32 devices in a mesh: shard: 4 (over x, core), ctx: 4 (over z), tp: 2 (over y).
Axes of the slice: x: 2, y: 2, z: 4, core: 2. Of those that a mesh axis runs over, the one named last changes fastest.
Arguments:
- tokens: bfloat16 [18432, 768], P(('shard', 'ctx')), may hold values from -6 to 6
- cotangent: bfloat16 [18432, 768], P(('shard', 'ctx')), may hold values from -6 to 6
- seq_lengths: int32 [4, 12], P('shard'), may hold values from 1 to 512, 4608 in all within a row
- dealing: int32 [4, 4608], P('shard'), may hold values from 0 to 4607, each once within a row
- query_weight: bfloat16 [768, 768], P('shard', 'tp'), may hold values from -0.21875 to 0.21875
- query_bias: bfloat16 [768], P('tp'), may hold values from -1.5 to 1.5
- key_weight: bfloat16 [768, 768], P('shard', 'tp'), may hold values from -0.21875 to 0.21875
- value_weight: bfloat16 [768, 768], P('shard', 'tp'), may hold values from -0.21875 to 0.21875
- value_bias: bfloat16 [768], P('tp'), may hold values from -0.14941406 to 0.14941406
- output_weight: bfloat16 [768, 768], P('tp', 'shard'), may hold values from -3.5 to 3.5
- output_bias: bfloat16 [768], replicated, may hold values from -2.5 to 2.5
- first_gain: bfloat16 [768], replicated, may hold values from 0.25 to 1.75
- first_shift: bfloat16 [768], replicated, may hold values from -1.5 to 1.5
- up_weight: bfloat16 [768, 3072], P('shard', 'tp'), may hold values from -0.21875 to 0.21875
- up_bias: bfloat16 [3072], P('tp'), may hold values from -2.5 to 2.5
- down_weight: bfloat16 [3072, 768], P('tp', 'shard'), may hold values from -0.109375 to 0.109375
- down_bias: bfloat16 [768], replicated, may hold values from -1.5 to 1.5
- second_gain: bfloat16 [768], replicated, may hold values from 0.25 to 1.75
- second_shift: bfloat16 [768], replicated, may hold values from -1.5 to 1.5
Outputs:
- layer_out: bfloat16 [18432, 768], P(('shard', 'ctx'))
- tokens_grad: bfloat16 [18432, 768], P(('shard', 'ctx'))
- query_weight_grad: float32 [768, 768], P('shard', 'tp')
- query_bias_grad: float32 [768], P('tp')
- key_weight_grad: float32 [768, 768], P('shard', 'tp')
- value_weight_grad: float32 [768, 768], P('shard', 'tp')
- value_bias_grad: float32 [768], P('tp')
- output_weight_grad: float32 [768, 768], P('tp', 'shard')
- output_bias_grad: float32 [768], replicated
- first_gain_grad: float32 [768], replicated
- first_shift_grad: float32 [768], replicated
- up_weight_grad: float32 [768, 3072], P('shard', 'tp')
- up_bias_grad: float32 [3072], P('tp')
- down_weight_grad: float32 [3072, 768], P('tp', 'shard')
- down_bias_grad: float32 [768], replicated
- second_gain_grad: float32 [768], replicated
- second_shift_grad: float32 [768], replicated
The draws below stay inside these ranges and needn't reach their ends.
Inputs may be any that keep to these rules, and one draw needn't show every extreme that they name: `seq_lengths`: each row holds 12 lengths that sum to 4608; the longest is exactly 512. `dealing`: each row is a permutation of the 4608 positions of its group.
All inputs are finite; a program needn't handle non-finite values.
Results may differ from the reference program's by a relative error of at most 0.02.
Values may be sent and summed in bfloat16 or wider, within the bound.
A program may use at most 128 MiB of HBM per device.

```python
import math
import jax
import jax.numpy as jnp
import numpy as np
from jax import lax

D = 768
FF = 3072
HEAD = 64
HEADS = 12
SEQ_MAX = 512
NSEQ = 12
GROUP = 4608
TOKENS = 18432
N_SHARD = 4


def levels(key, shape, split, least, high):
    loudness, own = 1.0, jax.random.fold_in(key, 6)
    for position, parts in split:
        draws = jnp.exp(jax.random.uniform(jax.random.fold_in(own, position), (parts,), jnp.float32, least / len(split), high / len(split)))
        loudness = loudness * jnp.repeat(draws, shape[position] // parts).reshape([-1 if axis == position else 1 for axis in range(len(shape))])
    return loudness


def profile(number_of, total, most, slope):
    portions = [(1 << 20) // math.isqrt(grade ** slope) + 1 for grade in range(2, number_of + 1)]
    rest, given = total - most - (number_of - 1), [1] * (number_of - 1)
    while rest > 0:
        free = [i for i in range(number_of - 1) if given[i] < most]
        whole, budget = sum([portions[i] for i in free]), rest
        for i in free:
            more = min(most - given[i], max(1, budget * portions[i] // whole), rest)
            given[i] = given[i] + more
            rest = rest - more
    return np.array([most] + given)


def ragged(key, number_of, total, limit, skew):
    if number_of == 2:
        one = jax.random.randint(key, (), max(1, total - limit), min(limit, total - 1) + 1)
        return jnp.stack([one, total - one])
    tallies = jnp.asarray(profile(number_of, total, limit, skew), jnp.int32)
    twos = (number_of - 1) // 2
    giver, receiver = tallies[1:1 + 2 * twos:2], tallies[2:2 + 2 * twos:2]
    margin = jnp.minimum(giver - 1, limit - receiver)
    moved = jax.random.randint(jax.random.fold_in(key, 1), (twos,), 0, 1 << 20) % (margin + 1)
    tallies = tallies.at[1:1 + 2 * twos:2].set(giver - moved).at[2:2 + 2 * twos:2].set(receiver + moved)
    return tallies[jax.random.permutation(jax.random.fold_in(key, 2), number_of)]


def centred(stream_key, shape, deviation, bound, cuts=(), kind=jnp.bfloat16):
    values = deviation * jax.random.normal(stream_key, shape, jnp.float32)
    if cuts:
        values = values * levels(stream_key, shape, cuts, -0.22, 0.18)
    return jnp.clip(values, -bound, bound).astype(kind)


def setup_inputs(seed: int = 0) -> dict:
    key_list = jax.random.split(jax.random.key(seed), 20)
    return {
        "tokens": centred(key_list[0], (TOKENS, D), 1.0, 6.0, ((0, 16),)),
        "cotangent": centred(key_list[1], (TOKENS, D), 1.0, 6.0, ((0, 16),)),
        "seq_lengths": jax.vmap(lambda own: ragged(own, NSEQ, GROUP, SEQ_MAX, 2))(jax.random.split(key_list[2], N_SHARD)).reshape((N_SHARD, NSEQ)).astype(jnp.int32),
        "dealing": jax.vmap(lambda own: jax.random.permutation(own, GROUP))(jax.random.split(key_list[3], N_SHARD)).reshape((N_SHARD, GROUP)).astype(jnp.int32),
        "query_weight": centred(key_list[4], (D, D), D ** -0.5, 0.21875, ((0, 4), (1, 2))),
        "query_bias": centred(key_list[5], (D,), 0.3, 1.5, ((0, 2),)),
        "key_weight": centred(key_list[6], (D, D), D ** -0.5, 0.21875, ((0, 4), (1, 2))),
        "value_weight": centred(key_list[7], (D, D), D ** -0.5, 0.21875, ((0, 4), (1, 2))),
        "value_bias": centred(key_list[8], (D,), 0.03, 0.14941406, ((0, 2),)),
        "output_weight": centred(key_list[9], (D, D), (max(D // 256, 1)) ** -0.5, 3.5, ((0, 2), (1, 4))),
        "output_bias": centred(key_list[10], (D,), 0.5, 2.5),
        "first_gain": jnp.clip(1.0 + 0.15 * jax.random.normal(key_list[11], (D,), jnp.float32), 0.25, 1.75).astype(jnp.bfloat16),
        "first_shift": centred(key_list[12], (D,), 0.3, 1.5),
        "up_weight": centred(key_list[13], (D, FF), D ** -0.5, 0.21875, ((0, 4), (1, 2))),
        "up_bias": centred(key_list[14], (FF,), 0.5, 2.5, ((0, 2),)),
        "down_weight": centred(key_list[15], (FF, D), FF ** -0.5, 0.109375, ((0, 2), (1, 4))),
        "down_bias": centred(key_list[16], (D,), 0.3, 1.5),
        "second_gain": jnp.clip(1.0 + 0.15 * jax.random.normal(key_list[17], (D,), jnp.float32), 0.25, 1.75).astype(jnp.bfloat16),
        "second_shift": centred(key_list[18], (D,), 0.3, 1.5),
    }


@jax.custom_vjp
def low(v):
    return lax.optimization_barrier(v.astype(jnp.bfloat16)).astype(jnp.float32)

@jax.custom_vjp
def low_back(v):
    return v

def low_keep(v):
    return (low(v), None)

def low_pass(kept, grad):
    return (grad,)

def back_keep(v):
    return (v, None)

def back_low(kept, grad):
    return (low(grad),)
low.defvjp(low_keep, low_pass)
low_back.defvjp(back_keep, back_low)

def both_ways(values):
    return low(low_back(values))

def matmul(former, latter):
    return jnp.dot(former, latter, precision=lax.Precision.HIGHEST)

def layer_norm(values, norm_gain, norm_shift):
    centre = values - lax.optimization_barrier(jnp.mean(values, axis=-1, keepdims=True))
    spread = lax.optimization_barrier(jnp.mean(centre * centre, axis=-1, keepdims=True))
    return norm_gain * (centre * lax.rsqrt(spread + 1e-06)) + norm_shift

def attend_head(query_head, key_head, value_head, allowed):
    scores = jnp.where(allowed, low_back(0.125 * matmul(query_head, key_head.T)), -1000000000.0)
    weights = low(jax.nn.softmax(scores, axis=-1))
    return matmul(weights, value_head)
checked_head = jax.checkpoint(attend_head)

def split_heads(matrix):
    return matrix.reshape(matrix.shape[0], HEADS, HEAD).transpose(1, 0, 2)

def group_forward(inputs, query_weight, query_bias, key_weight, value_weight, value_bias, output_weight, output_bias, first_gain, first_shift, up_weight, up_bias, down_weight, down_bias, second_gain, second_shift, allowed):
    queries = low(low_back(matmul(inputs, query_weight)) + query_bias)
    key_rows = low(low_back(matmul(inputs, key_weight)))
    value_rows = low(low_back(matmul(inputs, value_weight)) + value_bias)

    def one_head(packed):
        return checked_head(packed[0], packed[1], packed[2], allowed)
    head_out = lax.map(one_head, (split_heads(queries), split_heads(key_rows), split_heads(value_rows)))
    attended = both_ways(head_out.transpose(1, 0, 2).reshape(inputs.shape[0], HEADS * HEAD))
    attn_out = low_back(matmul(attended, output_weight)) + output_bias
    hidden_one = layer_norm(inputs + attn_out, first_gain, first_shift)
    hidden_low = low(hidden_one)
    pre_act = low_back(matmul(hidden_low, up_weight)) + up_bias
    act_low = low(jax.nn.gelu(pre_act, approximate=False))
    ffn_out = low_back(matmul(act_low, down_weight)) + down_bias
    return layer_norm(hidden_one + ffn_out, second_gain, second_shift)

def reference(tokens, cotangent, seq_lengths, dealing, query_weight, query_bias, key_weight, value_weight, value_bias, output_weight, output_bias, first_gain, first_shift, up_weight, up_bias, down_weight, down_bias, second_gain, second_shift):
    params = tuple((weight_arg.astype(jnp.float32) for weight_arg in (query_weight, query_bias, key_weight, value_weight, value_bias, output_weight, output_bias, first_gain, first_shift, up_weight, up_bias, down_weight, down_bias, second_gain, second_shift)))
    positions = jnp.arange(GROUP, dtype=jnp.int32)
    groups_in = tokens.reshape(-1, GROUP, D)
    groups_back = cotangent.reshape(-1, GROUP, D)

    def one_group(totals, packed):
        rows_in, rows_back, lengths, dealt_order = packed
        dealt_order = dealt_order.astype(jnp.int32)
        seq_ends = jnp.cumsum(lengths.astype(jnp.int32)).astype(jnp.int32)
        segment = lax.optimization_barrier(jnp.sum((positions[:, None] >= seq_ends[None, :-1]).astype(jnp.int32), axis=1))
        dealt_seg = jnp.take(segment, dealt_order)
        allowed = dealt_seg[:, None] == dealt_seg[None, :]
        inputs = jnp.take(rows_in, dealt_order, axis=0).astype(jnp.float32)
        grad_out = rows_back.astype(jnp.float32)

        def forward(inputs, *weights):
            return group_forward(inputs, *weights, allowed)
        result, pullback = jax.vjp(forward, inputs, *params)
        grads = pullback(grad_out)
        totals = tuple((running + gradient for running, gradient in zip(totals, grads[1:])))
        return (totals, (result.astype(jnp.bfloat16), grads[0].astype(jnp.bfloat16)))
    initial = tuple((jnp.zeros_like(weight_arg) for weight_arg in params))
    totals, outputs = lax.scan(one_group, initial, (groups_in, groups_back, seq_lengths, dealing))
    layer_out = outputs[0].reshape(-1, D)
    tokens_grad = outputs[1].reshape(-1, D)
    return (layer_out, tokens_grad, totals[0], totals[1], totals[2], totals[3], totals[4], totals[5], totals[6], totals[7], totals[8], totals[9], totals[10], totals[11], totals[12], totals[13], totals[14])
```

```python
import functools

import jax
import jax.numpy as jnp
from jax import lax
from jax.experimental import pallas as pl
from jax.experimental.pallas import tpu as pltpu
from jax.sharding import PartitionSpec as P

HEAD = 64
HALO = 512
HALF_ROOT = 0.7071067811865476
DENSITY = 0.3989422804014327
NEG_FILL = -1000000000.0
BF = jnp.bfloat16
F32 = jnp.float32
BLOCK = 256
VMEM_LIMIT = 56 * 1024 * 1024


def matmul(former, latter):
    return jnp.dot(former, latter, preferred_element_type=F32)


def matmul_first(former, latter):
    return lax.dot_general(former, latter, (((0,), (0,)), ((), ())), preferred_element_type=F32)


def matmul_second(former, latter):
    return lax.dot_general(former, latter, (((1,), (1,)), ((), ())), preferred_element_type=F32)


def norm_forward(values, norm_gain, norm_shift):
    centre = values - jnp.mean(values, axis=1, keepdims=True)
    spread = jnp.mean(centre * centre, axis=1, keepdims=True)
    inverse = lax.rsqrt(spread + 1e-06)
    normed = centre * inverse
    return (norm_gain * normed + norm_shift, normed, inverse)


def norm_backward(gradient, normed, inverse, norm_gain):
    scaled = gradient * norm_gain
    bracket = (
        scaled
        - jnp.mean(scaled, axis=1, keepdims=True)
        - normed * jnp.mean(scaled * normed, axis=1, keepdims=True)
    )
    return inverse * bracket


def low_lanes(rows):
    return lax.broadcasted_iota(jnp.int32, (rows, 128), 1) < HEAD


def stacked(pair):
    low = low_lanes(pair.shape[0])
    zero = jnp.zeros_like(pair)
    return jnp.concatenate([jnp.where(low, pair, zero), jnp.where(low, zero, pair)], axis=0)


def unstacked(both):
    rows = both.shape[0] // 2
    return jnp.where(low_lanes(rows), both[:rows], both[rows:])


def columns(ref_value, head, rows):
    return jnp.concatenate([ref_value[:, 2 * head : 2 * head + 1], ref_value[:, 2 * head + 1 : 2 * head + 2]], axis=0)


def bias_of(own_seg, other_seg):
    return jnp.where(own_seg == other_seg, 0.0, NEG_FILL)


def forward_kernel(dim, tile, bounds, qkv, seg_col, seg_row, out, logsum, query_st, bias_ref, acc, top, total):
    pairs = dim // 128
    own = out.shape[0]

    def one_tile(i, carry):
        first = pl.multiple_of(i * tile, tile)
        rows = pl.ds(pl.multiple_of(HALO + first, 64), tile)
        seg_here = seg_col[rows, :]
        for p in range(pairs):
            query_st[p] = stacked(qkv[rows, p * 128 : p * 128 + 128])
        acc[...] = jnp.zeros_like(acc)
        total[...] = jnp.zeros_like(total)
        top[...] = jnp.full_like(top, 2 * NEG_FILL)

        def one_block(j, inner):
            start = pl.multiple_of(j * BLOCK, BLOCK)
            bias = bias_of(seg_here, seg_row[:, pl.ds(start, BLOCK)])
            bias_ref[...] = jnp.concatenate([bias, bias], axis=0)
            for p in range(pairs):
                key = qkv[pl.ds(start, BLOCK), dim + p * 128 : dim + p * 128 + 128]
                value = qkv[pl.ds(start, BLOCK), 2 * dim + p * 128 : 2 * dim + p * 128 + 128]
                scores = matmul_second(query_st[p], key) + bias_ref[...]
                old = top[p]
                new = jnp.maximum(old, jnp.max(scores, axis=1, keepdims=True))
                keep = jnp.exp(old - new)
                raised = jnp.exp(scores - new[:, :1])
                total[p] = keep * total[p] + jnp.sum(raised, axis=1, keepdims=True)
                acc[p] = keep * acc[p] + matmul(raised.astype(BF), value)
                top[p] = new
            return inner

        lax.fori_loop(bounds[i, 0], bounds[i, 1], one_block, 0)
        lane = lax.broadcasted_iota(jnp.int32, (tile, 128), 1)
        sums = jnp.zeros((tile, 128), F32)
        for p in range(pairs):
            whole = total[p]
            out[pl.ds(first, tile), p * 128 : p * 128 + 128] = unstacked(acc[p] / whole).astype(BF)
            lse = top[p] + jnp.log(whole)
            sums = jnp.where(lane == 2 * p, lse[:tile], sums)
            sums = jnp.where(lane == 2 * p + 1, lse[tile:], sums)
        logsum[pl.ds(first, tile), :] = sums
        return carry

    lax.fori_loop(0, own // tile, one_tile, 0)


def query_kernel(dim, tile, bounds, qkv, seg_col, seg_row, grad, logsum, delta, out, query_st, grad_st, bias_ref, acc):
    pairs = dim // 128
    own = out.shape[0]

    def one_tile(i, carry):
        first = pl.multiple_of(i * tile, tile)
        own_rows = pl.ds(first, tile)
        rows = pl.ds(pl.multiple_of(HALO + first, 64), tile)
        seg_here = seg_col[rows, :]
        for p in range(pairs):
            query_st[p] = stacked(qkv[rows, p * 128 : p * 128 + 128])
            grad_st[p] = stacked(grad[own_rows, p * 128 : p * 128 + 128])
        acc[...] = jnp.zeros_like(acc)

        def one_block(j, inner):
            start = pl.multiple_of(j * BLOCK, BLOCK)
            bias = bias_of(seg_here, seg_row[:, pl.ds(start, BLOCK)])
            bias_ref[...] = jnp.concatenate([bias, bias], axis=0)
            for p in range(pairs):
                key = qkv[pl.ds(start, BLOCK), dim + p * 128 : dim + p * 128 + 128]
                value = qkv[pl.ds(start, BLOCK), 2 * dim + p * 128 : 2 * dim + p * 128 + 128]
                scores = matmul_second(query_st[p], key) + bias_ref[...]
                probs = jnp.exp(scores - columns(logsum[own_rows, :], p, tile))
                grad_probs = matmul_second(grad_st[p], value)
                grad_scores = (probs * (grad_probs - columns(delta[own_rows, :], p, tile))).astype(BF)
                acc[p] += matmul(grad_scores, key)
            return inner

        lax.fori_loop(bounds[i, 0], bounds[i, 1], one_block, 0)
        for p in range(pairs):
            out[own_rows, p * 128 : p * 128 + 128] = 0.125 * unstacked(acc[p])
        return carry

    lax.fori_loop(0, own // tile, one_tile, 0)


def key_kernel(dim, tile, bounds, qkv, seg_col, seg_row, grad, logsum, delta, out, key_st, value_st, bias_ref, key_acc, value_acc):
    pairs = dim // 128
    own = out.shape[0]

    def one_tile(i, carry):
        first = pl.multiple_of(i * tile, tile)
        own_rows = pl.ds(first, tile)
        rows = pl.ds(pl.multiple_of(HALO + first, 64), tile)
        seg_here = seg_col[rows, :]
        for p in range(pairs):
            key_st[p] = stacked(qkv[rows, dim + p * 128 : dim + p * 128 + 128])
            value_st[p] = stacked(qkv[rows, 2 * dim + p * 128 : 2 * dim + p * 128 + 128])
        key_acc[...] = jnp.zeros_like(key_acc)
        value_acc[...] = jnp.zeros_like(value_acc)

        def one_block(j, inner):
            start = pl.multiple_of(j * BLOCK, BLOCK)
            there = pl.ds(start, BLOCK)
            bias_ref[...] = bias_of(seg_here, seg_row[:, there])
            for p in range(pairs):
                query = qkv[there, p * 128 : p * 128 + 128]
                grad_pair = grad[there, p * 128 : p * 128 + 128]
                scores = matmul_second(key_st[p], query)
                grad_probs = matmul_second(value_st[p], grad_pair)
                probs_all, grads_all = [], []
                for half in range(2):
                    head = 2 * p + half
                    lines = slice(half * tile, half * tile + tile)
                    probs = jnp.exp(scores[lines] + bias_ref[...] - logsum[head : head + 1, there])
                    grads_all.append((probs * (grad_probs[lines] - delta[head : head + 1, there])).astype(BF))
                    probs_all.append(probs.astype(BF))
                key_acc[p] += matmul(jnp.concatenate(grads_all, axis=0), query)
                value_acc[p] += matmul(jnp.concatenate(probs_all, axis=0), grad_pair)
            return inner

        lax.fori_loop(bounds[i, 0], bounds[i, 1], one_block, 0)
        for p in range(pairs):
            out[own_rows, p * 128 : p * 128 + 128] = unstacked(key_acc[p])
            out[own_rows, dim + p * 128 : dim + p * 128 + 128] = unstacked(value_acc[p])
        return carry

    lax.fori_loop(0, own // tile, one_tile, 0)


def vmem_call(kernel, arrays, bounds, outs, scratch, flops):
    spec = pl.BlockSpec(memory_space=pltpu.VMEM)
    return pl.pallas_call(
        kernel,
        out_shape=outs,
        in_specs=[pl.BlockSpec(memory_space=pltpu.SMEM)] + [spec] * len(arrays),
        out_specs=jax.tree.map(lambda leaf: spec, outs),
        scratch_shapes=scratch,
        compiler_params=pltpu.CompilerParams(vmem_limit_bytes=VMEM_LIMIT),
        cost_estimate=pl.CostEstimate(flops=flops, bytes_accessed=12000000, transcendentals=6000000),
    )(bounds, *arrays)


def attention_tile(own):
    for tile in (192, 128, 64, 32, 16):
        if own % tile == 0:
            return tile
    raise ValueError("rows")


def attention_forward(qkv, seg_col, seg_row, bounds, own, dim):
    tile = attention_tile(own)
    pairs = dim // 128
    return vmem_call(
        functools.partial(forward_kernel, dim, tile),
        (qkv, seg_col, seg_row),
        bounds,
        (jax.ShapeDtypeStruct((own, dim), BF), jax.ShapeDtypeStruct((own, 128), F32)),
        [
            pltpu.VMEM((pairs, 2 * tile, 128), BF),
            pltpu.VMEM((2 * tile, BLOCK), F32),
            pltpu.VMEM((pairs, 2 * tile, 128), F32),
            pltpu.VMEM((pairs, 2 * tile, 128), F32),
            pltpu.VMEM((pairs, 2 * tile, 128), F32),
        ],
        10_000_000_000,
    )


def attention_query(qkv, seg_col, seg_row, bounds, grad, logsum, delta, dim):
    own = grad.shape[0]
    tile = attention_tile(own)
    pairs = dim // 128
    return vmem_call(
        functools.partial(query_kernel, dim, tile),
        (qkv, seg_col, seg_row, grad, logsum, delta),
        bounds,
        jax.ShapeDtypeStruct((own, dim), F32),
        [
            pltpu.VMEM((pairs, 2 * tile, 128), BF),
            pltpu.VMEM((pairs, 2 * tile, 128), BF),
            pltpu.VMEM((2 * tile, BLOCK), F32),
            pltpu.VMEM((pairs, 2 * tile, 128), F32),
        ],
        15_000_000_000,
    )


def attention_key(qkv, seg_col, seg_row, bounds, grad_win, logsum_rows, delta_rows, own, dim):
    tile = attention_tile(own)
    pairs = dim // 128
    return vmem_call(
        functools.partial(key_kernel, dim, tile),
        (qkv, seg_col, seg_row, grad_win, logsum_rows, delta_rows),
        bounds,
        jax.ShapeDtypeStruct((own, 2 * dim), F32),
        [
            pltpu.VMEM((pairs, 2 * tile, 128), BF),
            pltpu.VMEM((pairs, 2 * tile, 128), BF),
            pltpu.VMEM((tile, BLOCK), F32),
            pltpu.VMEM((pairs, 2 * tile, 128), F32),
            pltpu.VMEM((pairs, 2 * tile, 128), F32),
        ],
        20_000_000_000,
    )


def rows_to_slots(values, dealt, place_z, place_y):
    own, dim = values.shape
    half = dim // 2
    keep = lax.dynamic_slice_in_dim(values, place_y * half, half, axis=1)
    send = lax.dynamic_slice_in_dim(values, (1 - place_y) * half, half, axis=1)
    other = lax.ppermute(send, "tp", [(0, 1), (1, 0)])
    first = jnp.where(place_y == 0, keep, other)
    second = jnp.where(place_y == 0, other, keep)
    block = jnp.concatenate([first, second], axis=0)
    everything = lax.all_gather(block, "ctx", axis=0, tiled=True)
    slots = 2 * own
    mine = lax.dynamic_slice_in_dim(dealt, place_z * slots, slots)
    picked = jnp.take(everything, mine, axis=0, mode="clip")
    other_columns = lax.ppermute(picked, "tp", [(0, 1), (1, 0)])
    return jnp.concatenate(
        [jnp.where(place_y == 0, picked, other_columns), jnp.where(place_y == 0, other_columns, picked)], axis=1
    )


def slots_to_rows(values, dealt, place_z, place_y):
    slots, dim = values.shape
    half, own = dim // 2, slots // 2
    block = lax.dynamic_slice_in_dim(values, place_y * half, half, axis=1)
    everything = lax.all_gather(block, "ctx", axis=0, tiled=True)
    wanted = place_z * slots + lax.broadcasted_iota(jnp.int32, (slots, 1), 0)
    chosen = (wanted == dealt[None, :]).astype(BF)
    picked = matmul(chosen, everything).astype(BF)
    keep = lax.dynamic_slice_in_dim(picked, place_y * own, own, axis=0)
    send = lax.dynamic_slice_in_dim(picked, (1 - place_y) * own, own, axis=0)
    other = lax.ppermute(send, "tp", [(0, 1), (1, 0)])
    return jnp.concatenate([jnp.where(place_y == 0, keep, other), jnp.where(place_y == 0, other, keep)], axis=1)


def per_device(
    tokens,
    cotangent,
    seq_lengths,
    dealing,
    query_weight,
    query_bias,
    key_weight,
    value_weight,
    value_bias,
    output_weight,
    output_bias,
    first_gain,
    first_shift,
    up_weight,
    up_bias,
    down_weight,
    down_bias,
    second_gain,
    second_shift,
):
    rows, dim = tokens.shape
    ctx_size, tp_size = lax.axis_size("ctx"), lax.axis_size("tp")
    group_rows = rows * ctx_size
    own = rows // tp_size
    place_z, place_y = lax.axis_index("ctx"), lax.axis_index("tp")
    window = HALO + own + HALO
    padded = -(-window // BLOCK) * BLOCK
    heads = dim // HEAD
    dealt = dealing[0]

    lengths = seq_lengths[0]
    number = lengths.shape[0]
    upto = jnp.arange(number)[:, None] >= jnp.arange(number)[None, :]
    ends = jnp.sum(jnp.where(upto, lengths[None, :], 0), axis=1)
    starts = ends - lengths
    first_row = place_z * rows + place_y * own
    index = jnp.arange(padded, dtype=jnp.int32)
    position = first_row - HALO + index
    valid = (position >= 0) & (position < group_rows) & (index < window)
    segment = jnp.sum((position[:, None] >= ends[None, :-1]).astype(jnp.int32), axis=1)
    segment = jnp.where(valid, segment, -1)
    seg_row, seg_col = segment[None, :], segment[:, None]
    tile = attention_tile(own)
    tile_first = first_row + tile * jnp.arange(own // tile, dtype=jnp.int32)
    tile_last = tile_first + tile - 1
    begin = jnp.max(jnp.where(starts[None, :] <= tile_first[:, None], starts[None, :], 0), axis=1)
    finish = jnp.min(jnp.where(ends[None, :] > tile_last[:, None], ends[None, :], group_rows), axis=1)
    shift = HALO - first_row
    bounds = jnp.stack([(begin + shift) // BLOCK, (finish + shift + BLOCK - 1) // BLOCK], axis=1).astype(jnp.int32)

    def whole(weight, shard_axis):
        once = lax.all_gather(weight, "shard", axis=shard_axis, tiled=True)
        return lax.all_gather(once, "tp", axis=1 - shard_axis, tiled=True)

    edge = jnp.where(place_y == 0, tokens[rows - HALO :], tokens[:HALO])
    hops = [(2 * z, 2 * z + 2) for z in range(ctx_size - 1)] + [(2 * z + 1, 2 * z - 1) for z in range(1, ctx_size)]
    arrived = lax.ppermute(edge, ("ctx", "tp"), hops)
    x_window = jnp.where(
        place_y == 0,
        jnp.concatenate([arrived, tokens[: own + HALO]], axis=0),
        jnp.concatenate([tokens[own - HALO :], arrived], axis=0),
    )
    x_window = jnp.pad(x_window, ((0, padded - window), (0, 0)))
    inputs = lax.dynamic_slice_in_dim(tokens, place_y * own, own, axis=0)

    wide_qkv = jnp.concatenate([whole(query_weight, 0), whole(key_weight, 0), whole(value_weight, 0)], axis=1)
    wide_output = whole(output_weight, 1)
    wide_up = whole(up_weight, 0)
    wide_down = whole(down_weight, 1)
    whole_bias = lax.all_gather(jnp.stack([query_bias, value_bias]), "tp", axis=1, tiled=True).astype(F32)
    whole_up_bias = lax.all_gather(up_bias, "tp", axis=0, tiled=True).astype(F32)
    output_bias = output_bias.astype(F32)
    first_gain = first_gain.astype(F32)
    first_shift = first_shift.astype(F32)
    down_bias = down_bias.astype(F32)
    second_gain = second_gain.astype(F32)
    second_shift = second_shift.astype(F32)

    raw = matmul(x_window, wide_qkv)
    qkv = jnp.concatenate(
        [
            ((raw[:, :dim] + whole_bias[0]).astype(BF) * BF(0.125)),
            raw[:, dim : 2 * dim].astype(BF),
            (raw[:, 2 * dim :] + whole_bias[1]).astype(BF),
        ],
        axis=1,
    )
    attended, logsum = attention_forward(qkv, seg_col, seg_row, bounds, own, dim)
    grad_out = slots_to_rows(cotangent, dealt, place_z, place_y).astype(F32)
    hidden_one, normed_one, inverse_one = norm_forward(
        inputs.astype(F32) + matmul(attended, wide_output) + output_bias, first_gain, first_shift
    )
    hidden_low = hidden_one.astype(BF)
    pre_act = matmul(hidden_low, wide_up) + whole_up_bias
    erf_part = 0.5 * (1.0 + jax.scipy.special.erf(pre_act * HALF_ROOT))
    act_low = (pre_act * erf_part).astype(BF)
    layer_value, normed_two, inverse_two = norm_forward(
        hidden_one + matmul(act_low, wide_down) + down_bias, second_gain, second_shift
    )
    layer_out = rows_to_slots(layer_value.astype(BF), dealt, place_z, place_y)

    second_shift_grad = jnp.sum(grad_out, axis=0)
    second_gain_grad = jnp.sum(grad_out * normed_two, axis=0)
    grad_second = norm_backward(grad_out, normed_two, inverse_two, second_gain)
    down_bias_grad = jnp.sum(grad_second, axis=0)
    second_low = grad_second.astype(BF)
    slope = erf_part + pre_act * DENSITY * jnp.exp(-0.5 * pre_act * pre_act)
    grad_pre = matmul_second(second_low, wide_down) * slope
    up_bias_grad = jnp.sum(grad_pre, axis=0)
    pre_low = grad_pre.astype(BF)
    grad_hidden = grad_second + matmul_second(pre_low, wide_up)
    first_shift_grad = jnp.sum(grad_hidden, axis=0)
    first_gain_grad = jnp.sum(grad_hidden * normed_one, axis=0)
    grad_first = norm_backward(grad_hidden, normed_one, inverse_one, first_gain)
    output_bias_grad = jnp.sum(grad_first, axis=0)
    first_low = grad_first.astype(BF)
    attended_grad = matmul_second(first_low, wide_output).astype(BF)
    delta = jnp.sum(
        (attended_grad.astype(F32) * attended.astype(F32)).reshape(own, heads, HEAD), axis=2
    )
    delta = jnp.pad(delta, ((0, 0), (0, 128 - heads)))
    up_hops = [(i, i + 1) for i in range(ctx_size * tp_size - 1)]
    down_hops = [(i + 1, i) for i in range(ctx_size * tp_size - 1)]
    both = ("ctx", "tp")
    stats = jnp.concatenate([logsum[:, :16], delta[:, :16]], axis=1).T
    grad_win = jnp.concatenate(
        [
            lax.ppermute(attended_grad[own - HALO :], both, up_hops),
            attended_grad,
            lax.ppermute(attended_grad[:HALO], both, down_hops),
            jnp.zeros((padded - window, dim), BF),
        ],
        axis=0,
    )
    stats_win = jnp.concatenate(
        [
            lax.ppermute(stats[:, own - HALO :], both, up_hops),
            stats,
            lax.ppermute(stats[:, :HALO], both, down_hops),
            jnp.zeros((stats.shape[0], padded - window), F32),
        ],
        axis=1,
    )
    query_grad = attention_query(qkv, seg_col, seg_row, bounds, attended_grad, logsum, delta, dim)
    pair_grad = attention_key(
        qkv, seg_col, seg_row, bounds, grad_win, stats_win[:16], stats_win[16:], own, dim
    )
    query_bias_grad = jnp.sum(query_grad, axis=0)
    value_bias_grad = jnp.sum(pair_grad[:, dim:], axis=0)
    qkv_low = jnp.concatenate([query_grad.astype(BF), pair_grad.astype(BF)], axis=1)
    tokens_grad = (grad_first + matmul_second(qkv_low, wide_qkv)).astype(BF)
    tokens_grad = rows_to_slots(tokens_grad, dealt, place_z, place_y)

    def owned(full, shard_axis):
        part = lax.psum_scatter(full.astype(BF), "tp", scatter_dimension=1 - shard_axis, tiled=True)
        part = lax.psum_scatter(part, "shard", scatter_dimension=shard_axis, tiled=True)
        return lax.psum(part, "ctx").astype(F32)

    down_full = matmul_first(act_low, second_low)
    up_full = matmul_first(hidden_low, pre_low)
    output_full = matmul_first(attended, first_low)
    qkv_full = matmul_first(inputs, qkv_low)
    small = lax.psum(
        jnp.concatenate(
            [
                query_bias_grad,
                value_bias_grad,
                up_bias_grad,
                output_bias_grad,
                first_gain_grad,
                first_shift_grad,
                down_bias_grad,
                second_gain_grad,
                second_shift_grad,
            ]
        ),
        ("shard", "ctx", "tp"),
    )
    hidden = up_bias_grad.shape[0]
    sizes = [dim, dim, hidden] + [dim] * 6
    offsets = [sum(sizes[:i]) for i in range(len(sizes))]
    parts = [small[o : o + s] for o, s in zip(offsets, sizes)]

    def by_tp(vector):
        part = vector.shape[0] // tp_size
        return lax.dynamic_slice_in_dim(vector, place_y * part, part)

    return (
        layer_out,
        tokens_grad,
        owned(qkv_full[:, :dim], 0),
        by_tp(parts[0]),
        owned(qkv_full[:, dim : 2 * dim], 0),
        owned(qkv_full[:, 2 * dim :], 0),
        by_tp(parts[1]),
        owned(output_full, 1),
        parts[3],
        parts[4],
        parts[5],
        owned(up_full, 0),
        by_tp(parts[2]),
        owned(down_full, 1),
        parts[6],
        parts[7],
        parts[8],
    )


def solution(mesh):
    return jax.shard_map(
        per_device,
        mesh=mesh,
        in_specs=(
            P(("shard", "ctx"), None),
            P(("shard", "ctx"), None),
            P("shard", None),
            P("shard", None),
            P("shard", "tp"),
            P("tp"),
            P("shard", "tp"),
            P("shard", "tp"),
            P("tp"),
            P("tp", "shard"),
            P(),
            P(),
            P(),
            P("shard", "tp"),
            P("tp"),
            P("tp", "shard"),
            P(),
            P(),
            P(),
        ),
        out_specs=(
            P(("shard", "ctx"), None),
            P(("shard", "ctx"), None),
            P("shard", "tp"),
            P("tp"),
            P("shard", "tp"),
            P("shard", "tp"),
            P("tp"),
            P("tp", "shard"),
            P(),
            P(),
            P(),
            P("shard", "tp"),
            P("tp"),
            P("tp", "shard"),
            P(),
            P(),
            P(),
        ),
        check_vma=False,
    )
```

```python
import functools

import jax
import jax.numpy as jnp
from jax import lax
from jax.experimental import pallas as pl
from jax.experimental.pallas import tpu as pltpu
from jax.sharding import PartitionSpec as P

HEAD = 64
HALO = 512
HALF_ROOT = 0.7071067811865476
DENSITY = 0.3989422804014327
NEG_FILL = -1000000000.0
BF = jnp.bfloat16
F32 = jnp.float32
BLOCK = 256
VMEM_LIMIT = 56 * 1024 * 1024


def matmul(former, latter):
    return jnp.dot(former, latter, preferred_element_type=F32)


def matmul_first(former, latter):
    return lax.dot_general(former, latter, (((0,), (0,)), ((), ())), preferred_element_type=F32)


def matmul_second(former, latter):
    return lax.dot_general(former, latter, (((1,), (1,)), ((), ())), preferred_element_type=F32)


def norm_forward(values, norm_gain, norm_shift):
    centre = values - jnp.mean(values, axis=1, keepdims=True)
    spread = jnp.mean(centre * centre, axis=1, keepdims=True)
    inverse = lax.rsqrt(spread + 1e-06)
    normed = centre * inverse
    return (norm_gain * normed + norm_shift, normed, inverse)


def norm_backward(gradient, normed, inverse, norm_gain):
    scaled = gradient * norm_gain
    bracket = (
        scaled
        - jnp.mean(scaled, axis=1, keepdims=True)
        - normed * jnp.mean(scaled * normed, axis=1, keepdims=True)
    )
    return inverse * bracket


def places(pair, dim):
    half, inner = divmod(pair, dim // 256)
    base = half * (3 * dim // 2) + inner * 128
    return base, base + dim // 2, base + dim


def take(qkv, rows, pair, dim, which):
    first = places(pair, dim)[which]
    return qkv[rows, first : first + 128]


def low_lanes(rows):
    return lax.broadcasted_iota(jnp.int32, (rows, 128), 1) < HEAD


def stacked(pair):
    low = low_lanes(pair.shape[0])
    zero = jnp.zeros_like(pair)
    return jnp.concatenate([jnp.where(low, pair, zero), jnp.where(low, zero, pair)], axis=0)


def unstacked(both):
    rows = both.shape[0] // 2
    return jnp.where(low_lanes(rows), both[:rows], both[rows:])


def columns(ref_value, head, rows):
    return jnp.concatenate([ref_value[:, 2 * head : 2 * head + 1], ref_value[:, 2 * head + 1 : 2 * head + 2]], axis=0)


def bias_of(own_seg, other_seg):
    return jnp.where(own_seg == other_seg, 0.0, NEG_FILL)


def forward_kernel(dim, tile, bounds, qkv, seg_col, seg_row, out, logsum, query_st, bias_ref, acc, top, total):
    pairs = dim // 128
    own = out.shape[0]

    def one_tile(i, carry):
        first = pl.multiple_of(i * tile, tile)
        rows = pl.ds(pl.multiple_of(HALO + first, 64), tile)
        seg_here = seg_col[rows, :]
        for p in range(pairs):
            query_st[p] = stacked(take(qkv, rows, p, dim, 0))
        acc[...] = jnp.zeros_like(acc)
        total[...] = jnp.zeros_like(total)
        top[...] = jnp.full_like(top, 2 * NEG_FILL)

        def one_block(j, inner):
            start = pl.multiple_of(j * BLOCK, BLOCK)
            bias = bias_of(seg_here, seg_row[:, pl.ds(start, BLOCK)])
            bias_ref[...] = jnp.concatenate([bias, bias], axis=0)
            for p in range(pairs):
                key = take(qkv, pl.ds(start, BLOCK), p, dim, 1)
                value = take(qkv, pl.ds(start, BLOCK), p, dim, 2)
                scores = matmul_second(query_st[p], key) + bias_ref[...]
                old = top[p]
                new = jnp.maximum(old, jnp.max(scores, axis=1, keepdims=True))
                keep = jnp.exp(old - new)
                raised = jnp.exp(scores - new[:, :1])
                total[p] = keep * total[p] + jnp.sum(raised, axis=1, keepdims=True)
                acc[p] = keep * acc[p] + matmul(raised.astype(BF), value)
                top[p] = new
            return inner

        lax.fori_loop(bounds[i, 0], bounds[i, 1], one_block, 0)
        lane = lax.broadcasted_iota(jnp.int32, (tile, 128), 1)
        sums = jnp.zeros((tile, 128), F32)
        for p in range(pairs):
            whole = total[p]
            out[pl.ds(first, tile), p * 128 : p * 128 + 128] = unstacked(acc[p] / whole).astype(BF)
            lse = top[p] + jnp.log(whole)
            sums = jnp.where(lane == 2 * p, lse[:tile], sums)
            sums = jnp.where(lane == 2 * p + 1, lse[tile:], sums)
        logsum[pl.ds(first, tile), :] = sums
        return carry

    lax.fori_loop(0, own // tile, one_tile, 0)


def query_kernel(dim, tile, bounds, qkv, seg_col, seg_row, grad, logsum, delta, out, sums, query_st, grad_st, bias_ref, acc):
    pairs = dim // 128
    own = out.shape[0]

    def one_tile(i, carry):
        first = pl.multiple_of(i * tile, tile)
        own_rows = pl.ds(first, tile)
        rows = pl.ds(pl.multiple_of(HALO + first, 64), tile)
        seg_here = seg_col[rows, :]
        for p in range(pairs):
            query_st[p] = stacked(take(qkv, rows, p, dim, 0))
            grad_st[p] = stacked(grad[own_rows, p * 128 : p * 128 + 128])
        acc[...] = jnp.zeros_like(acc)

        def one_block(j, inner):
            start = pl.multiple_of(j * BLOCK, BLOCK)
            bias = bias_of(seg_here, seg_row[:, pl.ds(start, BLOCK)])
            bias_ref[...] = jnp.concatenate([bias, bias], axis=0)
            for p in range(pairs):
                key = take(qkv, pl.ds(start, BLOCK), p, dim, 1)
                value = take(qkv, pl.ds(start, BLOCK), p, dim, 2)
                scores = matmul_second(query_st[p], key) + bias_ref[...]
                probs = jnp.exp(scores - columns(logsum[own_rows, :], p, tile))
                grad_probs = matmul_second(grad_st[p], value)
                grad_scores = (probs * (grad_probs - columns(delta[own_rows, :], p, tile))).astype(BF)
                acc[p] += matmul(grad_scores, key)
            return inner

        lax.fori_loop(bounds[i, 0], bounds[i, 1], one_block, 0)
        for p in range(pairs):
            part = 0.125 * unstacked(acc[p])
            out[own_rows, p * 128 : p * 128 + 128] = part.astype(BF)
            sums[:, p * 128 : p * 128 + 128] += jnp.sum(part, axis=0, keepdims=True)
        return carry

    sums[...] = jnp.zeros_like(sums)
    lax.fori_loop(0, own // tile, one_tile, 0)


def key_kernel(dim, tile, bounds, qkv, seg_col, seg_row, grad, logsum, delta, query_low, out, sums, key_st, value_st, bias_ref, key_acc, value_acc):
    pairs = dim // 128
    own = out.shape[0]

    def one_tile(i, carry):
        first = pl.multiple_of(i * tile, tile)
        own_rows = pl.ds(first, tile)
        rows = pl.ds(pl.multiple_of(HALO + first, 64), tile)
        seg_here = seg_col[rows, :]
        for p in range(pairs):
            key_st[p] = stacked(take(qkv, rows, p, dim, 1))
            value_st[p] = stacked(take(qkv, rows, p, dim, 2))
        key_acc[...] = jnp.zeros_like(key_acc)
        value_acc[...] = jnp.zeros_like(value_acc)

        def one_block(j, inner):
            start = pl.multiple_of(j * BLOCK, BLOCK)
            there = pl.ds(start, BLOCK)
            bias_ref[...] = bias_of(seg_here, seg_row[:, there])
            for p in range(pairs):
                query = take(qkv, there, p, dim, 0)
                grad_pair = grad[there, p * 128 : p * 128 + 128]
                scores = matmul_second(key_st[p], query)
                grad_probs = matmul_second(value_st[p], grad_pair)
                probs_all, grads_all = [], []
                for half in range(2):
                    head = 2 * p + half
                    lines = slice(half * tile, half * tile + tile)
                    probs = jnp.exp(scores[lines] + bias_ref[...] - logsum[head : head + 1, there])
                    grads_all.append((probs * (grad_probs[lines] - delta[head : head + 1, there])).astype(BF))
                    probs_all.append(probs.astype(BF))
                key_acc[p] += matmul(jnp.concatenate(grads_all, axis=0), query)
                value_acc[p] += matmul(jnp.concatenate(probs_all, axis=0), grad_pair)
            return inner

        lax.fori_loop(bounds[i, 0], bounds[i, 1], one_block, 0)
        for p in range(pairs):
            at_query, at_key, at_value = places(p, dim)
            out[own_rows, at_query : at_query + 128] = query_low[own_rows, p * 128 : p * 128 + 128]
            out[own_rows, at_key : at_key + 128] = unstacked(key_acc[p]).astype(BF)
            part = unstacked(value_acc[p])
            out[own_rows, at_value : at_value + 128] = part.astype(BF)
            sums[:, p * 128 : p * 128 + 128] += jnp.sum(part, axis=0, keepdims=True)
        return carry

    sums[...] = jnp.zeros_like(sums)
    lax.fori_loop(0, own // tile, one_tile, 0)


def vmem_call(kernel, arrays, bounds, outs, scratch, flops):
    spec = pl.BlockSpec(memory_space=pltpu.VMEM)
    return pl.pallas_call(
        kernel,
        out_shape=outs,
        in_specs=[pl.BlockSpec(memory_space=pltpu.SMEM)] + [spec] * len(arrays),
        out_specs=jax.tree.map(lambda leaf: spec, outs),
        scratch_shapes=scratch,
        compiler_params=pltpu.CompilerParams(vmem_limit_bytes=VMEM_LIMIT),
        cost_estimate=pl.CostEstimate(flops=flops, bytes_accessed=12000000, transcendentals=6000000),
    )(bounds, *arrays)


def attention_tile(own):
    for tile in (192, 128, 64, 32, 16):
        if own % tile == 0:
            return tile
    raise ValueError("rows")


def attention_forward(qkv, seg_col, seg_row, bounds, own, dim):
    tile = attention_tile(own)
    pairs = dim // 128
    return vmem_call(
        functools.partial(forward_kernel, dim, tile),
        (qkv, seg_col, seg_row),
        bounds,
        (jax.ShapeDtypeStruct((own, dim), BF), jax.ShapeDtypeStruct((own, 128), F32)),
        [
            pltpu.VMEM((pairs, 2 * tile, 128), BF),
            pltpu.VMEM((2 * tile, BLOCK), F32),
            pltpu.VMEM((pairs, 2 * tile, 128), F32),
            pltpu.VMEM((pairs, 2 * tile, 128), F32),
            pltpu.VMEM((pairs, 2 * tile, 128), F32),
        ],
        10_000_000_000,
    )


def attention_query(qkv, seg_col, seg_row, bounds, grad, logsum, delta, dim):
    own = grad.shape[0]
    tile = attention_tile(own)
    pairs = dim // 128
    return vmem_call(
        functools.partial(query_kernel, dim, tile),
        (qkv, seg_col, seg_row, grad, logsum, delta),
        bounds,
        (jax.ShapeDtypeStruct((own, dim), BF), jax.ShapeDtypeStruct((1, dim), F32)),
        [
            pltpu.VMEM((pairs, 2 * tile, 128), BF),
            pltpu.VMEM((pairs, 2 * tile, 128), BF),
            pltpu.VMEM((2 * tile, BLOCK), F32),
            pltpu.VMEM((pairs, 2 * tile, 128), F32),
        ],
        15_000_000_000,
    )


def attention_key(qkv, seg_col, seg_row, bounds, grad_win, logsum_rows, delta_rows, query_low, own, dim):
    tile = attention_tile(own)
    pairs = dim // 128
    return vmem_call(
        functools.partial(key_kernel, dim, tile),
        (qkv, seg_col, seg_row, grad_win, logsum_rows, delta_rows, query_low),
        bounds,
        (jax.ShapeDtypeStruct((own, 3 * dim), BF), jax.ShapeDtypeStruct((1, dim), F32)),
        [
            pltpu.VMEM((pairs, 2 * tile, 128), BF),
            pltpu.VMEM((pairs, 2 * tile, 128), BF),
            pltpu.VMEM((tile, BLOCK), F32),
            pltpu.VMEM((pairs, 2 * tile, 128), F32),
            pltpu.VMEM((pairs, 2 * tile, 128), F32),
        ],
        20_000_000_000,
    )


def remote(src, dst, send_sem, recv_sem, where):
    return pltpu.make_async_remote_copy(
        src_ref=src,
        dst_ref=dst,
        send_sem=send_sem,
        recv_sem=recv_sem,
        device_id=where,
        device_id_type=pl.DeviceIdType.MESH,
    )


def greet(peers):
    barrier = pltpu.get_barrier_semaphore()
    for peer in peers:
        pl.semaphore_signal(barrier, inc=1, device_id=peer, device_id_type=pl.DeviceIdType.MESH)
    pl.semaphore_wait(barrier, len(peers))


def here():
    shard, z, y = lax.axis_index("shard"), lax.axis_index("ctx"), lax.axis_index("tp")
    return shard // 2, shard % 2, y, z


def gather_kernel(widths, *refs):
    count = len(widths)
    pieces, wholes = refs[:count], refs[count : 2 * count]
    small, small_whole = refs[2 * count], refs[2 * count + 1]
    send, recv, own_sem, small_sem = refs[2 * count + 2 :]
    x, c, y, z = here()
    at_x, at_y, at_c = {"shard": 2 * (1 - x) + c}, {"tp": 1 - y}, {"shard": 2 * x + 1 - c}
    greet((at_x, at_y, at_c))

    def slot(a, of_y, of_x, of_c, lines=None):
        cols = pl.ds(pl.multiple_of(of_y * widths[a], 128), widths[a])
        rows = wholes[a].shape[2]
        lines = slice(0, rows) if lines is None else slice(lines * rows // 2, (lines + 1) * rows // 2)
        return wholes[a].at[of_x, of_c, lines, cols]

    def copy(a, kind, src, dst, where):
        return remote(src, dst, send.at[a, kind], recv.at[a, kind], where)

    def moves(a):
        mine, from_x, from_y = slot(a, y, x, c), slot(a, y, 1 - x, c), slot(a, 1 - y, x, c)
        table = [
            (pieces[a], mine, at_x),
            (pieces[a], mine, at_y),
            (pieces[a], mine, at_c),
            (slot(a, y, 1 - x, c, 0), slot(a, y, 1 - x, c, 0), at_y),
            (slot(a, 1 - y, x, c, 1), slot(a, 1 - y, x, c, 1), at_x),
            (from_x, from_x, at_c),
            (from_y, from_y, at_c),
            (slot(a, 1 - y, 1 - x, c, 0), slot(a, 1 - y, 1 - x, c, 0), at_c),
            (slot(a, 1 - y, 1 - x, c, 1), slot(a, 1 - y, 1 - x, c, 1), at_c),
        ]
        return [copy(a, kind, *row) for kind, row in enumerate(table)]

    tables = [moves(a) for a in range(count)]
    lines = small_whole.shape[0] // 2
    small_at = small_whole.at[pl.ds(pl.multiple_of(y * lines, 16), lines)]
    small_copy = remote(small, small_at, small_sem.at[0], small_sem.at[1], at_y)
    small_copy.start()
    locals_ = [pltpu.make_async_copy(small, small_at, small_sem.at[2])]
    for a in range(count):
        for kind in range(3):
            tables[a][kind].start()
        locals_.append(pltpu.make_async_copy(pieces[a], slot(a, y, x, c), own_sem.at[a]))
    for item in locals_:
        item.start()
    for a in range(count):
        tables[a][0].wait_recv()
        tables[a][3].start()
        tables[a][5].start()
        tables[a][1].wait_recv()
        tables[a][4].start()
        tables[a][6].start()
    for a in range(count):
        tables[a][3].wait_recv()
        tables[a][7].start()
        tables[a][4].wait_recv()
        tables[a][8].start()
    for a in range(count):
        for kind in (2, 5, 6, 7, 8):
            tables[a][kind].wait_recv()
        for kind in range(9):
            tables[a][kind].wait_send()
    small_copy.wait()
    for item in locals_:
        item.wait()


def gather_weights(pieces, small):
    rows = pieces[0].shape[0]
    widths = tuple(piece.shape[1] for piece in pieces)
    outs = [jax.ShapeDtypeStruct((2, 2, rows, 2 * width), BF) for width in widths]
    outs.append(jax.ShapeDtypeStruct((2 * small.shape[0], small.shape[1]), BF))
    spec = pl.BlockSpec(memory_space=pl.ANY)
    count = len(pieces)

    def kernel(*refs):
        ins, rest = refs[: count + 1], refs[count + 1 :]
        gather_kernel(widths, *ins[:count], *rest[:count], ins[count], *rest[count:])

    gathered = pl.pallas_call(
        kernel,
        out_shape=outs,
        in_specs=[spec] * (count + 1),
        out_specs=[spec] * (count + 1),
        scratch_shapes=[
            pltpu.SemaphoreType.DMA((count, 9)),
            pltpu.SemaphoreType.DMA((count, 9)),
            pltpu.SemaphoreType.DMA((count,)),
            pltpu.SemaphoreType.DMA((3,)),
        ],
        compiler_params=pltpu.CompilerParams(collective_id=0, has_side_effects=True),
        cost_estimate=pl.CostEstimate(flops=0, bytes_accessed=100000000, transcendentals=0),
    )(*pieces, small)
    return [full.reshape(4 * rows, full.shape[3]) for full in gathered[:count]], gathered[count]


def add_lines(dst, first, second):
    rows = dst.shape[0]
    step = 48 if rows % 48 == 0 else 16

    def body(i, carry):
        lines = pl.ds(pl.multiple_of(i * step, 16), step)
        dst[lines, :] = (first[lines, :].astype(F32) + second[lines, :].astype(F32)).astype(dst.dtype)
        return carry

    lax.fori_loop(0, rows // step, body, 0)


def reduce_kernel(widths, chunks, *refs):
    count, number = len(widths), len(chunks)
    fulls, vector, outs, vector_out = refs[:count], refs[count], refs[count + 1 : 2 * count + 1], refs[2 * count + 1]
    rest = refs[2 * count + 2 :]
    by_core, by_x, by_y, plane, half_z, quarter_z, final = (rest[i * number : (i + 1) * number] for i in range(7))
    vector_in, vector_sum, send, recv, vector_send, vector_recv = rest[7 * number :]
    x, c, y, z = here()
    low_z, high_z = z % 2, z // 2
    at_x, at_y, at_c = {"shard": 2 * (1 - x) + c}, {"tp": 1 - y}, {"shard": 2 * x + 1 - c}
    at_one, at_two = {"ctx": 2 * high_z + 1 - low_z}, {"ctx": 2 * (1 - high_z) + low_z}
    greet((at_x, at_y, at_c, at_one, at_two))
    half = fulls[0].shape[2] // 2
    quarter = half // 2

    def part(k, of_core, of_y):
        a, first, width = chunks[k]
        cols = pl.ds(pl.multiple_of(of_y * widths[a] + first, 128), width)
        return fulls[a].at[:, of_core, :, cols]

    def copies(k, stage):
        if stage == 0:
            table = [(part(k, 1 - c, of_y), by_core[k].at[of_y], at_c) for of_y in range(2)]
        elif stage == 1:
            table = [
                (by_core[k].at[:, 1 - x, :half], by_x[k], at_x),
                (by_core[k].at[1 - y, :, half:], by_y[k], at_y),
            ]
        elif stage == 2:
            table = [(by_x[k].at[1 - y], plane[k].at[0], at_y), (by_y[k].at[1 - x], plane[k].at[1], at_x)]
        elif stage == 3:
            table = [(plane[k].at[1 - low_z], half_z[k], at_one)]
        elif stage == 4:
            lines = pl.ds(pl.multiple_of((1 - high_z) * quarter, 16), quarter)
            table = [(half_z[k].at[lines], quarter_z[k], at_two)]
        elif stage == 5:
            mine = final[k].at[2 * low_z + high_z]
            table = [(mine, mine, at_two)]
        else:
            mine = final[k].at[pl.ds(2 * low_z, 2)]
            table = [(mine, mine, at_one)]
        return [remote(s, d, send.at[k, stage, i], recv.at[k, stage, i], w) for i, (s, d, w) in enumerate(table)]

    def absorb(k, stage):
        if stage == 0:
            for of_y in range(2):
                mine = part(k, c, of_y)
                for of_x in range(2):
                    there = by_core[k].at[of_y, of_x]
                    add_lines(there, there, mine.at[of_x])
        elif stage == 1:
            for i in range(2):
                add_lines(by_x[k].at[i], by_x[k].at[i], by_core[k].at[i, x, pl.ds(0, half)])
                add_lines(by_y[k].at[i], by_y[k].at[i], by_core[k].at[y, i, pl.ds(half, half)])
        elif stage == 2:
            add_lines(plane[k].at[0], plane[k].at[0], by_x[k].at[y])
            add_lines(plane[k].at[1], plane[k].at[1], by_y[k].at[x])
        elif stage == 3:
            add_lines(half_z[k], half_z[k], plane[k].at[low_z])
        elif stage == 4:
            lines = pl.ds(pl.multiple_of(high_z * quarter, 16), quarter)
            add_lines(final[k].at[2 * low_z + high_z], quarter_z[k], half_z[k].at[lines])
        elif stage == 6:
            a, first, width = chunks[k]
            for i in range(4):
                outs[a][i * quarter : (i + 1) * quarter, first : first + width] = final[k][i].astype(F32)

    def vector_copy(stage):
        where = (at_c, at_x, at_y, at_one, at_two)[stage]
        return remote(vector_sum.at[stage], vector_in.at[stage], vector_send.at[stage], vector_recv.at[stage], where)

    stages = 7
    for k in range(number):
        for item in copies(k, 0):
            item.start()
    vector_sum[0] = vector[...]
    vector_copy(0).start()
    for step in range(number + stages - 1):
        for stage in reversed(range(stages)):
            k = step - stage
            if 0 <= k < number:
                for item in copies(k, stage):
                    item.wait_recv()
                absorb(k, stage)
                if stage + 1 < stages:
                    for item in copies(k, stage + 1):
                        item.start()
        if step < 5:
            vector_copy(step).wait_recv()
            total = vector_sum[step] + vector_in[step]
            if step < 4:
                vector_sum[step + 1] = total
                vector_copy(step + 1).start()
            else:
                vector_out[...] = total
    for k in range(number):
        for stage in range(stages):
            for item in copies(k, stage):
                item.wait_send()
    for stage in range(5):
        vector_copy(stage).wait_send()


def reduce_grads(fulls, vector):
    rows = fulls[0].shape[0] // 4
    widths = tuple(full.shape[1] // 2 for full in fulls)
    chunks = []
    for a, width in enumerate(widths):
        step = 768 if width % 768 == 0 else 384
        chunks += [(a, first, step) for first in range(0, width, step)]
    number = len(chunks)
    spec = pl.BlockSpec(memory_space=pltpu.VMEM)
    scratch = [pltpu.VMEM((2, 2, rows, width), BF) for _, _, width in chunks]
    scratch += [pltpu.VMEM((2, rows // 2, width), BF) for _ in range(3) for _, _, width in chunks]
    scratch += [pltpu.VMEM((rows // 2, width), BF) for _, _, width in chunks]
    scratch += [pltpu.VMEM((rows // 4, width), BF) for _, _, width in chunks]
    scratch += [pltpu.VMEM((4, rows // 4, width), BF) for _, _, width in chunks]
    scratch += [pltpu.VMEM((5,) + vector.shape, F32), pltpu.VMEM((5,) + vector.shape, F32)]
    scratch += [pltpu.SemaphoreType.DMA((number, 7, 2)), pltpu.SemaphoreType.DMA((number, 7, 2))]
    scratch += [pltpu.SemaphoreType.DMA((5,)), pltpu.SemaphoreType.DMA((5,))]
    outs = [jax.ShapeDtypeStruct((rows, width), F32) for width in widths]
    outs.append(jax.ShapeDtypeStruct(vector.shape, F32))
    result = pl.pallas_call(
        functools.partial(reduce_kernel, widths, tuple(chunks)),
        out_shape=outs,
        in_specs=[spec] * (len(fulls) + 1),
        out_specs=[spec] * len(outs),
        scratch_shapes=scratch,
        compiler_params=pltpu.CompilerParams(
            collective_id=1, has_side_effects=True, vmem_limit_bytes=VMEM_LIMIT
        ),
        cost_estimate=pl.CostEstimate(flops=0, bytes_accessed=200000000, transcendentals=0),
    )(*[full.reshape(2, 2, rows, full.shape[1]) for full in fulls], vector)
    return result[:-1], result[-1]


def slots_kernel(values, dealt_col, out, outgoing, blocks, acc, picked, sems, line_send, line_recv):
    own, dim = values.shape
    half, slots = dim // 2, 2 * own
    x, c, y, z = here()
    last = blocks.shape[0] - 1
    at_y, at_left, at_right = {"tp": 1 - y}, {"ctx": jnp.maximum(z - 1, 0)}, {"ctx": jnp.minimum(z + 1, last)}
    barrier = pltpu.get_barrier_semaphore()
    pl.semaphore_signal(barrier, inc=1, device_id=at_y, device_id_type=pl.DeviceIdType.MESH)

    @pl.when(z > 0)
    def _():
        pl.semaphore_signal(barrier, inc=1, device_id=at_left, device_id_type=pl.DeviceIdType.MESH)

    @pl.when(z < last)
    def _():
        pl.semaphore_signal(barrier, inc=1, device_id=at_right, device_id_type=pl.DeviceIdType.MESH)

    greetings = 1 + (z > 0).astype(jnp.int32) + (z < last).astype(jnp.int32)
    pl.semaphore_wait(barrier, greetings)
    mine_cols = pl.ds(pl.multiple_of(y * half, 128), half)
    other_cols = pl.ds(pl.multiple_of((1 - y) * half, 128), half)
    mine_rows = pl.ds(pl.multiple_of(y * own, 64), own)
    outgoing[...] = values[:, other_cols]
    first = remote(outgoing, blocks.at[z, mine_rows], sems.at[0], sems.at[1], at_y)
    first.start()
    blocks[z, mine_rows, :] = values[:, mine_cols]
    first.wait_recv()

    def to_right(block):
        return remote(blocks.at[block], blocks.at[block], line_send.at[0, block], line_recv.at[block], at_right)

    def to_left(block):
        return remote(blocks.at[block], blocks.at[block], line_send.at[1, block], line_recv.at[block], at_left)

    def select(block, start):
        wide = 384 if slots % 384 == 0 else 128

        def body(i, carry):
            lines = pl.ds(pl.multiple_of(i * wide, 128), wide)
            token = block * slots + lax.broadcasted_iota(jnp.int32, (wide, slots), 1)
            chosen = jnp.where(dealt_col[lines, :] == token, 1.0, 0.0).astype(BF)
            part = matmul(chosen, blocks[block])
            acc[lines, :] = part if start else acc[lines, :] + part
            return carry

        lax.fori_loop(0, slots // wide, body, 0)

    @pl.when(z < last)
    def _():
        to_right(z).start()

    @pl.when(z > 0)
    def _():
        to_left(z).start()

    select(z, True)
    for distance in range(1, last + 1):
        from_left, from_right = z - distance, z + distance

        @pl.when(from_left >= 0)
        def _():
            to_right(from_left).wait_recv()

            @pl.when(z < last)
            def _():
                to_right(from_left).start()

        @pl.when(from_right <= last)
        def _():
            to_left(from_right).wait_recv()

            @pl.when(z > 0)
            def _():
                to_left(from_right).start()

        @pl.when(from_left >= 0)
        def _():
            select(from_left, False)

        @pl.when(from_right <= last)
        def _():
            select(from_right, False)

    picked[...] = acc[...].astype(BF)
    back = remote(picked, out.at[:, mine_cols], sems.at[2], sems.at[3], at_y)
    back.start()
    out[:, mine_cols] = picked[...]
    first.wait_send()
    for block in range(last + 1):

        @pl.when((z < last) & (block <= z))
        def _():
            to_right(block).wait_send()

        @pl.when((z > 0) & (block >= z))
        def _():
            to_left(block).wait_send()

    back.wait()


def rows_to_slots_kernel(values, dealt, place_z):
    own, dim = values.shape
    slots = 2 * own
    ctx_size = lax.axis_size("ctx")
    mine = lax.dynamic_slice_in_dim(dealt, place_z * slots, slots)[:, None]
    spec = pl.BlockSpec(memory_space=pltpu.VMEM)
    return pl.pallas_call(
        slots_kernel,
        out_shape=jax.ShapeDtypeStruct((slots, dim), BF),
        in_specs=[spec, spec],
        out_specs=spec,
        scratch_shapes=[
            pltpu.VMEM((own, dim // 2), BF),
            pltpu.VMEM((ctx_size, slots, dim // 2), BF),
            pltpu.VMEM((slots, dim // 2), F32),
            pltpu.VMEM((slots, dim // 2), BF),
            pltpu.SemaphoreType.DMA((4,)),
            pltpu.SemaphoreType.DMA((2, ctx_size)),
            pltpu.SemaphoreType.DMA((ctx_size,)),
        ],
        compiler_params=pltpu.CompilerParams(
            collective_id=2, has_side_effects=True, vmem_limit_bytes=VMEM_LIMIT
        ),
        cost_estimate=pl.CostEstimate(flops=4000000000, bytes_accessed=150000000, transcendentals=0),
    )(values, mine)


def project_kernel(dim, x_ref, weight, bias, out):
    step = 256
    third = weight.shape[1] // 3

    def body(i, carry):
        lines = pl.ds(pl.multiple_of(i * step, step), step)
        value = (matmul(x_ref[lines, :], weight[...]) + bias[0]).astype(BF)
        scale = jnp.where(lax.broadcasted_iota(jnp.int32, (1, 3 * third), 1) < third, 0.125, 1.0).astype(BF)
        out[lines, :] = value * scale
        return carry

    lax.fori_loop(0, x_ref.shape[0] // step, body, 0)


def project(x_window, weight, bias):
    rows, dim = x_window.shape
    width = 3 * dim // 2
    return pl.pallas_call(
        functools.partial(project_kernel, dim),
        grid=(2,),
        out_shape=jax.ShapeDtypeStruct((rows, 2 * width), BF),
        in_specs=[
            pl.BlockSpec((rows, dim), lambda i: (0, 0)),
            pl.BlockSpec((dim, width), lambda i: (0, i)),
            pl.BlockSpec((1, 1, width), lambda i: (i, 0, 0)),
        ],
        out_specs=pl.BlockSpec((rows, width), lambda i: (0, i)),
        compiler_params=pltpu.CompilerParams(vmem_limit_bytes=VMEM_LIMIT),
        cost_estimate=pl.CostEstimate(flops=6000000000, bytes_accessed=14000000, transcendentals=0),
    )(x_window, weight, bias)


def rows_to_slots(values, dealt, place_z, place_y):
    own, dim = values.shape
    half = dim // 2
    keep = lax.dynamic_slice_in_dim(values, place_y * half, half, axis=1)
    send = lax.dynamic_slice_in_dim(values, (1 - place_y) * half, half, axis=1)
    other = lax.ppermute(send, "tp", [(0, 1), (1, 0)])
    first = jnp.where(place_y == 0, keep, other)
    second = jnp.where(place_y == 0, other, keep)
    block = jnp.concatenate([first, second], axis=0)
    everything = lax.all_gather(block, "ctx", axis=0, tiled=True)
    slots = 2 * own
    mine = lax.dynamic_slice_in_dim(dealt, place_z * slots, slots)
    picked = jnp.take(everything, mine, axis=0, mode="clip")
    other_columns = lax.ppermute(picked, "tp", [(0, 1), (1, 0)])
    return jnp.concatenate(
        [jnp.where(place_y == 0, picked, other_columns), jnp.where(place_y == 0, other_columns, picked)], axis=1
    )


def slots_to_rows(values, dealt, place_z, place_y):
    slots, dim = values.shape
    half, own = dim // 2, slots // 2
    block = lax.dynamic_slice_in_dim(values, place_y * half, half, axis=1)
    everything = lax.all_gather(block, "ctx", axis=0, tiled=True)
    wanted = place_z * slots + lax.broadcasted_iota(jnp.int32, (slots, 1), 0)
    chosen = (wanted == dealt[None, :]).astype(BF)
    picked = matmul(chosen, everything).astype(BF)
    keep = lax.dynamic_slice_in_dim(picked, place_y * own, own, axis=0)
    send = lax.dynamic_slice_in_dim(picked, (1 - place_y) * own, own, axis=0)
    other = lax.ppermute(send, "tp", [(0, 1), (1, 0)])
    return jnp.concatenate([jnp.where(place_y == 0, keep, other), jnp.where(place_y == 0, other, keep)], axis=1)


def per_device(
    tokens,
    cotangent,
    seq_lengths,
    dealing,
    query_weight,
    query_bias,
    key_weight,
    value_weight,
    value_bias,
    output_weight,
    output_bias,
    first_gain,
    first_shift,
    up_weight,
    up_bias,
    down_weight,
    down_bias,
    second_gain,
    second_shift,
):
    rows, dim = tokens.shape
    ctx_size, tp_size = lax.axis_size("ctx"), lax.axis_size("tp")
    group_rows = rows * ctx_size
    own = rows // tp_size
    place_z, place_y = lax.axis_index("ctx"), lax.axis_index("tp")
    window = HALO + own + HALO
    padded = -(-window // BLOCK) * BLOCK
    dealt = dealing[0]

    lengths = seq_lengths[0]
    number = lengths.shape[0]
    upto = jnp.arange(number)[:, None] >= jnp.arange(number)[None, :]
    ends = jnp.sum(jnp.where(upto, lengths[None, :], 0), axis=1)
    starts = ends - lengths
    first_row = place_z * rows + place_y * own
    index = jnp.arange(padded, dtype=jnp.int32)
    position = first_row - HALO + index
    valid = (position >= 0) & (position < group_rows) & (index < window)
    segment = jnp.sum((position[:, None] >= ends[None, :-1]).astype(jnp.int32), axis=1)
    segment = jnp.where(valid, segment, -1)
    seg_row, seg_col = segment[None, :], segment[:, None]
    tile = attention_tile(own)
    tile_first = first_row + tile * jnp.arange(own // tile, dtype=jnp.int32)
    tile_last = tile_first + tile - 1
    begin = jnp.max(jnp.where(starts[None, :] <= tile_first[:, None], starts[None, :], 0), axis=1)
    finish = jnp.min(jnp.where(ends[None, :] > tile_last[:, None], ends[None, :], group_rows), axis=1)
    shift = HALO - first_row
    bounds = jnp.stack([(begin + shift) // BLOCK, (finish + shift + BLOCK - 1) // BLOCK], axis=1).astype(jnp.int32)

    special = lax.axis_size("shard") == 4 and tp_size == 2 and ctx_size == 4
    half_dim = dim // tp_size
    pieces = [
        jnp.concatenate([query_weight, key_weight, value_weight], axis=1),
        output_weight.T,
        up_weight,
        down_weight.T,
    ]
    flat = jnp.concatenate([query_bias, value_bias, up_bias])
    small = jnp.broadcast_to(flat[None, :], (16, flat.shape[0]))
    if special:
        whole, biases = gather_weights(pieces, small)
    else:
        whole = [
            lax.all_gather(lax.all_gather(piece, "shard", axis=0, tiled=True), "tp", axis=1, tiled=True)
            for piece in pieces
        ]
        biases = lax.all_gather(small, "tp", axis=0, tiled=True)
    wide_qkv, wide_output, wide_up, wide_down = whole
    biases = biases[::16].astype(F32)
    qkv_bias = jnp.concatenate(
        [biases[:, :half_dim], jnp.zeros((tp_size, half_dim), F32), biases[:, half_dim:dim]], axis=1
    )[:, None, :]
    whole_up_bias = biases[:, dim:].reshape(-1)

    edge = jnp.where(place_y == 0, tokens[rows - HALO :], tokens[:HALO])
    hops = [(2 * z, 2 * z + 2) for z in range(ctx_size - 1)] + [(2 * z + 1, 2 * z - 1) for z in range(1, ctx_size)]
    arrived = lax.ppermute(edge, ("ctx", "tp"), hops)
    x_window = jnp.where(
        place_y == 0,
        jnp.concatenate([arrived, tokens[: own + HALO]], axis=0),
        jnp.concatenate([tokens[own - HALO :], arrived], axis=0),
    )
    x_window = jnp.pad(x_window, ((0, padded - window), (0, 0)))
    inputs = lax.dynamic_slice_in_dim(tokens, place_y * own, own, axis=0)

    output_bias = output_bias.astype(F32)
    first_gain = first_gain.astype(F32)
    first_shift = first_shift.astype(F32)
    down_bias = down_bias.astype(F32)
    second_gain = second_gain.astype(F32)
    second_shift = second_shift.astype(F32)

    qkv = project(x_window, wide_qkv, qkv_bias)
    attended, logsum = attention_forward(qkv, seg_col, seg_row, bounds, own, dim)
    grad_out = slots_to_rows(cotangent, dealt, place_z, place_y).astype(F32)
    hidden_one, normed_one, inverse_one = norm_forward(
        inputs.astype(F32) + matmul_second(attended, wide_output) + output_bias, first_gain, first_shift
    )
    hidden_low = hidden_one.astype(BF)
    pre_act = matmul(hidden_low, wide_up) + whole_up_bias
    erf_part = 0.5 * (1.0 + jax.scipy.special.erf(pre_act * HALF_ROOT))
    act_low = (pre_act * erf_part).astype(BF)
    layer_value, normed_two, inverse_two = norm_forward(
        hidden_one + matmul_second(act_low, wide_down) + down_bias, second_gain, second_shift
    )
    layer_out = rows_to_slots(layer_value.astype(BF), dealt, place_z, place_y)

    second_shift_grad = jnp.sum(grad_out, axis=0)
    second_gain_grad = jnp.sum(grad_out * normed_two, axis=0)
    grad_second = norm_backward(grad_out, normed_two, inverse_two, second_gain)
    down_bias_grad = jnp.sum(grad_second, axis=0)
    second_low = grad_second.astype(BF)
    slope = erf_part + pre_act * DENSITY * jnp.exp(-0.5 * pre_act * pre_act)
    grad_pre = matmul(second_low, wide_down) * slope
    up_bias_grad = jnp.sum(grad_pre, axis=0)
    pre_low = grad_pre.astype(BF)
    grad_hidden = grad_second + matmul_second(pre_low, wide_up)
    first_shift_grad = jnp.sum(grad_hidden, axis=0)
    first_gain_grad = jnp.sum(grad_hidden * normed_one, axis=0)
    grad_first = norm_backward(grad_hidden, normed_one, inverse_one, first_gain)
    output_bias_grad = jnp.sum(grad_first, axis=0)
    first_low = grad_first.astype(BF)
    attended_grad = matmul(first_low, wide_output).astype(BF)
    delta = jnp.sum(
        (attended_grad.astype(F32) * attended.astype(F32)).reshape(own, dim // HEAD, HEAD), axis=2
    )
    delta = jnp.pad(delta, ((0, 0), (0, 128 - dim // HEAD)))
    up_hops = [(i, i + 1) for i in range(ctx_size * tp_size - 1)]
    down_hops = [(i + 1, i) for i in range(ctx_size * tp_size - 1)]
    both = ("ctx", "tp")
    stats = jnp.concatenate([logsum[:, :16], delta[:, :16]], axis=1).T
    grad_win = jnp.concatenate(
        [
            lax.ppermute(attended_grad[own - HALO :], both, up_hops),
            attended_grad,
            lax.ppermute(attended_grad[:HALO], both, down_hops),
            jnp.zeros((padded - window, dim), BF),
        ],
        axis=0,
    )
    stats_win = jnp.concatenate(
        [
            lax.ppermute(stats[:, own - HALO :], both, up_hops),
            stats,
            lax.ppermute(stats[:, :HALO], both, down_hops),
            jnp.zeros((stats.shape[0], padded - window), F32),
        ],
        axis=1,
    )
    query_low, query_bias_grad = attention_query(qkv, seg_col, seg_row, bounds, attended_grad, logsum, delta, dim)
    qkv_low, value_bias_grad = attention_key(
        qkv, seg_col, seg_row, bounds, grad_win, stats_win[:16], stats_win[16:], query_low, own, dim
    )
    tokens_grad = (grad_first + matmul_second(qkv_low, wide_qkv)).astype(BF)
    fulls = [
        matmul_first(inputs, qkv_low).astype(BF),
        matmul_first(first_low, attended).astype(BF),
        matmul_first(hidden_low, pre_low).astype(BF),
        matmul_first(second_low, act_low).astype(BF),
    ]
    vectors = jnp.concatenate(
        [
            query_bias_grad[0],
            value_bias_grad[0],
            up_bias_grad,
            output_bias_grad,
            first_gain_grad,
            first_shift_grad,
            down_bias_grad,
            second_gain_grad,
            second_shift_grad,
        ]
    )
    if special:
        owned, small_sum = reduce_grads(fulls, vectors.reshape(-1, 128))
        small_sum = small_sum.reshape(-1)
        tokens_grad = rows_to_slots_kernel(tokens_grad, dealt, place_z)
    else:
        owned = []
        for full in fulls:
            part = lax.psum_scatter(full, "tp", scatter_dimension=1, tiled=True)
            part = lax.psum_scatter(part, "shard", scatter_dimension=0, tiled=True)
            owned.append(lax.psum(part, "ctx").astype(F32))
        small_sum = lax.psum(vectors, ("shard", "ctx", "tp"))
        tokens_grad = rows_to_slots(tokens_grad, dealt, place_z, place_y)
    hidden = up_bias_grad.shape[0]
    sizes = [dim, dim, hidden] + [dim] * 6
    offsets = [sum(sizes[:i]) for i in range(len(sizes))]
    parts = [small_sum[o : o + s] for o, s in zip(offsets, sizes)]

    def by_tp(vector):
        part = vector.shape[0] // tp_size
        return lax.dynamic_slice_in_dim(vector, place_y * part, part)

    return (
        layer_out,
        tokens_grad,
        owned[0][:, :half_dim],
        by_tp(parts[0]),
        owned[0][:, half_dim : 2 * half_dim],
        owned[0][:, 2 * half_dim :],
        by_tp(parts[1]),
        owned[1].T,
        parts[3],
        parts[4],
        parts[5],
        owned[2],
        by_tp(parts[2]),
        owned[3].T,
        parts[6],
        parts[7],
        parts[8],
    )


def solution(mesh):
    return jax.shard_map(
        per_device,
        mesh=mesh,
        in_specs=(
            P(("shard", "ctx"), None),
            P(("shard", "ctx"), None),
            P("shard", None),
            P("shard", None),
            P("shard", "tp"),
            P("tp"),
            P("shard", "tp"),
            P("shard", "tp"),
            P("tp"),
            P("tp", "shard"),
            P(),
            P(),
            P(),
            P("shard", "tp"),
            P("tp"),
            P("tp", "shard"),
            P(),
            P(),
            P(),
        ),
        out_specs=(
            P(("shard", "ctx"), None),
            P(("shard", "ctx"), None),
            P("shard", "tp"),
            P("tp"),
            P("shard", "tp"),
            P("shard", "tp"),
            P("tp"),
            P("tp", "shard"),
            P(),
            P(),
            P(),
            P("shard", "tp"),
            P("tp"),
            P("tp", "shard"),
            P(),
            P(),
            P(),
        ),
        check_vma=False,
    )
```

```python
import functools

import jax
import jax.numpy as jnp
from jax import lax
from jax.experimental import pallas as pl
from jax.experimental.pallas import tpu as pltpu
from jax.sharding import PartitionSpec as P

HEAD = 64
HALO = 512
HALF_ROOT = 0.7071067811865476
DENSITY = 0.3989422804014327
NEG_FILL = -1000000000.0
BF = jnp.bfloat16
F32 = jnp.float32
BLOCK = 256
VMEM_LIMIT = 56 * 1024 * 1024


def matmul(former, latter):
    return jnp.dot(former, latter, preferred_element_type=F32)


def matmul_first(former, latter):
    return lax.dot_general(former, latter, (((0,), (0,)), ((), ())), preferred_element_type=F32)


def matmul_second(former, latter):
    return lax.dot_general(former, latter, (((1,), (1,)), ((), ())), preferred_element_type=F32)


def norm_forward(values, norm_gain, norm_shift):
    centre = values - jnp.mean(values, axis=1, keepdims=True)
    spread = jnp.mean(centre * centre, axis=1, keepdims=True)
    inverse = lax.rsqrt(spread + 1e-06)
    normed = centre * inverse
    return (norm_gain * normed + norm_shift, normed, inverse)


def norm_backward(gradient, normed, inverse, norm_gain):
    scaled = gradient * norm_gain
    bracket = (
        scaled
        - jnp.mean(scaled, axis=1, keepdims=True)
        - normed * jnp.mean(scaled * normed, axis=1, keepdims=True)
    )
    return inverse * bracket


def places(pair, dim):
    half, inner = divmod(pair, dim // 256)
    base = half * (3 * dim // 2) + inner * 128
    return base, base + dim // 2, base + dim


def take(qkv, rows, pair, dim, which):
    first = places(pair, dim)[which]
    return qkv[rows, first : first + 128]


def low_lanes(rows):
    return lax.broadcasted_iota(jnp.int32, (rows, 128), 1) < HEAD


def stacked(pair):
    low = low_lanes(pair.shape[0])
    zero = jnp.zeros_like(pair)
    return jnp.concatenate([jnp.where(low, pair, zero), jnp.where(low, zero, pair)], axis=0)


def unstacked(both):
    rows = both.shape[0] // 2
    return jnp.where(low_lanes(rows), both[:rows], both[rows:])


def columns(ref_value, head, rows):
    return jnp.concatenate([ref_value[:, 2 * head : 2 * head + 1], ref_value[:, 2 * head + 1 : 2 * head + 2]], axis=0)


def bias_of(own_seg, other_seg):
    return jnp.where(own_seg == other_seg, 0.0, NEG_FILL)


def forward_kernel(dim, tile, bounds, qkv, seg_col, seg_row, out, logsum, query_st, bias_ref, acc, top, total):
    pairs = dim // 128
    own = out.shape[0]

    def one_tile(i, carry):
        first = pl.multiple_of(i * tile, tile)
        rows = pl.ds(pl.multiple_of(HALO + first, 64), tile)
        seg_here = seg_col[rows, :]
        for p in range(pairs):
            query_st[p] = stacked(take(qkv, rows, p, dim, 0))
        acc[...] = jnp.zeros_like(acc)
        total[...] = jnp.zeros_like(total)
        top[...] = jnp.full_like(top, 2 * NEG_FILL)

        def one_block(j, inner):
            start = pl.multiple_of(j * BLOCK, BLOCK)
            bias = bias_of(seg_here, seg_row[:, pl.ds(start, BLOCK)])
            bias_ref[...] = jnp.concatenate([bias, bias], axis=0)
            for p in range(pairs):
                key = take(qkv, pl.ds(start, BLOCK), p, dim, 1)
                value = take(qkv, pl.ds(start, BLOCK), p, dim, 2)
                scores = matmul_second(query_st[p], key) + bias_ref[...]
                old = top[p]
                new = jnp.maximum(old, jnp.max(scores, axis=1, keepdims=True))
                keep = jnp.exp(old - new)
                raised = jnp.exp(scores - new[:, :1])
                total[p] = keep * total[p] + jnp.sum(raised, axis=1, keepdims=True)
                acc[p] = keep * acc[p] + matmul(raised.astype(BF), value)
                top[p] = new
            return inner

        lax.fori_loop(bounds[i, 0], bounds[i, 1], one_block, 0)
        lane = lax.broadcasted_iota(jnp.int32, (tile, 128), 1)
        sums = jnp.zeros((tile, 128), F32)
        for p in range(pairs):
            whole = total[p]
            out[pl.ds(first, tile), p * 128 : p * 128 + 128] = unstacked(acc[p] / whole).astype(BF)
            lse = top[p] + jnp.log(whole)
            sums = jnp.where(lane == 2 * p, lse[:tile], sums)
            sums = jnp.where(lane == 2 * p + 1, lse[tile:], sums)
        logsum[pl.ds(first, tile), :] = sums
        return carry

    lax.fori_loop(0, own // tile, one_tile, 0)


def query_kernel(dim, tile, bounds, qkv, seg_col, seg_row, grad, stats, out, sums, query_st, grad_st, bias_ref, acc):
    pairs = dim // 128
    own = out.shape[0]

    def one_tile(i, carry):
        first = pl.multiple_of(i * tile, tile)
        own_rows = pl.ds(first, tile)
        rows = pl.ds(pl.multiple_of(HALO + first, 64), tile)
        seg_here = seg_col[rows, :]
        for p in range(pairs):
            query_st[p] = stacked(take(qkv, rows, p, dim, 0))
            grad_st[p] = stacked(grad[own_rows, p * 128 : p * 128 + 128])
        acc[...] = jnp.zeros_like(acc)

        def one_block(j, inner):
            start = pl.multiple_of(j * BLOCK, BLOCK)
            bias = bias_of(seg_here, seg_row[:, pl.ds(start, BLOCK)])
            bias_ref[...] = jnp.concatenate([bias, bias], axis=0)
            for p in range(pairs):
                key = take(qkv, pl.ds(start, BLOCK), p, dim, 1)
                value = take(qkv, pl.ds(start, BLOCK), p, dim, 2)
                scores = matmul_second(query_st[p], key) + bias_ref[...]
                probs = jnp.exp(scores - columns(stats[own_rows, :], p, tile))
                grad_probs = matmul_second(grad_st[p], value)
                grad_scores = (probs * (grad_probs - columns(stats[own_rows, :], p + 8, tile))).astype(BF)
                acc[p] += matmul(grad_scores, key)
            return inner

        lax.fori_loop(bounds[i, 0], bounds[i, 1], one_block, 0)
        for p in range(pairs):
            part = 0.125 * unstacked(acc[p])
            out[own_rows, p * 128 : p * 128 + 128] = part.astype(BF)
            sums[:, p * 128 : p * 128 + 128] += jnp.sum(part, axis=0, keepdims=True)
        return carry

    sums[...] = jnp.zeros_like(sums)
    lax.fori_loop(0, own // tile, one_tile, 0)


def key_kernel(dim, tile, bounds, qkv, seg_col, seg_row, grad, stats, query_low, out, sums, key_st, value_st, bias_ref, key_acc, value_acc, stats_t):
    pairs = dim // 128
    own = out.shape[0]

    def one_tile(i, carry):
        first = pl.multiple_of(i * tile, tile)
        own_rows = pl.ds(first, tile)
        rows = pl.ds(pl.multiple_of(HALO + first, 64), tile)
        seg_here = seg_col[rows, :]
        for p in range(pairs):
            key_st[p] = stacked(take(qkv, rows, p, dim, 1))
            value_st[p] = stacked(take(qkv, rows, p, dim, 2))
        key_acc[...] = jnp.zeros_like(key_acc)
        value_acc[...] = jnp.zeros_like(value_acc)

        def one_block(j, inner):
            start = pl.multiple_of(j * BLOCK, BLOCK)
            there = pl.ds(start, BLOCK)
            bias_ref[...] = bias_of(seg_here, seg_row[:, there])
            for p in range(pairs):
                query = take(qkv, there, p, dim, 0)
                grad_pair = grad[there, p * 128 : p * 128 + 128]
                scores = matmul_second(key_st[p], query)
                grad_probs = matmul_second(value_st[p], grad_pair)
                probs_all, grads_all = [], []
                for half in range(2):
                    head = 2 * p + half
                    lines = slice(half * tile, half * tile + tile)
                    probs = jnp.exp(scores[lines] + bias_ref[...] - stats_t[head : head + 1, there])
                    grads_all.append((probs * (grad_probs[lines] - stats_t[16 + head : 17 + head, there])).astype(BF))
                    probs_all.append(probs.astype(BF))
                key_acc[p] += matmul(jnp.concatenate(grads_all, axis=0), query)
                value_acc[p] += matmul(jnp.concatenate(probs_all, axis=0), grad_pair)
            return inner

        lax.fori_loop(bounds[i, 0], bounds[i, 1], one_block, 0)
        for p in range(pairs):
            at_query, at_key, at_value = places(p, dim)
            out[own_rows, at_query : at_query + 128] = query_low[own_rows, p * 128 : p * 128 + 128]
            out[own_rows, at_key : at_key + 128] = unstacked(key_acc[p]).astype(BF)
            part = unstacked(value_acc[p])
            out[own_rows, at_value : at_value + 128] = part.astype(BF)
            sums[:, p * 128 : p * 128 + 128] += jnp.sum(part, axis=0, keepdims=True)
        return carry

    stats_t[...] = stats[...].T
    sums[...] = jnp.zeros_like(sums)
    lax.fori_loop(0, own // tile, one_tile, 0)


def vmem_call(kernel, arrays, bounds, outs, scratch, flops):
    spec = pl.BlockSpec(memory_space=pltpu.VMEM)
    return pl.pallas_call(
        kernel,
        out_shape=outs,
        in_specs=[pl.BlockSpec(memory_space=pltpu.SMEM)] + [spec] * len(arrays),
        out_specs=jax.tree.map(lambda leaf: spec, outs),
        scratch_shapes=scratch,
        compiler_params=pltpu.CompilerParams(vmem_limit_bytes=VMEM_LIMIT),
        cost_estimate=pl.CostEstimate(flops=flops, bytes_accessed=12000000, transcendentals=6000000),
    )(bounds, *arrays)


def attention_tile(own):
    for tile in (192, 128, 64, 32, 16):
        if own % tile == 0:
            return tile
    raise ValueError("rows")


def attention_forward(qkv, seg_col, seg_row, bounds, own, dim):
    tile = attention_tile(own)
    pairs = dim // 128
    return vmem_call(
        functools.partial(forward_kernel, dim, tile),
        (qkv, seg_col, seg_row),
        bounds,
        (jax.ShapeDtypeStruct((own, dim), BF), jax.ShapeDtypeStruct((own, 128), F32)),
        [
            pltpu.VMEM((pairs, 2 * tile, 128), BF),
            pltpu.VMEM((2 * tile, BLOCK), F32),
            pltpu.VMEM((pairs, 2 * tile, 128), F32),
            pltpu.VMEM((pairs, 2 * tile, 128), F32),
            pltpu.VMEM((pairs, 2 * tile, 128), F32),
        ],
        10_000_000_000,
    )


def attention_query(qkv, seg_col, seg_row, bounds, grad, stats, dim):
    own = grad.shape[0]
    tile = attention_tile(own)
    pairs = dim // 128
    return vmem_call(
        functools.partial(query_kernel, dim, tile),
        (qkv, seg_col, seg_row, grad, stats),
        bounds,
        (jax.ShapeDtypeStruct((own, dim), BF), jax.ShapeDtypeStruct((1, dim), F32)),
        [
            pltpu.VMEM((pairs, 2 * tile, 128), BF),
            pltpu.VMEM((pairs, 2 * tile, 128), BF),
            pltpu.VMEM((2 * tile, BLOCK), F32),
            pltpu.VMEM((pairs, 2 * tile, 128), F32),
        ],
        15_000_000_000,
    )


def attention_key(qkv, seg_col, seg_row, bounds, grad_win, stats_win, query_low, own, dim):
    tile = attention_tile(own)
    pairs = dim // 128
    return vmem_call(
        functools.partial(key_kernel, dim, tile),
        (qkv, seg_col, seg_row, grad_win, stats_win, query_low),
        bounds,
        (jax.ShapeDtypeStruct((own, 3 * dim), BF), jax.ShapeDtypeStruct((1, dim), F32)),
        [
            pltpu.VMEM((pairs, 2 * tile, 128), BF),
            pltpu.VMEM((pairs, 2 * tile, 128), BF),
            pltpu.VMEM((tile, BLOCK), F32),
            pltpu.VMEM((pairs, 2 * tile, 128), F32),
            pltpu.VMEM((pairs, 2 * tile, 128), F32),
            pltpu.VMEM((128, qkv.shape[0]), F32),
        ],
        20_000_000_000,
    )


def remote(src, dst, send_sem, recv_sem, where):
    return pltpu.make_async_remote_copy(
        src_ref=src,
        dst_ref=dst,
        send_sem=send_sem,
        recv_sem=recv_sem,
        device_id=where,
        device_id_type=pl.DeviceIdType.MESH,
    )


def here():
    shard, z, y = lax.axis_index("shard"), lax.axis_index("ctx"), lax.axis_index("tp")
    return shard // 2, shard % 2, y, z


def interleave(tasks):
    running, turn = [], 0
    while tasks or running:
        running += [task for first, task in tasks if first <= turn]
        tasks = [item for item in tasks if item[0] > turn]
        alive = []
        for task in running:
            try:
                next(task)
                alive.append(task)
            except StopIteration:
                pass
        running, turn = alive, turn + 1


def greet_all(always, sometimes):
    barrier = pltpu.get_barrier_semaphore()
    number = jnp.int32(len(always))
    for peer in always:
        pl.semaphore_signal(barrier, inc=1, device_id=peer, device_id_type=pl.DeviceIdType.MESH)
    for condition, peer in sometimes:

        @pl.when(condition)
        def _():
            pl.semaphore_signal(barrier, inc=1, device_id=peer, device_id_type=pl.DeviceIdType.MESH)

        number = number + condition.astype(jnp.int32)
    pl.semaphore_wait(barrier, number)


class Line:
    SCRATCH = 4

    def __init__(self, z, dealt, to_slots, refs, sems):
        self.z, self.dealt, self.to_slots = z, dealt, to_slots
        self.blocks, self.picked, self.away, self.arrived = refs
        self.send, self.block_recv, self.away_recv = sems
        self.inner = (z == 1) | (z == 2)
        self.outer = (z == 0) | (z == 3)
        self.near = 1 + z // 3
        self.end = jnp.maximum(3 * (z - 1), 0) % 6
        self.middle = 3 - z
        self.far = 3 - self.end
        self.slots = refs[0].shape[1]

    def copy(self, what):
        if what == "own_near":
            block, where, sem = self.z, self.near, 0
        elif what == "own_middle":
            block, where, sem = self.z, self.middle, 0
        elif what == "forward":
            block, where, sem = self.end, self.middle, 1
        else:
            where = self.end
            return remote(self.away, self.arrived, self.send.at[2], self.away_recv, {"ctx": where})
        there = self.blocks.at[block]
        return remote(there, there, self.send.at[sem], self.block_recv.at[block], {"ctx": where})

    def wait_block(self, block):
        there = self.blocks.at[block]
        remote(there, there, self.send.at[0], self.block_recv.at[block], {"ctx": self.middle}).wait_recv()

    def select(self, target, wanted_by, block, start):
        slots = self.slots
        wide = 384 if slots % 384 == 0 else 128

        def body(i, carry):
            lines = pl.ds(pl.multiple_of(i * wide, 128), wide)
            if self.to_slots:
                wanted = self.dealt[pl.ds(pl.multiple_of(wanted_by * slots + i * wide, 128), wide), :]
                offered = block * slots + lax.broadcasted_iota(jnp.int32, (wide, slots), 1)
            else:
                wanted = wanted_by * slots + i * wide + lax.broadcasted_iota(jnp.int32, (wide, slots), 0)
                offered = self.dealt[:, pl.ds(pl.multiple_of(block * slots, 128), slots)]
            chosen = jnp.where(wanted == offered, 1.0, 0.0).astype(BF)
            part = matmul(chosen, self.blocks[block]).astype(BF)
            target[lines, :] = part if start else target[lines, :] + part
            return carry

        lax.fori_loop(0, slots // wide, body, 0)

    def run(self):
        @pl.when(self.outer)
        def _():
            self.copy("own_near").start()

        @pl.when(self.inner)
        def _():
            self.copy("own_middle").start()

        self.select(self.picked, self.z, self.z, True)
        yield

        @pl.when(self.inner)
        def _():
            self.wait_block(self.end)
            self.copy("forward").start()
            self.select(self.picked, self.z, self.end, False)
            self.select(self.away, self.end, self.z, True)

        yield

        @pl.when(self.inner)
        def _():
            self.wait_block(self.middle)
            self.select(self.away, self.end, self.middle, False)
            self.select(self.picked, self.z, self.middle, False)

        yield

        @pl.when(self.inner)
        def _():
            self.wait_block(self.far)
            self.select(self.away, self.end, self.far, False)
            self.copy("away").start()
            self.select(self.picked, self.z, self.far, False)

        yield

        @pl.when(self.outer)
        def _():
            self.copy("away").wait_recv()
            self.picked[...] = self.picked[...] + self.arrived[...]

    def settle(self):
        @pl.when(self.outer)
        def _():
            self.copy("own_near").wait_send()

        @pl.when(self.inner)
        def _():
            self.copy("own_middle").wait_send()
            self.copy("forward").wait_send()
            self.copy("away").wait_send()


def line_scratch(ctx_size, slots, chunks, columns):
    blocks = [pltpu.VMEM((ctx_size, slots, columns), BF) for _ in range(chunks)]
    others = [pltpu.VMEM((slots, columns), BF) for _ in range(3 * chunks)]
    sems = [pltpu.SemaphoreType.DMA((chunks, 3)), pltpu.SemaphoreType.DMA((chunks, ctx_size)), pltpu.SemaphoreType.DMA((chunks,))]
    return blocks + others + sems


def line_of(j, chunks, z, dealt, to_slots, refs):
    blocks, others, sems = refs[:chunks], refs[chunks : 4 * chunks], refs[4 * chunks :]
    return Line(
        z,
        dealt,
        to_slots,
        (blocks[j], others[3 * j], others[3 * j + 1], others[3 * j + 2]),
        (sems[0].at[j], sems[1].at[j], sems[2].at[j]),
    )


PERM = 3


def first_kernel(widths, padded, *refs):
    count = len(widths)
    pieces, (small, tokens, cotangent, dealt_row) = refs[:count], refs[count : count + 4]
    wholes, (small_whole, qkv, cot_rows) = refs[count + 4 : 2 * count + 4], refs[2 * count + 4 : 2 * count + 7]
    rest = refs[2 * count + 7 :]
    weight, window, send, recv, own_sem, small_sem, halo_sem, post_send, post_recv, bring = rest[:10]
    line_refs = rest[10:]
    x, c, y, z = here()
    rows, dim = tokens.shape
    own = rows // 2
    half = dim // 2
    last = 3
    at_x, at_y, at_c = {"shard": 2 * (1 - x) + c}, {"tp": 1 - y}, {"shard": 2 * x + 1 - c}
    left, right = {"ctx": jnp.maximum(z - 1, 0)}, {"ctx": jnp.minimum(z + 1, last)}
    greet_all((at_x, at_y, at_c), ((z > 0, left), (z < last, right)))

    def slot(a, of_y, of_x, of_c, lines=None):
        cols = pl.ds(pl.multiple_of(of_y * widths[a], 128), widths[a])
        depth = wholes[a].shape[2]
        lines = slice(0, depth) if lines is None else slice(lines * depth // 2, (lines + 1) * depth // 2)
        return (weight if a == 0 else wholes[a]).at[of_x, of_c, lines, cols]

    def moves(a):
        table = [
            (pieces[a], slot(a, y, x, c), at_x),
            (pieces[a], slot(a, y, x, c), at_y),
            (pieces[a], slot(a, y, x, c), at_c),
            (slot(a, y, 1 - x, c, 0), slot(a, y, 1 - x, c, 0), at_y),
            (slot(a, 1 - y, x, c, 1), slot(a, 1 - y, x, c, 1), at_x),
            (slot(a, y, 1 - x, c), slot(a, y, 1 - x, c), at_c),
            (slot(a, 1 - y, x, c), slot(a, 1 - y, x, c), at_c),
            (slot(a, 1 - y, 1 - x, c, 0), slot(a, 1 - y, 1 - x, c, 0), at_c),
            (slot(a, 1 - y, 1 - x, c, 1), slot(a, 1 - y, 1 - x, c, 1), at_c),
        ]
        return [remote(s, d, send.at[a, kind], recv.at[a, kind], w) for kind, (s, d, w) in enumerate(table)]

    tables = [moves(a) for a in range(count)]
    depth = small_whole.shape[0] // 2
    small_at = small_whole.at[pl.ds(pl.multiple_of(y * depth, 16), depth)]
    small_copy = remote(small, small_at, small_sem.at[0], small_sem.at[1], at_y)
    sends_right, sends_left = (y == 0) & (z < last), (y == 1) & (z > 0)
    gets_left, gets_right = (y == 0) & (z > 0), (y == 1) & (z < last)

    def halo(where):
        src = tokens.at[pl.ds(pl.multiple_of((1 - y) * (rows - HALO), 64), HALO)]
        dst = window.at[pl.ds(pl.multiple_of(y * (HALO + own), 64), HALO)]
        return remote(src, dst, halo_sem.at[0], halo_sem.at[1], where)

    inside = pltpu.make_async_copy(
        tokens.at[pl.ds(pl.multiple_of(y * (own - HALO), 64), own + HALO)],
        window.at[pl.ds(pl.multiple_of((1 - y) * HALO, 64), own + HALO)],
        halo_sem.at[2],
    )
    small_local = pltpu.make_async_copy(small, small_at, small_sem.at[2])
    piece_local = [pltpu.make_async_copy(pieces[a], slot(a, y, x, c), own_sem.at[a]) for a in range(count)]
    lines = [line_of(j, PERM, z, dealt_row, False, line_refs) for j in range(PERM)]

    def columns_of(j):
        return pl.ds(pl.multiple_of(y * half + j * (half // PERM), 128), half // PERM)

    bring_cot = [
        pltpu.make_async_copy(cotangent.at[:, columns_of(j)], lines[j].blocks.at[z], bring.at[j]) for j in range(PERM)
    ]
    for kind in range(3):
        tables[0][kind].start()
    small_copy.start()

    @pl.when(sends_right)
    def _():
        halo(right).start()

    @pl.when(sends_left)
    def _():
        halo(left).start()

    for item in (small_local, *piece_local, inside, *bring_cot):
        item.start()
    window[padded - (padded - 2 * HALO - own) :, :] = jnp.zeros((padded - 2 * HALO - own, dim), BF)

    @pl.when((y == 0) & (z == 0))
    def _():
        window[:HALO, :] = jnp.zeros((HALO, dim), BF)

    @pl.when((y == 1) & (z == last))
    def _():
        window[HALO + own : 2 * HALO + own, :] = jnp.zeros((HALO, dim), BF)

    def weights_task(a):
        if a:
            for kind in range(3):
                tables[a][kind].start()
            yield
        tables[a][0].wait_recv()
        tables[a][3].start()
        tables[a][5].start()
        tables[a][1].wait_recv()
        tables[a][4].start()
        tables[a][6].start()
        yield
        tables[a][3].wait_recv()
        tables[a][7].start()
        tables[a][4].wait_recv()
        tables[a][8].start()
        yield
        for kind in (2, 5, 6, 7, 8):
            tables[a][kind].wait_recv()
        if a == 0:
            yield from project_task()

    def project_task():
        piece_local[0].wait()
        pltpu.make_async_copy(weight, wholes[0], own_sem.at[0]).start()
        inside.wait()
        small_copy.wait()
        small_local.wait()

        @pl.when(gets_left | gets_right)
        def _():
            halo(left).wait_recv()

        depth_w, width = weight.shape[2], widths[0]
        third = width // 3
        step = 256
        for of_y in range(2):
            bias = small_whole[of_y * depth : of_y * depth + 1, :].astype(F32)
            bias = jnp.concatenate([bias[:, :third], jnp.zeros((1, third), F32), bias[:, third : 2 * third]], axis=1)
            scale = jnp.where(lax.broadcasted_iota(jnp.int32, (1, width), 1) < third, 0.125, 1.0).astype(BF)
            full = jnp.concatenate(
                [weight[i // 2, i % 2, :, of_y * width : (of_y + 1) * width] for i in range(4)], axis=0
            )

            def body(i, carry):
                there = pl.ds(pl.multiple_of(i * step, step), step)
                value = (matmul(window[there, :], full) + bias).astype(BF)
                qkv[there, of_y * width : (of_y + 1) * width] = value * scale
                return carry

            lax.fori_loop(0, padded // step, body, 0)
            yield

    def post(j):
        there = lines[j].picked.at[pl.ds(pl.multiple_of((1 - y) * own, 64), own)]
        return remote(there, cot_rows.at[:, columns_of(j)], post_send.at[j], post_recv.at[j], at_y)

    def cotangent_task(j):
        bring_cot[j].wait()
        yield from lines[j].run()
        post(j).start()
        cot_rows[:, columns_of(j)] = lines[j].picked[pl.ds(pl.multiple_of(y * own, 64), own), :]
        yield
        post(j).wait_recv()

    tasks = [(a, weights_task(a)) for a in range(count)] + [(1 + j, cotangent_task(j)) for j in range(PERM)]
    interleave(sorted(tasks, key=lambda item: item[0]))
    for a in range(count):
        for kind in range(9):
            tables[a][kind].wait_send()
        if a:
            piece_local[a].wait()
    pltpu.make_async_copy(weight, wholes[0], own_sem.at[0]).wait()

    @pl.when(sends_right | sends_left)
    def _():
        halo(left).wait_send()

    for j in range(PERM):
        lines[j].settle()
        post(j).wait_send()


def first_stage(pieces, small, tokens, cotangent, dealt, padded):
    rows, dim = tokens.shape
    depth = pieces[0].shape[0]
    own = rows // 2
    widths = tuple(piece.shape[1] for piece in pieces)
    count = len(pieces)
    ctx_size = lax.axis_size("ctx")
    outs = [jax.ShapeDtypeStruct((2, 2, depth, 2 * width), BF) for width in widths]
    outs += [
        jax.ShapeDtypeStruct((2 * small.shape[0], small.shape[1]), BF),
        jax.ShapeDtypeStruct((padded, 3 * dim), BF),
        jax.ShapeDtypeStruct((own, dim), BF),
    ]
    anywhere, vmem = pl.BlockSpec(memory_space=pl.ANY), pl.BlockSpec(memory_space=pltpu.VMEM)
    result = pl.pallas_call(
        functools.partial(first_kernel, widths, padded),
        out_shape=outs,
        in_specs=[anywhere] * (count + 3) + [vmem],
        out_specs=[anywhere] * count + [vmem] * 3,
        scratch_shapes=[
            pltpu.VMEM((2, 2, depth, 2 * widths[0]), BF),
            pltpu.VMEM((padded, dim), BF),
            pltpu.SemaphoreType.DMA((count, 9)),
            pltpu.SemaphoreType.DMA((count, 9)),
            pltpu.SemaphoreType.DMA((count,)),
            pltpu.SemaphoreType.DMA((3,)),
            pltpu.SemaphoreType.DMA((3,)),
            pltpu.SemaphoreType.DMA((PERM,)),
            pltpu.SemaphoreType.DMA((PERM,)),
            pltpu.SemaphoreType.DMA((PERM,)),
        ]
        + line_scratch(ctx_size, rows, PERM, dim // 2 // PERM),
        compiler_params=pltpu.CompilerParams(
            collective_id=0, has_side_effects=True, vmem_limit_bytes=VMEM_LIMIT
        ),
        cost_estimate=pl.CostEstimate(flops=10000000000, bytes_accessed=100000000, transcendentals=0),
    )(*pieces, small, tokens, cotangent, dealt[None, :])
    whole = [full.reshape(4 * depth, full.shape[3]) for full in result[:count]]
    return whole, result[count], result[count + 1], result[count + 2]


def add_lines(dst, first, second):
    rows = dst.shape[0]
    step = 48 if rows % 48 == 0 else 16

    def body(i, carry):
        lines = pl.ds(pl.multiple_of(i * step, 16), step)
        dst[lines, :] = (first[lines, :].astype(F32) + second[lines, :].astype(F32)).astype(dst.dtype)
        return carry

    lax.fori_loop(0, rows // step, body, 0)


class Reduction:
    def __init__(self, chunks, outs, refs):
        number = len(chunks)
        self.chunks, self.outs = chunks, outs
        self.full, self.by_core, self.by_x, self.by_y, self.plane, self.half_z, self.quarter_z, self.final = (
            refs[i * number : (i + 1) * number] for i in range(8)
        )
        self.send, self.recv = refs[8 * number :]
        self.place = here()
        self.rows = self.full[0].shape[3]

    def peers(self):
        x, c, y, z = self.place
        low, high = z % 2, z // 2
        return (
            {"shard": 2 * x + 1 - c},
            {"shard": 2 * (1 - x) + c},
            {"tp": 1 - y},
            {"ctx": 2 * high + 1 - low},
            {"ctx": 2 * (1 - high) + low},
        )

    def copies(self, k, stage):
        x, c, y, z = self.place
        low, high = z % 2, z // 2
        at_c, at_x, at_y, at_one, at_two = self.peers()
        half, quarter = self.rows // 2, self.rows // 4
        if stage == 0:
            table = [(self.full[k].at[:, :, 1 - c], self.by_core[k], at_c)]
        elif stage == 1:
            table = [
                (self.by_core[k].at[:, 1 - x, :half], self.by_x[k], at_x),
                (self.by_core[k].at[1 - y, :, half:], self.by_y[k], at_y),
            ]
        elif stage == 2:
            table = [
                (self.by_x[k].at[1 - y], self.plane[k].at[0], at_y),
                (self.by_y[k].at[1 - x], self.plane[k].at[1], at_x),
            ]
        elif stage == 3:
            table = [(self.plane[k].at[1 - low], self.half_z[k], at_one)]
        elif stage == 4:
            lines = pl.ds(pl.multiple_of((1 - high) * quarter, 16), quarter)
            table = [(self.half_z[k].at[lines], self.quarter_z[k], at_two)]
        elif stage == 5:
            mine = self.final[k].at[2 * low + high]
            table = [(mine, mine, at_two)]
        else:
            mine = self.final[k].at[pl.ds(2 * low, 2)]
            table = [(mine, mine, at_one)]
        return [
            remote(s, d, self.send.at[k, stage, i], self.recv.at[k, stage, i], w) for i, (s, d, w) in enumerate(table)
        ]

    def absorb(self, k, stage):
        x, c, y, z = self.place
        low, high = z % 2, z // 2
        half, quarter = self.rows // 2, self.rows // 4
        if stage == 0:
            for of_y in range(2):
                for of_x in range(2):
                    there = self.by_core[k].at[of_y, of_x]
                    add_lines(there, there, self.full[k].at[of_y, of_x, c])
        elif stage == 1:
            for i in range(2):
                add_lines(self.by_x[k].at[i], self.by_x[k].at[i], self.by_core[k].at[i, x, pl.ds(0, half)])
                add_lines(self.by_y[k].at[i], self.by_y[k].at[i], self.by_core[k].at[y, i, pl.ds(half, half)])
        elif stage == 2:
            add_lines(self.plane[k].at[0], self.plane[k].at[0], self.by_x[k].at[y])
            add_lines(self.plane[k].at[1], self.plane[k].at[1], self.by_y[k].at[x])
        elif stage == 3:
            add_lines(self.half_z[k], self.half_z[k], self.plane[k].at[low])
        elif stage == 4:
            lines = pl.ds(pl.multiple_of(high * quarter, 16), quarter)
            add_lines(self.final[k].at[2 * low + high], self.quarter_z[k], self.half_z[k].at[lines])
        elif stage == 6:
            a, first, width = self.chunks[k]
            for i in range(4):
                self.outs[a][i * quarter : (i + 1) * quarter, first : first + width] = self.final[k][i].astype(F32)

    def task(self, k, produce):
        produce(k)
        for stage in range(7):
            for item in self.copies(k, stage):
                item.start()
            yield
            for item in self.copies(k, stage):
                item.wait_recv()
            self.absorb(k, stage)

    def settle(self):
        for k in range(len(self.chunks)):
            for stage in range(7):
                for item in self.copies(k, stage):
                    item.wait_send()

    def product(self, k, turned, other, half_columns):
        _, first, width = self.chunks[k]
        for of_y in range(2):
            right = other[:, of_y * half_columns + first : of_y * half_columns + first + width]
            for i in range(4):
                value = matmul(turned[i * self.rows : (i + 1) * self.rows, :], right)
                self.full[k][of_y, i // 2, i % 2] = value.astype(BF)


def reduction_scratch(rows, chunks):
    shapes = [
        lambda w: (2, 2, 2, rows, w),
        lambda w: (2, 2, rows, w),
        lambda w: (2, rows // 2, w),
        lambda w: (2, rows // 2, w),
        lambda w: (2, rows // 2, w),
        lambda w: (rows // 2, w),
        lambda w: (rows // 4, w),
        lambda w: (4, rows // 4, w),
    ]
    scratch = [pltpu.VMEM(shape(width), BF) for shape in shapes for _, _, width in chunks]
    return scratch + [pltpu.SemaphoreType.DMA((len(chunks), 7, 2)), pltpu.SemaphoreType.DMA((len(chunks), 7, 2))]


CHUNK = 384


def chunks_of(widths):
    return tuple((a, first, CHUNK) for a, width in enumerate(widths) for first in range(0, width, CHUNK))


def slots_task(line, j, y, values, out, pre, post_sem, at_y):
    slots = line.slots
    own = slots // 2
    outgoing, pre_send, pre_recv = pre
    post_send, post_recv = post_sem
    width = line.picked.shape[1]
    mine_rows = pl.ds(pl.multiple_of(y * own, 64), own)
    half = out.shape[1] // 2
    outgoing[...] = values(j, 1 - y)
    before = remote(outgoing, line.blocks.at[line.z, mine_rows], pre_send, pre_recv, at_y)
    before.start()
    line.blocks[line.z, mine_rows, :] = values(j, y)
    yield
    before.wait_recv()
    yield from line.run()
    cols = pl.ds(pl.multiple_of(y * half + j * width, 128), width)
    after = remote(line.picked, out.at[:, cols], post_send, post_recv, at_y)
    after.start()
    out[:, cols] = line.picked[...]
    yield
    after.wait_recv()
    before.wait_send()
    after.wait_send()
    line.settle()


def middle_kernel(chunks, padded, *refs):
    first_low, attended, hidden_low, pre_low, second_low, act_low, layer_low, grad, stats, dealt_col = refs[:10]
    outs, layer_out, grad_win, stats_win = refs[10:13], refs[13], refs[14], refs[15]
    rest = refs[16:]
    turned, halo_sem, outgoing, pre_send, pre_recv, post_send, post_recv = (
        rest[0:3],
        rest[3],
        rest[4 : 4 + PERM],
        rest[4 + PERM],
        rest[5 + PERM],
        rest[6 + PERM],
        rest[7 + PERM],
    )
    rest = rest[8 + PERM :]
    line_number = 4 * PERM + 3
    line_refs, reduction_refs = rest[:line_number], rest[line_number:]
    reduction = Reduction(chunks, outs, reduction_refs)
    x, c, y, z = reduction.place
    own, dim = grad.shape
    at_y = {"tp": 1 - y}
    last = 3
    inner = (z == 1) | (z == 2)
    diagonal = {"ctx": jnp.clip(z - 1 + 2 * y, 0, last), "tp": 1 - y}
    has_diagonal = ((y == 0) & (z > 0)) | ((y == 1) & (z < last))
    greet_all(reduction.peers(), ((inner, {"ctx": 3 - z}), (has_diagonal, diagonal)))
    halos = []
    for i, (src, dst) in enumerate(((grad, grad_win), (stats, stats_win))):
        to_y = remote(
            src.at[pl.ds(pl.multiple_of((1 - y) * (own - HALO), 64), HALO)],
            dst.at[pl.ds(pl.multiple_of(y * (HALO + own), 64), HALO)],
            halo_sem.at[i, 0],
            halo_sem.at[i, 1],
            at_y,
        )
        to_diagonal = remote(
            src.at[pl.ds(pl.multiple_of(y * (own - HALO), 64), HALO)],
            dst.at[pl.ds(pl.multiple_of((1 - y) * (HALO + own), 64), HALO)],
            halo_sem.at[i, 2],
            halo_sem.at[i, 3],
            diagonal,
        )
        to_y.start()

        @pl.when(has_diagonal)
        def _():
            to_diagonal.start()

        halos.append((to_y, to_diagonal))
    lines = [line_of(j, PERM, z, dealt_col, True, line_refs) for j in range(PERM)]
    width = dim // 2 // PERM

    def layer_values(j, half):
        return layer_low[:, pl.ds(pl.multiple_of(half * (dim // 2) + j * width, 128), width)]

    factors = ((first_low, attended), (hidden_low, pre_low), (second_low, act_low))

    def produce(k):
        a, first, _ = chunks[k]
        if first == 0:
            turned[a][...] = factors[a][0][...].T
        reduction.product(k, turned[a], factors[a][1], factors[a][1].shape[1] // 2)

    tasks = [(k, reduction.task(k, produce)) for k in range(len(chunks))]
    tasks += [
        (
            2 * j,
            slots_task(
                lines[j],
                j,
                y,
                layer_values,
                layer_out,
                (outgoing[j], pre_send.at[j], pre_recv.at[j]),
                (post_send.at[j], post_recv.at[j]),
                at_y,
            ),
        )
        for j in range(PERM)
    ]
    for src, dst in ((grad, grad_win), (stats, stats_win)):
        dst[HALO : HALO + own, :] = src[...]
        rest_rows = padded - 2 * HALO - own
        dst[2 * HALO + own :, :] = jnp.zeros((rest_rows, dst.shape[1]), dst.dtype)

        @pl.when((y == 0) & (z == 0))
        def _():
            dst[:HALO, :] = jnp.zeros((HALO, dst.shape[1]), dst.dtype)

        @pl.when((y == 1) & (z == last))
        def _():
            dst[HALO + own : 2 * HALO + own, :] = jnp.zeros((HALO, dst.shape[1]), dst.dtype)

    interleave(sorted(tasks, key=lambda item: item[0]))
    for to_y, to_diagonal in halos:
        to_y.wait()

        @pl.when(has_diagonal)
        def _():
            to_diagonal.wait()

    reduction.settle()


def middle_stage(first_low, attended, hidden_low, pre_low, second_low, act_low, layer_low, grad, stats, dealt, padded):
    own, dim = grad.shape
    ctx_size = lax.axis_size("ctx")
    rows = dim // 4
    widths = (attended.shape[1] // 2, pre_low.shape[1] // 2, act_low.shape[1] // 2)
    chunks = chunks_of(widths)
    spec = pl.BlockSpec(memory_space=pltpu.VMEM)
    outs = [jax.ShapeDtypeStruct((rows, width), F32) for width in widths]
    outs += [
        jax.ShapeDtypeStruct((2 * own, dim), BF),
        jax.ShapeDtypeStruct((padded, dim), BF),
        jax.ShapeDtypeStruct((padded, 128), F32),
    ]
    scratch = [pltpu.VMEM((dim, own), BF) for _ in range(3)]
    scratch += [pltpu.SemaphoreType.DMA((2, 4))]
    scratch += [pltpu.VMEM((own, dim // 2 // PERM), BF) for _ in range(PERM)]
    scratch += [pltpu.SemaphoreType.DMA((PERM,)) for _ in range(4)]
    scratch += line_scratch(ctx_size, 2 * own, PERM, dim // 2 // PERM)
    scratch += reduction_scratch(rows, chunks)
    return pl.pallas_call(
        functools.partial(middle_kernel, chunks, padded),
        out_shape=outs,
        in_specs=[spec] * 10,
        out_specs=[spec] * len(outs),
        scratch_shapes=scratch,
        compiler_params=pltpu.CompilerParams(
            collective_id=1, has_side_effects=True, vmem_limit_bytes=VMEM_LIMIT
        ),
        cost_estimate=pl.CostEstimate(flops=20000000000, bytes_accessed=100000000, transcendentals=0),
    )(first_low, attended, hidden_low, pre_low, second_low, act_low, layer_low, grad, stats, dealt[:, None])


def last_kernel(chunks, *refs):
    inputs, qkv_low, weight, grad_first, dealt_col, vector = refs[:6]
    out, tokens_grad, vector_out = refs[6:9]
    rest = refs[9:]
    turned, outgoing, pre_send, pre_recv, post_send, post_recv = (
        rest[0],
        rest[1 : 1 + PERM],
        rest[1 + PERM],
        rest[2 + PERM],
        rest[3 + PERM],
        rest[4 + PERM],
    )
    vector_in, vector_sum, vector_send, vector_recv = rest[5 + PERM : 9 + PERM]
    rest = rest[9 + PERM :]
    line_number = 4 * PERM + 3
    line_refs, reduction_refs = rest[:line_number], rest[line_number:]
    reduction = Reduction(chunks, (out,), reduction_refs)
    x, c, y, z = reduction.place
    own, dim = inputs.shape
    at_y = {"tp": 1 - y}
    inner = (z == 1) | (z == 2)
    peers = reduction.peers()
    greet_all(peers, ((inner, {"ctx": 3 - z}),))
    lines = [line_of(j, PERM, z, dealt_col, True, line_refs) for j in range(PERM)]
    width = dim // 2 // PERM

    def vector_copy(stage):
        return remote(
            vector_sum.at[stage], vector_in.at[stage], vector_send.at[stage], vector_recv.at[stage], peers[stage]
        )

    def vector_task():
        vector_sum[0] = vector[...]
        for stage in range(5):
            vector_copy(stage).start()
            yield
            vector_copy(stage).wait_recv()
            total = vector_sum[stage] + vector_in[stage]
            if stage < 4:
                vector_sum[stage + 1] = total
            else:
                vector_out[...] = total

    def grad_values(j, half):
        first = pl.ds(pl.multiple_of(half * (dim // 2) + j * width, 128), width)
        return (grad_first[:, first] + matmul_second(qkv_low[...], weight[first, :])).astype(BF)

    def produce(k):
        if k == 0:
            turned[...] = inputs[...].T
        reduction.product(k, turned, qkv_low, qkv_low.shape[1] // 2)

    tasks = [
        (
            j,
            slots_task(
                lines[j],
                j,
                y,
                grad_values,
                tokens_grad,
                (outgoing[j], pre_send.at[j], pre_recv.at[j]),
                (post_send.at[j], post_recv.at[j]),
                at_y,
            ),
        )
        for j in range(PERM)
    ]
    tasks += [(k, reduction.task(k, produce)) for k in range(len(chunks))]
    tasks += [(1, vector_task())]
    interleave(sorted(tasks, key=lambda item: item[0]))
    reduction.settle()
    for stage in range(5):
        vector_copy(stage).wait_send()


def last_stage(inputs, qkv_low, weight, grad_first, dealt, vector):
    own, dim = inputs.shape
    ctx_size = lax.axis_size("ctx")
    rows = dim // 4
    width = qkv_low.shape[1] // 2
    chunks = chunks_of((width,))
    spec = pl.BlockSpec(memory_space=pltpu.VMEM)
    outs = [
        jax.ShapeDtypeStruct((rows, width), F32),
        jax.ShapeDtypeStruct((2 * own, dim), BF),
        jax.ShapeDtypeStruct(vector.shape, F32),
    ]
    scratch = [pltpu.VMEM((dim, own), BF)]
    scratch += [pltpu.VMEM((own, dim // 2 // PERM), BF) for _ in range(PERM)]
    scratch += [pltpu.SemaphoreType.DMA((PERM,)) for _ in range(4)]
    scratch += [pltpu.VMEM((5,) + vector.shape, F32), pltpu.VMEM((5,) + vector.shape, F32)]
    scratch += [pltpu.SemaphoreType.DMA((5,)), pltpu.SemaphoreType.DMA((5,))]
    scratch += line_scratch(ctx_size, 2 * own, PERM, dim // 2 // PERM)
    scratch += reduction_scratch(rows, chunks)
    return pl.pallas_call(
        functools.partial(last_kernel, chunks),
        out_shape=outs,
        in_specs=[spec] * 6,
        out_specs=[spec] * len(outs),
        scratch_shapes=scratch,
        compiler_params=pltpu.CompilerParams(
            collective_id=2, has_side_effects=True, vmem_limit_bytes=VMEM_LIMIT
        ),
        cost_estimate=pl.CostEstimate(flops=10000000000, bytes_accessed=100000000, transcendentals=0),
    )(inputs, qkv_low, weight, grad_first, dealt[:, None], vector)


def project_kernel(dim, x_ref, weight, bias, out):
    step = 256
    third = weight.shape[1] // 3

    def body(i, carry):
        lines = pl.ds(pl.multiple_of(i * step, step), step)
        value = (matmul(x_ref[lines, :], weight[...]) + bias[0]).astype(BF)
        scale = jnp.where(lax.broadcasted_iota(jnp.int32, (1, 3 * third), 1) < third, 0.125, 1.0).astype(BF)
        out[lines, :] = value * scale
        return carry

    lax.fori_loop(0, x_ref.shape[0] // step, body, 0)


def project(x_window, weight, bias):
    rows, dim = x_window.shape
    width = 3 * dim // 2
    return pl.pallas_call(
        functools.partial(project_kernel, dim),
        grid=(2,),
        out_shape=jax.ShapeDtypeStruct((rows, 2 * width), BF),
        in_specs=[
            pl.BlockSpec((rows, dim), lambda i: (0, 0)),
            pl.BlockSpec((dim, width), lambda i: (0, i)),
            pl.BlockSpec((1, 1, width), lambda i: (i, 0, 0)),
        ],
        out_specs=pl.BlockSpec((rows, width), lambda i: (0, i)),
        compiler_params=pltpu.CompilerParams(vmem_limit_bytes=VMEM_LIMIT),
        cost_estimate=pl.CostEstimate(flops=6000000000, bytes_accessed=14000000, transcendentals=0),
    )(x_window, weight, bias)


def rows_to_slots(values, dealt, place_z, place_y):
    own, dim = values.shape
    half = dim // 2
    keep = lax.dynamic_slice_in_dim(values, place_y * half, half, axis=1)
    send = lax.dynamic_slice_in_dim(values, (1 - place_y) * half, half, axis=1)
    other = lax.ppermute(send, "tp", [(0, 1), (1, 0)])
    first = jnp.where(place_y == 0, keep, other)
    second = jnp.where(place_y == 0, other, keep)
    block = jnp.concatenate([first, second], axis=0)
    everything = lax.all_gather(block, "ctx", axis=0, tiled=True)
    slots = 2 * own
    mine = lax.dynamic_slice_in_dim(dealt, place_z * slots, slots)
    picked = jnp.take(everything, mine, axis=0, mode="clip")
    other_columns = lax.ppermute(picked, "tp", [(0, 1), (1, 0)])
    return jnp.concatenate(
        [jnp.where(place_y == 0, picked, other_columns), jnp.where(place_y == 0, other_columns, picked)], axis=1
    )


def slots_to_rows(values, dealt, place_z, place_y):
    slots, dim = values.shape
    half, own = dim // 2, slots // 2
    block = lax.dynamic_slice_in_dim(values, place_y * half, half, axis=1)
    everything = lax.all_gather(block, "ctx", axis=0, tiled=True)
    wanted = place_z * slots + lax.broadcasted_iota(jnp.int32, (slots, 1), 0)
    chosen = (wanted == dealt[None, :]).astype(BF)
    picked = matmul(chosen, everything).astype(BF)
    keep = lax.dynamic_slice_in_dim(picked, place_y * own, own, axis=0)
    send = lax.dynamic_slice_in_dim(picked, (1 - place_y) * own, own, axis=0)
    other = lax.ppermute(send, "tp", [(0, 1), (1, 0)])
    return jnp.concatenate([jnp.where(place_y == 0, keep, other), jnp.where(place_y == 0, other, keep)], axis=1)


def per_device(
    tokens,
    cotangent,
    seq_lengths,
    dealing,
    query_weight,
    query_bias,
    key_weight,
    value_weight,
    value_bias,
    output_weight,
    output_bias,
    first_gain,
    first_shift,
    up_weight,
    up_bias,
    down_weight,
    down_bias,
    second_gain,
    second_shift,
):
    rows, dim = tokens.shape
    ctx_size, tp_size = lax.axis_size("ctx"), lax.axis_size("tp")
    group_rows = rows * ctx_size
    own = rows // tp_size
    place_z, place_y = lax.axis_index("ctx"), lax.axis_index("tp")
    window = HALO + own + HALO
    padded = -(-window // BLOCK) * BLOCK
    dealt = dealing[0]

    lengths = seq_lengths[0]
    number = lengths.shape[0]
    upto = jnp.arange(number)[:, None] >= jnp.arange(number)[None, :]
    ends = jnp.sum(jnp.where(upto, lengths[None, :], 0), axis=1)
    starts = ends - lengths
    first_row = place_z * rows + place_y * own
    index = jnp.arange(padded, dtype=jnp.int32)
    position = first_row - HALO + index
    valid = (position >= 0) & (position < group_rows) & (index < window)
    segment = jnp.sum((position[:, None] >= ends[None, :-1]).astype(jnp.int32), axis=1)
    segment = jnp.where(valid, segment, -1)
    seg_row, seg_col = segment[None, :], segment[:, None]
    tile = attention_tile(own)
    tile_first = first_row + tile * jnp.arange(own // tile, dtype=jnp.int32)
    tile_last = tile_first + tile - 1
    begin = jnp.max(jnp.where(starts[None, :] <= tile_first[:, None], starts[None, :], 0), axis=1)
    finish = jnp.min(jnp.where(ends[None, :] > tile_last[:, None], ends[None, :], group_rows), axis=1)
    shift = HALO - first_row
    bounds = jnp.stack([(begin + shift) // BLOCK, (finish + shift + BLOCK - 1) // BLOCK], axis=1).astype(jnp.int32)

    special = lax.axis_size("shard") == 4 and tp_size == 2 and ctx_size == 4
    half_dim = dim // tp_size
    pieces = [
        jnp.concatenate([query_weight, key_weight, value_weight], axis=1),
        output_weight.T,
        up_weight,
        down_weight.T,
    ]
    flat = jnp.concatenate([query_bias, value_bias, up_bias])
    small = jnp.broadcast_to(flat[None, :], (16, flat.shape[0]))
    inputs = lax.dynamic_slice_in_dim(tokens, place_y * own, own, axis=0)
    if special:
        whole, biases, qkv, cot_rows = first_stage(pieces, small, tokens, cotangent, dealt, padded)
        whole_up_bias = biases[::16, dim:].reshape(-1).astype(F32)
    else:
        whole = [
            lax.all_gather(lax.all_gather(piece, "shard", axis=0, tiled=True), "tp", axis=1, tiled=True)
            for piece in pieces
        ]
        biases = lax.all_gather(small, "tp", axis=0, tiled=True)[::16].astype(F32)
        qkv_bias = jnp.concatenate(
            [biases[:, :half_dim], jnp.zeros((tp_size, half_dim), F32), biases[:, half_dim:dim]], axis=1
        )[:, None, :]
        whole_up_bias = biases[:, dim:].reshape(-1)
        edge = jnp.where(place_y == 0, tokens[rows - HALO :], tokens[:HALO])
        hops = [(2 * z, 2 * z + 2) for z in range(ctx_size - 1)] + [(2 * z + 1, 2 * z - 1) for z in range(1, ctx_size)]
        arrived = lax.ppermute(edge, ("ctx", "tp"), hops)
        x_window = jnp.where(
            place_y == 0,
            jnp.concatenate([arrived, tokens[: own + HALO]], axis=0),
            jnp.concatenate([tokens[own - HALO :], arrived], axis=0),
        )
        x_window = jnp.pad(x_window, ((0, padded - window), (0, 0)))
        qkv = project(x_window, whole[0], qkv_bias)
        cot_rows = slots_to_rows(cotangent, dealt, place_z, place_y)
    wide_qkv, wide_output, wide_up, wide_down = whole
    output_bias = output_bias.astype(F32)
    first_gain = first_gain.astype(F32)
    first_shift = first_shift.astype(F32)
    down_bias = down_bias.astype(F32)
    second_gain = second_gain.astype(F32)
    second_shift = second_shift.astype(F32)

    attended, logsum = attention_forward(qkv, seg_col, seg_row, bounds, own, dim)
    grad_out = cot_rows.astype(F32)
    hidden_one, normed_one, inverse_one = norm_forward(
        inputs.astype(F32) + matmul_second(attended, wide_output) + output_bias, first_gain, first_shift
    )
    hidden_low = hidden_one.astype(BF)
    pre_act = matmul(hidden_low, wide_up) + whole_up_bias
    erf_part = 0.5 * (1.0 + jax.scipy.special.erf(pre_act * HALF_ROOT))
    act_low = (pre_act * erf_part).astype(BF)
    layer_value, normed_two, inverse_two = norm_forward(
        hidden_one + matmul_second(act_low, wide_down) + down_bias, second_gain, second_shift
    )
    layer_low = layer_value.astype(BF)

    second_shift_grad = jnp.sum(grad_out, axis=0)
    second_gain_grad = jnp.sum(grad_out * normed_two, axis=0)
    grad_second = norm_backward(grad_out, normed_two, inverse_two, second_gain)
    down_bias_grad = jnp.sum(grad_second, axis=0)
    second_low = grad_second.astype(BF)
    slope = erf_part + pre_act * DENSITY * jnp.exp(-0.5 * pre_act * pre_act)
    grad_pre = matmul(second_low, wide_down) * slope
    up_bias_grad = jnp.sum(grad_pre, axis=0)
    pre_low = grad_pre.astype(BF)
    grad_hidden = grad_second + matmul_second(pre_low, wide_up)
    first_shift_grad = jnp.sum(grad_hidden, axis=0)
    first_gain_grad = jnp.sum(grad_hidden * normed_one, axis=0)
    grad_first = norm_backward(grad_hidden, normed_one, inverse_one, first_gain)
    output_bias_grad = jnp.sum(grad_first, axis=0)
    first_low = grad_first.astype(BF)
    attended_grad = matmul(first_low, wide_output).astype(BF)
    delta = jnp.sum(
        (attended_grad.astype(F32) * attended.astype(F32)).reshape(own, dim // HEAD, HEAD), axis=2
    )
    stats = logsum + jnp.pad(delta, ((0, 0), (16, 112 - dim // HEAD)))
    if special:
        output_own, up_own, down_own, layer_out, grad_win, stats_win = middle_stage(
            first_low, attended, hidden_low, pre_low, second_low, act_low, layer_low, attended_grad, stats, dealt, padded
        )
    else:
        layer_out = rows_to_slots(layer_low, dealt, place_z, place_y)
        up_hops = [(i, i + 1) for i in range(ctx_size * tp_size - 1)]
        down_hops = [(i + 1, i) for i in range(ctx_size * tp_size - 1)]
        grad_win, stats_win = [
            jnp.concatenate(
                [
                    lax.ppermute(array[own - HALO :], ("ctx", "tp"), up_hops),
                    array,
                    lax.ppermute(array[:HALO], ("ctx", "tp"), down_hops),
                    jnp.zeros((padded - window, array.shape[1]), array.dtype),
                ],
                axis=0,
            )
            for array in (attended_grad, stats)
        ]
    query_low, query_bias_grad = attention_query(qkv, seg_col, seg_row, bounds, attended_grad, stats, dim)
    qkv_low, value_bias_grad = attention_key(
        qkv, seg_col, seg_row, bounds, grad_win, stats_win, query_low, own, dim
    )
    vectors = jnp.concatenate(
        [
            query_bias_grad[0],
            value_bias_grad[0],
            up_bias_grad,
            output_bias_grad,
            first_gain_grad,
            first_shift_grad,
            down_bias_grad,
            second_gain_grad,
            second_shift_grad,
        ]
    )
    if special:
        qkv_own, tokens_grad, small_sum = last_stage(
            inputs, qkv_low, wide_qkv, grad_first, dealt, vectors.reshape(-1, 128)
        )
        small_sum = small_sum.reshape(-1)
        owned = [qkv_own, output_own, up_own, down_own]
    else:
        owned = []
        for full in (
            matmul_first(inputs, qkv_low),
            matmul_first(first_low, attended),
            matmul_first(hidden_low, pre_low),
            matmul_first(second_low, act_low),
        ):
            part = lax.psum_scatter(full.astype(BF), "tp", scatter_dimension=1, tiled=True)
            part = lax.psum_scatter(part, "shard", scatter_dimension=0, tiled=True)
            owned.append(lax.psum(part, "ctx").astype(F32))
        small_sum = lax.psum(vectors, ("shard", "ctx", "tp"))
        tokens_grad = (grad_first + matmul_second(qkv_low, wide_qkv)).astype(BF)
        tokens_grad = rows_to_slots(tokens_grad, dealt, place_z, place_y)
    hidden = up_bias_grad.shape[0]
    sizes = [dim, dim, hidden] + [dim] * 6
    offsets = [sum(sizes[:i]) for i in range(len(sizes))]
    parts = [small_sum[o : o + s] for o, s in zip(offsets, sizes)]

    def by_tp(vector):
        part = vector.shape[0] // tp_size
        return lax.dynamic_slice_in_dim(vector, place_y * part, part)

    return (
        layer_out,
        tokens_grad,
        owned[0][:, :half_dim],
        by_tp(parts[0]),
        owned[0][:, half_dim : 2 * half_dim],
        owned[0][:, 2 * half_dim :],
        by_tp(parts[1]),
        owned[1].T,
        parts[3],
        parts[4],
        parts[5],
        owned[2],
        by_tp(parts[2]),
        owned[3].T,
        parts[6],
        parts[7],
        parts[8],
    )


def solution(mesh):
    return jax.shard_map(
        per_device,
        mesh=mesh,
        in_specs=(
            P(("shard", "ctx"), None),
            P(("shard", "ctx"), None),
            P("shard", None),
            P("shard", None),
            P("shard", "tp"),
            P("tp"),
            P("shard", "tp"),
            P("shard", "tp"),
            P("tp"),
            P("tp", "shard"),
            P(),
            P(),
            P(),
            P("shard", "tp"),
            P("tp"),
            P("tp", "shard"),
            P(),
            P(),
            P(),
        ),
        out_specs=(
            P(("shard", "ctx"), None),
            P(("shard", "ctx"), None),
            P("shard", "tp"),
            P("tp"),
            P("shard", "tp"),
            P("shard", "tp"),
            P("tp"),
            P("tp", "shard"),
            P(),
            P(),
            P(),
            P("shard", "tp"),
            P("tp"),
            P("tp", "shard"),
            P(),
            P(),
            P(),
        ),
        check_vma=False,
    )
```

```python
import functools

import jax
import jax.numpy as jnp
from jax import lax
from jax.experimental import pallas as pl
from jax.experimental.pallas import tpu as pltpu
from jax.sharding import PartitionSpec as P

HEAD = 64
HALO = 512
HALF_ROOT = 0.7071067811865476
DENSITY = 0.3989422804014327
NEG_FILL = -1000000000.0
BF = jnp.bfloat16
F32 = jnp.float32
BLOCK = 256
VMEM_LIMIT = 56 * 1024 * 1024


def matmul(former, latter):
    return jnp.dot(former, latter, preferred_element_type=F32)


def matmul_first(former, latter):
    return lax.dot_general(former, latter, (((0,), (0,)), ((), ())), preferred_element_type=F32)


def matmul_second(former, latter):
    return lax.dot_general(former, latter, (((1,), (1,)), ((), ())), preferred_element_type=F32)


def norm_forward(values, norm_gain, norm_shift):
    centre = values - jnp.mean(values, axis=1, keepdims=True)
    spread = jnp.mean(centre * centre, axis=1, keepdims=True)
    inverse = lax.rsqrt(spread + 1e-06)
    normed = centre * inverse
    return (norm_gain * normed + norm_shift, normed, inverse)


def norm_backward(gradient, normed, inverse, norm_gain):
    scaled = gradient * norm_gain
    bracket = (
        scaled
        - jnp.mean(scaled, axis=1, keepdims=True)
        - normed * jnp.mean(scaled * normed, axis=1, keepdims=True)
    )
    return inverse * bracket


def places(pair, dim):
    half, inner = divmod(pair, dim // 256)
    base = half * (3 * dim // 2) + inner * 128
    return base, base + dim // 2, base + dim


def take(qkv, rows, pair, dim, which):
    first = places(pair, dim)[which]
    return qkv[rows, first : first + 128]


def low_lanes(rows):
    return lax.broadcasted_iota(jnp.int32, (rows, 128), 1) < HEAD


def stacked(pair):
    low = low_lanes(pair.shape[0])
    zero = jnp.zeros_like(pair)
    return jnp.concatenate([jnp.where(low, pair, zero), jnp.where(low, zero, pair)], axis=0)


def unstacked(both):
    rows = both.shape[0] // 2
    return jnp.where(low_lanes(rows), both[:rows], both[rows:])


def bias_of(own_seg, other_seg):
    return jnp.where(own_seg == other_seg, 0.0, NEG_FILL)


def turn_columns(qkv, pair, dim, which, turned):
    turned[pair * 128 : pair * 128 + 128, :] = take(qkv, slice(0, qkv.shape[0]), pair, dim, which).T


def twice(row_pair):
    return jnp.concatenate([row_pair[0:1], row_pair[1:2]], axis=1)


def forward_kernel(dim, tile, bounds, qkv, seg_col, seg_tile, out, logsum, value_t, query_st, bias_ref, acc, top, total):
    pairs = dim // 128
    own = out.shape[0]
    for p in range(pairs):
        turn_columns(qkv, p, dim, 2, value_t)

    def one_tile(i, carry):
        first = pl.multiple_of(i * tile, tile)
        rows = pl.ds(pl.multiple_of(HALO + first, 64), tile)
        seg_here = seg_tile[i]
        for p in range(pairs):
            query_st[p] = stacked(take(qkv, rows, p, dim, 0))
        acc[...] = jnp.zeros_like(acc)
        total[...] = jnp.zeros_like(total)
        top[...] = jnp.full_like(top, 2 * NEG_FILL)

        def one_block(j, inner):
            start = pl.multiple_of(j * BLOCK, BLOCK)
            bias_ref[...] = bias_of(seg_col[pl.ds(start, BLOCK), :], seg_here)
            for p in range(pairs):
                key = take(qkv, pl.ds(start, BLOCK), p, dim, 1)
                scores = matmul_second(key, query_st[p]) + bias_ref[...]
                old = top[p]
                new = jnp.maximum(old, jnp.max(scores, axis=0, keepdims=True))
                keep = jnp.exp(old - new)
                raised = jnp.exp(scores - new)
                total[p] = keep * total[p] + jnp.sum(raised, axis=0, keepdims=True)
                value = value_t[p * 128 : p * 128 + 128, pl.ds(start, BLOCK)]
                acc[p] = keep * acc[p] + matmul(value, raised.astype(BF))
                top[p] = new
            return inner

        lax.fori_loop(bounds[i, 0], bounds[i, 1], one_block, 0)
        for p in range(pairs):
            whole = total[p]
            out[pl.ds(first, tile), p * 128 : p * 128 + 128] = unstacked((acc[p] / whole).T).astype(BF)
            lse = top[p] + jnp.log(whole)
            logsum[i, 2 * p : 2 * p + 1, :] = lse[:, :tile]
            logsum[i, 2 * p + 1 : 2 * p + 2, :] = lse[:, tile:]
        for p in range(2 * pairs, 16):
            logsum[i, p : p + 1, :] = jnp.zeros((1, tile), F32)
        return carry

    lax.fori_loop(0, own // tile, one_tile, 0)


def query_kernel(dim, tile, bounds, qkv, seg_col, seg_tile, grad, stats, out, sums, key_t, query_st, grad_st, bias_ref, acc):
    pairs = dim // 128
    own = out.shape[0]
    for p in range(pairs):
        turn_columns(qkv, p, dim, 1, key_t)

    def one_tile(i, carry):
        first = pl.multiple_of(i * tile, tile)
        own_rows = pl.ds(first, tile)
        rows = pl.ds(pl.multiple_of(HALO + first, 64), tile)
        seg_here = seg_tile[i]
        for p in range(pairs):
            query_st[p] = stacked(take(qkv, rows, p, dim, 0))
            grad_st[p] = stacked(grad[own_rows, p * 128 : p * 128 + 128])
        acc[...] = jnp.zeros_like(acc)

        def one_block(j, inner):
            start = pl.multiple_of(j * BLOCK, BLOCK)
            there = pl.ds(start, BLOCK)
            bias_ref[...] = bias_of(seg_col[there, :], seg_here)
            for p in range(pairs):
                scores = matmul_second(take(qkv, there, p, dim, 1), query_st[p]) + bias_ref[...]
                probs = jnp.exp(scores - twice(stats[i, 2 * p : 2 * p + 2, :]))
                grad_probs = matmul_second(take(qkv, there, p, dim, 2), grad_st[p])
                grad_scores = (probs * (grad_probs - twice(stats[i, 16 + 2 * p : 18 + 2 * p, :]))).astype(BF)
                acc[p] += matmul(key_t[p * 128 : p * 128 + 128, there], grad_scores)
            return inner

        lax.fori_loop(bounds[i, 0], bounds[i, 1], one_block, 0)
        for p in range(pairs):
            part = 0.125 * unstacked(acc[p].T)
            out[own_rows, p * 128 : p * 128 + 128] = part.astype(BF)
            sums[:, p * 128 : p * 128 + 128] += jnp.sum(part, axis=0, keepdims=True)
        return carry

    sums[...] = jnp.zeros_like(sums)
    lax.fori_loop(0, own // tile, one_tile, 0)


def key_kernel(dim, tile, bounds, qkv, seg_col, seg_row, grad, stats, query_low, out, sums, key_st, value_st, bias_ref, key_acc, value_acc):
    pairs = dim // 128
    own = out.shape[0]

    def one_tile(i, carry):
        first = pl.multiple_of(i * tile, tile)
        own_rows = pl.ds(first, tile)
        rows = pl.ds(pl.multiple_of(HALO + first, 64), tile)
        seg_here = seg_col[rows, :]
        for p in range(pairs):
            key_st[p] = stacked(take(qkv, rows, p, dim, 1))
            value_st[p] = stacked(take(qkv, rows, p, dim, 2))
        key_acc[...] = jnp.zeros_like(key_acc)
        value_acc[...] = jnp.zeros_like(value_acc)

        def one_block(j, inner):
            start = pl.multiple_of(j * BLOCK, BLOCK)
            there = pl.ds(start, BLOCK)
            bias_ref[...] = bias_of(seg_here, seg_row[:, there])
            for p in range(pairs):
                query = take(qkv, there, p, dim, 0)
                grad_pair = grad[there, p * 128 : p * 128 + 128]
                scores = matmul_second(key_st[p], query)
                grad_probs = matmul_second(value_st[p], grad_pair)
                probs_all, grads_all = [], []
                for half in range(2):
                    head = 2 * p + half
                    lines = slice(half * tile, half * tile + tile)
                    probs = jnp.exp(scores[lines] + bias_ref[...] - stats[head : head + 1, there])
                    grads_all.append((probs * (grad_probs[lines] - stats[16 + head : 17 + head, there])).astype(BF))
                    probs_all.append(probs.astype(BF))
                key_acc[p] += matmul(jnp.concatenate(grads_all, axis=0), query)
                value_acc[p] += matmul(jnp.concatenate(probs_all, axis=0), grad_pair)
            return inner

        lax.fori_loop(bounds[i, 0], bounds[i, 1], one_block, 0)
        for p in range(pairs):
            at_query, at_key, at_value = places(p, dim)
            out[own_rows, at_query : at_query + 128] = query_low[own_rows, p * 128 : p * 128 + 128]
            out[own_rows, at_key : at_key + 128] = unstacked(key_acc[p]).astype(BF)
            part = unstacked(value_acc[p])
            out[own_rows, at_value : at_value + 128] = part.astype(BF)
            sums[:, p * 128 : p * 128 + 128] += jnp.sum(part, axis=0, keepdims=True)
        return carry

    sums[...] = jnp.zeros_like(sums)
    lax.fori_loop(0, own // tile, one_tile, 0)


def vmem_call(kernel, arrays, bounds, outs, scratch, flops):
    spec = pl.BlockSpec(memory_space=pltpu.VMEM)
    return pl.pallas_call(
        kernel,
        out_shape=outs,
        in_specs=[pl.BlockSpec(memory_space=pltpu.SMEM)] + [spec] * len(arrays),
        out_specs=jax.tree.map(lambda leaf: spec, outs),
        scratch_shapes=scratch,
        compiler_params=pltpu.CompilerParams(vmem_limit_bytes=VMEM_LIMIT),
        cost_estimate=pl.CostEstimate(flops=flops, bytes_accessed=12000000, transcendentals=6000000),
    )(bounds, *arrays)


def attention_tile(own):
    for tile in (192, 128, 64, 32, 16):
        if own % tile == 0:
            return tile
    raise ValueError("rows")


def by_tile(rows_last, own):
    tile = attention_tile(own)
    return rows_last.reshape(rows_last.shape[0], own // tile, tile).transpose(1, 0, 2)


def segments_by_tile(seg_row, own):
    tiles = by_tile(lax.slice_in_dim(seg_row, HALO, HALO + own, axis=1), own)
    return jnp.concatenate([tiles, tiles], axis=2)


def attention_forward(qkv, seg_col, seg_row, bounds, own, dim):
    tile = attention_tile(own)
    pairs = dim // 128
    out, logsum = vmem_call(
        functools.partial(forward_kernel, dim, tile),
        (qkv, seg_col, segments_by_tile(seg_row, own)),
        bounds,
        (jax.ShapeDtypeStruct((own, dim), BF), jax.ShapeDtypeStruct((own // tile, 16, tile), F32)),
        [
            pltpu.VMEM((dim, qkv.shape[0]), BF),
            pltpu.VMEM((pairs, 2 * tile, 128), BF),
            pltpu.VMEM((BLOCK, 2 * tile), F32),
            pltpu.VMEM((pairs, 128, 2 * tile), F32),
            pltpu.VMEM((pairs, 1, 2 * tile), F32),
            pltpu.VMEM((pairs, 1, 2 * tile), F32),
        ],
        10_000_000_000,
    )
    return out, logsum.transpose(1, 0, 2).reshape(16, own)


def attention_query(qkv, seg_col, seg_row, bounds, grad, stats, dim):
    own = grad.shape[0]
    tile = attention_tile(own)
    pairs = dim // 128
    return vmem_call(
        functools.partial(query_kernel, dim, tile),
        (qkv, seg_col, segments_by_tile(seg_row, own), grad, by_tile(stats, own)),
        bounds,
        (jax.ShapeDtypeStruct((own, dim), BF), jax.ShapeDtypeStruct((1, dim), F32)),
        [
            pltpu.VMEM((dim, qkv.shape[0]), BF),
            pltpu.VMEM((pairs, 2 * tile, 128), BF),
            pltpu.VMEM((pairs, 2 * tile, 128), BF),
            pltpu.VMEM((BLOCK, 2 * tile), F32),
            pltpu.VMEM((pairs, 128, 2 * tile), F32),
        ],
        15_000_000_000,
    )


def attention_key(qkv, seg_col, seg_row, bounds, grad_win, stats_win, query_low, own, dim):
    tile = attention_tile(own)
    pairs = dim // 128
    return vmem_call(
        functools.partial(key_kernel, dim, tile),
        (qkv, seg_col, seg_row, grad_win, stats_win, query_low),
        bounds,
        (jax.ShapeDtypeStruct((own, 3 * dim), BF), jax.ShapeDtypeStruct((1, dim), F32)),
        [
            pltpu.VMEM((pairs, 2 * tile, 128), BF),
            pltpu.VMEM((pairs, 2 * tile, 128), BF),
            pltpu.VMEM((tile, BLOCK), F32),
            pltpu.VMEM((pairs, 2 * tile, 128), F32),
            pltpu.VMEM((pairs, 2 * tile, 128), F32),
        ],
        20_000_000_000,
    )


def remote(src, dst, send_sem, recv_sem, where):
    return pltpu.make_async_remote_copy(
        src_ref=src,
        dst_ref=dst,
        send_sem=send_sem,
        recv_sem=recv_sem,
        device_id=where,
        device_id_type=pl.DeviceIdType.MESH,
    )


def here():
    shard, z, y = lax.axis_index("shard"), lax.axis_index("ctx"), lax.axis_index("tp")
    return shard // 2, shard % 2, y, z


def half_of(y, z):
    return (y + z) % 2


def interleave(tasks):
    running, turn = [], 0
    while tasks or running:
        running += [task for first, task in tasks if first <= turn]
        tasks = [item for item in tasks if item[0] > turn]
        alive = []
        for task in running:
            try:
                next(task)
                alive.append(task)
            except StopIteration:
                pass
        running, turn = alive, turn + 1


def greet_all(always, sometimes):
    barrier = pltpu.get_barrier_semaphore()
    number = jnp.int32(len(always))
    for peer in always:
        pl.semaphore_signal(barrier, inc=1, device_id=peer, device_id_type=pl.DeviceIdType.MESH)
    for condition, peer in sometimes:

        @pl.when(condition)
        def _():
            pl.semaphore_signal(barrier, inc=1, device_id=peer, device_id_type=pl.DeviceIdType.MESH)

        number = number + condition.astype(jnp.int32)
    pl.semaphore_wait(barrier, number)


class Line:
    SCRATCH = 4

    def __init__(self, z, dealt, to_slots, refs, sems):
        self.z, self.dealt, self.to_slots = z, dealt, to_slots
        self.blocks, self.picked, self.away, self.arrived = refs
        self.send, self.block_recv, self.away_recv = sems
        self.inner = (z == 1) | (z == 2)
        self.outer = (z == 0) | (z == 3)
        self.near = 1 + z // 3
        self.end = jnp.maximum(3 * (z - 1), 0) % 6
        self.middle = 3 - z
        self.far = 3 - self.end
        self.slots = refs[0].shape[1]

    def copy(self, what):
        if what == "own_near":
            block, where, sem = self.z, self.near, 0
        elif what == "own_middle":
            block, where, sem = self.z, self.middle, 0
        elif what == "forward":
            block, where, sem = self.end, self.middle, 1
        else:
            where = self.end
            return remote(self.away, self.arrived, self.send.at[2], self.away_recv, {"ctx": where})
        there = self.blocks.at[block]
        return remote(there, there, self.send.at[sem], self.block_recv.at[block], {"ctx": where})

    def wait_block(self, block):
        there = self.blocks.at[block]
        remote(there, there, self.send.at[0], self.block_recv.at[block], {"ctx": self.middle}).wait_recv()

    def select(self, target, wanted_by, block, start):
        slots = self.slots
        wide = 384 if slots % 384 == 0 else 128

        def body(i, carry):
            lines = pl.ds(pl.multiple_of(i * wide, 128), wide)
            if self.to_slots:
                wanted = self.dealt[pl.ds(pl.multiple_of(wanted_by * slots + i * wide, 128), wide), :]
                offered = block * slots + lax.broadcasted_iota(jnp.int32, (wide, slots), 1)
            else:
                wanted = wanted_by * slots + i * wide + lax.broadcasted_iota(jnp.int32, (wide, slots), 0)
                offered = self.dealt[:, pl.ds(pl.multiple_of(block * slots, 128), slots)]
            chosen = jnp.where(wanted == offered, 1.0, 0.0).astype(BF)
            part = matmul(chosen, self.blocks[block]).astype(BF)
            target[lines, :] = part if start else target[lines, :] + part
            return carry

        lax.fori_loop(0, slots // wide, body, 0)

    def run(self):
        @pl.when(self.outer)
        def _():
            self.copy("own_near").start()

        @pl.when(self.inner)
        def _():
            self.copy("own_middle").start()

        self.select(self.picked, self.z, self.z, True)
        yield

        @pl.when(self.inner)
        def _():
            self.wait_block(self.end)
            self.copy("forward").start()
            self.select(self.picked, self.z, self.end, False)
            self.select(self.away, self.end, self.z, True)

        yield

        @pl.when(self.inner)
        def _():
            self.wait_block(self.middle)
            self.select(self.away, self.end, self.middle, False)
            self.select(self.picked, self.z, self.middle, False)

        yield

        @pl.when(self.inner)
        def _():
            self.wait_block(self.far)
            self.select(self.away, self.end, self.far, False)
            self.copy("away").start()
            self.select(self.picked, self.z, self.far, False)

        yield

        @pl.when(self.outer)
        def _():
            self.copy("away").wait_recv()
            self.picked[...] = self.picked[...] + self.arrived[...]

    def settle(self):
        @pl.when(self.outer)
        def _():
            self.copy("own_near").wait_send()

        @pl.when(self.inner)
        def _():
            self.copy("own_middle").wait_send()
            self.copy("forward").wait_send()
            self.copy("away").wait_send()


def line_scratch(ctx_size, slots, chunks, columns):
    blocks = [pltpu.VMEM((ctx_size, slots, columns), BF) for _ in range(chunks)]
    others = [pltpu.VMEM((slots, columns), BF) for _ in range(3 * chunks)]
    sems = [pltpu.SemaphoreType.DMA((chunks, 3)), pltpu.SemaphoreType.DMA((chunks, ctx_size)), pltpu.SemaphoreType.DMA((chunks,))]
    return blocks + others + sems


def line_of(j, chunks, z, dealt, to_slots, refs):
    blocks, others, sems = refs[:chunks], refs[chunks : 4 * chunks], refs[4 * chunks :]
    return Line(
        z,
        dealt,
        to_slots,
        (blocks[j], others[3 * j], others[3 * j + 1], others[3 * j + 2]),
        (sems[0].at[j], sems[1].at[j], sems[2].at[j]),
    )


PERM = 3


def first_kernel(widths, padded, *refs):
    count = len(widths)
    pieces, (small, tokens, cotangent, dealt_row) = refs[:count], refs[count : count + 4]
    wholes, (small_whole, qkv, cot_rows) = refs[count + 4 : 2 * count + 4], refs[2 * count + 4 : 2 * count + 7]
    rest = refs[2 * count + 7 :]
    weight, window, send, recv, own_sem, small_sem, halo_sem, post_send, post_recv, bring = rest[:10]
    line_refs = rest[10:]
    x, c, y, z = here()
    h = half_of(y, z)
    rows, dim = tokens.shape
    own = rows // 2
    half = dim // 2
    last = 3
    at_x, at_y, at_c = {"shard": 2 * (1 - x) + c}, {"tp": 1 - y}, {"shard": 2 * x + 1 - c}
    left, right = {"ctx": jnp.maximum(z - 1, 0)}, {"ctx": jnp.minimum(z + 1, last)}
    greet_all((at_x, at_y, at_c), ((z > 0, left), (z < last, right)))

    def slot(a, of_y, of_x, of_c, lines=None):
        cols = pl.ds(pl.multiple_of(of_y * widths[a], 128), widths[a])
        depth = wholes[a].shape[2]
        lines = slice(0, depth) if lines is None else slice(lines * depth // 2, (lines + 1) * depth // 2)
        return (weight if a == 0 else wholes[a]).at[of_x, of_c, lines, cols]

    def moves(a):
        table = [
            (pieces[a], slot(a, y, x, c), at_x),
            (pieces[a], slot(a, y, x, c), at_y),
            (pieces[a], slot(a, y, x, c), at_c),
            (slot(a, y, 1 - x, c, 0), slot(a, y, 1 - x, c, 0), at_y),
            (slot(a, 1 - y, x, c, 1), slot(a, 1 - y, x, c, 1), at_x),
            (slot(a, y, 1 - x, c), slot(a, y, 1 - x, c), at_c),
            (slot(a, 1 - y, x, c), slot(a, 1 - y, x, c), at_c),
            (slot(a, 1 - y, 1 - x, c, 0), slot(a, 1 - y, 1 - x, c, 0), at_c),
            (slot(a, 1 - y, 1 - x, c, 1), slot(a, 1 - y, 1 - x, c, 1), at_c),
        ]
        return [remote(s, d, send.at[a, kind], recv.at[a, kind], w) for kind, (s, d, w) in enumerate(table)]

    tables = [moves(a) for a in range(count)]
    depth = small_whole.shape[0] // 2
    small_at = small_whole.at[pl.ds(pl.multiple_of(y * depth, 16), depth)]
    small_copy = remote(small, small_at, small_sem.at[0], small_sem.at[1], at_y)
    sends_right, sends_left = (h == 1) & (z < last), (h == 0) & (z > 0)
    gets_left, gets_right = (h == 0) & (z > 0), (h == 1) & (z < last)

    def halo(where):
        src = tokens.at[pl.ds(pl.multiple_of(h * (rows - HALO), 64), HALO)]
        dst = window.at[pl.ds(pl.multiple_of((1 - h) * (HALO + own), 64), HALO)]
        return remote(src, dst, halo_sem.at[0], halo_sem.at[1], where)

    inside = pltpu.make_async_copy(
        tokens.at[pl.ds(pl.multiple_of(h * (own - HALO), 64), own + HALO)],
        window.at[pl.ds(pl.multiple_of((1 - h) * HALO, 64), own + HALO)],
        halo_sem.at[2],
    )
    small_local = pltpu.make_async_copy(small, small_at, small_sem.at[2])
    piece_local = [pltpu.make_async_copy(pieces[a], slot(a, y, x, c), own_sem.at[a]) for a in range(count)]
    lines = [line_of(j, PERM, z, dealt_row, False, line_refs) for j in range(PERM)]

    def columns_of(j):
        return pl.ds(pl.multiple_of(y * half + j * (half // PERM), 128), half // PERM)

    bring_cot = [
        pltpu.make_async_copy(cotangent.at[:, columns_of(j)], lines[j].blocks.at[z], bring.at[j]) for j in range(PERM)
    ]
    for kind in range(3):
        tables[0][kind].start()
    small_copy.start()

    @pl.when(sends_right)
    def _():
        halo(right).start()

    @pl.when(sends_left)
    def _():
        halo(left).start()

    for item in (small_local, *piece_local, inside, *bring_cot):
        item.start()
    window[padded - (padded - 2 * HALO - own) :, :] = jnp.zeros((padded - 2 * HALO - own, dim), BF)

    @pl.when((h == 0) & (z == 0))
    def _():
        window[:HALO, :] = jnp.zeros((HALO, dim), BF)

    @pl.when((h == 1) & (z == last))
    def _():
        window[HALO + own : 2 * HALO + own, :] = jnp.zeros((HALO, dim), BF)

    def weights_task(a):
        if a:
            for kind in range(3):
                tables[a][kind].start()
            yield
        tables[a][0].wait_recv()
        tables[a][3].start()
        tables[a][5].start()
        tables[a][1].wait_recv()
        tables[a][4].start()
        tables[a][6].start()
        yield
        tables[a][3].wait_recv()
        tables[a][7].start()
        tables[a][4].wait_recv()
        tables[a][8].start()
        yield
        for kind in (2, 5, 6, 7, 8):
            tables[a][kind].wait_recv()
        if a == 0:
            yield from project_task()

    def project_task():
        piece_local[0].wait()
        pltpu.make_async_copy(weight, wholes[0], own_sem.at[0]).start()
        inside.wait()
        small_copy.wait()
        small_local.wait()

        @pl.when(gets_left | gets_right)
        def _():
            halo(left).wait_recv()

        depth_w, width = weight.shape[2], widths[0]
        third = width // 3
        step = 256
        for of_y in range(2):
            bias = small_whole[of_y * depth : of_y * depth + 1, :].astype(F32)
            bias = jnp.concatenate([bias[:, :third], jnp.zeros((1, third), F32), bias[:, third : 2 * third]], axis=1)
            scale = jnp.where(lax.broadcasted_iota(jnp.int32, (1, width), 1) < third, 0.125, 1.0).astype(BF)
            full = jnp.concatenate(
                [weight[i // 2, i % 2, :, of_y * width : (of_y + 1) * width] for i in range(4)], axis=0
            )

            def body(i, carry):
                there = pl.ds(pl.multiple_of(i * step, step), step)
                value = (matmul(window[there, :], full) + bias).astype(BF)
                qkv[there, of_y * width : (of_y + 1) * width] = value * scale
                return carry

            lax.fori_loop(0, padded // step, body, 0)
            yield

    def post(j):
        there = lines[j].picked.at[pl.ds(pl.multiple_of((1 - h) * own, 64), own)]
        return remote(there, cot_rows.at[:, columns_of(j)], post_send.at[j], post_recv.at[j], at_y)

    def cotangent_task(j):
        bring_cot[j].wait()
        yield from lines[j].run()
        post(j).start()
        cot_rows[:, columns_of(j)] = lines[j].picked[pl.ds(pl.multiple_of(h * own, 64), own), :]
        yield
        post(j).wait_recv()

    tasks = [(a, weights_task(a)) for a in range(count)] + [(1 + j, cotangent_task(j)) for j in range(PERM)]
    interleave(sorted(tasks, key=lambda item: item[0]))
    for a in range(count):
        for kind in range(9):
            tables[a][kind].wait_send()
        if a:
            piece_local[a].wait()
    pltpu.make_async_copy(weight, wholes[0], own_sem.at[0]).wait()

    @pl.when(sends_right | sends_left)
    def _():
        halo(left).wait_send()

    for j in range(PERM):
        lines[j].settle()
        post(j).wait_send()


def first_stage(pieces, small, tokens, cotangent, dealt, padded):
    rows, dim = tokens.shape
    depth = pieces[0].shape[0]
    own = rows // 2
    widths = tuple(piece.shape[1] for piece in pieces)
    count = len(pieces)
    ctx_size = lax.axis_size("ctx")
    outs = [jax.ShapeDtypeStruct((2, 2, depth, 2 * width), BF) for width in widths]
    outs += [
        jax.ShapeDtypeStruct((2 * small.shape[0], small.shape[1]), BF),
        jax.ShapeDtypeStruct((padded, 3 * dim), BF),
        jax.ShapeDtypeStruct((own, dim), BF),
    ]
    anywhere, vmem = pl.BlockSpec(memory_space=pl.ANY), pl.BlockSpec(memory_space=pltpu.VMEM)
    result = pl.pallas_call(
        functools.partial(first_kernel, widths, padded),
        out_shape=outs,
        in_specs=[anywhere] * (count + 3) + [vmem],
        out_specs=[anywhere] * count + [vmem] * 3,
        scratch_shapes=[
            pltpu.VMEM((2, 2, depth, 2 * widths[0]), BF),
            pltpu.VMEM((padded, dim), BF),
            pltpu.SemaphoreType.DMA((count, 9)),
            pltpu.SemaphoreType.DMA((count, 9)),
            pltpu.SemaphoreType.DMA((count,)),
            pltpu.SemaphoreType.DMA((3,)),
            pltpu.SemaphoreType.DMA((3,)),
            pltpu.SemaphoreType.DMA((PERM,)),
            pltpu.SemaphoreType.DMA((PERM,)),
            pltpu.SemaphoreType.DMA((PERM,)),
        ]
        + line_scratch(ctx_size, rows, PERM, dim // 2 // PERM),
        compiler_params=pltpu.CompilerParams(
            collective_id=0, has_side_effects=True, vmem_limit_bytes=VMEM_LIMIT
        ),
        cost_estimate=pl.CostEstimate(flops=10000000000, bytes_accessed=100000000, transcendentals=0),
    )(*pieces, small, tokens, cotangent, dealt[None, :])
    whole = [full.reshape(4 * depth, full.shape[3]) for full in result[:count]]
    return whole, result[count], result[count + 1], result[count + 2]


def add_lines(dst, first, second):
    rows = dst.shape[0]
    step = 48 if rows % 48 == 0 else 16

    def body(i, carry):
        lines = pl.ds(pl.multiple_of(i * step, 16), step)
        dst[lines, :] = (first[lines, :].astype(F32) + second[lines, :].astype(F32)).astype(dst.dtype)
        return carry

    lax.fori_loop(0, rows // step, body, 0)


class Reduction:
    STAGES = 7

    def __init__(self, chunks, outs, refs):
        number = len(chunks)
        self.chunks, self.outs = chunks, outs
        self.full, self.by_core, self.by_x, self.plane, self.from_end, self.half_z, self.final = (
            refs[i * number : (i + 1) * number] for i in range(7)
        )
        self.send, self.recv = refs[7 * number :]
        self.place = here()
        z = self.place[3]
        self.inner, self.outer = (z == 1) | (z == 2), (z == 0) | (z == 3)
        self.near, self.end, self.middle = 1 + z // 3, jnp.maximum(3 * (z - 1), 0) % 6, 3 - z
        self.rows = self.full[0].shape[3]

    def copy(self, k, stage):
        x, c, y, z = self.place
        half = self.rows // 2
        side = z // 2
        if stage == 0:
            src, dst, where = self.full[k].at[:, :, 1 - c], self.by_core[k], {"shard": 2 * x + 1 - c}
        elif stage == 1:
            src, dst, where = self.by_core[k].at[:, 1 - x], self.by_x[k], {"shard": 2 * (1 - x) + c}
        elif stage == 2:
            src, dst, where = self.by_x[k].at[1 - y], self.plane[k], {"tp": 1 - y}
        elif stage == 3:
            src, dst, where = self.plane[k], self.from_end[k], {"ctx": self.near}
        elif stage == 4:
            src = self.plane[k].at[pl.ds(pl.multiple_of((1 - side) * half, 16), half)]
            dst, where = self.half_z[k], {"ctx": self.middle}
        elif stage == 5:
            src = dst = self.final[k].at[pl.ds(pl.multiple_of(side * half, 16), half)]
            where = {"ctx": self.middle}
        else:
            src = dst = self.final[k]
            where = {"ctx": self.end}
        return remote(src, dst, self.send.at[k, stage], self.recv.at[k, stage], where)

    def sender(self, stage):
        return None if stage < 3 else (self.outer if stage == 3 else self.inner)

    def receiver(self, stage):
        return None if stage < 3 else (self.outer if stage == 6 else self.inner)

    def guarded(self, condition, action):
        if condition is None:
            action()
        else:
            pl.when(condition)(action)

    def start(self, k, stage):
        self.guarded(self.sender(stage), lambda: self.copy(k, stage).start())

    def absorb(self, k, stage):
        x, c, y, z = self.place
        half = self.rows // 2
        side = z // 2
        self.copy(k, stage).wait_recv()
        if stage == 0:
            for of_y in range(2):
                for of_x in range(2):
                    there = self.by_core[k].at[of_y, of_x]
                    add_lines(there, there, self.full[k].at[of_y, of_x, c])
        elif stage == 1:
            for i in range(2):
                add_lines(self.by_x[k].at[i], self.by_x[k].at[i], self.by_core[k].at[i, x])
        elif stage == 2:
            add_lines(self.plane[k], self.plane[k], self.by_x[k].at[y])
        elif stage == 3:
            add_lines(self.plane[k], self.plane[k], self.from_end[k])
        elif stage == 4:
            lines = pl.ds(pl.multiple_of(side * half, 16), half)
            add_lines(self.final[k].at[lines], self.half_z[k], self.plane[k].at[lines])

    def task(self, k, produce):
        produce(k)
        for stage in range(self.STAGES):
            self.start(k, stage)
            yield
            self.guarded(self.receiver(stage), lambda: self.absorb(k, stage))
        a, first, width = self.chunks[k]
        self.outs[a][:, first : first + width] = self.final[k][...].astype(F32)

    def settle(self):
        for k in range(len(self.chunks)):
            for stage in range(self.STAGES):
                self.guarded(self.sender(stage), lambda: self.copy(k, stage).wait_send())

    def product(self, k, turned, other, half_columns):
        _, first, width = self.chunks[k]
        for of_y in range(2):
            right = other[:, of_y * half_columns + first : of_y * half_columns + first + width]
            for i in range(4):
                value = matmul(turned[i * self.rows : (i + 1) * self.rows, :], right)
                self.full[k][of_y, i // 2, i % 2] = value.astype(BF)


def reduction_scratch(rows, chunks):
    shapes = [
        lambda w: (2, 2, 2, rows, w),
        lambda w: (2, 2, rows, w),
        lambda w: (2, rows, w),
        lambda w: (rows, w),
        lambda w: (rows, w),
        lambda w: (rows // 2, w),
        lambda w: (rows, w),
    ]
    scratch = [pltpu.VMEM(shape(width), BF) for shape in shapes for _, _, width in chunks]
    return scratch + [pltpu.SemaphoreType.DMA((len(chunks), 7)), pltpu.SemaphoreType.DMA((len(chunks), 7))]


def wide_peers():
    x, c, y, z = here()
    return (
        {"shard": 2 * x + 1 - c},
        {"shard": 2 * (1 - x) + c},
        {"tp": 1 - y},
        {"ctx": z + 1 - 2 * (z % 2)},
    )


CHUNK = 384


def chunks_of(widths):
    return tuple((a, first, CHUNK) for a, width in enumerate(widths) for first in range(0, width, CHUNK))


def slots_task(line, j, y, values, out, pre, post_sem, at_y):
    slots = line.slots
    own = slots // 2
    outgoing, pre_send, pre_recv = pre
    post_send, post_recv = post_sem
    width = line.picked.shape[1]
    mine_rows = pl.ds(pl.multiple_of(half_of(y, line.z) * own, 64), own)
    half = out.shape[1] // 2
    outgoing[...] = values(j, 1 - y)
    before = remote(outgoing, line.blocks.at[line.z, mine_rows], pre_send, pre_recv, at_y)
    before.start()
    line.blocks[line.z, mine_rows, :] = values(j, y)
    yield
    before.wait_recv()
    yield from line.run()
    cols = pl.ds(pl.multiple_of(y * half + j * width, 128), width)
    after = remote(line.picked, out.at[:, cols], post_send, post_recv, at_y)
    after.start()
    out[:, cols] = line.picked[...]
    yield
    after.wait_recv()
    before.wait_send()
    after.wait_send()
    line.settle()


def middle_kernel(chunks, *refs):
    first_low, attended, hidden_low, pre_low, second_low, act_low, layer_low, dealt_col = refs[:8]
    outs, layer_out = refs[8:11], refs[11]
    rest = refs[12:]
    turned, outgoing, pre_send, pre_recv, post_send, post_recv = (
        rest[0:3],
        rest[3 : 3 + PERM],
        rest[3 + PERM],
        rest[4 + PERM],
        rest[5 + PERM],
        rest[6 + PERM],
    )
    rest = rest[7 + PERM :]
    line_number = 4 * PERM + 3
    line_refs, reduction_refs = rest[:line_number], rest[line_number:]
    reduction = Reduction(chunks, outs, reduction_refs)
    x, c, y, z = reduction.place
    dim = layer_low.shape[1]
    at_y = {"tp": 1 - y}
    greet_all(wide_peers(), ((reduction.inner, {"ctx": 3 - z}),))
    lines = [line_of(j, PERM, z, dealt_col, True, line_refs) for j in range(PERM)]
    width = dim // 2 // PERM

    def layer_values(j, half):
        return layer_low[:, pl.ds(pl.multiple_of(half * (dim // 2) + j * width, 128), width)]

    factors = ((first_low, attended), (hidden_low, pre_low), (second_low, act_low))

    def produce(k):
        a, first, _ = chunks[k]
        if first == 0:
            turned[a][...] = factors[a][0][...].T
        reduction.product(k, turned[a], factors[a][1], factors[a][1].shape[1] // 2)

    tasks = [(k, reduction.task(k, produce)) for k in range(len(chunks))]
    tasks += [
        (
            2 * j,
            slots_task(
                lines[j],
                j,
                y,
                layer_values,
                layer_out,
                (outgoing[j], pre_send.at[j], pre_recv.at[j]),
                (post_send.at[j], post_recv.at[j]),
                at_y,
            ),
        )
        for j in range(PERM)
    ]
    interleave(sorted(tasks, key=lambda item: item[0]))
    reduction.settle()


def middle_stage(first_low, attended, hidden_low, pre_low, second_low, act_low, layer_low, dealt):
    own, dim = layer_low.shape
    ctx_size = lax.axis_size("ctx")
    rows = dim // 4
    widths = (attended.shape[1] // 2, pre_low.shape[1] // 2, act_low.shape[1] // 2)
    chunks = chunks_of(widths)
    spec = pl.BlockSpec(memory_space=pltpu.VMEM)
    outs = [jax.ShapeDtypeStruct((rows, width), F32) for width in widths]
    outs += [
        jax.ShapeDtypeStruct((2 * own, dim), BF),
    ]
    scratch = [pltpu.VMEM((dim, own), BF) for _ in range(3)]
    scratch += [pltpu.VMEM((own, dim // 2 // PERM), BF) for _ in range(PERM)]
    scratch += [pltpu.SemaphoreType.DMA((PERM,)) for _ in range(4)]
    scratch += line_scratch(ctx_size, 2 * own, PERM, dim // 2 // PERM)
    scratch += reduction_scratch(rows, chunks)
    return pl.pallas_call(
        functools.partial(middle_kernel, chunks),
        out_shape=outs,
        in_specs=[spec] * 8,
        out_specs=[spec] * len(outs),
        scratch_shapes=scratch,
        compiler_params=pltpu.CompilerParams(
            collective_id=1, has_side_effects=True, vmem_limit_bytes=VMEM_LIMIT
        ),
        cost_estimate=pl.CostEstimate(flops=20000000000, bytes_accessed=100000000, transcendentals=0),
    )(first_low, attended, hidden_low, pre_low, second_low, act_low, layer_low, dealt[:, None])


def last_kernel(chunks, *refs):
    inputs, qkv_low, weight, grad_first, dealt_col, vector = refs[:6]
    out, tokens_grad, vector_out = refs[6:9]
    rest = refs[9:]
    turned, outgoing, pre_send, pre_recv, post_send, post_recv = (
        rest[0],
        rest[1 : 1 + PERM],
        rest[1 + PERM],
        rest[2 + PERM],
        rest[3 + PERM],
        rest[4 + PERM],
    )
    vector_in, vector_sum, vector_send, vector_recv = rest[5 + PERM : 9 + PERM]
    rest = rest[9 + PERM :]
    line_number = 4 * PERM + 3
    line_refs, reduction_refs = rest[:line_number], rest[line_number:]
    reduction = Reduction(chunks, (out,), reduction_refs)
    x, c, y, z = reduction.place
    own, dim = inputs.shape
    at_y = {"tp": 1 - y}
    inner = (z == 1) | (z == 2)
    peers = wide_peers() + ({"ctx": (z + 2) % 4},)
    greet_all(peers, ((inner, {"ctx": 3 - z}),))
    lines = [line_of(j, PERM, z, dealt_col, True, line_refs) for j in range(PERM)]
    width = dim // 2 // PERM

    def vector_copy(stage):
        return remote(
            vector_sum.at[stage], vector_in.at[stage], vector_send.at[stage], vector_recv.at[stage], peers[stage]
        )

    def vector_task():
        vector_sum[0] = vector[...]
        for stage in range(5):
            vector_copy(stage).start()
            yield
            vector_copy(stage).wait_recv()
            total = vector_sum[stage] + vector_in[stage]
            if stage < 4:
                vector_sum[stage + 1] = total
            else:
                vector_out[...] = total

    def grad_values(j, half):
        first = pl.ds(pl.multiple_of(half * (dim // 2) + j * width, 128), width)
        return (grad_first[:, first] + matmul_second(qkv_low[...], weight[first, :])).astype(BF)

    def produce(k):
        if k == 0:
            turned[...] = inputs[...].T
        reduction.product(k, turned, qkv_low, qkv_low.shape[1] // 2)

    tasks = [
        (
            j,
            slots_task(
                lines[j],
                j,
                y,
                grad_values,
                tokens_grad,
                (outgoing[j], pre_send.at[j], pre_recv.at[j]),
                (post_send.at[j], post_recv.at[j]),
                at_y,
            ),
        )
        for j in range(PERM)
    ]
    tasks += [(k, reduction.task(k, produce)) for k in range(len(chunks))]
    tasks += [(1, vector_task())]
    interleave(sorted(tasks, key=lambda item: item[0]))
    reduction.settle()
    for stage in range(5):
        vector_copy(stage).wait_send()


def last_stage(inputs, qkv_low, weight, grad_first, dealt, vector):
    own, dim = inputs.shape
    ctx_size = lax.axis_size("ctx")
    rows = dim // 4
    width = qkv_low.shape[1] // 2
    chunks = chunks_of((width,))
    spec = pl.BlockSpec(memory_space=pltpu.VMEM)
    outs = [
        jax.ShapeDtypeStruct((rows, width), F32),
        jax.ShapeDtypeStruct((2 * own, dim), BF),
        jax.ShapeDtypeStruct(vector.shape, F32),
    ]
    scratch = [pltpu.VMEM((dim, own), BF)]
    scratch += [pltpu.VMEM((own, dim // 2 // PERM), BF) for _ in range(PERM)]
    scratch += [pltpu.SemaphoreType.DMA((PERM,)) for _ in range(4)]
    scratch += [pltpu.VMEM((5,) + vector.shape, F32), pltpu.VMEM((5,) + vector.shape, F32)]
    scratch += [pltpu.SemaphoreType.DMA((5,)), pltpu.SemaphoreType.DMA((5,))]
    scratch += line_scratch(ctx_size, 2 * own, PERM, dim // 2 // PERM)
    scratch += reduction_scratch(rows, chunks)
    return pl.pallas_call(
        functools.partial(last_kernel, chunks),
        out_shape=outs,
        in_specs=[spec] * 6,
        out_specs=[spec] * len(outs),
        scratch_shapes=scratch,
        compiler_params=pltpu.CompilerParams(
            collective_id=2, has_side_effects=True, vmem_limit_bytes=VMEM_LIMIT
        ),
        cost_estimate=pl.CostEstimate(flops=10000000000, bytes_accessed=100000000, transcendentals=0),
    )(inputs, qkv_low, weight, grad_first, dealt[:, None], vector)


def project_kernel(dim, x_ref, weight, bias, out):
    step = 256
    third = weight.shape[1] // 3

    def body(i, carry):
        lines = pl.ds(pl.multiple_of(i * step, step), step)
        value = (matmul(x_ref[lines, :], weight[...]) + bias[0]).astype(BF)
        scale = jnp.where(lax.broadcasted_iota(jnp.int32, (1, 3 * third), 1) < third, 0.125, 1.0).astype(BF)
        out[lines, :] = value * scale
        return carry

    lax.fori_loop(0, x_ref.shape[0] // step, body, 0)


def project(x_window, weight, bias):
    rows, dim = x_window.shape
    width = 3 * dim // 2
    return pl.pallas_call(
        functools.partial(project_kernel, dim),
        grid=(2,),
        out_shape=jax.ShapeDtypeStruct((rows, 2 * width), BF),
        in_specs=[
            pl.BlockSpec((rows, dim), lambda i: (0, 0)),
            pl.BlockSpec((dim, width), lambda i: (0, i)),
            pl.BlockSpec((1, 1, width), lambda i: (i, 0, 0)),
        ],
        out_specs=pl.BlockSpec((rows, width), lambda i: (0, i)),
        compiler_params=pltpu.CompilerParams(vmem_limit_bytes=VMEM_LIMIT),
        cost_estimate=pl.CostEstimate(flops=6000000000, bytes_accessed=14000000, transcendentals=0),
    )(x_window, weight, bias)


def rows_to_slots(values, dealt, place_z, place_y):
    own, dim = values.shape
    half = dim // 2
    keep = lax.dynamic_slice_in_dim(values, place_y * half, half, axis=1)
    send = lax.dynamic_slice_in_dim(values, (1 - place_y) * half, half, axis=1)
    other = lax.ppermute(send, "tp", [(0, 1), (1, 0)])
    first = jnp.where(place_y == 0, keep, other)
    second = jnp.where(place_y == 0, other, keep)
    block = jnp.concatenate([first, second], axis=0)
    everything = lax.all_gather(block, "ctx", axis=0, tiled=True)
    slots = 2 * own
    mine = lax.dynamic_slice_in_dim(dealt, place_z * slots, slots)
    picked = jnp.take(everything, mine, axis=0, mode="clip")
    other_columns = lax.ppermute(picked, "tp", [(0, 1), (1, 0)])
    return jnp.concatenate(
        [jnp.where(place_y == 0, picked, other_columns), jnp.where(place_y == 0, other_columns, picked)], axis=1
    )


def slots_to_rows(values, dealt, place_z, place_y):
    slots, dim = values.shape
    half, own = dim // 2, slots // 2
    block = lax.dynamic_slice_in_dim(values, place_y * half, half, axis=1)
    everything = lax.all_gather(block, "ctx", axis=0, tiled=True)
    wanted = place_z * slots + lax.broadcasted_iota(jnp.int32, (slots, 1), 0)
    chosen = (wanted == dealt[None, :]).astype(BF)
    picked = matmul(chosen, everything).astype(BF)
    keep = lax.dynamic_slice_in_dim(picked, place_y * own, own, axis=0)
    send = lax.dynamic_slice_in_dim(picked, (1 - place_y) * own, own, axis=0)
    other = lax.ppermute(send, "tp", [(0, 1), (1, 0)])
    return jnp.concatenate([jnp.where(place_y == 0, keep, other), jnp.where(place_y == 0, other, keep)], axis=1)


def per_device(
    tokens,
    cotangent,
    seq_lengths,
    dealing,
    query_weight,
    query_bias,
    key_weight,
    value_weight,
    value_bias,
    output_weight,
    output_bias,
    first_gain,
    first_shift,
    up_weight,
    up_bias,
    down_weight,
    down_bias,
    second_gain,
    second_shift,
):
    rows, dim = tokens.shape
    ctx_size, tp_size = lax.axis_size("ctx"), lax.axis_size("tp")
    group_rows = rows * ctx_size
    own = rows // tp_size
    place_z, place_y = lax.axis_index("ctx"), lax.axis_index("tp")
    window = HALO + own + HALO
    padded = -(-window // BLOCK) * BLOCK
    dealt = dealing[0]

    lengths = seq_lengths[0]
    number = lengths.shape[0]
    upto = jnp.arange(number)[:, None] >= jnp.arange(number)[None, :]
    ends = jnp.sum(jnp.where(upto, lengths[None, :], 0), axis=1)
    starts = ends - lengths
    special = lax.axis_size("shard") == 4 and tp_size == 2 and ctx_size == 4
    place_h = half_of(place_y, place_z) if special else place_y
    first_row = place_z * rows + place_h * own
    index = jnp.arange(padded, dtype=jnp.int32)
    position = first_row - HALO + index
    valid = (position >= 0) & (position < group_rows) & (index < window)
    segment = jnp.sum((position[:, None] >= ends[None, :-1]).astype(jnp.int32), axis=1)
    segment = jnp.where(valid, segment, -1)
    seg_row, seg_col = segment[None, :], segment[:, None]
    tile = attention_tile(own)
    tile_first = first_row + tile * jnp.arange(own // tile, dtype=jnp.int32)
    tile_last = tile_first + tile - 1
    begin = jnp.max(jnp.where(starts[None, :] <= tile_first[:, None], starts[None, :], 0), axis=1)
    finish = jnp.min(jnp.where(ends[None, :] > tile_last[:, None], ends[None, :], group_rows), axis=1)
    shift = HALO - first_row
    bounds = jnp.stack([(begin + shift) // BLOCK, (finish + shift + BLOCK - 1) // BLOCK], axis=1).astype(jnp.int32)

    half_dim = dim // tp_size
    pieces = [
        jnp.concatenate([query_weight, key_weight, value_weight], axis=1),
        output_weight.T,
        up_weight,
        down_weight.T,
    ]
    flat = jnp.concatenate([query_bias, value_bias, up_bias])
    small = jnp.broadcast_to(flat[None, :], (16, flat.shape[0]))
    inputs = lax.dynamic_slice_in_dim(tokens, place_h * own, own, axis=0)
    if special:
        whole, biases, qkv, cot_rows = first_stage(pieces, small, tokens, cotangent, dealt, padded)
        whole_up_bias = biases[::16, dim:].reshape(-1).astype(F32)
    else:
        whole = [
            lax.all_gather(lax.all_gather(piece, "shard", axis=0, tiled=True), "tp", axis=1, tiled=True)
            for piece in pieces
        ]
        biases = lax.all_gather(small, "tp", axis=0, tiled=True)[::16].astype(F32)
        qkv_bias = jnp.concatenate(
            [biases[:, :half_dim], jnp.zeros((tp_size, half_dim), F32), biases[:, half_dim:dim]], axis=1
        )[:, None, :]
        whole_up_bias = biases[:, dim:].reshape(-1)
        edge = jnp.where(place_y == 0, tokens[rows - HALO :], tokens[:HALO])
        hops = [(2 * z, 2 * z + 2) for z in range(ctx_size - 1)] + [(2 * z + 1, 2 * z - 1) for z in range(1, ctx_size)]
        arrived = lax.ppermute(edge, ("ctx", "tp"), hops)
        x_window = jnp.where(
            place_y == 0,
            jnp.concatenate([arrived, tokens[: own + HALO]], axis=0),
            jnp.concatenate([tokens[own - HALO :], arrived], axis=0),
        )
        x_window = jnp.pad(x_window, ((0, padded - window), (0, 0)))
        qkv = project(x_window, whole[0], qkv_bias)
        cot_rows = slots_to_rows(cotangent, dealt, place_z, place_y)
    wide_qkv, wide_output, wide_up, wide_down = whole
    output_bias = output_bias.astype(F32)
    first_gain = first_gain.astype(F32)
    first_shift = first_shift.astype(F32)
    down_bias = down_bias.astype(F32)
    second_gain = second_gain.astype(F32)
    second_shift = second_shift.astype(F32)

    attended, logsum = attention_forward(qkv, seg_col, seg_row, bounds, own, dim)
    grad_out = cot_rows.astype(F32)
    hidden_one, normed_one, inverse_one = norm_forward(
        inputs.astype(F32) + matmul_second(attended, wide_output) + output_bias, first_gain, first_shift
    )
    hidden_low = hidden_one.astype(BF)
    pre_act = matmul(hidden_low, wide_up) + whole_up_bias
    erf_part = 0.5 * (1.0 + jax.scipy.special.erf(pre_act * HALF_ROOT))
    act_low = (pre_act * erf_part).astype(BF)
    layer_value, normed_two, inverse_two = norm_forward(
        hidden_one + matmul_second(act_low, wide_down) + down_bias, second_gain, second_shift
    )
    layer_low = layer_value.astype(BF)

    second_shift_grad = jnp.sum(grad_out, axis=0)
    second_gain_grad = jnp.sum(grad_out * normed_two, axis=0)
    grad_second = norm_backward(grad_out, normed_two, inverse_two, second_gain)
    down_bias_grad = jnp.sum(grad_second, axis=0)
    second_low = grad_second.astype(BF)
    slope = erf_part + pre_act * DENSITY * jnp.exp(-0.5 * pre_act * pre_act)
    grad_pre = matmul(second_low, wide_down) * slope
    up_bias_grad = jnp.sum(grad_pre, axis=0)
    pre_low = grad_pre.astype(BF)
    grad_hidden = grad_second + matmul_second(pre_low, wide_up)
    first_shift_grad = jnp.sum(grad_hidden, axis=0)
    first_gain_grad = jnp.sum(grad_hidden * normed_one, axis=0)
    grad_first = norm_backward(grad_hidden, normed_one, inverse_one, first_gain)
    output_bias_grad = jnp.sum(grad_first, axis=0)
    first_low = grad_first.astype(BF)
    attended_grad = matmul(first_low, wide_output).astype(BF)
    head_of = (jnp.arange(dim)[None, :] // HEAD == jnp.arange(16)[:, None]).astype(F32)
    delta = lax.dot_general(
        head_of,
        attended_grad.astype(F32) * attended.astype(F32),
        (((1,), (1,)), ((), ())),
        precision=lax.Precision.HIGHEST,
        preferred_element_type=F32,
    )
    stats = jnp.concatenate([logsum, delta], axis=0)
    if special:
        output_own, up_own, down_own, layer_out = middle_stage(
            first_low, attended, hidden_low, pre_low, second_low, act_low, layer_low, dealt
        )
        path = [2 * (i // 2) + (i + i // 2) % 2 for i in range(2 * ctx_size)]
        attended_grad, stats, up_own = lax.optimization_barrier((attended_grad, stats, up_own))
    else:
        layer_out = rows_to_slots(layer_low, dealt, place_z, place_y)
        path = list(range(ctx_size * tp_size))
    up_hops, down_hops = list(zip(path[:-1], path[1:])), list(zip(path[1:], path[:-1]))
    grad_win, stats_win = [
        jnp.concatenate(
            [
                lax.ppermute(lax.slice_in_dim(array, own - HALO, own, axis=axis), ("ctx", "tp"), up_hops),
                array,
                lax.ppermute(lax.slice_in_dim(array, 0, HALO, axis=axis), ("ctx", "tp"), down_hops),
                jnp.zeros((padded - window, dim) if axis == 0 else (32, padded - window), array.dtype),
            ],
            axis=axis,
        )
        for array, axis in ((attended_grad, 0), (stats, 1))
    ]
    query_low, query_bias_grad = attention_query(qkv, seg_col, seg_row, bounds, attended_grad, stats, dim)
    qkv_low, value_bias_grad = attention_key(
        qkv, seg_col, seg_row, bounds, grad_win, stats_win, query_low, own, dim
    )
    vectors = jnp.concatenate(
        [
            query_bias_grad[0],
            value_bias_grad[0],
            up_bias_grad,
            output_bias_grad,
            first_gain_grad,
            first_shift_grad,
            down_bias_grad,
            second_gain_grad,
            second_shift_grad,
        ]
    )
    if special:
        qkv_own, tokens_grad, small_sum = last_stage(
            inputs, qkv_low, wide_qkv, grad_first, dealt, vectors.reshape(-1, 128)
        )
        small_sum = small_sum.reshape(-1)
        owned = [qkv_own, output_own, up_own, down_own]
    else:
        owned = []
        for full in (
            matmul_first(inputs, qkv_low),
            matmul_first(first_low, attended),
            matmul_first(hidden_low, pre_low),
            matmul_first(second_low, act_low),
        ):
            part = lax.psum_scatter(full.astype(BF), "tp", scatter_dimension=1, tiled=True)
            part = lax.psum_scatter(part, "shard", scatter_dimension=0, tiled=True)
            owned.append(lax.psum(part, "ctx").astype(F32))
        small_sum = lax.psum(vectors, ("shard", "ctx", "tp"))
        tokens_grad = (grad_first + matmul_second(qkv_low, wide_qkv)).astype(BF)
        tokens_grad = rows_to_slots(tokens_grad, dealt, place_z, place_y)
    hidden = up_bias_grad.shape[0]
    sizes = [dim, dim, hidden] + [dim] * 6
    offsets = [sum(sizes[:i]) for i in range(len(sizes))]
    parts = [small_sum[o : o + s] for o, s in zip(offsets, sizes)]

    def by_tp(vector):
        part = vector.shape[0] // tp_size
        return lax.dynamic_slice_in_dim(vector, place_y * part, part)

    return (
        layer_out,
        tokens_grad,
        owned[0][:, :half_dim],
        by_tp(parts[0]),
        owned[0][:, half_dim : 2 * half_dim],
        owned[0][:, 2 * half_dim :],
        by_tp(parts[1]),
        owned[1].T,
        parts[3],
        parts[4],
        parts[5],
        owned[2],
        by_tp(parts[2]),
        owned[3].T,
        parts[6],
        parts[7],
        parts[8],
    )


def solution(mesh):
    return jax.shard_map(
        per_device,
        mesh=mesh,
        in_specs=(
            P(("shard", "ctx"), None),
            P(("shard", "ctx"), None),
            P("shard", None),
            P("shard", None),
            P("shard", "tp"),
            P("tp"),
            P("shard", "tp"),
            P("shard", "tp"),
            P("tp"),
            P("tp", "shard"),
            P(),
            P(),
            P(),
            P("shard", "tp"),
            P("tp"),
            P("tp", "shard"),
            P(),
            P(),
            P(),
        ),
        out_specs=(
            P(("shard", "ctx"), None),
            P(("shard", "ctx"), None),
            P("shard", "tp"),
            P("tp"),
            P("shard", "tp"),
            P("shard", "tp"),
            P("tp"),
            P("tp", "shard"),
            P(),
            P(),
            P(),
            P("shard", "tp"),
            P("tp"),
            P("tp", "shard"),
            P(),
            P(),
            P(),
        ),
        check_vma=False,
    )
```

```python
import functools

import jax
import jax.numpy as jnp
from jax import lax
from jax.experimental import pallas as pl
from jax.experimental.pallas import tpu as pltpu
from jax.sharding import PartitionSpec as P

HEAD = 64
HALO = 512
HALF_ROOT = 0.7071067811865476
DENSITY = 0.3989422804014327
NEG_FILL = -1000000000.0
BF = jnp.bfloat16
F32 = jnp.float32
BLOCK = 256
VMEM_LIMIT = 56 * 1024 * 1024


def matmul(former, latter):
    return jnp.dot(former, latter, preferred_element_type=F32)


def matmul_first(former, latter):
    return lax.dot_general(former, latter, (((0,), (0,)), ((), ())), preferred_element_type=F32)


def matmul_second(former, latter):
    return lax.dot_general(former, latter, (((1,), (1,)), ((), ())), preferred_element_type=F32)


def norm_forward(values, norm_gain, norm_shift):
    centre = values - jnp.mean(values, axis=1, keepdims=True)
    spread = jnp.mean(centre * centre, axis=1, keepdims=True)
    inverse = lax.rsqrt(spread + 1e-06)
    normed = centre * inverse
    return (norm_gain * normed + norm_shift, normed, inverse)


def norm_backward(gradient, normed, inverse, norm_gain):
    scaled = gradient * norm_gain
    bracket = (
        scaled
        - jnp.mean(scaled, axis=1, keepdims=True)
        - normed * jnp.mean(scaled * normed, axis=1, keepdims=True)
    )
    return inverse * bracket


def places(pair, dim):
    half, inner = divmod(pair, dim // 256)
    base = half * (3 * dim // 2) + inner * 128
    return base, base + dim // 2, base + dim


def take(qkv, rows, pair, dim, which):
    first = places(pair, dim)[which]
    return qkv[rows, first : first + 128]


def low_lanes(rows):
    return lax.broadcasted_iota(jnp.int32, (rows, 128), 1) < HEAD


def stacked(pair):
    low = low_lanes(pair.shape[0])
    zero = jnp.zeros_like(pair)
    return jnp.concatenate([jnp.where(low, pair, zero), jnp.where(low, zero, pair)], axis=0)


def unstacked(both):
    rows = both.shape[0] // 2
    return jnp.where(low_lanes(rows), both[:rows], both[rows:])


def bias_of(own_seg, other_seg):
    return jnp.where(own_seg == other_seg, 0.0, NEG_FILL)


def turn_columns(qkv, pair, dim, which, turned):
    turned[pair * 128 : pair * 128 + 128, :] = take(qkv, slice(0, qkv.shape[0]), pair, dim, which).T


def twice(row_pair):
    return jnp.concatenate([row_pair[0:1], row_pair[1:2]], axis=1)


def forward_steps(dim, tile, qkv, seg_col, seg_tile, out, logsum, value_t, query_st, bias_ref, acc, top, total):
    pairs = dim // 128

    def prepare():
        for p in range(pairs):
            turn_columns(qkv, p, dim, 2, value_t)

    def begin(i):
        rows = pl.ds(pl.multiple_of(HALO + i * tile, 64), tile)
        for p in range(pairs):
            query_st[p] = stacked(take(qkv, rows, p, dim, 0))
        acc[...] = jnp.zeros_like(acc)
        total[...] = jnp.zeros_like(total)
        top[...] = jnp.full_like(top, 2 * NEG_FILL)

    def block(i, j):
        start = pl.multiple_of(j * BLOCK, BLOCK)
        bias_ref[...] = bias_of(seg_col[pl.ds(start, BLOCK), :], seg_tile[i])
        for p in range(pairs):
            key = take(qkv, pl.ds(start, BLOCK), p, dim, 1)
            scores = matmul_second(key, query_st[p]) + bias_ref[...]
            old = top[p]
            new = jnp.maximum(old, jnp.max(scores, axis=0, keepdims=True))
            keep = jnp.exp(old - new)
            raised = jnp.exp(scores - new)
            total[p] = keep * total[p] + jnp.sum(raised, axis=0, keepdims=True)
            value = value_t[p * 128 : p * 128 + 128, pl.ds(start, BLOCK)]
            acc[p] = keep * acc[p] + matmul(value, raised.astype(BF))
            top[p] = new

    def finish(i):
        lines = pl.ds(pl.multiple_of(i * tile, tile), tile)
        for p in range(pairs):
            whole = total[p]
            out[lines, p * 128 : p * 128 + 128] = unstacked((acc[p] / whole).T).astype(BF)
            lse = top[p] + jnp.log(whole)
            logsum[i, 2 * p : 2 * p + 1, :] = lse[:, :tile]
            logsum[i, 2 * p + 1 : 2 * p + 2, :] = lse[:, tile:]
        for p in range(2 * pairs, 16):
            logsum[i, p : p + 1, :] = jnp.zeros((1, tile), F32)

    return prepare, begin, block, finish


def query_steps(dim, tile, qkv, seg_col, seg_tile, grad, stats, store, sums, key_t, query_st, grad_st, bias_ref, acc):
    pairs = dim // 128

    def prepare():
        sums[...] = jnp.zeros_like(sums)
        for p in range(pairs):
            turn_columns(qkv, p, dim, 1, key_t)

    def begin(i):
        own_rows = pl.ds(pl.multiple_of(i * tile, tile), tile)
        rows = pl.ds(pl.multiple_of(HALO + i * tile, 64), tile)
        for p in range(pairs):
            query_st[p] = stacked(take(qkv, rows, p, dim, 0))
            grad_st[p] = stacked(grad[own_rows, p * 128 : p * 128 + 128])
        acc[...] = jnp.zeros_like(acc)

    def block(i, j):
        there = pl.ds(pl.multiple_of(j * BLOCK, BLOCK), BLOCK)
        bias_ref[...] = bias_of(seg_col[there, :], seg_tile[i])
        for p in range(pairs):
            scores = matmul_second(take(qkv, there, p, dim, 1), query_st[p]) + bias_ref[...]
            probs = jnp.exp(scores - twice(stats[i, 2 * p : 2 * p + 2, :]))
            grad_probs = matmul_second(take(qkv, there, p, dim, 2), grad_st[p])
            grad_scores = (probs * (grad_probs - twice(stats[i, 16 + 2 * p : 18 + 2 * p, :]))).astype(BF)
            acc[p] += matmul(key_t[p * 128 : p * 128 + 128, there], grad_scores)

    def finish(i):
        own_rows = pl.ds(pl.multiple_of(i * tile, tile), tile)
        for p in range(pairs):
            part = 0.125 * unstacked(acc[p].T)
            store(own_rows, p, part.astype(BF))
            sums[:, p * 128 : p * 128 + 128] += jnp.sum(part, axis=0, keepdims=True)

    return prepare, begin, block, finish


def key_steps(dim, tile, qkv, seg_col, seg_row, grad, stats, out, sums, key_st, value_st, bias_ref, key_acc, value_acc):
    pairs = dim // 128

    def prepare():
        sums[...] = jnp.zeros_like(sums)

    def begin(i):
        rows = pl.ds(pl.multiple_of(HALO + i * tile, 64), tile)
        for p in range(pairs):
            key_st[p] = stacked(take(qkv, rows, p, dim, 1))
            value_st[p] = stacked(take(qkv, rows, p, dim, 2))
        key_acc[...] = jnp.zeros_like(key_acc)
        value_acc[...] = jnp.zeros_like(value_acc)

    def block(i, j):
        there = pl.ds(pl.multiple_of(j * BLOCK, BLOCK), BLOCK)
        seg_here = seg_col[pl.ds(pl.multiple_of(HALO + i * tile, 64), tile), :]
        bias_ref[...] = bias_of(seg_here, seg_row[:, there])
        for p in range(pairs):
            query = take(qkv, there, p, dim, 0)
            grad_pair = grad[there, p * 128 : p * 128 + 128]
            scores = matmul_second(key_st[p], query)
            grad_probs = matmul_second(value_st[p], grad_pair)
            probs_all, grads_all = [], []
            for half in range(2):
                head = 2 * p + half
                lines = slice(half * tile, half * tile + tile)
                probs = jnp.exp(scores[lines] + bias_ref[...] - stats[head : head + 1, there])
                grads_all.append((probs * (grad_probs[lines] - stats[16 + head : 17 + head, there])).astype(BF))
                probs_all.append(probs.astype(BF))
            key_acc[p] += matmul(jnp.concatenate(grads_all, axis=0), query)
            value_acc[p] += matmul(jnp.concatenate(probs_all, axis=0), grad_pair)

    def finish(i):
        own_rows = pl.ds(pl.multiple_of(i * tile, tile), tile)
        for p in range(pairs):
            _, at_key, at_value = places(p, dim)
            out[own_rows, at_key : at_key + 128] = unstacked(key_acc[p]).astype(BF)
            part = unstacked(value_acc[p])
            out[own_rows, at_value : at_value + 128] = part.astype(BF)
            sums[:, p * 128 : p * 128 + 128] += jnp.sum(part, axis=0, keepdims=True)

    return prepare, begin, block, finish


def run_dynamic(steps, bounds, tiles):
    prepare, begin, block, finish = steps
    prepare()

    def one_tile(i, carry):
        begin(i)

        def one_block(j, inner):
            block(i, j)
            return inner

        lax.fori_loop(bounds[i, 0], bounds[i, 1], one_block, 0)
        finish(i)
        return carry

    lax.fori_loop(0, tiles, one_tile, 0)


PIECE = 2


def run_static(steps, tile, tiles):
    prepare, begin, block, finish = steps
    prepare()
    yield
    for i in range(tiles):
        first = (HALO + i * tile - HALO + 1) // BLOCK
        after = -(-(HALO + i * tile + tile + HALO - 1) // BLOCK)
        begin(i)
        for piece in range(first, after, PIECE):

            def one_block(j, inner):
                block(i, j)
                return inner

            lax.fori_loop(piece, min(piece + PIECE, after), one_block, 0)
            if piece + PIECE >= after:
                finish(i)
            yield


def forward_kernel(dim, tile, bounds, *refs):
    run_dynamic(forward_steps(dim, tile, *refs), bounds, refs[3].shape[0] // tile)


def query_kernel(dim, tile, bounds, qkv, seg_col, seg_tile, grad, stats, out, sums, *scratch):
    def store(rows, p, part):
        out[rows, p * 128 : p * 128 + 128] = part

    run_dynamic(
        query_steps(dim, tile, qkv, seg_col, seg_tile, grad, stats, store, sums, *scratch), bounds, out.shape[0] // tile
    )


def key_kernel(dim, tile, bounds, qkv, seg_col, seg_row, grad, stats, query_low, out, sums, *scratch):
    for p in range(dim // 128):
        at_query = places(p, dim)[0]
        out[:, at_query : at_query + 128] = query_low[:, p * 128 : p * 128 + 128]
    run_dynamic(
        key_steps(dim, tile, qkv, seg_col, seg_row, grad, stats, out, sums, *scratch), bounds, out.shape[0] // tile
    )


def vmem_call(kernel, arrays, bounds, outs, scratch, flops):
    spec = pl.BlockSpec(memory_space=pltpu.VMEM)
    return pl.pallas_call(
        kernel,
        out_shape=outs,
        in_specs=[pl.BlockSpec(memory_space=pltpu.SMEM)] + [spec] * len(arrays),
        out_specs=jax.tree.map(lambda leaf: spec, outs),
        scratch_shapes=scratch,
        compiler_params=pltpu.CompilerParams(vmem_limit_bytes=VMEM_LIMIT),
        cost_estimate=pl.CostEstimate(flops=flops, bytes_accessed=12000000, transcendentals=6000000),
    )(bounds, *arrays)


def attention_tile(own):
    for tile in (192, 128, 64, 32, 16):
        if own % tile == 0:
            return tile
    raise ValueError("rows")


def by_tile(rows_last, own):
    tile = attention_tile(own)
    return rows_last.reshape(rows_last.shape[0], own // tile, tile).transpose(1, 0, 2)


def segments_by_tile(seg_row, own):
    tiles = by_tile(lax.slice_in_dim(seg_row, HALO, HALO + own, axis=1), own)
    return jnp.concatenate([tiles, tiles], axis=2)


def forward_scratch(padded, tile, dim):
    pairs = dim // 128
    return [
        pltpu.VMEM((dim, padded), BF),
        pltpu.VMEM((pairs, 2 * tile, 128), BF),
        pltpu.VMEM((BLOCK, 2 * tile), F32),
        pltpu.VMEM((pairs, 128, 2 * tile), F32),
        pltpu.VMEM((pairs, 1, 2 * tile), F32),
        pltpu.VMEM((pairs, 1, 2 * tile), F32),
    ]


def attention_forward(qkv, seg_col, seg_row, bounds, own, dim):
    tile = attention_tile(own)
    pairs = dim // 128
    out, logsum = vmem_call(
        functools.partial(forward_kernel, dim, tile),
        (qkv, seg_col, segments_by_tile(seg_row, own)),
        bounds,
        (jax.ShapeDtypeStruct((own, dim), BF), jax.ShapeDtypeStruct((own // tile, 16, tile), F32)),
        forward_scratch(qkv.shape[0], tile, dim),
        10_000_000_000,
    )
    return out, logsum.transpose(1, 0, 2).reshape(16, own)


def attention_query(qkv, seg_col, seg_row, bounds, grad, stats, dim):
    own = grad.shape[0]
    tile = attention_tile(own)
    pairs = dim // 128
    return vmem_call(
        functools.partial(query_kernel, dim, tile),
        (qkv, seg_col, segments_by_tile(seg_row, own), grad, by_tile(stats, own)),
        bounds,
        (jax.ShapeDtypeStruct((own, dim), BF), jax.ShapeDtypeStruct((1, dim), F32)),
        [
            pltpu.VMEM((dim, qkv.shape[0]), BF),
            pltpu.VMEM((pairs, 2 * tile, 128), BF),
            pltpu.VMEM((pairs, 2 * tile, 128), BF),
            pltpu.VMEM((BLOCK, 2 * tile), F32),
            pltpu.VMEM((pairs, 128, 2 * tile), F32),
        ],
        15_000_000_000,
    )


def attention_key(qkv, seg_col, seg_row, bounds, grad_win, stats_win, query_low, own, dim):
    tile = attention_tile(own)
    pairs = dim // 128
    return vmem_call(
        functools.partial(key_kernel, dim, tile),
        (qkv, seg_col, seg_row, grad_win, stats_win, query_low),
        bounds,
        (jax.ShapeDtypeStruct((own, 3 * dim), BF), jax.ShapeDtypeStruct((1, dim), F32)),
        [
            pltpu.VMEM((pairs, 2 * tile, 128), BF),
            pltpu.VMEM((pairs, 2 * tile, 128), BF),
            pltpu.VMEM((tile, BLOCK), F32),
            pltpu.VMEM((pairs, 2 * tile, 128), F32),
            pltpu.VMEM((pairs, 2 * tile, 128), F32),
        ],
        20_000_000_000,
    )


def remote(src, dst, send_sem, recv_sem, where):
    return pltpu.make_async_remote_copy(
        src_ref=src,
        dst_ref=dst,
        send_sem=send_sem,
        recv_sem=recv_sem,
        device_id=where,
        device_id_type=pl.DeviceIdType.MESH,
    )


def here():
    shard, z, y = lax.axis_index("shard"), lax.axis_index("ctx"), lax.axis_index("tp")
    return shard // 2, shard % 2, y, z


def half_of(y, z):
    return (y + z) % 2


def interleave(tasks):
    running, turn = [], 0
    while tasks or running:
        running += [task for first, task in tasks if first <= turn]
        tasks = [item for item in tasks if item[0] > turn]
        alive = []
        for task in running:
            try:
                next(task)
                alive.append(task)
            except StopIteration:
                pass
        running, turn = alive, turn + 1


def greet_all(always, sometimes):
    barrier = pltpu.get_barrier_semaphore()
    number = jnp.int32(len(always))
    for peer in always:
        pl.semaphore_signal(barrier, inc=1, device_id=peer, device_id_type=pl.DeviceIdType.MESH)
    for condition, peer in sometimes:

        @pl.when(condition)
        def _():
            pl.semaphore_signal(barrier, inc=1, device_id=peer, device_id_type=pl.DeviceIdType.MESH)

        number = number + condition.astype(jnp.int32)
    pl.semaphore_wait(barrier, number)


class Line:
    SCRATCH = 4

    def __init__(self, z, dealt, to_slots, refs, sems):
        self.z, self.dealt, self.to_slots = z, dealt, to_slots
        self.blocks, self.picked, self.away, self.arrived = refs
        self.send, self.block_recv, self.away_recv = sems
        self.inner = (z == 1) | (z == 2)
        self.outer = (z == 0) | (z == 3)
        self.near = 1 + z // 3
        self.end = jnp.maximum(3 * (z - 1), 0) % 6
        self.middle = 3 - z
        self.far = 3 - self.end
        self.slots = refs[0].shape[1]

    def copy(self, what):
        if what == "own_near":
            block, where, sem = self.z, self.near, 0
        elif what == "own_middle":
            block, where, sem = self.z, self.middle, 0
        elif what == "forward":
            block, where, sem = self.end, self.middle, 1
        else:
            where = self.end
            return remote(self.away, self.arrived, self.send.at[2], self.away_recv, {"ctx": where})
        there = self.blocks.at[block]
        return remote(there, there, self.send.at[sem], self.block_recv.at[block], {"ctx": where})

    def wait_block(self, block):
        there = self.blocks.at[block]
        remote(there, there, self.send.at[0], self.block_recv.at[block], {"ctx": self.middle}).wait_recv()

    def select(self, target, wanted_by, block, start):
        slots = self.slots
        wide = 384 if slots % 384 == 0 else 128

        def body(i, carry):
            lines = pl.ds(pl.multiple_of(i * wide, 128), wide)
            if self.to_slots:
                wanted = self.dealt[pl.ds(pl.multiple_of(wanted_by * slots + i * wide, 128), wide), :]
                offered = block * slots + lax.broadcasted_iota(jnp.int32, (wide, slots), 1)
            else:
                wanted = wanted_by * slots + i * wide + lax.broadcasted_iota(jnp.int32, (wide, slots), 0)
                offered = self.dealt[:, pl.ds(pl.multiple_of(block * slots, 128), slots)]
            chosen = jnp.where(wanted == offered, 1.0, 0.0).astype(BF)
            part = matmul(chosen, self.blocks[block]).astype(BF)
            target[lines, :] = part if start else target[lines, :] + part
            return carry

        lax.fori_loop(0, slots // wide, body, 0)

    def run(self):
        @pl.when(self.outer)
        def _():
            self.copy("own_near").start()

        @pl.when(self.inner)
        def _():
            self.copy("own_middle").start()

        self.select(self.picked, self.z, self.z, True)
        yield

        @pl.when(self.inner)
        def _():
            self.wait_block(self.end)
            self.copy("forward").start()
            self.select(self.picked, self.z, self.end, False)
            self.select(self.away, self.end, self.z, True)

        yield

        @pl.when(self.inner)
        def _():
            self.wait_block(self.middle)
            self.select(self.away, self.end, self.middle, False)
            self.select(self.picked, self.z, self.middle, False)

        yield

        @pl.when(self.inner)
        def _():
            self.wait_block(self.far)
            self.select(self.away, self.end, self.far, False)
            self.copy("away").start()
            self.select(self.picked, self.z, self.far, False)

        yield

        @pl.when(self.outer)
        def _():
            self.copy("away").wait_recv()
            self.picked[...] = self.picked[...] + self.arrived[...]

    def settle(self):
        @pl.when(self.outer)
        def _():
            self.copy("own_near").wait_send()

        @pl.when(self.inner)
        def _():
            self.copy("own_middle").wait_send()
            self.copy("forward").wait_send()
            self.copy("away").wait_send()


def line_scratch(ctx_size, slots, chunks, columns):
    blocks = [pltpu.VMEM((ctx_size, slots, columns), BF) for _ in range(chunks)]
    others = [pltpu.VMEM((slots, columns), BF) for _ in range(3 * chunks)]
    sems = [pltpu.SemaphoreType.DMA((chunks, 3)), pltpu.SemaphoreType.DMA((chunks, ctx_size)), pltpu.SemaphoreType.DMA((chunks,))]
    return blocks + others + sems


def line_of(j, chunks, z, dealt, to_slots, refs):
    blocks, others, sems = refs[:chunks], refs[chunks : 4 * chunks], refs[4 * chunks :]
    return Line(
        z,
        dealt,
        to_slots,
        (blocks[j], others[3 * j], others[3 * j + 1], others[3 * j + 2]),
        (sems[0].at[j], sems[1].at[j], sems[2].at[j]),
    )


PERM = 3


FIRST_WAIT = (0, 1, 4, 6)
SECOND_WAIT = (0, 1, 1, 2)
THIRD_WAIT = (0, 1, 1, 1)
COTANGENT_AT = (1, 2, 4)
COTANGENT_PAUSE = 0


def first_kernel(widths, padded, *refs):
    count = len(widths)
    pieces, (small, tokens, cotangent, dealt_row, seg_col, seg_tile) = refs[:count], refs[count : count + 6]
    refs = refs[count + 6 :]
    wholes, (small_whole, qkv, cot_rows, attended, logsum) = refs[:count], refs[count : count + 5]
    rest = refs[count + 5 :]
    attention_refs, rest = rest[:6], rest[6:]
    weight, window, send, recv, own_sem, small_sem, halo_sem, post_send, post_recv, bring = rest[:10]
    line_refs = rest[10:]
    x, c, y, z = here()
    h = half_of(y, z)
    rows, dim = tokens.shape
    own = rows // 2
    half = dim // 2
    last = 3
    tile = attention_tile(own)
    at_x, at_y, at_c = {"shard": 2 * (1 - x) + c}, {"tp": 1 - y}, {"shard": 2 * x + 1 - c}
    left, right = {"ctx": jnp.maximum(z - 1, 0)}, {"ctx": jnp.minimum(z + 1, last)}
    greet_all((at_x, at_y, at_c), ((z > 0, left), (z < last, right)))

    def slot(a, of_y, of_x, of_c, lines=None):
        cols = pl.ds(pl.multiple_of(of_y * widths[a], 128), widths[a])
        depth = wholes[a].shape[2]
        lines = slice(0, depth) if lines is None else slice(lines * depth // 2, (lines + 1) * depth // 2)
        return (weight if a == 0 else wholes[a]).at[of_x, of_c, lines, cols]

    def moves(a):
        table = [
            (pieces[a], slot(a, y, x, c), at_x),
            (pieces[a], slot(a, y, x, c), at_y),
            (pieces[a], slot(a, y, x, c), at_c),
            (slot(a, y, 1 - x, c, 0), slot(a, y, 1 - x, c, 0), at_y),
            (slot(a, 1 - y, x, c, 1), slot(a, 1 - y, x, c, 1), at_x),
            (slot(a, y, 1 - x, c), slot(a, y, 1 - x, c), at_c),
            (slot(a, 1 - y, x, c), slot(a, 1 - y, x, c), at_c),
            (slot(a, 1 - y, 1 - x, c, 0), slot(a, 1 - y, 1 - x, c, 0), at_c),
            (slot(a, 1 - y, 1 - x, c, 1), slot(a, 1 - y, 1 - x, c, 1), at_c),
        ]
        return [remote(s, d, send.at[a, kind], recv.at[a, kind], w) for kind, (s, d, w) in enumerate(table)]

    tables = [moves(a) for a in range(count)]
    depth = small_whole.shape[0] // 2
    small_at = small_whole.at[pl.ds(pl.multiple_of(y * depth, 16), depth)]
    small_copy = remote(small, small_at, small_sem.at[0], small_sem.at[1], at_y)
    sends_right, sends_left = (h == 1) & (z < last), (h == 0) & (z > 0)
    gets_left, gets_right = (h == 0) & (z > 0), (h == 1) & (z < last)

    def halo(where):
        src = tokens.at[pl.ds(pl.multiple_of(h * (rows - HALO), 64), HALO)]
        dst = window.at[pl.ds(pl.multiple_of((1 - h) * (HALO + own), 64), HALO)]
        return remote(src, dst, halo_sem.at[0], halo_sem.at[1], where)

    inside = pltpu.make_async_copy(
        tokens.at[pl.ds(pl.multiple_of(h * (own - HALO), 64), own + HALO)],
        window.at[pl.ds(pl.multiple_of((1 - h) * HALO, 64), own + HALO)],
        halo_sem.at[2],
    )
    small_local = pltpu.make_async_copy(small, small_at, small_sem.at[2])
    piece_local = [pltpu.make_async_copy(pieces[a], slot(a, y, x, c), own_sem.at[a]) for a in range(count)]
    lines = [line_of(j, PERM, z, dealt_row, False, line_refs) for j in range(PERM)]

    def columns_of(j):
        return pl.ds(pl.multiple_of(y * half + j * (half // PERM), 128), half // PERM)

    bring_cot = [
        pltpu.make_async_copy(cotangent.at[:, columns_of(j)], lines[j].blocks.at[z], bring.at[j]) for j in range(PERM)
    ]
    def spread(a):
        for kind in range(3):
            tables[a][kind].start()

    spread(0)
    small_copy.start()

    @pl.when(sends_right)
    def _():
        halo(right).start()

    @pl.when(sends_left)
    def _():
        halo(left).start()

    for item in (small_local, *piece_local, inside, *bring_cot):
        item.start()
    window[padded - (padded - 2 * HALO - own) :, :] = jnp.zeros((padded - 2 * HALO - own, dim), BF)

    @pl.when((h == 0) & (z == 0))
    def _():
        window[:HALO, :] = jnp.zeros((HALO, dim), BF)

    @pl.when((h == 1) & (z == last))
    def _():
        window[HALO + own : 2 * HALO + own, :] = jnp.zeros((HALO, dim), BF)

    def pause(number):
        for _ in range(number):
            yield

    def weights_task(a):
        tables[a][0].wait_recv()
        tables[a][3].start()
        tables[a][5].start()
        tables[a][1].wait_recv()
        tables[a][4].start()
        tables[a][6].start()
        if a + 2 < count:
            spread(a + 2)
        yield
        yield from pause(SECOND_WAIT[a])
        tables[a][3].wait_recv()
        tables[a][7].start()
        tables[a][4].wait_recv()
        tables[a][8].start()
        yield
        yield from pause(THIRD_WAIT[a])
        for kind in (2, 5, 6, 7, 8):
            tables[a][kind].wait_recv()
        if a == 0:
            yield from project_task()
            yield from run_static(
                forward_steps(dim, tile, qkv, seg_col, seg_tile, attended, logsum, *attention_refs), tile, own // tile
            )

    def project_task():
        piece_local[0].wait()
        pltpu.make_async_copy(weight, wholes[0], own_sem.at[0]).start()
        inside.wait()
        small_copy.wait()
        small_local.wait()

        @pl.when(gets_left | gets_right)
        def _():
            halo(left).wait_recv()

        depth_w, width = weight.shape[2], widths[0]
        third = width // 3
        step = 256
        for of_y in range(2):
            bias = small_whole[of_y * depth : of_y * depth + 1, :].astype(F32)
            bias = jnp.concatenate([bias[:, :third], jnp.zeros((1, third), F32), bias[:, third : 2 * third]], axis=1)
            scale = jnp.where(lax.broadcasted_iota(jnp.int32, (1, width), 1) < third, 0.125, 1.0).astype(BF)
            full = jnp.concatenate(
                [weight[i // 2, i % 2, :, of_y * width : (of_y + 1) * width] for i in range(4)], axis=0
            )

            def body(i, carry):
                there = pl.ds(pl.multiple_of(i * step, step), step)
                value = (matmul(window[there, :], full) + bias).astype(BF)
                qkv[there, of_y * width : (of_y + 1) * width] = value * scale
                return carry

            lax.fori_loop(0, padded // step, body, 0)
            yield

    def post(j):
        there = lines[j].picked.at[pl.ds(pl.multiple_of((1 - h) * own, 64), own)]
        return remote(there, cot_rows.at[:, columns_of(j)], post_send.at[j], post_recv.at[j], at_y)

    def cotangent_task(j):
        bring_cot[j].wait()
        for _ in lines[j].run():
            yield
            yield from pause(COTANGENT_PAUSE)
        post(j).start()
        cot_rows[:, columns_of(j)] = lines[j].picked[pl.ds(pl.multiple_of(h * own, 64), own), :]
        yield
        post(j).wait_recv()

    if count > 1:
        spread(1)
    tasks = [(FIRST_WAIT[a], weights_task(a)) for a in range(count)]
    tasks += [(COTANGENT_AT[j], cotangent_task(j)) for j in range(PERM)]
    interleave(sorted(tasks, key=lambda item: item[0]))
    for a in range(count):
        for kind in range(9):
            tables[a][kind].wait_send()
        if a:
            piece_local[a].wait()
    pltpu.make_async_copy(weight, wholes[0], own_sem.at[0]).wait()

    @pl.when(sends_right | sends_left)
    def _():
        halo(left).wait_send()

    for j in range(PERM):
        lines[j].settle()
        post(j).wait_send()


def first_stage(pieces, small, tokens, cotangent, dealt, seg_col, seg_row, padded):
    rows, dim = tokens.shape
    depth = pieces[0].shape[0]
    own = rows // 2
    tile = attention_tile(own)
    widths = tuple(piece.shape[1] for piece in pieces)
    count = len(pieces)
    ctx_size = lax.axis_size("ctx")
    outs = [jax.ShapeDtypeStruct((2, 2, depth, 2 * width), BF) for width in widths]
    outs += [
        jax.ShapeDtypeStruct((2 * small.shape[0], small.shape[1]), BF),
        jax.ShapeDtypeStruct((padded, 3 * dim), BF),
        jax.ShapeDtypeStruct((own, dim), BF),
        jax.ShapeDtypeStruct((own, dim), BF),
        jax.ShapeDtypeStruct((own // tile, 16, tile), F32),
    ]
    anywhere, vmem = pl.BlockSpec(memory_space=pl.ANY), pl.BlockSpec(memory_space=pltpu.VMEM)
    result = pl.pallas_call(
        functools.partial(first_kernel, widths, padded),
        out_shape=outs,
        in_specs=[anywhere] * (count + 3) + [vmem] * 3,
        out_specs=[anywhere] * count + [vmem] * 5,
        scratch_shapes=forward_scratch(padded, tile, dim)
        + [
            pltpu.VMEM((2, 2, depth, 2 * widths[0]), BF),
            pltpu.VMEM((padded, dim), BF),
            pltpu.SemaphoreType.DMA((count, 9)),
            pltpu.SemaphoreType.DMA((count, 9)),
            pltpu.SemaphoreType.DMA((count,)),
            pltpu.SemaphoreType.DMA((3,)),
            pltpu.SemaphoreType.DMA((3,)),
            pltpu.SemaphoreType.DMA((PERM,)),
            pltpu.SemaphoreType.DMA((PERM,)),
            pltpu.SemaphoreType.DMA((PERM,)),
        ]
        + line_scratch(ctx_size, rows, PERM, dim // 2 // PERM),
        compiler_params=pltpu.CompilerParams(
            collective_id=0, has_side_effects=True, vmem_limit_bytes=VMEM_LIMIT
        ),
        cost_estimate=pl.CostEstimate(flops=10000000000, bytes_accessed=100000000, transcendentals=0),
    )(*pieces, small, tokens, cotangent, dealt[None, :], seg_col, segments_by_tile(seg_row, own))
    whole = [full.reshape(4 * depth, full.shape[3]) for full in result[:count]]
    logsum = result[count + 4].transpose(1, 0, 2).reshape(16, own)
    return whole, result[count], result[count + 1], result[count + 2], result[count + 3], logsum


def add_lines(dst, first, second):
    rows = dst.shape[0]
    step = 48 if rows % 48 == 0 else 16

    def body(i, carry):
        lines = pl.ds(pl.multiple_of(i * step, 16), step)
        dst[lines, :] = (first[lines, :].astype(F32) + second[lines, :].astype(F32)).astype(dst.dtype)
        return carry

    lax.fori_loop(0, rows // step, body, 0)


RING = 3


class Reduction:
    STAGES = 7

    def __init__(self, chunks, outs, refs):
        number = len(chunks)
        self.chunks, self.outs = chunks, outs
        ring = min(RING, number)
        self.full = [refs[k % ring] for k in range(number)]
        refs = refs[ring:]
        self.by_core, self.by_x, self.plane, self.from_end, self.half_z, self.final = (
            refs[i * number : (i + 1) * number] for i in range(6)
        )
        self.send, self.recv = refs[6 * number :]
        self.place = here()
        z = self.place[3]
        self.inner, self.outer = (z == 1) | (z == 2), (z == 0) | (z == 3)
        self.near, self.end, self.middle = 1 + z // 3, jnp.maximum(3 * (z - 1), 0) % 6, 3 - z
        self.rows = self.full[0].shape[3]

    def copy(self, k, stage):
        x, c, y, z = self.place
        half = self.rows // 2
        side = z // 2
        if stage == 0:
            src, dst, where = self.full[k].at[:, :, 1 - c], self.by_core[k], {"shard": 2 * x + 1 - c}
        elif stage == 1:
            src, dst, where = self.by_core[k].at[:, 1 - x], self.by_x[k], {"shard": 2 * (1 - x) + c}
        elif stage == 2:
            src, dst, where = self.by_x[k].at[1 - y], self.plane[k], {"tp": 1 - y}
        elif stage == 3:
            src, dst, where = self.plane[k], self.from_end[k], {"ctx": self.near}
        elif stage == 4:
            src = self.plane[k].at[pl.ds(pl.multiple_of((1 - side) * half, 16), half)]
            dst, where = self.half_z[k], {"ctx": self.middle}
        elif stage == 5:
            src = dst = self.final[k].at[pl.ds(pl.multiple_of(side * half, 16), half)]
            where = {"ctx": self.middle}
        else:
            src = dst = self.final[k]
            where = {"ctx": self.end}
        return remote(src, dst, self.send.at[k, stage], self.recv.at[k, stage], where)

    def sender(self, stage):
        return None if stage < 3 else (self.outer if stage == 3 else self.inner)

    def receiver(self, stage):
        return None if stage < 3 else (self.outer if stage == 6 else self.inner)

    def guarded(self, condition, action):
        if condition is None:
            action()
        else:
            pl.when(condition)(action)

    def start(self, k, stage):
        self.guarded(self.sender(stage), lambda: self.copy(k, stage).start())

    def absorb(self, k, stage):
        x, c, y, z = self.place
        half = self.rows // 2
        side = z // 2
        self.copy(k, stage).wait_recv()
        if stage == 0:
            for of_y in range(2):
                for of_x in range(2):
                    there = self.by_core[k].at[of_y, of_x]
                    add_lines(there, there, self.full[k].at[of_y, of_x, c])
            self.copy(k, 0).wait_send()
        elif stage == 1:
            for i in range(2):
                add_lines(self.by_x[k].at[i], self.by_x[k].at[i], self.by_core[k].at[i, x])
        elif stage == 2:
            add_lines(self.plane[k], self.plane[k], self.by_x[k].at[y])
        elif stage == 3:
            add_lines(self.plane[k], self.plane[k], self.from_end[k])
        elif stage == 4:
            lines = pl.ds(pl.multiple_of(side * half, 16), half)
            add_lines(self.final[k].at[lines], self.half_z[k], self.plane[k].at[lines])

    def task(self, k, produce):
        produce(k)
        for stage in range(self.STAGES):
            self.start(k, stage)
            yield
            self.guarded(self.receiver(stage), lambda: self.absorb(k, stage))
        a, first, width = self.chunks[k]
        self.outs[a][:, first : first + width] = self.final[k][...].astype(F32)

    def settle(self):
        for k in range(len(self.chunks)):
            for stage in range(1, self.STAGES):
                self.guarded(self.sender(stage), lambda: self.copy(k, stage).wait_send())

    def product(self, k, turned, other, half_columns):
        _, first, width = self.chunks[k]
        for of_y in range(2):
            right = other[:, of_y * half_columns + first : of_y * half_columns + first + width]
            for i in range(4):
                value = matmul(turned[i * self.rows : (i + 1) * self.rows, :], right)
                self.full[k][of_y, i // 2, i % 2] = value.astype(BF)


def reduction_scratch(rows, chunks):
    shapes = [
        lambda w: (2, 2, rows, w),
        lambda w: (2, rows, w),
        lambda w: (rows, w),
        lambda w: (rows, w),
        lambda w: (rows // 2, w),
        lambda w: (rows, w),
    ]
    scratch = [pltpu.VMEM((2, 2, 2, rows, CHUNK), BF) for _ in range(min(RING, len(chunks)))]
    scratch += [pltpu.VMEM(shape(width), BF) for shape in shapes for _, _, width in chunks]
    return scratch + [pltpu.SemaphoreType.DMA((len(chunks), 7)), pltpu.SemaphoreType.DMA((len(chunks), 7))]


def wide_peers():
    x, c, y, z = here()
    return (
        {"shard": 2 * x + 1 - c},
        {"shard": 2 * (1 - x) + c},
        {"tp": 1 - y},
        {"ctx": z + 1 - 2 * (z % 2)},
    )


CHUNK = 384


def chunks_of(widths):
    return tuple((a, first, CHUNK) for a, width in enumerate(widths) for first in range(0, width, CHUNK))


def slots_task(line, j, y, values, out, pre, post_sem, at_y):
    slots = line.slots
    own = slots // 2
    outgoing, pre_send, pre_recv = pre
    post_send, post_recv = post_sem
    width = line.picked.shape[1]
    mine_rows = pl.ds(pl.multiple_of(half_of(y, line.z) * own, 64), own)
    half = out.shape[1] // 2
    outgoing[...] = values(j, 1 - y)
    before = remote(outgoing, line.blocks.at[line.z, mine_rows], pre_send, pre_recv, at_y)
    before.start()
    line.blocks[line.z, mine_rows, :] = values(j, y)
    yield
    before.wait_recv()
    yield from line.run()
    cols = pl.ds(pl.multiple_of(y * half + j * width, 128), width)
    after = remote(line.picked, out.at[:, cols], post_send, post_recv, at_y)
    after.start()
    out[:, cols] = line.picked[...]
    yield
    after.wait_recv()
    before.wait_send()
    after.wait_send()
    line.settle()


def backward_kernel(chunks, *refs):
    first_low, attended, hidden_low, pre_low, second_low, act_low, grad, stats, stats_tile, qkv, seg_col, seg_row, seg_tile = refs[:13]
    outs, qkv_low, query_sums, value_sums = refs[13:16], refs[16], refs[17], refs[18]
    rest = refs[19:]
    turned, grad_win, stats_side, stats_win, halo_sem = rest[0:3], rest[3], rest[4], rest[5], rest[6]
    key_t, first_st, second_st, bias_query, bias_key, acc, first_acc, second_acc = rest[7:15]
    reduction = Reduction(chunks, outs, rest[15:])
    x, c, y, z = reduction.place
    h = half_of(y, z)
    own, dim = grad.shape
    padded = qkv.shape[0]
    tile = attention_tile(own)
    last = 3
    at_y, at_z = {"tp": 1 - y}, {"ctx": jnp.clip(z - 1 + 2 * h, 0, last)}
    has_z = ((h == 0) & (z > 0)) | ((h == 1) & (z < last))
    greet_all(wide_peers(), ((reduction.inner, {"ctx": 3 - z}),))

    def halos(where, same):
        first = (1 - h) if same else h
        side = h if same else 1 - h
        base = 0 if same else 4
        return (
            remote(
                grad.at[pl.ds(pl.multiple_of(first * (own - HALO), 64), HALO)],
                grad_win.at[pl.ds(pl.multiple_of(side * (HALO + own), 64), HALO)],
                halo_sem.at[base],
                halo_sem.at[base + 1],
                where,
            ),
            remote(stats, stats_side.at[side], halo_sem.at[base + 2], halo_sem.at[base + 3], where),
        )

    for item in halos(at_y, True):
        item.start()

    @pl.when(has_z)
    def _():
        for item in halos(at_z, False):
            item.start()

    grad_win[HALO : HALO + own, :] = grad[...]
    grad_win[2 * HALO + own :, :] = jnp.zeros((padded - 2 * HALO - own, dim), BF)
    for missing, side in (((h == 0) & (z == 0), 0), ((h == 1) & (z == last), 1)):

        @pl.when(missing)
        def _():
            grad_win[side * (HALO + own) : side * (HALO + own) + HALO, :] = jnp.zeros((HALO, dim), BF)
            stats_side[side] = jnp.zeros(stats.shape, F32)

    factors = ((first_low, attended), (hidden_low, pre_low), (second_low, act_low))

    def produce(k):
        a, first, _ = chunks[k]
        if first == 0:
            turned[a][...] = factors[a][0][...].T
        reduction.product(k, turned[a], factors[a][1], factors[a][1].shape[1] // 2)

    def store(rows, p, part):
        at_query = places(p, dim)[0]
        qkv_low[rows, at_query : at_query + 128] = part

    def attention_task():
        yield from run_static(
            query_steps(
                dim, tile, qkv, seg_col, seg_tile, grad, stats_tile, store, query_sums, key_t, first_st, second_st, bias_query, acc
            ),
            tile,
            own // tile,
        )
        for item in halos(at_y, True):
            item.wait()

        @pl.when(has_z)
        def _():
            for item in halos(at_z, False):
                item.wait()

        stats_win[...] = jnp.concatenate(
            [
                stats_side[0][:, own - HALO :],
                stats[...],
                stats_side[1][:, :HALO],
                jnp.zeros((stats.shape[0], padded - 2 * HALO - own), F32),
            ],
            axis=1,
        )
        yield from run_static(
            key_steps(
                dim,
                tile,
                qkv,
                seg_col,
                seg_row,
                grad_win,
                stats_win,
                qkv_low,
                value_sums,
                first_st,
                second_st,
                bias_key,
                first_acc,
                second_acc,
            ),
            tile,
            own // tile,
        )

    tasks = [(k, reduction.task(k, produce)) for k in range(len(chunks))]
    interleave(sorted([(0, attention_task())] + tasks, key=lambda item: item[0]))
    reduction.settle()


def backward_stage(first_low, attended, hidden_low, pre_low, second_low, act_low, grad, stats, qkv, seg_col, seg_row):
    own, dim = grad.shape
    padded = qkv.shape[0]
    rows = dim // 4
    tile = attention_tile(own)
    pairs = dim // 128
    widths = (attended.shape[1] // 2, pre_low.shape[1] // 2, act_low.shape[1] // 2)
    chunks = chunks_of(widths)
    spec = pl.BlockSpec(memory_space=pltpu.VMEM)
    outs = [jax.ShapeDtypeStruct((rows, width), F32) for width in widths]
    outs += [
        jax.ShapeDtypeStruct((own, 3 * dim), BF),
        jax.ShapeDtypeStruct((1, dim), F32),
        jax.ShapeDtypeStruct((1, dim), F32),
    ]
    scratch = [pltpu.VMEM((dim, own), BF) for _ in range(3)]
    scratch += [
        pltpu.VMEM((padded, dim), BF),
        pltpu.VMEM((2, 32, own), F32),
        pltpu.VMEM((32, padded), F32),
        pltpu.SemaphoreType.DMA((8,)),
        pltpu.VMEM((dim, padded), BF),
        pltpu.VMEM((pairs, 2 * tile, 128), BF),
        pltpu.VMEM((pairs, 2 * tile, 128), BF),
        pltpu.VMEM((BLOCK, 2 * tile), F32),
        pltpu.VMEM((tile, BLOCK), F32),
        pltpu.VMEM((pairs, 128, 2 * tile), F32),
        pltpu.VMEM((pairs, 2 * tile, 128), F32),
        pltpu.VMEM((pairs, 2 * tile, 128), F32),
    ]
    scratch += reduction_scratch(rows, chunks)
    args = (first_low, attended, hidden_low, pre_low, second_low, act_low, grad, stats, by_tile(stats, own), qkv, seg_col, seg_row)
    return pl.pallas_call(
        functools.partial(backward_kernel, chunks),
        out_shape=outs,
        in_specs=[spec] * (len(args) + 1),
        out_specs=[spec] * len(outs),
        scratch_shapes=scratch,
        compiler_params=pltpu.CompilerParams(
            collective_id=1, has_side_effects=True, vmem_limit_bytes=VMEM_LIMIT
        ),
        cost_estimate=pl.CostEstimate(flops=50000000000, bytes_accessed=100000000, transcendentals=0),
    )(*args, segments_by_tile(seg_row, own))


LAYER_AT = 1


def last_kernel(chunks, *refs):
    inputs, qkv_low, weight, grad_first, dealt_col, vector, layer_low = refs[:7]
    out, tokens_grad, layer_out, vector_out = refs[7:11]
    rest = refs[11:]
    number = 2 * PERM
    turned, outgoing, pre_send, pre_recv, post_send, post_recv = (
        rest[0],
        rest[1 : 1 + number],
        rest[1 + number],
        rest[2 + number],
        rest[3 + number],
        rest[4 + number],
    )
    vector_in, vector_sum, vector_send, vector_recv = rest[5 + number : 9 + number]
    rest = rest[9 + number :]
    line_number = 4 * number + 3
    line_refs, reduction_refs = rest[:line_number], rest[line_number:]
    reduction = Reduction(chunks, (out,), reduction_refs)
    x, c, y, z = reduction.place
    own, dim = inputs.shape
    at_y = {"tp": 1 - y}
    inner = (z == 1) | (z == 2)
    peers = wide_peers() + ({"ctx": (z + 2) % 4},)
    greet_all(peers, ((inner, {"ctx": 3 - z}),))
    lines = [line_of(j, number, z, dealt_col, True, line_refs) for j in range(number)]
    width = dim // 2 // PERM

    def vector_copy(stage):
        return remote(
            vector_sum.at[stage], vector_in.at[stage], vector_send.at[stage], vector_recv.at[stage], peers[stage]
        )

    def vector_task():
        vector_sum[0] = vector[...]
        for stage in range(5):
            vector_copy(stage).start()
            yield
            vector_copy(stage).wait_recv()
            total = vector_sum[stage] + vector_in[stage]
            if stage < 4:
                vector_sum[stage + 1] = total
            else:
                vector_out[...] = total

    def grad_values(j, half):
        first = pl.ds(pl.multiple_of(half * (dim // 2) + j * width, 128), width)
        return (grad_first[:, first] + matmul_second(qkv_low[...], weight[first, :])).astype(BF)

    def layer_values(j, half):
        return layer_low[:, pl.ds(pl.multiple_of(half * (dim // 2) + j * width, 128), width)]

    def produce(k):
        if k == 0:
            turned[...] = inputs[...].T
        reduction.product(k, turned, qkv_low, qkv_low.shape[1] // 2)

    def slots(values, j, index, out_ref):
        return slots_task(
            lines[index],
            j,
            y,
            values,
            out_ref,
            (outgoing[index], pre_send.at[index], pre_recv.at[index]),
            (post_send.at[index], post_recv.at[index]),
            at_y,
        )

    tasks = [(j, slots(grad_values, j, j, tokens_grad)) for j in range(PERM)]
    tasks += [(LAYER_AT + j, slots(layer_values, j, PERM + j, layer_out)) for j in range(PERM)]
    tasks += [(k, reduction.task(k, produce)) for k in range(len(chunks))]
    tasks += [(1, vector_task())]
    interleave(sorted(tasks, key=lambda item: item[0]))
    reduction.settle()
    for stage in range(5):
        vector_copy(stage).wait_send()


def last_stage(inputs, qkv_low, weight, grad_first, dealt, vector, layer_low):
    own, dim = inputs.shape
    ctx_size = lax.axis_size("ctx")
    rows = dim // 4
    width = qkv_low.shape[1] // 2
    chunks = chunks_of((width,))
    spec = pl.BlockSpec(memory_space=pltpu.VMEM)
    outs = [
        jax.ShapeDtypeStruct((rows, width), F32),
        jax.ShapeDtypeStruct((2 * own, dim), BF),
        jax.ShapeDtypeStruct((2 * own, dim), BF),
        jax.ShapeDtypeStruct(vector.shape, F32),
    ]
    scratch = [pltpu.VMEM((dim, own), BF)]
    scratch += [pltpu.VMEM((own, dim // 2 // PERM), BF) for _ in range(2 * PERM)]
    scratch += [pltpu.SemaphoreType.DMA((2 * PERM,)) for _ in range(4)]
    scratch += [pltpu.VMEM((5,) + vector.shape, F32), pltpu.VMEM((5,) + vector.shape, F32)]
    scratch += [pltpu.SemaphoreType.DMA((5,)), pltpu.SemaphoreType.DMA((5,))]
    scratch += line_scratch(ctx_size, 2 * own, 2 * PERM, dim // 2 // PERM)
    scratch += reduction_scratch(rows, chunks)
    return pl.pallas_call(
        functools.partial(last_kernel, chunks),
        out_shape=outs,
        in_specs=[spec] * 7,
        out_specs=[spec] * len(outs),
        scratch_shapes=scratch,
        compiler_params=pltpu.CompilerParams(
            collective_id=2, has_side_effects=True, vmem_limit_bytes=VMEM_LIMIT
        ),
        cost_estimate=pl.CostEstimate(flops=10000000000, bytes_accessed=100000000, transcendentals=0),
    )(inputs, qkv_low, weight, grad_first, dealt[:, None], vector, layer_low)


def project_kernel(dim, x_ref, weight, bias, out):
    step = 256
    third = weight.shape[1] // 3

    def body(i, carry):
        lines = pl.ds(pl.multiple_of(i * step, step), step)
        value = (matmul(x_ref[lines, :], weight[...]) + bias[0]).astype(BF)
        scale = jnp.where(lax.broadcasted_iota(jnp.int32, (1, 3 * third), 1) < third, 0.125, 1.0).astype(BF)
        out[lines, :] = value * scale
        return carry

    lax.fori_loop(0, x_ref.shape[0] // step, body, 0)


def project(x_window, weight, bias):
    rows, dim = x_window.shape
    width = 3 * dim // 2
    return pl.pallas_call(
        functools.partial(project_kernel, dim),
        grid=(2,),
        out_shape=jax.ShapeDtypeStruct((rows, 2 * width), BF),
        in_specs=[
            pl.BlockSpec((rows, dim), lambda i: (0, 0)),
            pl.BlockSpec((dim, width), lambda i: (0, i)),
            pl.BlockSpec((1, 1, width), lambda i: (i, 0, 0)),
        ],
        out_specs=pl.BlockSpec((rows, width), lambda i: (0, i)),
        compiler_params=pltpu.CompilerParams(vmem_limit_bytes=VMEM_LIMIT),
        cost_estimate=pl.CostEstimate(flops=6000000000, bytes_accessed=14000000, transcendentals=0),
    )(x_window, weight, bias)


def rows_to_slots(values, dealt, place_z, place_y):
    own, dim = values.shape
    half = dim // 2
    keep = lax.dynamic_slice_in_dim(values, place_y * half, half, axis=1)
    send = lax.dynamic_slice_in_dim(values, (1 - place_y) * half, half, axis=1)
    other = lax.ppermute(send, "tp", [(0, 1), (1, 0)])
    first = jnp.where(place_y == 0, keep, other)
    second = jnp.where(place_y == 0, other, keep)
    block = jnp.concatenate([first, second], axis=0)
    everything = lax.all_gather(block, "ctx", axis=0, tiled=True)
    slots = 2 * own
    mine = lax.dynamic_slice_in_dim(dealt, place_z * slots, slots)
    picked = jnp.take(everything, mine, axis=0, mode="clip")
    other_columns = lax.ppermute(picked, "tp", [(0, 1), (1, 0)])
    return jnp.concatenate(
        [jnp.where(place_y == 0, picked, other_columns), jnp.where(place_y == 0, other_columns, picked)], axis=1
    )


def slots_to_rows(values, dealt, place_z, place_y):
    slots, dim = values.shape
    half, own = dim // 2, slots // 2
    block = lax.dynamic_slice_in_dim(values, place_y * half, half, axis=1)
    everything = lax.all_gather(block, "ctx", axis=0, tiled=True)
    wanted = place_z * slots + lax.broadcasted_iota(jnp.int32, (slots, 1), 0)
    chosen = (wanted == dealt[None, :]).astype(BF)
    picked = matmul(chosen, everything).astype(BF)
    keep = lax.dynamic_slice_in_dim(picked, place_y * own, own, axis=0)
    send = lax.dynamic_slice_in_dim(picked, (1 - place_y) * own, own, axis=0)
    other = lax.ppermute(send, "tp", [(0, 1), (1, 0)])
    return jnp.concatenate([jnp.where(place_y == 0, keep, other), jnp.where(place_y == 0, other, keep)], axis=1)


def per_device(
    tokens,
    cotangent,
    seq_lengths,
    dealing,
    query_weight,
    query_bias,
    key_weight,
    value_weight,
    value_bias,
    output_weight,
    output_bias,
    first_gain,
    first_shift,
    up_weight,
    up_bias,
    down_weight,
    down_bias,
    second_gain,
    second_shift,
):
    rows, dim = tokens.shape
    ctx_size, tp_size = lax.axis_size("ctx"), lax.axis_size("tp")
    group_rows = rows * ctx_size
    own = rows // tp_size
    place_z, place_y = lax.axis_index("ctx"), lax.axis_index("tp")
    window = HALO + own + HALO
    padded = -(-window // BLOCK) * BLOCK
    dealt = dealing[0]

    lengths = seq_lengths[0]
    number = lengths.shape[0]
    upto = jnp.arange(number)[:, None] >= jnp.arange(number)[None, :]
    ends = jnp.sum(jnp.where(upto, lengths[None, :], 0), axis=1)
    starts = ends - lengths
    special = lax.axis_size("shard") == 4 and tp_size == 2 and ctx_size == 4
    place_h = half_of(place_y, place_z) if special else place_y
    first_row = place_z * rows + place_h * own
    index = jnp.arange(padded, dtype=jnp.int32)
    position = first_row - HALO + index
    valid = (position >= 0) & (position < group_rows) & (index < window)
    segment = jnp.sum((position[:, None] >= ends[None, :-1]).astype(jnp.int32), axis=1)
    segment = jnp.where(valid, segment, -1)
    seg_row, seg_col = segment[None, :], segment[:, None]
    tile = attention_tile(own)
    tile_first = first_row + tile * jnp.arange(own // tile, dtype=jnp.int32)
    tile_last = tile_first + tile - 1
    begin = jnp.max(jnp.where(starts[None, :] <= tile_first[:, None], starts[None, :], 0), axis=1)
    finish = jnp.min(jnp.where(ends[None, :] > tile_last[:, None], ends[None, :], group_rows), axis=1)
    shift = HALO - first_row
    bounds = jnp.stack([(begin + shift) // BLOCK, (finish + shift + BLOCK - 1) // BLOCK], axis=1).astype(jnp.int32)

    half_dim = dim // tp_size
    pieces = [
        jnp.concatenate([query_weight, key_weight, value_weight], axis=1),
        output_weight.T,
        up_weight,
        down_weight.T,
    ]
    flat = jnp.concatenate([query_bias, value_bias, up_bias])
    small = jnp.broadcast_to(flat[None, :], (16, flat.shape[0]))
    inputs = lax.dynamic_slice_in_dim(tokens, place_h * own, own, axis=0)
    if special:
        whole, biases, qkv, cot_rows, attended, logsum = first_stage(
            pieces, small, tokens, cotangent, dealt, seg_col, seg_row, padded
        )
        whole_up_bias = biases[::16, dim:].reshape(-1).astype(F32)
    else:
        whole = [
            lax.all_gather(lax.all_gather(piece, "shard", axis=0, tiled=True), "tp", axis=1, tiled=True)
            for piece in pieces
        ]
        biases = lax.all_gather(small, "tp", axis=0, tiled=True)[::16].astype(F32)
        qkv_bias = jnp.concatenate(
            [biases[:, :half_dim], jnp.zeros((tp_size, half_dim), F32), biases[:, half_dim:dim]], axis=1
        )[:, None, :]
        whole_up_bias = biases[:, dim:].reshape(-1)
        edge = jnp.where(place_y == 0, tokens[rows - HALO :], tokens[:HALO])
        hops = [(2 * z, 2 * z + 2) for z in range(ctx_size - 1)] + [(2 * z + 1, 2 * z - 1) for z in range(1, ctx_size)]
        arrived = lax.ppermute(edge, ("ctx", "tp"), hops)
        x_window = jnp.where(
            place_y == 0,
            jnp.concatenate([arrived, tokens[: own + HALO]], axis=0),
            jnp.concatenate([tokens[own - HALO :], arrived], axis=0),
        )
        x_window = jnp.pad(x_window, ((0, padded - window), (0, 0)))
        qkv = project(x_window, whole[0], qkv_bias)
        cot_rows = slots_to_rows(cotangent, dealt, place_z, place_y)
        attended, logsum = attention_forward(qkv, seg_col, seg_row, bounds, own, dim)
    wide_qkv, wide_output, wide_up, wide_down = whole
    output_bias = output_bias.astype(F32)
    first_gain = first_gain.astype(F32)
    first_shift = first_shift.astype(F32)
    down_bias = down_bias.astype(F32)
    second_gain = second_gain.astype(F32)
    second_shift = second_shift.astype(F32)

    grad_out = cot_rows.astype(F32)
    hidden_one, normed_one, inverse_one = norm_forward(
        inputs.astype(F32) + matmul_second(attended, wide_output) + output_bias, first_gain, first_shift
    )
    hidden_low = hidden_one.astype(BF)
    pre_act = matmul(hidden_low, wide_up) + whole_up_bias
    erf_part = 0.5 * (1.0 + jax.scipy.special.erf(pre_act * HALF_ROOT))
    act_low = (pre_act * erf_part).astype(BF)
    layer_value, normed_two, inverse_two = norm_forward(
        hidden_one + matmul_second(act_low, wide_down) + down_bias, second_gain, second_shift
    )
    layer_low = layer_value.astype(BF)

    second_shift_grad = jnp.sum(grad_out, axis=0)
    second_gain_grad = jnp.sum(grad_out * normed_two, axis=0)
    grad_second = norm_backward(grad_out, normed_two, inverse_two, second_gain)
    down_bias_grad = jnp.sum(grad_second, axis=0)
    second_low = grad_second.astype(BF)
    slope = erf_part + pre_act * DENSITY * jnp.exp(-0.5 * pre_act * pre_act)
    grad_pre = matmul(second_low, wide_down) * slope
    up_bias_grad = jnp.sum(grad_pre, axis=0)
    pre_low = grad_pre.astype(BF)
    grad_hidden = grad_second + matmul_second(pre_low, wide_up)
    first_shift_grad = jnp.sum(grad_hidden, axis=0)
    first_gain_grad = jnp.sum(grad_hidden * normed_one, axis=0)
    grad_first = norm_backward(grad_hidden, normed_one, inverse_one, first_gain)
    output_bias_grad = jnp.sum(grad_first, axis=0)
    first_low = grad_first.astype(BF)
    attended_grad = matmul(first_low, wide_output).astype(BF)
    head_of = (jnp.arange(dim)[None, :] // HEAD == jnp.arange(16)[:, None]).astype(F32)
    delta = lax.dot_general(
        head_of,
        attended_grad.astype(F32) * attended.astype(F32),
        (((1,), (1,)), ((), ())),
        precision=lax.Precision.HIGHEST,
        preferred_element_type=F32,
    )
    stats = jnp.concatenate([logsum, delta], axis=0)
    if special:
        output_own, up_own, down_own, qkv_low, query_bias_grad, value_bias_grad = backward_stage(
            first_low, attended, hidden_low, pre_low, second_low, act_low, attended_grad, stats, qkv, seg_col, seg_row
        )
    else:
        layer_out = rows_to_slots(layer_low, dealt, place_z, place_y)
        up_hops = [(i, i + 1) for i in range(ctx_size * tp_size - 1)]
        down_hops = [(i + 1, i) for i in range(ctx_size * tp_size - 1)]
        grad_win, stats_win = [
            jnp.concatenate(
                [
                    lax.ppermute(lax.slice_in_dim(array, own - HALO, own, axis=axis), ("ctx", "tp"), up_hops),
                    array,
                    lax.ppermute(lax.slice_in_dim(array, 0, HALO, axis=axis), ("ctx", "tp"), down_hops),
                    jnp.zeros((padded - window, dim) if axis == 0 else (32, padded - window), array.dtype),
                ],
                axis=axis,
            )
            for array, axis in ((attended_grad, 0), (stats, 1))
        ]
        query_low, query_bias_grad = attention_query(qkv, seg_col, seg_row, bounds, attended_grad, stats, dim)
        qkv_low, value_bias_grad = attention_key(
            qkv, seg_col, seg_row, bounds, grad_win, stats_win, query_low, own, dim
        )
    vectors = jnp.concatenate(
        [
            query_bias_grad[0],
            value_bias_grad[0],
            up_bias_grad,
            output_bias_grad,
            first_gain_grad,
            first_shift_grad,
            down_bias_grad,
            second_gain_grad,
            second_shift_grad,
        ]
    )
    if special:
        qkv_own, tokens_grad, layer_out, small_sum = last_stage(
            inputs, qkv_low, wide_qkv, grad_first, dealt, vectors.reshape(-1, 128), layer_low
        )
        small_sum = small_sum.reshape(-1)
        owned = [qkv_own, output_own, up_own, down_own]
    else:
        owned = []
        for full in (
            matmul_first(inputs, qkv_low),
            matmul_first(first_low, attended),
            matmul_first(hidden_low, pre_low),
            matmul_first(second_low, act_low),
        ):
            part = lax.psum_scatter(full.astype(BF), "tp", scatter_dimension=1, tiled=True)
            part = lax.psum_scatter(part, "shard", scatter_dimension=0, tiled=True)
            owned.append(lax.psum(part, "ctx").astype(F32))
        small_sum = lax.psum(vectors, ("shard", "ctx", "tp"))
        tokens_grad = (grad_first + matmul_second(qkv_low, wide_qkv)).astype(BF)
        tokens_grad = rows_to_slots(tokens_grad, dealt, place_z, place_y)
    hidden = up_bias_grad.shape[0]
    sizes = [dim, dim, hidden] + [dim] * 6
    offsets = [sum(sizes[:i]) for i in range(len(sizes))]
    parts = [small_sum[o : o + s] for o, s in zip(offsets, sizes)]

    def by_tp(vector):
        part = vector.shape[0] // tp_size
        return lax.dynamic_slice_in_dim(vector, place_y * part, part)

    return (
        layer_out,
        tokens_grad,
        owned[0][:, :half_dim],
        by_tp(parts[0]),
        owned[0][:, half_dim : 2 * half_dim],
        owned[0][:, 2 * half_dim :],
        by_tp(parts[1]),
        owned[1].T,
        parts[3],
        parts[4],
        parts[5],
        owned[2],
        by_tp(parts[2]),
        owned[3].T,
        parts[6],
        parts[7],
        parts[8],
    )


def solution(mesh):
    return jax.shard_map(
        per_device,
        mesh=mesh,
        in_specs=(
            P(("shard", "ctx"), None),
            P(("shard", "ctx"), None),
            P("shard", None),
            P("shard", None),
            P("shard", "tp"),
            P("tp"),
            P("shard", "tp"),
            P("shard", "tp"),
            P("tp"),
            P("tp", "shard"),
            P(),
            P(),
            P(),
            P("shard", "tp"),
            P("tp"),
            P("tp", "shard"),
            P(),
            P(),
            P(),
        ),
        out_specs=(
            P(("shard", "ctx"), None),
            P(("shard", "ctx"), None),
            P("shard", "tp"),
            P("tp"),
            P("shard", "tp"),
            P("shard", "tp"),
            P("tp"),
            P("tp", "shard"),
            P(),
            P(),
            P(),
            P("shard", "tp"),
            P("tp"),
            P("tp", "shard"),
            P(),
            P(),
            P(),
        ),
        check_vma=False,
    )
```

```python
import functools

import jax
import jax.numpy as jnp
from jax import lax
from jax.experimental import pallas as pl
from jax.experimental.pallas import tpu as pltpu
from jax.sharding import PartitionSpec as P

HEAD = 64
HALO = 512
HALF_ROOT = 0.7071067811865476
DENSITY = 0.3989422804014327
NEG_FILL = -1000000000.0
BF = jnp.bfloat16
F32 = jnp.float32
BLOCK = 256
VMEM_LIMIT = 60 * 1024 * 1024


def matmul(former, latter):
    return jnp.dot(former, latter, preferred_element_type=F32)


def matmul_first(former, latter):
    return lax.dot_general(former, latter, (((0,), (0,)), ((), ())), preferred_element_type=F32)


def matmul_second(former, latter):
    return lax.dot_general(former, latter, (((1,), (1,)), ((), ())), preferred_element_type=F32)


def norm_forward(values, norm_gain, norm_shift):
    centre = values - jnp.mean(values, axis=1, keepdims=True)
    spread = jnp.mean(centre * centre, axis=1, keepdims=True)
    inverse = lax.rsqrt(spread + 1e-06)
    normed = centre * inverse
    return (norm_gain * normed + norm_shift, normed, inverse)


def norm_backward(gradient, normed, inverse, norm_gain):
    scaled = gradient * norm_gain
    bracket = (
        scaled
        - jnp.mean(scaled, axis=1, keepdims=True)
        - normed * jnp.mean(scaled * normed, axis=1, keepdims=True)
    )
    return inverse * bracket


def places(pair, dim):
    half, inner = divmod(pair, dim // 256)
    base = half * (3 * dim // 2) + inner * 128
    return base, base + dim // 2, base + dim


def take(qkv, rows, pair, dim, which):
    first = places(pair, dim)[which]
    return qkv[rows, first : first + 128]


def low_lanes(rows):
    return lax.broadcasted_iota(jnp.int32, (rows, 128), 1) < HEAD


def stacked(pair):
    low = low_lanes(pair.shape[0])
    zero = jnp.zeros_like(pair)
    return jnp.concatenate([jnp.where(low, pair, zero), jnp.where(low, zero, pair)], axis=0)


def unstacked(both):
    rows = both.shape[0] // 2
    return jnp.where(low_lanes(rows), both[:rows], both[rows:])


def bias_of(own_seg, other_seg):
    return jnp.where(own_seg == other_seg, 0.0, NEG_FILL)


def turn_columns(qkv, pair, dim, which, turned):
    turned[pair * 128 : pair * 128 + 128, :] = take(qkv, slice(0, qkv.shape[0]), pair, dim, which).T


def twice(row_pair):
    return jnp.concatenate([row_pair[0:1], row_pair[1:2]], axis=1)


def forward_steps(dim, tile, qkv, seg_col, seg_tile, out, logsum, value_t, query_st, bias_ref, acc, top, total):
    pairs = dim // 128

    def prepare():
        for p in range(pairs):
            turn_columns(qkv, p, dim, 2, value_t)

    def begin(i):
        rows = pl.ds(pl.multiple_of(HALO + i * tile, 64), tile)
        for p in range(pairs):
            query_st[p] = stacked(take(qkv, rows, p, dim, 0))
        acc[...] = jnp.zeros_like(acc)
        total[...] = jnp.zeros_like(total)
        top[...] = jnp.full_like(top, 2 * NEG_FILL)

    def block(i, j):
        start = pl.multiple_of(j * BLOCK, BLOCK)
        bias_ref[...] = bias_of(seg_col[pl.ds(start, BLOCK), :], seg_tile[i])
        for p in range(pairs):
            key = take(qkv, pl.ds(start, BLOCK), p, dim, 1)
            scores = matmul_second(key, query_st[p]) + bias_ref[...]
            old = top[p]
            new = jnp.maximum(old, jnp.max(scores, axis=0, keepdims=True))
            keep = jnp.exp(old - new)
            raised = jnp.exp(scores - new)
            total[p] = keep * total[p] + jnp.sum(raised, axis=0, keepdims=True)
            value = value_t[p * 128 : p * 128 + 128, pl.ds(start, BLOCK)]
            acc[p] = keep * acc[p] + matmul(value, raised.astype(BF))
            top[p] = new

    def finish(i):
        lines = pl.ds(pl.multiple_of(i * tile, tile), tile)
        for p in range(pairs):
            whole = total[p]
            out[lines, p * 128 : p * 128 + 128] = unstacked((acc[p] / whole).T).astype(BF)
            lse = top[p] + jnp.log(whole)
            logsum[i, 2 * p : 2 * p + 1, :] = lse[:, :tile]
            logsum[i, 2 * p + 1 : 2 * p + 2, :] = lse[:, tile:]
        for p in range(2 * pairs, 16):
            logsum[i, p : p + 1, :] = jnp.zeros((1, tile), F32)

    return prepare, begin, block, finish


def query_steps(dim, tile, qkv, seg_col, seg_tile, grad, stats, store, sums, key_t, query_st, grad_st, bias_ref, acc):
    pairs = dim // 128

    def prepare():
        sums[...] = jnp.zeros_like(sums)
        for p in range(pairs):
            turn_columns(qkv, p, dim, 1, key_t)

    def begin(i):
        own_rows = pl.ds(pl.multiple_of(i * tile, tile), tile)
        rows = pl.ds(pl.multiple_of(HALO + i * tile, 64), tile)
        for p in range(pairs):
            query_st[p] = stacked(take(qkv, rows, p, dim, 0))
            grad_st[p] = stacked(grad[own_rows, p * 128 : p * 128 + 128])
        acc[...] = jnp.zeros_like(acc)

    def block(i, j):
        there = pl.ds(pl.multiple_of(j * BLOCK, BLOCK), BLOCK)
        bias_ref[...] = bias_of(seg_col[there, :], seg_tile[i])
        for p in range(pairs):
            scores = matmul_second(take(qkv, there, p, dim, 1), query_st[p]) + bias_ref[...]
            probs = jnp.exp(scores - twice(stats[i, 2 * p : 2 * p + 2, :]))
            grad_probs = matmul_second(take(qkv, there, p, dim, 2), grad_st[p])
            grad_scores = (probs * (grad_probs - twice(stats[i, 16 + 2 * p : 18 + 2 * p, :]))).astype(BF)
            acc[p] += matmul(key_t[p * 128 : p * 128 + 128, there], grad_scores)

    def finish(i):
        own_rows = pl.ds(pl.multiple_of(i * tile, tile), tile)
        for p in range(pairs):
            part = 0.125 * unstacked(acc[p].T)
            store(own_rows, p, part.astype(BF))
            sums[:, p * 128 : p * 128 + 128] += jnp.sum(part, axis=0, keepdims=True)

    return prepare, begin, block, finish


def key_steps(dim, tile, qkv, seg_col, seg_row, grad, stats, out, sums, key_st, value_st, bias_ref, key_acc, value_acc):
    pairs = dim // 128

    def prepare():
        sums[...] = jnp.zeros_like(sums)

    def begin(i):
        rows = pl.ds(pl.multiple_of(HALO + i * tile, 64), tile)
        for p in range(pairs):
            key_st[p] = stacked(take(qkv, rows, p, dim, 1))
            value_st[p] = stacked(take(qkv, rows, p, dim, 2))
        key_acc[...] = jnp.zeros_like(key_acc)
        value_acc[...] = jnp.zeros_like(value_acc)

    def block(i, j):
        there = pl.ds(pl.multiple_of(j * BLOCK, BLOCK), BLOCK)
        seg_here = seg_col[pl.ds(pl.multiple_of(HALO + i * tile, 64), tile), :]
        bias_ref[...] = bias_of(seg_here, seg_row[:, there])
        for p in range(pairs):
            query = take(qkv, there, p, dim, 0)
            grad_pair = grad[there, p * 128 : p * 128 + 128]
            scores = matmul_second(key_st[p], query)
            grad_probs = matmul_second(value_st[p], grad_pair)
            probs_all, grads_all = [], []
            for half in range(2):
                head = 2 * p + half
                lines = slice(half * tile, half * tile + tile)
                probs = jnp.exp(scores[lines] + bias_ref[...] - stats[head : head + 1, there])
                grads_all.append((probs * (grad_probs[lines] - stats[16 + head : 17 + head, there])).astype(BF))
                probs_all.append(probs.astype(BF))
            key_acc[p] += matmul(jnp.concatenate(grads_all, axis=0), query)
            value_acc[p] += matmul(jnp.concatenate(probs_all, axis=0), grad_pair)

    def finish(i):
        own_rows = pl.ds(pl.multiple_of(i * tile, tile), tile)
        for p in range(pairs):
            _, at_key, at_value = places(p, dim)
            out[own_rows, at_key : at_key + 128] = unstacked(key_acc[p]).astype(BF)
            part = unstacked(value_acc[p])
            out[own_rows, at_value : at_value + 128] = part.astype(BF)
            sums[:, p * 128 : p * 128 + 128] += jnp.sum(part, axis=0, keepdims=True)

    return prepare, begin, block, finish


def run_dynamic(steps, bounds, tiles):
    prepare, begin, block, finish = steps
    prepare()

    def one_tile(i, carry):
        begin(i)

        def one_block(j, inner):
            block(i, j)
            return inner

        lax.fori_loop(bounds[i, 0], bounds[i, 1], one_block, 0)
        finish(i)
        return carry

    lax.fori_loop(0, tiles, one_tile, 0)


PIECE = 2


def run_static(steps, tile, tiles):
    prepare, begin, block, finish = steps
    prepare()
    yield
    for i in range(tiles):
        first = (HALO + i * tile - HALO + 1) // BLOCK
        after = -(-(HALO + i * tile + tile + HALO - 1) // BLOCK)
        begin(i)
        for piece in range(first, after, PIECE):

            def one_block(j, inner):
                block(i, j)
                return inner

            lax.fori_loop(piece, min(piece + PIECE, after), one_block, 0)
            if piece + PIECE >= after:
                finish(i)
            yield


def forward_kernel(dim, tile, bounds, *refs):
    run_dynamic(forward_steps(dim, tile, *refs), bounds, refs[3].shape[0] // tile)


def query_kernel(dim, tile, bounds, qkv, seg_col, seg_tile, grad, stats, out, sums, *scratch):
    def store(rows, p, part):
        out[rows, p * 128 : p * 128 + 128] = part

    run_dynamic(
        query_steps(dim, tile, qkv, seg_col, seg_tile, grad, stats, store, sums, *scratch), bounds, out.shape[0] // tile
    )


def key_kernel(dim, tile, bounds, qkv, seg_col, seg_row, grad, stats, query_low, out, sums, *scratch):
    for p in range(dim // 128):
        at_query = places(p, dim)[0]
        out[:, at_query : at_query + 128] = query_low[:, p * 128 : p * 128 + 128]
    run_dynamic(
        key_steps(dim, tile, qkv, seg_col, seg_row, grad, stats, out, sums, *scratch), bounds, out.shape[0] // tile
    )


def vmem_call(kernel, arrays, bounds, outs, scratch, flops):
    spec = pl.BlockSpec(memory_space=pltpu.VMEM)
    return pl.pallas_call(
        kernel,
        out_shape=outs,
        in_specs=[pl.BlockSpec(memory_space=pltpu.SMEM)] + [spec] * len(arrays),
        out_specs=jax.tree.map(lambda leaf: spec, outs),
        scratch_shapes=scratch,
        compiler_params=pltpu.CompilerParams(vmem_limit_bytes=VMEM_LIMIT),
        cost_estimate=pl.CostEstimate(flops=flops, bytes_accessed=12000000, transcendentals=6000000),
    )(bounds, *arrays)


def attention_tile(own):
    for tile in (192, 128, 64, 32, 16):
        if own % tile == 0:
            return tile
    raise ValueError("rows")


def by_tile(rows_last, own):
    tile = attention_tile(own)
    return rows_last.reshape(rows_last.shape[0], own // tile, tile).transpose(1, 0, 2)


def segments_by_tile(seg_row, own):
    tiles = by_tile(lax.slice_in_dim(seg_row, HALO, HALO + own, axis=1), own)
    return jnp.concatenate([tiles, tiles], axis=2)


def forward_scratch(padded, tile, dim):
    pairs = dim // 128
    return [
        pltpu.VMEM((dim, padded), BF),
        pltpu.VMEM((pairs, 2 * tile, 128), BF),
        pltpu.VMEM((BLOCK, 2 * tile), F32),
        pltpu.VMEM((pairs, 128, 2 * tile), F32),
        pltpu.VMEM((pairs, 1, 2 * tile), F32),
        pltpu.VMEM((pairs, 1, 2 * tile), F32),
    ]


def attention_forward(qkv, seg_col, seg_row, bounds, own, dim):
    tile = attention_tile(own)
    pairs = dim // 128
    out, logsum = vmem_call(
        functools.partial(forward_kernel, dim, tile),
        (qkv, seg_col, segments_by_tile(seg_row, own)),
        bounds,
        (jax.ShapeDtypeStruct((own, dim), BF), jax.ShapeDtypeStruct((own // tile, 16, tile), F32)),
        forward_scratch(qkv.shape[0], tile, dim),
        10_000_000_000,
    )
    return out, logsum.transpose(1, 0, 2).reshape(16, own)


def attention_query(qkv, seg_col, seg_row, bounds, grad, stats, dim):
    own = grad.shape[0]
    tile = attention_tile(own)
    pairs = dim // 128
    return vmem_call(
        functools.partial(query_kernel, dim, tile),
        (qkv, seg_col, segments_by_tile(seg_row, own), grad, by_tile(stats, own)),
        bounds,
        (jax.ShapeDtypeStruct((own, dim), BF), jax.ShapeDtypeStruct((1, dim), F32)),
        [
            pltpu.VMEM((dim, qkv.shape[0]), BF),
            pltpu.VMEM((pairs, 2 * tile, 128), BF),
            pltpu.VMEM((pairs, 2 * tile, 128), BF),
            pltpu.VMEM((BLOCK, 2 * tile), F32),
            pltpu.VMEM((pairs, 128, 2 * tile), F32),
        ],
        15_000_000_000,
    )


def attention_key(qkv, seg_col, seg_row, bounds, grad_win, stats_win, query_low, own, dim):
    tile = attention_tile(own)
    pairs = dim // 128
    return vmem_call(
        functools.partial(key_kernel, dim, tile),
        (qkv, seg_col, seg_row, grad_win, stats_win, query_low),
        bounds,
        (jax.ShapeDtypeStruct((own, 3 * dim), BF), jax.ShapeDtypeStruct((1, dim), F32)),
        [
            pltpu.VMEM((pairs, 2 * tile, 128), BF),
            pltpu.VMEM((pairs, 2 * tile, 128), BF),
            pltpu.VMEM((tile, BLOCK), F32),
            pltpu.VMEM((pairs, 2 * tile, 128), F32),
            pltpu.VMEM((pairs, 2 * tile, 128), F32),
        ],
        20_000_000_000,
    )


def remote(src, dst, send_sem, recv_sem, where):
    return pltpu.make_async_remote_copy(
        src_ref=src,
        dst_ref=dst,
        send_sem=send_sem,
        recv_sem=recv_sem,
        device_id=where,
        device_id_type=pl.DeviceIdType.MESH,
    )


def here():
    shard, z, y = lax.axis_index("shard"), lax.axis_index("ctx"), lax.axis_index("tp")
    return shard // 2, shard % 2, y, z


def half_of(y, z):
    return (y + z) % 2


def interleave(tasks):
    running, turn = [], 0
    while tasks or running:
        running += [task for first, task in tasks if first <= turn]
        tasks = [item for item in tasks if item[0] > turn]
        alive = []
        for task in running:
            try:
                next(task)
                alive.append(task)
            except StopIteration:
                pass
        running, turn = alive, turn + 1


def timed(task, gaps):
    for stage, _ in enumerate(task):
        yield
        for _ in range(gaps[min(stage, len(gaps) - 1)]):
            yield


def greet_all(always, sometimes):
    barrier = pltpu.get_barrier_semaphore()
    number = jnp.int32(len(always))
    for peer in always:
        pl.semaphore_signal(barrier, inc=1, device_id=peer, device_id_type=pl.DeviceIdType.MESH)
    for condition, peer in sometimes:

        @pl.when(condition)
        def _():
            pl.semaphore_signal(barrier, inc=1, device_id=peer, device_id_type=pl.DeviceIdType.MESH)

        number = number + condition.astype(jnp.int32)
    pl.semaphore_wait(barrier, number)


class Line:
    SCRATCH = 4

    def __init__(self, z, dealt, to_slots, refs, sems):
        self.z, self.dealt, self.to_slots = z, dealt, to_slots
        self.blocks, self.picked, self.away, self.arrived = refs
        self.send, self.block_recv, self.away_recv = sems
        self.inner = (z == 1) | (z == 2)
        self.outer = (z == 0) | (z == 3)
        self.near = 1 + z // 3
        self.end = jnp.maximum(3 * (z - 1), 0) % 6
        self.middle = 3 - z
        self.far = 3 - self.end
        self.slots = refs[0].shape[1]

    def copy(self, what):
        if what == "own_near":
            block, where, sem = self.z, self.near, 0
        elif what == "own_middle":
            block, where, sem = self.z, self.middle, 0
        elif what == "forward":
            block, where, sem = self.end, self.middle, 1
        else:
            where = self.end
            return remote(self.away, self.arrived, self.send.at[2], self.away_recv, {"ctx": where})
        there = self.blocks.at[block]
        return remote(there, there, self.send.at[sem], self.block_recv.at[block], {"ctx": where})

    def wait_block(self, block):
        there = self.blocks.at[block]
        remote(there, there, self.send.at[0], self.block_recv.at[block], {"ctx": self.middle}).wait_recv()

    def select(self, target, wanted_by, block, start):
        slots = self.slots
        wide = 384 if slots % 384 == 0 else 128

        def body(i, carry):
            lines = pl.ds(pl.multiple_of(i * wide, 128), wide)
            if self.to_slots:
                row = self.dealt[:, pl.ds(pl.multiple_of(wanted_by * slots + i * wide, 128), wide)]
                wanted = jnp.broadcast_to(row, (8, wide)).T[:, :1]
                offered = (block * slots + lax.broadcasted_iota(jnp.int32, (wide, slots), 1)).astype(F32)
            else:
                wanted = wanted_by * slots + i * wide + lax.broadcasted_iota(jnp.int32, (wide, slots), 0)
                offered = self.dealt[:, pl.ds(pl.multiple_of(block * slots, 128), slots)]
            chosen = jnp.where(wanted == offered, 1.0, 0.0).astype(BF)
            part = matmul(chosen, self.blocks[block]).astype(BF)
            target[lines, :] = part if start else target[lines, :] + part
            return carry

        lax.fori_loop(0, slots // wide, body, 0)

    def run(self):
        @pl.when(self.outer)
        def _():
            self.copy("own_near").start()

        @pl.when(self.inner)
        def _():
            self.copy("own_middle").start()

        self.select(self.picked, self.z, self.z, True)
        yield

        @pl.when(self.inner)
        def _():
            self.wait_block(self.end)
            self.copy("forward").start()
            self.select(self.picked, self.z, self.end, False)
            self.select(self.away, self.end, self.z, True)

        yield

        @pl.when(self.inner)
        def _():
            self.wait_block(self.middle)
            self.select(self.away, self.end, self.middle, False)
            self.select(self.picked, self.z, self.middle, False)

        yield

        @pl.when(self.inner)
        def _():
            self.wait_block(self.far)
            self.select(self.away, self.end, self.far, False)
            self.copy("away").start()
            self.select(self.picked, self.z, self.far, False)

        yield

        @pl.when(self.outer)
        def _():
            self.copy("away").wait_recv()
            self.picked[...] = self.picked[...] + self.arrived[...]

    def settle(self):
        @pl.when(self.outer)
        def _():
            self.copy("own_near").wait_send()

        @pl.when(self.inner)
        def _():
            self.copy("own_middle").wait_send()
            self.copy("forward").wait_send()
            self.copy("away").wait_send()


def line_scratch(ctx_size, slots, chunks, columns):
    blocks = [pltpu.VMEM((ctx_size, slots, columns), BF) for _ in range(chunks)]
    others = [pltpu.VMEM((slots, columns), BF) for _ in range(3 * chunks)]
    sems = [pltpu.SemaphoreType.DMA((chunks, 3)), pltpu.SemaphoreType.DMA((chunks, ctx_size)), pltpu.SemaphoreType.DMA((chunks,))]
    return blocks + others + sems


def line_of(j, chunks, z, dealt, to_slots, refs):
    blocks, others, sems = refs[:chunks], refs[chunks : 4 * chunks], refs[4 * chunks :]
    return Line(
        z,
        dealt,
        to_slots,
        (blocks[j], others[3 * j], others[3 * j + 1], others[3 * j + 2]),
        (sems[0].at[j], sems[1].at[j], sems[2].at[j]),
    )


PERM = 3


FIRST_WAIT = (0, 1, 4, 6)
SECOND_WAIT = (0, 1, 1, 2)
THIRD_WAIT = (0, 1, 1, 1)
COTANGENT_AT = (1, 2, 4)
COTANGENT_PAUSE = 0


def first_kernel(widths, padded, *refs):
    count = len(widths)
    pieces, (small, tokens, cotangent, dealt_row, seg_col, seg_tile) = refs[:count], refs[count : count + 6]
    refs = refs[count + 6 :]
    wholes, (small_whole, qkv, cot_rows, attended, logsum) = refs[:count], refs[count : count + 5]
    rest = refs[count + 5 :]
    attention_refs, rest = rest[:6], rest[6:]
    weight, window, send, recv, own_sem, small_sem, halo_sem, post_send, post_recv, bring = rest[:10]
    line_refs = rest[10:]
    x, c, y, z = here()
    h = half_of(y, z)
    rows, dim = tokens.shape
    own = rows // 2
    half = dim // 2
    last = 3
    tile = attention_tile(own)
    at_x, at_y, at_c = {"shard": 2 * (1 - x) + c}, {"tp": 1 - y}, {"shard": 2 * x + 1 - c}
    left, right = {"ctx": jnp.maximum(z - 1, 0)}, {"ctx": jnp.minimum(z + 1, last)}
    greet_all((at_x, at_y, at_c), ((z > 0, left), (z < last, right)))

    def slot(a, of_y, of_x, of_c, lines=None):
        cols = pl.ds(pl.multiple_of(of_y * widths[a], 128), widths[a])
        depth = wholes[a].shape[2]
        lines = slice(0, depth) if lines is None else slice(lines * depth // 2, (lines + 1) * depth // 2)
        return (weight if a == 0 else wholes[a]).at[of_x, of_c, lines, cols]

    def moves(a):
        table = [
            (pieces[a], slot(a, y, x, c), at_x),
            (pieces[a], slot(a, y, x, c), at_y),
            (pieces[a], slot(a, y, x, c), at_c),
            (slot(a, y, 1 - x, c, 0), slot(a, y, 1 - x, c, 0), at_y),
            (slot(a, 1 - y, x, c, 1), slot(a, 1 - y, x, c, 1), at_x),
            (slot(a, y, 1 - x, c), slot(a, y, 1 - x, c), at_c),
            (slot(a, 1 - y, x, c), slot(a, 1 - y, x, c), at_c),
            (slot(a, 1 - y, 1 - x, c, 0), slot(a, 1 - y, 1 - x, c, 0), at_c),
            (slot(a, 1 - y, 1 - x, c, 1), slot(a, 1 - y, 1 - x, c, 1), at_c),
        ]
        return [remote(s, d, send.at[a, kind], recv.at[a, kind], w) for kind, (s, d, w) in enumerate(table)]

    tables = [moves(a) for a in range(count)]
    depth = small_whole.shape[0] // 2
    small_at = small_whole.at[pl.ds(pl.multiple_of(y * depth, 16), depth)]
    small_copy = remote(small, small_at, small_sem.at[0], small_sem.at[1], at_y)
    sends_right, sends_left = (h == 1) & (z < last), (h == 0) & (z > 0)
    gets_left, gets_right = (h == 0) & (z > 0), (h == 1) & (z < last)

    def halo(where):
        src = tokens.at[pl.ds(pl.multiple_of(h * (rows - HALO), 64), HALO)]
        dst = window.at[pl.ds(pl.multiple_of((1 - h) * (HALO + own), 64), HALO)]
        return remote(src, dst, halo_sem.at[0], halo_sem.at[1], where)

    inside = pltpu.make_async_copy(
        tokens.at[pl.ds(pl.multiple_of(h * (own - HALO), 64), own + HALO)],
        window.at[pl.ds(pl.multiple_of((1 - h) * HALO, 64), own + HALO)],
        halo_sem.at[2],
    )
    small_local = pltpu.make_async_copy(small, small_at, small_sem.at[2])
    piece_local = [pltpu.make_async_copy(pieces[a], slot(a, y, x, c), own_sem.at[a]) for a in range(count)]
    lines = [line_of(j, PERM, z, dealt_row, False, line_refs) for j in range(PERM)]

    def columns_of(j):
        return pl.ds(pl.multiple_of(y * half + j * (half // PERM), 128), half // PERM)

    bring_cot = [
        pltpu.make_async_copy(cotangent.at[:, columns_of(j)], lines[j].blocks.at[z], bring.at[j]) for j in range(PERM)
    ]
    def spread(a):
        for kind in range(3):
            tables[a][kind].start()

    spread(0)
    small_copy.start()

    @pl.when(sends_right)
    def _():
        halo(right).start()

    @pl.when(sends_left)
    def _():
        halo(left).start()

    for item in (small_local, *piece_local, inside, *bring_cot):
        item.start()
    window[padded - (padded - 2 * HALO - own) :, :] = jnp.zeros((padded - 2 * HALO - own, dim), BF)

    @pl.when((h == 0) & (z == 0))
    def _():
        window[:HALO, :] = jnp.zeros((HALO, dim), BF)

    @pl.when((h == 1) & (z == last))
    def _():
        window[HALO + own : 2 * HALO + own, :] = jnp.zeros((HALO, dim), BF)

    def pause(number):
        for _ in range(number):
            yield

    def weights_task(a):
        tables[a][0].wait_recv()
        tables[a][3].start()
        tables[a][5].start()
        tables[a][1].wait_recv()
        tables[a][4].start()
        tables[a][6].start()
        if a + 2 < count:
            spread(a + 2)
        yield
        yield from pause(SECOND_WAIT[a])
        tables[a][3].wait_recv()
        tables[a][7].start()
        tables[a][4].wait_recv()
        tables[a][8].start()
        yield
        yield from pause(THIRD_WAIT[a])
        for kind in (2, 5, 6, 7, 8):
            tables[a][kind].wait_recv()
        if a == 0:
            yield from project_task()
            yield from run_static(
                forward_steps(dim, tile, qkv, seg_col, seg_tile, attended, logsum, *attention_refs), tile, own // tile
            )

    def project_task():
        piece_local[0].wait()
        pltpu.make_async_copy(weight, wholes[0], own_sem.at[0]).start()
        inside.wait()
        small_copy.wait()
        small_local.wait()

        @pl.when(gets_left | gets_right)
        def _():
            halo(left).wait_recv()

        depth_w, width = weight.shape[2], widths[0]
        third = width // 3
        step = 256
        for of_y in range(2):
            bias = small_whole[of_y * depth : of_y * depth + 1, :].astype(F32)
            bias = jnp.concatenate([bias[:, :third], jnp.zeros((1, third), F32), bias[:, third : 2 * third]], axis=1)
            scale = jnp.where(lax.broadcasted_iota(jnp.int32, (1, width), 1) < third, 0.125, 1.0).astype(BF)
            full = jnp.concatenate(
                [weight[i // 2, i % 2, :, of_y * width : (of_y + 1) * width] for i in range(4)], axis=0
            )

            def body(i, carry):
                there = pl.ds(pl.multiple_of(i * step, step), step)
                value = (matmul(window[there, :], full) + bias).astype(BF)
                qkv[there, of_y * width : (of_y + 1) * width] = value * scale
                return carry

            lax.fori_loop(0, padded // step, body, 0)
            yield

    def post(j):
        there = lines[j].picked.at[pl.ds(pl.multiple_of((1 - h) * own, 64), own)]
        return remote(there, cot_rows.at[:, columns_of(j)], post_send.at[j], post_recv.at[j], at_y)

    def cotangent_task(j):
        bring_cot[j].wait()
        for _ in lines[j].run():
            yield
            yield from pause(COTANGENT_PAUSE)
        post(j).start()
        cot_rows[:, columns_of(j)] = lines[j].picked[pl.ds(pl.multiple_of(h * own, 64), own), :]
        yield
        post(j).wait_recv()

    if count > 1:
        spread(1)
    tasks = [(FIRST_WAIT[a], weights_task(a)) for a in range(count)]
    tasks += [(COTANGENT_AT[j], cotangent_task(j)) for j in range(PERM)]
    interleave(sorted(tasks, key=lambda item: item[0]))
    for a in range(count):
        for kind in range(9):
            tables[a][kind].wait_send()
        if a:
            piece_local[a].wait()
    pltpu.make_async_copy(weight, wholes[0], own_sem.at[0]).wait()

    @pl.when(sends_right | sends_left)
    def _():
        halo(left).wait_send()

    for j in range(PERM):
        lines[j].settle()
        post(j).wait_send()


def first_stage(pieces, small, tokens, cotangent, dealt, seg_col, seg_row, padded):
    rows, dim = tokens.shape
    depth = pieces[0].shape[0]
    own = rows // 2
    tile = attention_tile(own)
    widths = tuple(piece.shape[1] for piece in pieces)
    count = len(pieces)
    ctx_size = lax.axis_size("ctx")
    outs = [jax.ShapeDtypeStruct((2, 2, depth, 2 * width), BF) for width in widths]
    outs += [
        jax.ShapeDtypeStruct((2 * small.shape[0], small.shape[1]), BF),
        jax.ShapeDtypeStruct((padded, 3 * dim), BF),
        jax.ShapeDtypeStruct((own, dim), BF),
        jax.ShapeDtypeStruct((own, dim), BF),
        jax.ShapeDtypeStruct((own // tile, 16, tile), F32),
    ]
    anywhere, vmem = pl.BlockSpec(memory_space=pl.ANY), pl.BlockSpec(memory_space=pltpu.VMEM)
    result = pl.pallas_call(
        functools.partial(first_kernel, widths, padded),
        out_shape=outs,
        in_specs=[anywhere] * (count + 3) + [vmem] * 3,
        out_specs=[anywhere] * count + [vmem] * 5,
        scratch_shapes=forward_scratch(padded, tile, dim)
        + [
            pltpu.VMEM((2, 2, depth, 2 * widths[0]), BF),
            pltpu.VMEM((padded, dim), BF),
            pltpu.SemaphoreType.DMA((count, 9)),
            pltpu.SemaphoreType.DMA((count, 9)),
            pltpu.SemaphoreType.DMA((count,)),
            pltpu.SemaphoreType.DMA((3,)),
            pltpu.SemaphoreType.DMA((3,)),
            pltpu.SemaphoreType.DMA((PERM,)),
            pltpu.SemaphoreType.DMA((PERM,)),
            pltpu.SemaphoreType.DMA((PERM,)),
        ]
        + line_scratch(ctx_size, rows, PERM, dim // 2 // PERM),
        compiler_params=pltpu.CompilerParams(
            collective_id=0, has_side_effects=True, vmem_limit_bytes=VMEM_LIMIT
        ),
        cost_estimate=pl.CostEstimate(flops=10000000000, bytes_accessed=100000000, transcendentals=0),
    )(*pieces, small, tokens, cotangent, dealt[None, :], seg_col, segments_by_tile(seg_row, own))
    whole = [full.reshape(4 * depth, full.shape[3]) for full in result[:count]]
    logsum = result[count + 4].transpose(1, 0, 2).reshape(16, own)
    return whole, result[count], result[count + 1], result[count + 2], result[count + 3], logsum


def add_lines(dst, first, second):
    rows = dst.shape[0]
    step = 48 if rows % 48 == 0 else 16

    def body(i, carry):
        lines = pl.ds(pl.multiple_of(i * step, 16), step)
        dst[lines, :] = (first[lines, :].astype(F32) + second[lines, :].astype(F32)).astype(dst.dtype)
        return carry

    lax.fori_loop(0, rows // step, body, 0)


RING = 4


class Reduction:
    STAGES = 7

    def __init__(self, chunks, outs, refs):
        number = len(chunks)
        self.chunks, self.outs = chunks, outs
        ring = min(RING, number)
        self.full = [refs[k % ring] for k in range(number)]
        refs = refs[ring:]
        self.by_core, self.by_x, self.plane, self.from_end, self.half_z, self.final = (
            refs[i * number : (i + 1) * number] for i in range(6)
        )
        self.send, self.recv = refs[6 * number :]
        self.place = here()
        z = self.place[3]
        self.inner, self.outer = (z == 1) | (z == 2), (z == 0) | (z == 3)
        self.near, self.end, self.middle = 1 + z // 3, jnp.maximum(3 * (z - 1), 0) % 6, 3 - z
        self.rows = self.full[0].shape[3]

    def copy(self, k, stage):
        x, c, y, z = self.place
        half = self.rows // 2
        side = z // 2
        if stage == 0:
            src, dst, where = self.full[k].at[:, :, 1 - c], self.by_core[k], {"shard": 2 * x + 1 - c}
        elif stage == 1:
            src, dst, where = self.by_core[k].at[:, 1 - x], self.by_x[k], {"shard": 2 * (1 - x) + c}
        elif stage == 2:
            src, dst, where = self.by_x[k].at[1 - y], self.plane[k], {"tp": 1 - y}
        elif stage == 3:
            src, dst, where = self.plane[k], self.from_end[k], {"ctx": self.near}
        elif stage == 4:
            src = self.plane[k].at[pl.ds(pl.multiple_of((1 - side) * half, 16), half)]
            dst, where = self.half_z[k], {"ctx": self.middle}
        elif stage == 5:
            src = dst = self.final[k].at[pl.ds(pl.multiple_of(side * half, 16), half)]
            where = {"ctx": self.middle}
        else:
            src = dst = self.final[k]
            where = {"ctx": self.end}
        return remote(src, dst, self.send.at[k, stage], self.recv.at[k, stage], where)

    def sender(self, stage):
        return None if stage < 3 else (self.outer if stage == 3 else self.inner)

    def receiver(self, stage):
        return None if stage < 3 else (self.outer if stage == 6 else self.inner)

    def guarded(self, condition, action):
        if condition is None:
            action()
        else:
            pl.when(condition)(action)

    def start(self, k, stage):
        self.guarded(self.sender(stage), lambda: self.copy(k, stage).start())

    def absorb(self, k, stage):
        x, c, y, z = self.place
        half = self.rows // 2
        side = z // 2
        self.copy(k, stage).wait_recv()
        if stage == 0:
            for of_y in range(2):
                for of_x in range(2):
                    there = self.by_core[k].at[of_y, of_x]
                    add_lines(there, there, self.full[k].at[of_y, of_x, c])
            self.copy(k, 0).wait_send()
        elif stage == 1:
            for i in range(2):
                add_lines(self.by_x[k].at[i], self.by_x[k].at[i], self.by_core[k].at[i, x])
        elif stage == 2:
            add_lines(self.plane[k], self.plane[k], self.by_x[k].at[y])
        elif stage == 3:
            add_lines(self.plane[k], self.plane[k], self.from_end[k])
        elif stage == 4:
            lines = pl.ds(pl.multiple_of(side * half, 16), half)
            add_lines(self.final[k].at[lines], self.half_z[k], self.plane[k].at[lines])

    def task(self, k, produce):
        produce(k)
        for stage in range(self.STAGES):
            self.start(k, stage)
            yield
            self.guarded(self.receiver(stage), lambda: self.absorb(k, stage))
        a, first, width = self.chunks[k]
        self.outs[a][:, first : first + width] = self.final[k][...].astype(F32)

    def settle(self):
        for k in range(len(self.chunks)):
            for stage in range(1, self.STAGES):
                self.guarded(self.sender(stage), lambda: self.copy(k, stage).wait_send())

    def product(self, k, turned, other):
        for of_y in range(2):
            right = other(of_y)
            for i in range(4):
                value = matmul(turned[i * self.rows : (i + 1) * self.rows, :], right)
                self.full[k][of_y, i // 2, i % 2] = value.astype(BF)


def reduction_scratch(rows, chunks):
    shapes = [
        lambda w: (2, 2, rows, w),
        lambda w: (2, rows, w),
        lambda w: (rows, w),
        lambda w: (rows, w),
        lambda w: (rows // 2, w),
        lambda w: (rows, w),
    ]
    scratch = [pltpu.VMEM((2, 2, 2, rows, CHUNK), BF) for _ in range(min(RING, len(chunks)))]
    scratch += [pltpu.VMEM(shape(width), BF) for shape in shapes for _, _, width in chunks]
    return scratch + [pltpu.SemaphoreType.DMA((len(chunks), 7)), pltpu.SemaphoreType.DMA((len(chunks), 7))]


def wide_peers():
    x, c, y, z = here()
    return (
        {"shard": 2 * x + 1 - c},
        {"shard": 2 * (1 - x) + c},
        {"tp": 1 - y},
        {"ctx": z + 1 - 2 * (z % 2)},
    )


CHUNK = 384


def chunks_of(widths):
    return tuple((a, first, CHUNK) for a, width in enumerate(widths) for first in range(0, width, CHUNK))


def slots_task(line, j, y, values, out, pre, post_sem, at_y):
    slots = line.slots
    own = slots // 2
    outgoing, pre_send, pre_recv = pre
    post_send, post_recv = post_sem
    width = line.picked.shape[1]
    mine_rows = pl.ds(pl.multiple_of(half_of(y, line.z) * own, 64), own)
    half = out.shape[1] // 2
    outgoing[...] = values(j, 1 - y)
    before = remote(outgoing, line.blocks.at[line.z, mine_rows], pre_send, pre_recv, at_y)
    before.start()
    line.blocks[line.z, mine_rows, :] = values(j, y)
    yield
    before.wait_recv()
    yield from line.run()
    cols = pl.ds(pl.multiple_of(y * half + j * width, 128), width)
    after = remote(line.picked, out.at[:, cols], post_send, post_recv, at_y)
    after.start()
    out[:, cols] = line.picked[...]
    yield
    after.wait_recv()
    before.wait_send()
    after.wait_send()
    line.settle()


LAYER_AT = (2, 5, 8)
LAYER_GAPS = (1, 1, 1, 1, 1, 1)
AHEAD = 2
X_FIRST = 3
LATER_GAPS = (1, 1, 1, 0, 1)


def chunk_round(k):
    return k // AHEAD


def chunk_gaps(k):
    return (0, max(0, X_FIRST + 5 * k // 4 - chunk_round(k) - 2)) + LATER_GAPS


def backward_kernel(chunks, *refs):
    first_low, attended, hidden_low, pre_low, second_low, act_low, grad, stats, stats_tile, qkv, seg_col, seg_row, seg_tile, layer_low, dealt_row = refs[:15]
    outs, qkv_low, query_sums, value_sums, layer_out = refs[15:18], refs[18], refs[19], refs[20], refs[21]
    rest = refs[22:]
    turned, grad_win, stats_side, stats_win, halo_sem = rest[0:3], rest[3], rest[4], rest[5], rest[6]
    key_t, first_st, second_st, bias_query, bias_key, acc, first_acc, second_acc = rest[7:15]
    stream, stream_sem = rest[15:17]
    outgoing, rest = rest[17 : 17 + PERM], rest[17 + PERM :]
    pre_send, pre_recv, post_send, post_recv = rest[:4]
    line_number = 4 * PERM + 3
    line_refs, reduction_refs = rest[4 : 4 + line_number], rest[4 + line_number :]
    reduction = Reduction(chunks, outs, reduction_refs)
    x, c, y, z = reduction.place
    h = half_of(y, z)
    own, dim = grad.shape
    padded = qkv.shape[0]
    tile = attention_tile(own)
    last = 3
    at_y, at_z = {"tp": 1 - y}, {"ctx": jnp.clip(z - 1 + 2 * h, 0, last)}
    has_z = ((h == 0) & (z > 0)) | ((h == 1) & (z < last))
    greet_all(wide_peers(), ((reduction.inner, {"ctx": 3 - z}),))

    def halos(where, same):
        first = (1 - h) if same else h
        side = h if same else 1 - h
        base = 0 if same else 4
        return (
            remote(
                grad.at[pl.ds(pl.multiple_of(first * (own - HALO), 64), HALO)],
                grad_win.at[pl.ds(pl.multiple_of(side * (HALO + own), 64), HALO)],
                halo_sem.at[base],
                halo_sem.at[base + 1],
                where,
            ),
            remote(stats, stats_side.at[side], halo_sem.at[base + 2], halo_sem.at[base + 3], where),
        )

    for item in halos(at_y, True):
        item.start()

    @pl.when(has_z)
    def _():
        for item in halos(at_z, False):
            item.start()

    grad_win[HALO : HALO + own, :] = grad[...]
    grad_win[2 * HALO + own :, :] = jnp.zeros((padded - 2 * HALO - own, dim), BF)
    for missing, side in (((h == 0) & (z == 0), 0), ((h == 1) & (z == last), 1)):

        @pl.when(missing)
        def _():
            grad_win[side * (HALO + own) : side * (HALO + own) + HALO, :] = jnp.zeros((HALO, dim), BF)
            stats_side[side] = jnp.zeros(stats.shape, F32)

    lefts, rights = (first_low, hidden_low, second_low), (attended, pre_low, act_low)

    def bring(k, of_y):
        a, first, columns = chunks[k]
        half = rights[a].shape[1] // 2
        return pltpu.make_async_copy(
            rights[a].at[:, of_y * half + first : of_y * half + first + columns],
            stream.at[k % 2, of_y],
            stream_sem.at[k % 2, of_y],
        )

    for k in range(min(2, len(chunks))):
        for of_y in range(2):
            bring(k, of_y).start()

    def produce(k):
        a, first, _ = chunks[k]
        if first == 0:
            turned[a][...] = lefts[a][...].T
        for of_y in range(2):
            bring(k, of_y).wait()
        reduction.product(k, turned[a], lambda of_y: stream[k % 2, of_y])
        if k + 2 < len(chunks):
            for of_y in range(2):
                bring(k + 2, of_y).start()

    lines = [line_of(j, PERM, z, dealt_row, True, line_refs) for j in range(PERM)]
    width = dim // 2 // PERM

    def layer_values(j, half):
        return layer_low[:, pl.ds(pl.multiple_of(half * (dim // 2) + j * width, 128), width)]

    def store(rows, p, part):
        at_query = places(p, dim)[0]
        qkv_low[rows, at_query : at_query + 128] = part

    def attention_task():
        yield from run_static(
            query_steps(
                dim, tile, qkv, seg_col, seg_tile, grad, stats_tile, store, query_sums, key_t, first_st, second_st, bias_query, acc
            ),
            tile,
            own // tile,
        )
        for item in halos(at_y, True):
            item.wait()

        @pl.when(has_z)
        def _():
            for item in halos(at_z, False):
                item.wait()

        stats_win[...] = jnp.concatenate(
            [
                stats_side[0][:, own - HALO :],
                stats[...],
                stats_side[1][:, :HALO],
                jnp.zeros((stats.shape[0], padded - 2 * HALO - own), F32),
            ],
            axis=1,
        )
        yield from run_static(
            key_steps(
                dim,
                tile,
                qkv,
                seg_col,
                seg_row,
                grad_win,
                stats_win,
                qkv_low,
                value_sums,
                first_st,
                second_st,
                bias_key,
                first_acc,
                second_acc,
            ),
            tile,
            own // tile,
        )

    tasks = [(chunk_round(k), timed(reduction.task(k, produce), chunk_gaps(k))) for k in range(len(chunks))]
    tasks += [
        (
            LAYER_AT[j],
            timed(
                slots_task(
                lines[j],
                j,
                y,
                layer_values,
                layer_out,
                (outgoing[j], pre_send.at[j], pre_recv.at[j]),
                (post_send.at[j], post_recv.at[j]),
                at_y,
            ), LAYER_GAPS),
        )
        for j in range(PERM)
    ]
    interleave(sorted([(0, attention_task())] + tasks, key=lambda item: item[0]))
    reduction.settle()


def backward_stage(first_low, attended, hidden_low, pre_low, second_low, act_low, grad, stats, qkv, seg_col, seg_row, layer_low, dealt):
    own, dim = grad.shape
    padded = qkv.shape[0]
    rows = dim // 4
    tile = attention_tile(own)
    pairs = dim // 128
    widths = (attended.shape[1] // 2, pre_low.shape[1] // 2, act_low.shape[1] // 2)
    chunks = chunks_of(widths)
    spec = pl.BlockSpec(memory_space=pltpu.VMEM)
    outs = [jax.ShapeDtypeStruct((rows, width), F32) for width in widths]
    outs += [
        jax.ShapeDtypeStruct((own, 3 * dim), BF),
        jax.ShapeDtypeStruct((1, dim), F32),
        jax.ShapeDtypeStruct((1, dim), F32),
        jax.ShapeDtypeStruct((2 * own, dim), BF),
    ]
    scratch = [pltpu.VMEM((dim, own), BF) for _ in range(3)]
    scratch += [
        pltpu.VMEM((padded, dim), BF),
        pltpu.VMEM((2, 32, own), F32),
        pltpu.VMEM((32, padded), F32),
        pltpu.SemaphoreType.DMA((8,)),
        pltpu.VMEM((dim, padded), BF),
        pltpu.VMEM((pairs, 2 * tile, 128), BF),
        pltpu.VMEM((pairs, 2 * tile, 128), BF),
        pltpu.VMEM((BLOCK, 2 * tile), F32),
        pltpu.VMEM((tile, BLOCK), F32),
        pltpu.VMEM((pairs, 128, 2 * tile), F32),
        pltpu.VMEM((pairs, 2 * tile, 128), F32),
        pltpu.VMEM((pairs, 2 * tile, 128), F32),
    ]
    scratch += [pltpu.VMEM((2, 2, own, CHUNK), BF), pltpu.SemaphoreType.DMA((2, 2))]
    scratch += [pltpu.VMEM((own, dim // 2 // PERM), BF) for _ in range(PERM)]
    scratch += [pltpu.SemaphoreType.DMA((PERM,)) for _ in range(4)]
    scratch += line_scratch(lax.axis_size("ctx"), 2 * own, PERM, dim // 2 // PERM)
    scratch += reduction_scratch(rows, chunks)
    args = (
        first_low,
        attended,
        hidden_low,
        pre_low,
        second_low,
        act_low,
        grad,
        stats,
        by_tile(stats, own),
        qkv,
        seg_col,
        seg_row,
        segments_by_tile(seg_row, own),
        layer_low,
        dealt[None, :].astype(F32),
    )
    anywhere = pl.BlockSpec(memory_space=pl.ANY)
    return pl.pallas_call(
        functools.partial(backward_kernel, chunks),
        out_shape=outs,
        in_specs=[anywhere if i in (1, 3, 5) else spec for i in range(len(args))],
        out_specs=[spec] * len(outs),
        scratch_shapes=scratch,
        compiler_params=pltpu.CompilerParams(
            collective_id=1, has_side_effects=True, vmem_limit_bytes=VMEM_LIMIT
        ),
        cost_estimate=pl.CostEstimate(flops=50000000000, bytes_accessed=100000000, transcendentals=0),
    )(*args)


def last_kernel(chunks, *refs):
    inputs, qkv_low, weight, grad_first, dealt_row, vector = refs[:6]
    out, tokens_grad, vector_out = refs[6:9]
    rest = refs[9:]
    number = PERM
    turned, outgoing, pre_send, pre_recv, post_send, post_recv = (
        rest[0],
        rest[1 : 1 + number],
        rest[1 + number],
        rest[2 + number],
        rest[3 + number],
        rest[4 + number],
    )
    vector_in, vector_sum, vector_send, vector_recv = rest[5 + number : 9 + number]
    rest = rest[9 + number :]
    line_number = 4 * number + 3
    line_refs, reduction_refs = rest[:line_number], rest[line_number:]
    reduction = Reduction(chunks, (out,), reduction_refs)
    x, c, y, z = reduction.place
    own, dim = inputs.shape
    at_y = {"tp": 1 - y}
    inner = (z == 1) | (z == 2)
    peers = wide_peers() + ({"ctx": (z + 2) % 4},)
    greet_all(peers, ((inner, {"ctx": 3 - z}),))
    lines = [line_of(j, number, z, dealt_row, True, line_refs) for j in range(number)]
    width = dim // 2 // PERM

    def vector_copy(stage):
        return remote(
            vector_sum.at[stage], vector_in.at[stage], vector_send.at[stage], vector_recv.at[stage], peers[stage]
        )

    def vector_task():
        vector_sum[0] = vector[...]
        for stage in range(5):
            vector_copy(stage).start()
            yield
            vector_copy(stage).wait_recv()
            total = vector_sum[stage] + vector_in[stage]
            if stage < 4:
                vector_sum[stage + 1] = total
            else:
                vector_out[...] = total

    def grad_values(j, half):
        first = pl.ds(pl.multiple_of(half * (dim // 2) + j * width, 128), width)
        return (grad_first[:, first] + matmul_second(qkv_low[...], weight[first, :])).astype(BF)

    def produce(k):
        if k == 0:
            turned[...] = inputs[...].T
        columns, half = pl.ds, qkv_low.shape[1] // 2
        _, first, number_of = chunks[k]
        reduction.product(k, turned, lambda of_y: qkv_low[:, columns(of_y * half + first, number_of)])

    def slots(values, j, index, out_ref):
        return slots_task(
            lines[index],
            j,
            y,
            values,
            out_ref,
            (outgoing[index], pre_send.at[index], pre_recv.at[index]),
            (post_send.at[index], post_recv.at[index]),
            at_y,
        )

    tasks = [(j, slots(grad_values, j, j, tokens_grad)) for j in range(PERM)]
    tasks += [(k, reduction.task(k, produce)) for k in range(len(chunks))]
    tasks += [(1, vector_task())]
    interleave(sorted(tasks, key=lambda item: item[0]))
    reduction.settle()
    for stage in range(5):
        vector_copy(stage).wait_send()


def last_stage(inputs, qkv_low, weight, grad_first, dealt, vector):
    own, dim = inputs.shape
    ctx_size = lax.axis_size("ctx")
    rows = dim // 4
    width = qkv_low.shape[1] // 2
    chunks = chunks_of((width,))
    spec = pl.BlockSpec(memory_space=pltpu.VMEM)
    outs = [
        jax.ShapeDtypeStruct((rows, width), F32),
        jax.ShapeDtypeStruct((2 * own, dim), BF),
        jax.ShapeDtypeStruct(vector.shape, F32),
    ]
    scratch = [pltpu.VMEM((dim, own), BF)]
    scratch += [pltpu.VMEM((own, dim // 2 // PERM), BF) for _ in range(PERM)]
    scratch += [pltpu.SemaphoreType.DMA((PERM,)) for _ in range(4)]
    scratch += [pltpu.VMEM((5,) + vector.shape, F32), pltpu.VMEM((5,) + vector.shape, F32)]
    scratch += [pltpu.SemaphoreType.DMA((5,)), pltpu.SemaphoreType.DMA((5,))]
    scratch += line_scratch(ctx_size, 2 * own, PERM, dim // 2 // PERM)
    scratch += reduction_scratch(rows, chunks)
    return pl.pallas_call(
        functools.partial(last_kernel, chunks),
        out_shape=outs,
        in_specs=[spec] * 6,
        out_specs=[spec] * len(outs),
        scratch_shapes=scratch,
        compiler_params=pltpu.CompilerParams(
            collective_id=2, has_side_effects=True, vmem_limit_bytes=VMEM_LIMIT
        ),
        cost_estimate=pl.CostEstimate(flops=10000000000, bytes_accessed=100000000, transcendentals=0),
    )(inputs, qkv_low, weight, grad_first, dealt[None, :].astype(F32), vector)


def project_kernel(dim, x_ref, weight, bias, out):
    step = 256
    third = weight.shape[1] // 3

    def body(i, carry):
        lines = pl.ds(pl.multiple_of(i * step, step), step)
        value = (matmul(x_ref[lines, :], weight[...]) + bias[0]).astype(BF)
        scale = jnp.where(lax.broadcasted_iota(jnp.int32, (1, 3 * third), 1) < third, 0.125, 1.0).astype(BF)
        out[lines, :] = value * scale
        return carry

    lax.fori_loop(0, x_ref.shape[0] // step, body, 0)


def project(x_window, weight, bias):
    rows, dim = x_window.shape
    width = 3 * dim // 2
    return pl.pallas_call(
        functools.partial(project_kernel, dim),
        grid=(2,),
        out_shape=jax.ShapeDtypeStruct((rows, 2 * width), BF),
        in_specs=[
            pl.BlockSpec((rows, dim), lambda i: (0, 0)),
            pl.BlockSpec((dim, width), lambda i: (0, i)),
            pl.BlockSpec((1, 1, width), lambda i: (i, 0, 0)),
        ],
        out_specs=pl.BlockSpec((rows, width), lambda i: (0, i)),
        compiler_params=pltpu.CompilerParams(vmem_limit_bytes=VMEM_LIMIT),
        cost_estimate=pl.CostEstimate(flops=6000000000, bytes_accessed=14000000, transcendentals=0),
    )(x_window, weight, bias)


def rows_to_slots(values, dealt, place_z, place_y):
    own, dim = values.shape
    half = dim // 2
    keep = lax.dynamic_slice_in_dim(values, place_y * half, half, axis=1)
    send = lax.dynamic_slice_in_dim(values, (1 - place_y) * half, half, axis=1)
    other = lax.ppermute(send, "tp", [(0, 1), (1, 0)])
    first = jnp.where(place_y == 0, keep, other)
    second = jnp.where(place_y == 0, other, keep)
    block = jnp.concatenate([first, second], axis=0)
    everything = lax.all_gather(block, "ctx", axis=0, tiled=True)
    slots = 2 * own
    mine = lax.dynamic_slice_in_dim(dealt, place_z * slots, slots)
    picked = jnp.take(everything, mine, axis=0, mode="clip")
    other_columns = lax.ppermute(picked, "tp", [(0, 1), (1, 0)])
    return jnp.concatenate(
        [jnp.where(place_y == 0, picked, other_columns), jnp.where(place_y == 0, other_columns, picked)], axis=1
    )


def slots_to_rows(values, dealt, place_z, place_y):
    slots, dim = values.shape
    half, own = dim // 2, slots // 2
    block = lax.dynamic_slice_in_dim(values, place_y * half, half, axis=1)
    everything = lax.all_gather(block, "ctx", axis=0, tiled=True)
    wanted = place_z * slots + lax.broadcasted_iota(jnp.int32, (slots, 1), 0)
    chosen = (wanted == dealt[None, :]).astype(BF)
    picked = matmul(chosen, everything).astype(BF)
    keep = lax.dynamic_slice_in_dim(picked, place_y * own, own, axis=0)
    send = lax.dynamic_slice_in_dim(picked, (1 - place_y) * own, own, axis=0)
    other = lax.ppermute(send, "tp", [(0, 1), (1, 0)])
    return jnp.concatenate([jnp.where(place_y == 0, keep, other), jnp.where(place_y == 0, other, keep)], axis=1)


def per_device(
    tokens,
    cotangent,
    seq_lengths,
    dealing,
    query_weight,
    query_bias,
    key_weight,
    value_weight,
    value_bias,
    output_weight,
    output_bias,
    first_gain,
    first_shift,
    up_weight,
    up_bias,
    down_weight,
    down_bias,
    second_gain,
    second_shift,
):
    rows, dim = tokens.shape
    ctx_size, tp_size = lax.axis_size("ctx"), lax.axis_size("tp")
    group_rows = rows * ctx_size
    own = rows // tp_size
    place_z, place_y = lax.axis_index("ctx"), lax.axis_index("tp")
    window = HALO + own + HALO
    padded = -(-window // BLOCK) * BLOCK
    dealt = dealing[0]

    lengths = seq_lengths[0]
    number = lengths.shape[0]
    upto = jnp.arange(number)[:, None] >= jnp.arange(number)[None, :]
    ends = jnp.sum(jnp.where(upto, lengths[None, :], 0), axis=1)
    starts = ends - lengths
    special = lax.axis_size("shard") == 4 and tp_size == 2 and ctx_size == 4
    place_h = half_of(place_y, place_z) if special else place_y
    first_row = place_z * rows + place_h * own
    index = jnp.arange(padded, dtype=jnp.int32)
    position = first_row - HALO + index
    valid = (position >= 0) & (position < group_rows) & (index < window)
    segment = jnp.sum((position[:, None] >= ends[None, :-1]).astype(jnp.int32), axis=1)
    segment = jnp.where(valid, segment, -1)
    seg_row, seg_col = segment[None, :], segment[:, None]
    tile = attention_tile(own)
    tile_first = first_row + tile * jnp.arange(own // tile, dtype=jnp.int32)
    tile_last = tile_first + tile - 1
    begin = jnp.max(jnp.where(starts[None, :] <= tile_first[:, None], starts[None, :], 0), axis=1)
    finish = jnp.min(jnp.where(ends[None, :] > tile_last[:, None], ends[None, :], group_rows), axis=1)
    shift = HALO - first_row
    bounds = jnp.stack([(begin + shift) // BLOCK, (finish + shift + BLOCK - 1) // BLOCK], axis=1).astype(jnp.int32)

    half_dim = dim // tp_size
    pieces = [
        jnp.concatenate([query_weight, key_weight, value_weight], axis=1),
        output_weight.T,
        up_weight,
        down_weight.T,
    ]
    flat = jnp.concatenate([query_bias, value_bias, up_bias])
    small = jnp.broadcast_to(flat[None, :], (16, flat.shape[0]))
    inputs = lax.dynamic_slice_in_dim(tokens, place_h * own, own, axis=0)
    if special:
        whole, biases, qkv, cot_rows, attended, logsum = first_stage(
            pieces, small, tokens, cotangent, dealt, seg_col, seg_row, padded
        )
        whole_up_bias = biases[::16, dim:].reshape(-1).astype(F32)
    else:
        whole = [
            lax.all_gather(lax.all_gather(piece, "shard", axis=0, tiled=True), "tp", axis=1, tiled=True)
            for piece in pieces
        ]
        biases = lax.all_gather(small, "tp", axis=0, tiled=True)[::16].astype(F32)
        qkv_bias = jnp.concatenate(
            [biases[:, :half_dim], jnp.zeros((tp_size, half_dim), F32), biases[:, half_dim:dim]], axis=1
        )[:, None, :]
        whole_up_bias = biases[:, dim:].reshape(-1)
        edge = jnp.where(place_y == 0, tokens[rows - HALO :], tokens[:HALO])
        hops = [(2 * z, 2 * z + 2) for z in range(ctx_size - 1)] + [(2 * z + 1, 2 * z - 1) for z in range(1, ctx_size)]
        arrived = lax.ppermute(edge, ("ctx", "tp"), hops)
        x_window = jnp.where(
            place_y == 0,
            jnp.concatenate([arrived, tokens[: own + HALO]], axis=0),
            jnp.concatenate([tokens[own - HALO :], arrived], axis=0),
        )
        x_window = jnp.pad(x_window, ((0, padded - window), (0, 0)))
        qkv = project(x_window, whole[0], qkv_bias)
        cot_rows = slots_to_rows(cotangent, dealt, place_z, place_y)
        attended, logsum = attention_forward(qkv, seg_col, seg_row, bounds, own, dim)
    wide_qkv, wide_output, wide_up, wide_down = whole
    output_bias = output_bias.astype(F32)
    first_gain = first_gain.astype(F32)
    first_shift = first_shift.astype(F32)
    down_bias = down_bias.astype(F32)
    second_gain = second_gain.astype(F32)
    second_shift = second_shift.astype(F32)

    grad_out = cot_rows.astype(F32)
    hidden_one, normed_one, inverse_one = norm_forward(
        inputs.astype(F32) + matmul_second(attended, wide_output) + output_bias, first_gain, first_shift
    )
    hidden_low = hidden_one.astype(BF)
    pre_act = matmul(hidden_low, wide_up) + whole_up_bias
    erf_part = 0.5 * (1.0 + jax.scipy.special.erf(pre_act * HALF_ROOT))
    act_low = (pre_act * erf_part).astype(BF)
    layer_value, normed_two, inverse_two = norm_forward(
        hidden_one + matmul_second(act_low, wide_down) + down_bias, second_gain, second_shift
    )
    layer_low = layer_value.astype(BF)

    second_shift_grad = jnp.sum(grad_out, axis=0)
    second_gain_grad = jnp.sum(grad_out * normed_two, axis=0)
    grad_second = norm_backward(grad_out, normed_two, inverse_two, second_gain)
    down_bias_grad = jnp.sum(grad_second, axis=0)
    second_low = grad_second.astype(BF)
    slope = erf_part + pre_act * DENSITY * jnp.exp(-0.5 * pre_act * pre_act)
    grad_pre = matmul(second_low, wide_down) * slope
    up_bias_grad = jnp.sum(grad_pre, axis=0)
    pre_low = grad_pre.astype(BF)
    grad_hidden = grad_second + matmul_second(pre_low, wide_up)
    first_shift_grad = jnp.sum(grad_hidden, axis=0)
    first_gain_grad = jnp.sum(grad_hidden * normed_one, axis=0)
    grad_first = norm_backward(grad_hidden, normed_one, inverse_one, first_gain)
    output_bias_grad = jnp.sum(grad_first, axis=0)
    first_low = grad_first.astype(BF)
    attended_grad = matmul(first_low, wide_output).astype(BF)
    head_of = (jnp.arange(dim)[None, :] // HEAD == jnp.arange(16)[:, None]).astype(F32)
    delta = lax.dot_general(
        head_of,
        attended_grad.astype(F32) * attended.astype(F32),
        (((1,), (1,)), ((), ())),
        precision=lax.Precision.HIGHEST,
        preferred_element_type=F32,
    )
    stats = jnp.concatenate([logsum, delta], axis=0)
    if special:
        output_own, up_own, down_own, qkv_low, query_bias_grad, value_bias_grad, layer_out = backward_stage(
            first_low,
            attended,
            hidden_low,
            pre_low,
            second_low,
            act_low,
            attended_grad,
            stats,
            qkv,
            seg_col,
            seg_row,
            layer_low,
            dealt,
        )
    else:
        layer_out = rows_to_slots(layer_low, dealt, place_z, place_y)
        up_hops = [(i, i + 1) for i in range(ctx_size * tp_size - 1)]
        down_hops = [(i + 1, i) for i in range(ctx_size * tp_size - 1)]
        grad_win, stats_win = [
            jnp.concatenate(
                [
                    lax.ppermute(lax.slice_in_dim(array, own - HALO, own, axis=axis), ("ctx", "tp"), up_hops),
                    array,
                    lax.ppermute(lax.slice_in_dim(array, 0, HALO, axis=axis), ("ctx", "tp"), down_hops),
                    jnp.zeros((padded - window, dim) if axis == 0 else (32, padded - window), array.dtype),
                ],
                axis=axis,
            )
            for array, axis in ((attended_grad, 0), (stats, 1))
        ]
        query_low, query_bias_grad = attention_query(qkv, seg_col, seg_row, bounds, attended_grad, stats, dim)
        qkv_low, value_bias_grad = attention_key(
            qkv, seg_col, seg_row, bounds, grad_win, stats_win, query_low, own, dim
        )
    vectors = jnp.concatenate(
        [
            query_bias_grad[0],
            value_bias_grad[0],
            up_bias_grad,
            output_bias_grad,
            first_gain_grad,
            first_shift_grad,
            down_bias_grad,
            second_gain_grad,
            second_shift_grad,
        ]
    )
    if special:
        qkv_own, tokens_grad, small_sum = last_stage(
            inputs, qkv_low, wide_qkv, grad_first, dealt, vectors.reshape(-1, 128)
        )
        small_sum = small_sum.reshape(-1)
        owned = [qkv_own, output_own, up_own, down_own]
    else:
        owned = []
        for full in (
            matmul_first(inputs, qkv_low),
            matmul_first(first_low, attended),
            matmul_first(hidden_low, pre_low),
            matmul_first(second_low, act_low),
        ):
            part = lax.psum_scatter(full.astype(BF), "tp", scatter_dimension=1, tiled=True)
            part = lax.psum_scatter(part, "shard", scatter_dimension=0, tiled=True)
            owned.append(lax.psum(part, "ctx").astype(F32))
        small_sum = lax.psum(vectors, ("shard", "ctx", "tp"))
        tokens_grad = (grad_first + matmul_second(qkv_low, wide_qkv)).astype(BF)
        tokens_grad = rows_to_slots(tokens_grad, dealt, place_z, place_y)
    hidden = up_bias_grad.shape[0]
    sizes = [dim, dim, hidden] + [dim] * 6
    offsets = [sum(sizes[:i]) for i in range(len(sizes))]
    parts = [small_sum[o : o + s] for o, s in zip(offsets, sizes)]

    def by_tp(vector):
        part = vector.shape[0] // tp_size
        return lax.dynamic_slice_in_dim(vector, place_y * part, part)

    return (
        layer_out,
        tokens_grad,
        owned[0][:, :half_dim],
        by_tp(parts[0]),
        owned[0][:, half_dim : 2 * half_dim],
        owned[0][:, 2 * half_dim :],
        by_tp(parts[1]),
        owned[1].T,
        parts[3],
        parts[4],
        parts[5],
        owned[2],
        by_tp(parts[2]),
        owned[3].T,
        parts[6],
        parts[7],
        parts[8],
    )


def solution(mesh):
    return jax.shard_map(
        per_device,
        mesh=mesh,
        in_specs=(
            P(("shard", "ctx"), None),
            P(("shard", "ctx"), None),
            P("shard", None),
            P("shard", None),
            P("shard", "tp"),
            P("tp"),
            P("shard", "tp"),
            P("shard", "tp"),
            P("tp"),
            P("tp", "shard"),
            P(),
            P(),
            P(),
            P("shard", "tp"),
            P("tp"),
            P("tp", "shard"),
            P(),
            P(),
            P(),
        ),
        out_specs=(
            P(("shard", "ctx"), None),
            P(("shard", "ctx"), None),
            P("shard", "tp"),
            P("tp"),
            P("shard", "tp"),
            P("shard", "tp"),
            P("tp"),
            P("tp", "shard"),
            P(),
            P(),
            P(),
            P("shard", "tp"),
            P("tp"),
            P("tp", "shard"),
            P(),
            P(),
            P(),
        ),
        check_vma=False,
    )
```

```python
import functools

import jax
import jax.numpy as jnp
from jax import lax
from jax.experimental import pallas as pl
from jax.experimental.pallas import tpu as pltpu
from jax.sharding import PartitionSpec as P

HEAD = 64
HALO = 512
HALF_ROOT = 0.7071067811865476
DENSITY = 0.3989422804014327
NEG_FILL = -1000000000.0
BF = jnp.bfloat16
F32 = jnp.float32
BLOCK = 256
VMEM_LIMIT = 60 * 1024 * 1024


def matmul(former, latter):
    return jnp.dot(former, latter, preferred_element_type=F32)


def matmul_first(former, latter):
    return lax.dot_general(former, latter, (((0,), (0,)), ((), ())), preferred_element_type=F32)


def matmul_second(former, latter):
    return lax.dot_general(former, latter, (((1,), (1,)), ((), ())), preferred_element_type=F32)


def norm_forward(values, norm_gain, norm_shift):
    centre = values - jnp.mean(values, axis=1, keepdims=True)
    spread = jnp.mean(centre * centre, axis=1, keepdims=True)
    inverse = lax.rsqrt(spread + 1e-06)
    normed = centre * inverse
    return (norm_gain * normed + norm_shift, normed, inverse)


def norm_backward(gradient, normed, inverse, norm_gain):
    scaled = gradient * norm_gain
    bracket = (
        scaled
        - jnp.mean(scaled, axis=1, keepdims=True)
        - normed * jnp.mean(scaled * normed, axis=1, keepdims=True)
    )
    return inverse * bracket


def places(pair, dim):
    half, inner = divmod(pair, dim // 256)
    base = half * (3 * dim // 2) + inner * 128
    return base, base + dim // 2, base + dim


def take(qkv, rows, pair, dim, which):
    first = places(pair, dim)[which]
    return qkv[rows, first : first + 128]


def low_lanes(rows):
    return lax.broadcasted_iota(jnp.int32, (rows, 128), 1) < HEAD


def stacked(pair):
    low = low_lanes(pair.shape[0])
    zero = jnp.zeros_like(pair)
    return jnp.concatenate([jnp.where(low, pair, zero), jnp.where(low, zero, pair)], axis=0)


def unstacked(both):
    rows = both.shape[0] // 2
    return jnp.where(low_lanes(rows), both[:rows], both[rows:])


def bias_of(own_seg, other_seg):
    return jnp.where(own_seg == other_seg, 0.0, NEG_FILL)


def turn_columns(qkv, pair, dim, which, turned):
    turned[pair * 128 : pair * 128 + 128, :] = take(qkv, slice(0, qkv.shape[0]), pair, dim, which).T


def twice(row_pair):
    return jnp.concatenate([row_pair[0:1], row_pair[1:2]], axis=1)


def forward_steps(dim, tile, qkv, seg_col, seg_tile, out, logsum, value_t, query_st, bias_ref, acc, top, total):
    pairs = dim // 128

    def prepare():
        for p in range(pairs):
            turn_columns(qkv, p, dim, 2, value_t)

    def begin(i):
        rows = pl.ds(pl.multiple_of(HALO + i * tile, 64), tile)
        for p in range(pairs):
            query_st[p] = stacked(take(qkv, rows, p, dim, 0))
        acc[...] = jnp.zeros_like(acc)
        total[...] = jnp.zeros_like(total)
        top[...] = jnp.full_like(top, 2 * NEG_FILL)

    def block(i, j):
        start = pl.multiple_of(j * BLOCK, BLOCK)
        bias_ref[...] = bias_of(seg_col[pl.ds(start, BLOCK), :], seg_tile[i])
        for p in range(pairs):
            key = take(qkv, pl.ds(start, BLOCK), p, dim, 1)
            scores = matmul_second(key, query_st[p]) + bias_ref[...]
            old = top[p]
            new = jnp.maximum(old, jnp.max(scores, axis=0, keepdims=True))
            keep = jnp.exp(old - new)
            raised = jnp.exp(scores - new)
            total[p] = keep * total[p] + jnp.sum(raised, axis=0, keepdims=True)
            value = value_t[p * 128 : p * 128 + 128, pl.ds(start, BLOCK)]
            acc[p] = keep * acc[p] + matmul(value, raised.astype(BF))
            top[p] = new

    def finish(i):
        lines = pl.ds(pl.multiple_of(i * tile, tile), tile)
        for p in range(pairs):
            whole = total[p]
            out[lines, p * 128 : p * 128 + 128] = unstacked((acc[p] / whole).T).astype(BF)
            lse = top[p] + jnp.log(whole)
            logsum[i, 2 * p : 2 * p + 1, :] = lse[:, :tile]
            logsum[i, 2 * p + 1 : 2 * p + 2, :] = lse[:, tile:]
        for p in range(2 * pairs, 16):
            logsum[i, p : p + 1, :] = jnp.zeros((1, tile), F32)

    return prepare, begin, block, finish


def query_steps(dim, tile, qkv, seg_col, seg_tile, grad, stats, store, sums, key_t, query_st, grad_st, bias_ref, acc):
    pairs = dim // 128

    def prepare():
        sums[...] = jnp.zeros_like(sums)
        for p in range(pairs):
            turn_columns(qkv, p, dim, 1, key_t)

    def begin(i):
        own_rows = pl.ds(pl.multiple_of(i * tile, tile), tile)
        rows = pl.ds(pl.multiple_of(HALO + i * tile, 64), tile)
        for p in range(pairs):
            query_st[p] = stacked(take(qkv, rows, p, dim, 0))
            grad_st[p] = stacked(grad[own_rows, p * 128 : p * 128 + 128])
        acc[...] = jnp.zeros_like(acc)

    def block(i, j):
        there = pl.ds(pl.multiple_of(j * BLOCK, BLOCK), BLOCK)
        bias_ref[...] = bias_of(seg_col[there, :], seg_tile[i])
        for p in range(pairs):
            scores = matmul_second(take(qkv, there, p, dim, 1), query_st[p]) + bias_ref[...]
            probs = jnp.exp(scores - twice(stats[i, 2 * p : 2 * p + 2, :]))
            grad_probs = matmul_second(take(qkv, there, p, dim, 2), grad_st[p])
            grad_scores = (probs * (grad_probs - twice(stats[i, 16 + 2 * p : 18 + 2 * p, :]))).astype(BF)
            acc[p] += matmul(key_t[p * 128 : p * 128 + 128, there], grad_scores)

    def finish(i):
        own_rows = pl.ds(pl.multiple_of(i * tile, tile), tile)
        for p in range(pairs):
            part = 0.125 * unstacked(acc[p].T)
            store(own_rows, p, part.astype(BF))
            sums[:, p * 128 : p * 128 + 128] += jnp.sum(part, axis=0, keepdims=True)

    return prepare, begin, block, finish


def key_steps(dim, tile, qkv, seg_col, seg_row, grad, stats, out, sums, key_st, value_st, bias_ref, key_acc, value_acc):
    pairs = dim // 128

    def prepare():
        sums[...] = jnp.zeros_like(sums)

    def begin(i):
        rows = pl.ds(pl.multiple_of(HALO + i * tile, 64), tile)
        for p in range(pairs):
            key_st[p] = stacked(take(qkv, rows, p, dim, 1))
            value_st[p] = stacked(take(qkv, rows, p, dim, 2))
        key_acc[...] = jnp.zeros_like(key_acc)
        value_acc[...] = jnp.zeros_like(value_acc)

    def block(i, j):
        there = pl.ds(pl.multiple_of(j * BLOCK, BLOCK), BLOCK)
        seg_here = seg_col[pl.ds(pl.multiple_of(HALO + i * tile, 64), tile), :]
        bias_ref[...] = bias_of(seg_here, seg_row[:, there])
        for p in range(pairs):
            query = take(qkv, there, p, dim, 0)
            grad_pair = grad[there, p * 128 : p * 128 + 128]
            scores = matmul_second(key_st[p], query)
            grad_probs = matmul_second(value_st[p], grad_pair)
            probs_all, grads_all = [], []
            for half in range(2):
                head = 2 * p + half
                lines = slice(half * tile, half * tile + tile)
                probs = jnp.exp(scores[lines] + bias_ref[...] - stats[head : head + 1, there])
                grads_all.append((probs * (grad_probs[lines] - stats[16 + head : 17 + head, there])).astype(BF))
                probs_all.append(probs.astype(BF))
            key_acc[p] += matmul(jnp.concatenate(grads_all, axis=0), query)
            value_acc[p] += matmul(jnp.concatenate(probs_all, axis=0), grad_pair)

    def finish(i):
        own_rows = pl.ds(pl.multiple_of(i * tile, tile), tile)
        for p in range(pairs):
            _, at_key, at_value = places(p, dim)
            out[own_rows, at_key : at_key + 128] = unstacked(key_acc[p]).astype(BF)
            part = unstacked(value_acc[p])
            out[own_rows, at_value : at_value + 128] = part.astype(BF)
            sums[:, p * 128 : p * 128 + 128] += jnp.sum(part, axis=0, keepdims=True)

    return prepare, begin, block, finish


def run_dynamic(steps, bounds, tiles):
    prepare, begin, block, finish = steps
    prepare()

    def one_tile(i, carry):
        begin(i)

        def one_block(j, inner):
            block(i, j)
            return inner

        lax.fori_loop(bounds[i, 0], bounds[i, 1], one_block, 0)
        finish(i)
        return carry

    lax.fori_loop(0, tiles, one_tile, 0)


PIECE = 2


def run_static(steps, tile, tiles):
    prepare, begin, block, finish = steps
    prepare()
    yield
    for i in range(tiles):
        first = (HALO + i * tile - HALO + 1) // BLOCK
        after = -(-(HALO + i * tile + tile + HALO - 1) // BLOCK)
        begin(i)
        for piece in range(first, after, PIECE):

            def one_block(j, inner):
                block(i, j)
                return inner

            lax.fori_loop(piece, min(piece + PIECE, after), one_block, 0)
            if piece + PIECE >= after:
                finish(i)
            yield


def forward_kernel(dim, tile, bounds, *refs):
    run_dynamic(forward_steps(dim, tile, *refs), bounds, refs[3].shape[0] // tile)


def query_kernel(dim, tile, bounds, qkv, seg_col, seg_tile, grad, stats, out, sums, *scratch):
    def store(rows, p, part):
        out[rows, p * 128 : p * 128 + 128] = part

    run_dynamic(
        query_steps(dim, tile, qkv, seg_col, seg_tile, grad, stats, store, sums, *scratch), bounds, out.shape[0] // tile
    )


def key_kernel(dim, tile, bounds, qkv, seg_col, seg_row, grad, stats, query_low, out, sums, *scratch):
    for p in range(dim // 128):
        at_query = places(p, dim)[0]
        out[:, at_query : at_query + 128] = query_low[:, p * 128 : p * 128 + 128]
    run_dynamic(
        key_steps(dim, tile, qkv, seg_col, seg_row, grad, stats, out, sums, *scratch), bounds, out.shape[0] // tile
    )


def vmem_call(kernel, arrays, bounds, outs, scratch, flops):
    spec = pl.BlockSpec(memory_space=pltpu.VMEM)
    return pl.pallas_call(
        kernel,
        out_shape=outs,
        in_specs=[pl.BlockSpec(memory_space=pltpu.SMEM)] + [spec] * len(arrays),
        out_specs=jax.tree.map(lambda leaf: spec, outs),
        scratch_shapes=scratch,
        compiler_params=pltpu.CompilerParams(vmem_limit_bytes=VMEM_LIMIT),
        cost_estimate=pl.CostEstimate(flops=flops, bytes_accessed=12000000, transcendentals=6000000),
    )(bounds, *arrays)


def attention_tile(own):
    for tile in (192, 128, 64, 32, 16):
        if own % tile == 0:
            return tile
    raise ValueError("rows")


def by_tile(rows_last, own):
    tile = attention_tile(own)
    return rows_last.reshape(rows_last.shape[0], own // tile, tile).transpose(1, 0, 2)


def segments_by_tile(seg_row, own):
    tiles = by_tile(lax.slice_in_dim(seg_row, HALO, HALO + own, axis=1), own)
    return jnp.concatenate([tiles, tiles], axis=2)


def forward_scratch(padded, tile, dim):
    pairs = dim // 128
    return [
        pltpu.VMEM((dim, padded), BF),
        pltpu.VMEM((pairs, 2 * tile, 128), BF),
        pltpu.VMEM((BLOCK, 2 * tile), F32),
        pltpu.VMEM((pairs, 128, 2 * tile), F32),
        pltpu.VMEM((pairs, 1, 2 * tile), F32),
        pltpu.VMEM((pairs, 1, 2 * tile), F32),
    ]


def attention_forward(qkv, seg_col, seg_row, bounds, own, dim):
    tile = attention_tile(own)
    pairs = dim // 128
    out, logsum = vmem_call(
        functools.partial(forward_kernel, dim, tile),
        (qkv, seg_col, segments_by_tile(seg_row, own)),
        bounds,
        (jax.ShapeDtypeStruct((own, dim), BF), jax.ShapeDtypeStruct((own // tile, 16, tile), F32)),
        forward_scratch(qkv.shape[0], tile, dim),
        10_000_000_000,
    )
    return out, logsum.transpose(1, 0, 2).reshape(16, own)


def attention_query(qkv, seg_col, seg_row, bounds, grad, stats, dim):
    own = grad.shape[0]
    tile = attention_tile(own)
    pairs = dim // 128
    return vmem_call(
        functools.partial(query_kernel, dim, tile),
        (qkv, seg_col, segments_by_tile(seg_row, own), grad, by_tile(stats, own)),
        bounds,
        (jax.ShapeDtypeStruct((own, dim), BF), jax.ShapeDtypeStruct((1, dim), F32)),
        [
            pltpu.VMEM((dim, qkv.shape[0]), BF),
            pltpu.VMEM((pairs, 2 * tile, 128), BF),
            pltpu.VMEM((pairs, 2 * tile, 128), BF),
            pltpu.VMEM((BLOCK, 2 * tile), F32),
            pltpu.VMEM((pairs, 128, 2 * tile), F32),
        ],
        15_000_000_000,
    )


def attention_key(qkv, seg_col, seg_row, bounds, grad_win, stats_win, query_low, own, dim):
    tile = attention_tile(own)
    pairs = dim // 128
    return vmem_call(
        functools.partial(key_kernel, dim, tile),
        (qkv, seg_col, seg_row, grad_win, stats_win, query_low),
        bounds,
        (jax.ShapeDtypeStruct((own, 3 * dim), BF), jax.ShapeDtypeStruct((1, dim), F32)),
        [
            pltpu.VMEM((pairs, 2 * tile, 128), BF),
            pltpu.VMEM((pairs, 2 * tile, 128), BF),
            pltpu.VMEM((tile, BLOCK), F32),
            pltpu.VMEM((pairs, 2 * tile, 128), F32),
            pltpu.VMEM((pairs, 2 * tile, 128), F32),
        ],
        20_000_000_000,
    )


def remote(src, dst, send_sem, recv_sem, where):
    return pltpu.make_async_remote_copy(
        src_ref=src,
        dst_ref=dst,
        send_sem=send_sem,
        recv_sem=recv_sem,
        device_id=where,
        device_id_type=pl.DeviceIdType.MESH,
    )


def here():
    shard, z, y = lax.axis_index("shard"), lax.axis_index("ctx"), lax.axis_index("tp")
    return shard // 2, shard % 2, y, z


def half_of(y, z):
    return (y + z) % 2


def interleave(tasks):
    running, turn = [], 0
    while tasks or running:
        running += [task for first, task in tasks if first <= turn]
        tasks = [item for item in tasks if item[0] > turn]
        alive = []
        for task in running:
            try:
                next(task)
                alive.append(task)
            except StopIteration:
                pass
        running, turn = alive, turn + 1


def timed(task, gaps):
    for stage, _ in enumerate(task):
        yield
        for _ in range(gaps[min(stage, len(gaps) - 1)]):
            yield


def greet_all(always, sometimes):
    barrier = pltpu.get_barrier_semaphore()
    number = jnp.int32(len(always))
    for peer in always:
        pl.semaphore_signal(barrier, inc=1, device_id=peer, device_id_type=pl.DeviceIdType.MESH)
    for condition, peer in sometimes:

        @pl.when(condition)
        def _():
            pl.semaphore_signal(barrier, inc=1, device_id=peer, device_id_type=pl.DeviceIdType.MESH)

        number = number + condition.astype(jnp.int32)
    pl.semaphore_wait(barrier, number)


class Line:
    SCRATCH = 4

    def __init__(self, z, dealt, to_slots, refs, sems):
        self.z, self.dealt, self.to_slots = z, dealt, to_slots
        self.blocks, self.picked, self.away, self.arrived = refs
        self.send, self.block_recv, self.away_recv = sems
        self.inner = (z == 1) | (z == 2)
        self.outer = (z == 0) | (z == 3)
        self.near = 1 + z // 3
        self.end = jnp.maximum(3 * (z - 1), 0) % 6
        self.middle = 3 - z
        self.far = 3 - self.end
        self.slots = refs[0].shape[1]

    def copy(self, what):
        if what == "own_near":
            block, where, sem = self.z, self.near, 0
        elif what == "own_middle":
            block, where, sem = self.z, self.middle, 0
        elif what == "forward":
            block, where, sem = self.end, self.middle, 1
        else:
            where = self.end
            return remote(self.away, self.arrived, self.send.at[2], self.away_recv, {"ctx": where})
        there = self.blocks.at[block]
        return remote(there, there, self.send.at[sem], self.block_recv.at[block], {"ctx": where})

    def wait_block(self, block):
        there = self.blocks.at[block]
        remote(there, there, self.send.at[0], self.block_recv.at[block], {"ctx": self.middle}).wait_recv()

    def select(self, target, wanted_by, block, start):
        slots = self.slots
        wide = 384 if slots % 384 == 0 else 128

        def body(i, carry):
            lines = pl.ds(pl.multiple_of(i * wide, 128), wide)
            if self.to_slots:
                row = self.dealt[:, pl.ds(pl.multiple_of(wanted_by * slots + i * wide, 128), wide)]
                wanted = jnp.broadcast_to(row, (8, wide)).T[:, :1]
                offered = (block * slots + lax.broadcasted_iota(jnp.int32, (wide, slots), 1)).astype(F32)
            else:
                wanted = wanted_by * slots + i * wide + lax.broadcasted_iota(jnp.int32, (wide, slots), 0)
                offered = self.dealt[:, pl.ds(pl.multiple_of(block * slots, 128), slots)]
            chosen = jnp.where(wanted == offered, 1.0, 0.0).astype(BF)
            part = matmul(chosen, self.blocks[block]).astype(BF)
            target[lines, :] = part if start else target[lines, :] + part
            return carry

        lax.fori_loop(0, slots // wide, body, 0)

    def run(self):
        @pl.when(self.outer)
        def _():
            self.copy("own_near").start()

        @pl.when(self.inner)
        def _():
            self.copy("own_middle").start()

        self.select(self.picked, self.z, self.z, True)
        yield

        @pl.when(self.inner)
        def _():
            self.wait_block(self.end)
            self.copy("forward").start()
            self.select(self.picked, self.z, self.end, False)
            self.select(self.away, self.end, self.z, True)

        yield

        @pl.when(self.inner)
        def _():
            self.wait_block(self.middle)
            self.select(self.away, self.end, self.middle, False)
            self.select(self.picked, self.z, self.middle, False)

        yield

        @pl.when(self.inner)
        def _():
            self.wait_block(self.far)
            self.select(self.away, self.end, self.far, False)
            self.copy("away").start()
            self.select(self.picked, self.z, self.far, False)

        yield

        @pl.when(self.outer)
        def _():
            self.copy("away").wait_recv()
            self.picked[...] = self.picked[...] + self.arrived[...]

    def settle(self):
        @pl.when(self.outer)
        def _():
            self.copy("own_near").wait_send()

        @pl.when(self.inner)
        def _():
            self.copy("own_middle").wait_send()
            self.copy("forward").wait_send()
            self.copy("away").wait_send()


def line_scratch(ctx_size, slots, chunks, columns):
    blocks = [pltpu.VMEM((ctx_size, slots, columns), BF) for _ in range(chunks)]
    others = [pltpu.VMEM((slots, columns), BF) for _ in range(3 * chunks)]
    sems = [pltpu.SemaphoreType.DMA((chunks, 3)), pltpu.SemaphoreType.DMA((chunks, ctx_size)), pltpu.SemaphoreType.DMA((chunks,))]
    return blocks + others + sems


def line_of(j, chunks, z, dealt, to_slots, refs):
    blocks, others, sems = refs[:chunks], refs[chunks : 4 * chunks], refs[4 * chunks :]
    return Line(
        z,
        dealt,
        to_slots,
        (blocks[j], others[3 * j], others[3 * j + 1], others[3 * j + 2]),
        (sems[0].at[j], sems[1].at[j], sems[2].at[j]),
    )


PERM = 3


MIDDLE_AT = (4, 8, 12)
COTANGENT_AT = (1, 2, 3)
COTANGENT_PAUSE = 1


def first_kernel(widths, padded, *refs):
    count = len(widths)
    pieces, (small, tokens, cotangent, dealt_row, seg_col, seg_tile) = refs[:count], refs[count : count + 6]
    refs = refs[count + 6 :]
    wholes, (small_whole, qkv_out, cot_rows, attended, logsum) = refs[:count], refs[count : count + 5]
    rest = refs[count + 5 :]
    attention_refs, qkv, qkv_sem, rest = rest[:6], rest[6], rest[7], rest[8:]
    weight, window, send, recv, own_sem, small_sem, halo_sem, post_send, post_recv, bring = rest[:10]
    line_refs = rest[10:]
    x, c, y, z = here()
    h = half_of(y, z)
    rows, dim = tokens.shape
    own = rows // 2
    half = dim // 2
    last = 3
    tile = attention_tile(own)
    at_x, at_y, at_c = {"shard": 2 * (1 - x) + c}, {"tp": 1 - y}, {"shard": 2 * x + 1 - c}
    left, right = {"ctx": jnp.maximum(z - 1, 0)}, {"ctx": jnp.minimum(z + 1, last)}
    greet_all((at_x, at_y, at_c), ((z > 0, left), (z < last, right)))

    def slot(a, of_y, of_x, of_c, lines=None):
        cols = pl.ds(pl.multiple_of(of_y * widths[a], 128), widths[a])
        depth = wholes[a].shape[2]
        lines = slice(0, depth) if lines is None else slice(lines * depth // 2, (lines + 1) * depth // 2)
        return (weight if a == 0 else wholes[a]).at[of_x, of_c, lines, cols]

    def moves(a):
        table = [
            (pieces[a], slot(a, y, x, c), at_x),
            (pieces[a], slot(a, y, x, c), at_y),
            (pieces[a], slot(a, y, x, c), at_c),
            (slot(a, y, 1 - x, c, 0), slot(a, y, 1 - x, c, 0), at_y),
            (slot(a, 1 - y, x, c, 1), slot(a, 1 - y, x, c, 1), at_x),
            (slot(a, y, 1 - x, c), slot(a, y, 1 - x, c), at_c),
            (slot(a, 1 - y, x, c), slot(a, 1 - y, x, c), at_c),
            (slot(a, 1 - y, 1 - x, c, 0), slot(a, 1 - y, 1 - x, c, 0), at_c),
            (slot(a, 1 - y, 1 - x, c, 1), slot(a, 1 - y, 1 - x, c, 1), at_c),
        ]
        return [remote(s, d, send.at[a, kind], recv.at[a, kind], w) for kind, (s, d, w) in enumerate(table)]

    tables = [moves(a) for a in range(count)]
    depth = small_whole.shape[0] // 2
    small_at = small_whole.at[pl.ds(pl.multiple_of(y * depth, 16), depth)]
    small_copy = remote(small, small_at, small_sem.at[0], small_sem.at[1], at_y)
    sends_right, sends_left = (h == 1) & (z < last), (h == 0) & (z > 0)
    gets_left, gets_right = (h == 0) & (z > 0), (h == 1) & (z < last)

    def halo(where):
        src = tokens.at[pl.ds(pl.multiple_of(h * (rows - HALO), 64), HALO)]
        dst = window.at[pl.ds(pl.multiple_of((1 - h) * (HALO + own), 64), HALO)]
        return remote(src, dst, halo_sem.at[0], halo_sem.at[1], where)

    inside = pltpu.make_async_copy(
        tokens.at[pl.ds(pl.multiple_of(h * (own - HALO), 64), own + HALO)],
        window.at[pl.ds(pl.multiple_of((1 - h) * HALO, 64), own + HALO)],
        halo_sem.at[2],
    )
    small_local = pltpu.make_async_copy(small, small_at, small_sem.at[2])
    piece_local = [pltpu.make_async_copy(pieces[a], slot(a, y, x, c), own_sem.at[a]) for a in range(count)]
    lines = [line_of(j, PERM, z, dealt_row, False, line_refs) for j in range(PERM)]

    def columns_of(j):
        return pl.ds(pl.multiple_of(y * half + j * (half // PERM), 128), half // PERM)

    bring_cot = [
        pltpu.make_async_copy(cotangent.at[:, columns_of(j)], lines[j].blocks.at[z], bring.at[j]) for j in range(PERM)
    ]
    def spread(a):
        for kind in range(3):
            tables[a][kind].start()

    spread(0)
    small_copy.start()

    @pl.when(sends_right)
    def _():
        halo(right).start()

    @pl.when(sends_left)
    def _():
        halo(left).start()

    for item in (small_local, *piece_local, inside, *bring_cot):
        item.start()
    window[padded - (padded - 2 * HALO - own) :, :] = jnp.zeros((padded - 2 * HALO - own, dim), BF)

    @pl.when((h == 0) & (z == 0))
    def _():
        window[:HALO, :] = jnp.zeros((HALO, dim), BF)

    @pl.when((h == 1) & (z == last))
    def _():
        window[HALO + own : 2 * HALO + own, :] = jnp.zeros((HALO, dim), BF)

    def pause(number):
        for _ in range(number):
            yield

    def forward_first(a):
        tables[a][0].wait_recv()
        tables[a][3].start()
        tables[a][5].start()
        tables[a][1].wait_recv()
        tables[a][4].start()
        tables[a][6].start()

    def forward_second(a):
        tables[a][3].wait_recv()
        tables[a][7].start()
        tables[a][4].wait_recv()
        tables[a][8].start()

    def collect(a):
        for kind in (2, 5, 6, 7, 8):
            tables[a][kind].wait_recv()

    early, late = tuple(range(1, count - 1)), count - 1

    def qkv_task():
        forward_first(0)
        yield
        forward_second(0)
        for a in early:
            spread(a)
        yield
        collect(0)
        yield from project_task()
        qkv_copy.start()
        yield from run_static(
            forward_steps(dim, tile, qkv, seg_col, seg_tile, attended, logsum, *attention_refs), tile, own // tile
        )

    def others_task():
        for a in early:
            forward_first(a)
        spread(late)
        yield from pause(MIDDLE_AT[1] - MIDDLE_AT[0])
        forward_first(late)
        for a in early:
            forward_second(a)
        yield from pause(MIDDLE_AT[2] - MIDDLE_AT[1])
        forward_second(late)
        for a in (*early, late):
            collect(a)

    qkv_copy = pltpu.make_async_copy(qkv, qkv_out, qkv_sem)

    def project_task():
        piece_local[0].wait()
        pltpu.make_async_copy(weight, wholes[0], own_sem.at[0]).start()
        inside.wait()
        small_copy.wait()
        small_local.wait()

        @pl.when(gets_left | gets_right)
        def _():
            halo(left).wait_recv()

        depth_w, width = weight.shape[2], widths[0]
        third = width // 3
        step = 256
        for of_y in range(2):
            bias = small_whole[of_y * depth : of_y * depth + 1, :].astype(F32)
            bias = jnp.concatenate([bias[:, :third], jnp.zeros((1, third), F32), bias[:, third : 2 * third]], axis=1)
            scale = jnp.where(lax.broadcasted_iota(jnp.int32, (1, width), 1) < third, 0.125, 1.0).astype(BF)
            full = jnp.concatenate(
                [weight[i // 2, i % 2, :, of_y * width : (of_y + 1) * width] for i in range(4)], axis=0
            )

            def body(i, carry):
                there = pl.ds(pl.multiple_of(i * step, step), step)
                value = (matmul(window[there, :], full) + bias).astype(BF)
                qkv[there, of_y * width : (of_y + 1) * width] = value * scale
                return carry

            lax.fori_loop(0, padded // step, body, 0)
            yield

    def post(j):
        there = lines[j].picked.at[pl.ds(pl.multiple_of((1 - h) * own, 64), own)]
        return remote(there, cot_rows.at[:, columns_of(j)], post_send.at[j], post_recv.at[j], at_y)

    def cotangent_task(j):
        bring_cot[j].wait()
        for _ in lines[j].run():
            yield
            yield from pause(COTANGENT_PAUSE)
        post(j).start()
        cot_rows[:, columns_of(j)] = lines[j].picked[pl.ds(pl.multiple_of(h * own, 64), own), :]
        yield
        post(j).wait_recv()

    tasks = [(0, qkv_task()), (MIDDLE_AT[0], others_task())]
    tasks += [(COTANGENT_AT[j], cotangent_task(j)) for j in range(PERM)]
    interleave(sorted(tasks, key=lambda item: item[0]))
    for a in range(count):
        for kind in range(9):
            tables[a][kind].wait_send()
        if a:
            piece_local[a].wait()
    pltpu.make_async_copy(weight, wholes[0], own_sem.at[0]).wait()
    qkv_copy.wait()

    @pl.when(sends_right | sends_left)
    def _():
        halo(left).wait_send()

    for j in range(PERM):
        lines[j].settle()
        post(j).wait_send()


def first_stage(pieces, small, tokens, cotangent, dealt, seg_col, seg_row, padded):
    rows, dim = tokens.shape
    depth = pieces[0].shape[0]
    own = rows // 2
    tile = attention_tile(own)
    widths = tuple(piece.shape[1] for piece in pieces)
    count = len(pieces)
    ctx_size = lax.axis_size("ctx")
    outs = [jax.ShapeDtypeStruct((2, 2, depth, 2 * width), BF) for width in widths]
    outs += [
        jax.ShapeDtypeStruct((2 * small.shape[0], small.shape[1]), BF),
        jax.ShapeDtypeStruct((padded, 3 * dim), BF),
        jax.ShapeDtypeStruct((own, dim), BF),
        jax.ShapeDtypeStruct((own, dim), BF),
        jax.ShapeDtypeStruct((own // tile, 16, tile), F32),
    ]
    anywhere, vmem = pl.BlockSpec(memory_space=pl.ANY), pl.BlockSpec(memory_space=pltpu.VMEM)
    result = pl.pallas_call(
        functools.partial(first_kernel, widths, padded),
        out_shape=outs,
        in_specs=[anywhere] * (count + 3) + [vmem] * 3,
        out_specs=[anywhere] * count + [vmem, anywhere] + [vmem] * 3,
        scratch_shapes=forward_scratch(padded, tile, dim)
        + [
            pltpu.VMEM((padded, 3 * dim), BF),
            pltpu.SemaphoreType.DMA,
            pltpu.VMEM((2, 2, depth, 2 * widths[0]), BF),
            pltpu.VMEM((padded, dim), BF),
            pltpu.SemaphoreType.DMA((count, 9)),
            pltpu.SemaphoreType.DMA((count, 9)),
            pltpu.SemaphoreType.DMA((count,)),
            pltpu.SemaphoreType.DMA((3,)),
            pltpu.SemaphoreType.DMA((3,)),
            pltpu.SemaphoreType.DMA((PERM,)),
            pltpu.SemaphoreType.DMA((PERM,)),
            pltpu.SemaphoreType.DMA((PERM,)),
        ]
        + line_scratch(ctx_size, rows, PERM, dim // 2 // PERM),
        compiler_params=pltpu.CompilerParams(
            collective_id=0, has_side_effects=True, vmem_limit_bytes=VMEM_LIMIT
        ),
        cost_estimate=pl.CostEstimate(flops=10000000000, bytes_accessed=100000000, transcendentals=0),
    )(*pieces, small, tokens, cotangent, dealt[None, :], seg_col, segments_by_tile(seg_row, own))
    whole = [full.reshape(4 * depth, full.shape[3]) for full in result[:count]]
    logsum = result[count + 4].transpose(1, 0, 2).reshape(16, own)
    return whole, result[count], result[count + 1], result[count + 2], result[count + 3], logsum


def add_lines(dst, first, second):
    rows = dst.shape[0]
    step = 48 if rows % 48 == 0 else 16

    def body(i, carry):
        lines = pl.ds(pl.multiple_of(i * step, 16), step)
        dst[lines, :] = (first[lines, :].astype(F32) + second[lines, :].astype(F32)).astype(dst.dtype)
        return carry

    lax.fori_loop(0, rows // step, body, 0)


RING = 4


class Reduction:
    STAGES = 7

    def __init__(self, chunks, outs, refs):
        number = len(chunks)
        self.chunks, self.outs = chunks, outs
        ring = min(RING, number)
        self.full = [refs[k % ring] for k in range(number)]
        refs = refs[ring:]
        self.by_core, self.by_x, self.plane, self.from_end, self.half_z, self.final = (
            refs[i * number : (i + 1) * number] for i in range(6)
        )
        self.send, self.recv = refs[6 * number :]
        self.place = here()
        z = self.place[3]
        self.inner, self.outer = (z == 1) | (z == 2), (z == 0) | (z == 3)
        self.near, self.end, self.middle = 1 + z // 3, jnp.maximum(3 * (z - 1), 0) % 6, 3 - z
        self.rows = self.full[0].shape[3]

    def copy(self, k, stage):
        x, c, y, z = self.place
        half = self.rows // 2
        side = z // 2
        if stage == 0:
            src, dst, where = self.full[k].at[:, :, 1 - c], self.by_core[k], {"shard": 2 * x + 1 - c}
        elif stage == 1:
            src, dst, where = self.by_core[k].at[:, 1 - x], self.by_x[k], {"shard": 2 * (1 - x) + c}
        elif stage == 2:
            src, dst, where = self.by_x[k].at[1 - y], self.plane[k], {"tp": 1 - y}
        elif stage == 3:
            src, dst, where = self.plane[k], self.from_end[k], {"ctx": self.near}
        elif stage == 4:
            src = self.plane[k].at[pl.ds(pl.multiple_of((1 - side) * half, 16), half)]
            dst, where = self.half_z[k], {"ctx": self.middle}
        elif stage == 5:
            src = dst = self.final[k].at[pl.ds(pl.multiple_of(side * half, 16), half)]
            where = {"ctx": self.middle}
        else:
            src = dst = self.final[k]
            where = {"ctx": self.end}
        return remote(src, dst, self.send.at[k, stage], self.recv.at[k, stage], where)

    def sender(self, stage):
        return None if stage < 3 else (self.outer if stage == 3 else self.inner)

    def receiver(self, stage):
        return None if stage < 3 else (self.outer if stage == 6 else self.inner)

    def guarded(self, condition, action):
        if condition is None:
            action()
        else:
            pl.when(condition)(action)

    def start(self, k, stage):
        self.guarded(self.sender(stage), lambda: self.copy(k, stage).start())

    def absorb(self, k, stage):
        x, c, y, z = self.place
        half = self.rows // 2
        side = z // 2
        self.copy(k, stage).wait_recv()
        if stage == 0:
            for of_y in range(2):
                for of_x in range(2):
                    there = self.by_core[k].at[of_y, of_x]
                    add_lines(there, there, self.full[k].at[of_y, of_x, c])
            self.copy(k, 0).wait_send()
        elif stage == 1:
            for i in range(2):
                add_lines(self.by_x[k].at[i], self.by_x[k].at[i], self.by_core[k].at[i, x])
        elif stage == 2:
            add_lines(self.plane[k], self.plane[k], self.by_x[k].at[y])
        elif stage == 3:
            add_lines(self.plane[k], self.plane[k], self.from_end[k])
        elif stage == 4:
            lines = pl.ds(pl.multiple_of(side * half, 16), half)
            add_lines(self.final[k].at[lines], self.half_z[k], self.plane[k].at[lines])

    def task(self, k, produce):
        produce(k)
        for stage in range(self.STAGES):
            self.start(k, stage)
            yield
            self.guarded(self.receiver(stage), lambda: self.absorb(k, stage))
        a, first, width = self.chunks[k]
        self.outs[a][:, first : first + width] = self.final[k][...].astype(F32)

    def settle(self):
        for k in range(len(self.chunks)):
            for stage in range(1, self.STAGES):
                self.guarded(self.sender(stage), lambda: self.copy(k, stage).wait_send())

    def product(self, k, turned, other):
        for of_y in range(2):
            right = other(of_y)
            for i in range(4):
                value = matmul(turned[i * self.rows : (i + 1) * self.rows, :], right)
                self.full[k][of_y, i // 2, i % 2] = value.astype(BF)


def reduction_scratch(rows, chunks):
    shapes = [
        lambda w: (2, 2, rows, w),
        lambda w: (2, rows, w),
        lambda w: (rows, w),
        lambda w: (rows, w),
        lambda w: (rows // 2, w),
        lambda w: (rows, w),
    ]
    scratch = [pltpu.VMEM((2, 2, 2, rows, CHUNK), BF) for _ in range(min(RING, len(chunks)))]
    scratch += [pltpu.VMEM(shape(width), BF) for shape in shapes for _, _, width in chunks]
    return scratch + [pltpu.SemaphoreType.DMA((len(chunks), 7)), pltpu.SemaphoreType.DMA((len(chunks), 7))]


def wide_peers():
    x, c, y, z = here()
    return (
        {"shard": 2 * x + 1 - c},
        {"shard": 2 * (1 - x) + c},
        {"tp": 1 - y},
        {"ctx": z + 1 - 2 * (z % 2)},
    )


CHUNK = 384


def chunks_of(widths):
    return tuple((a, first, CHUNK) for a, width in enumerate(widths) for first in range(0, width, CHUNK))


def slots_task(line, j, y, values, out, pre, post_sem, at_y):
    slots = line.slots
    own = slots // 2
    outgoing, pre_send, pre_recv = pre
    post_send, post_recv = post_sem
    width = line.picked.shape[1]
    mine_rows = pl.ds(pl.multiple_of(half_of(y, line.z) * own, 64), own)
    half = out.shape[1] // 2
    outgoing[...] = values(j, 1 - y)
    before = remote(outgoing, line.blocks.at[line.z, mine_rows], pre_send, pre_recv, at_y)
    before.start()
    line.blocks[line.z, mine_rows, :] = values(j, y)
    yield
    before.wait_recv()
    yield from line.run()
    cols = pl.ds(pl.multiple_of(y * half + j * width, 128), width)
    after = remote(line.picked, out.at[:, cols], post_send, post_recv, at_y)
    after.start()
    out[:, cols] = line.picked[...]
    yield
    after.wait_recv()
    before.wait_send()
    after.wait_send()
    line.settle()


LAYER_AT = (2, 5, 8)
LAYER_GAPS = (1, 1, 1, 1, 1, 1)
AHEAD = 2
X_FIRST = 3
LATER_GAPS = (1, 1, 1, 0, 1)


def chunk_round(k):
    return k // AHEAD


def chunk_gaps(k):
    return (0, max(0, X_FIRST + 5 * k // 4 - chunk_round(k) - 2)) + LATER_GAPS


def backward_kernel(chunks, *refs):
    first_low, attended, hidden_low, pre_low, second_low, act_low, grad, stats, stats_tile, qkv_in, seg_col, seg_row, seg_tile, layer_low, dealt_row = refs[:15]
    outs, qkv_low, query_sums, value_sums, layer_out = refs[15:18], refs[18], refs[19], refs[20], refs[21]
    rest = refs[22:]
    turned, grad_win, stats_side, stats_win, halo_sem = rest[0:3], rest[3], rest[4], rest[5], rest[6]
    key_t, first_st, second_st, bias_query, bias_key, acc, first_acc, second_acc = rest[7:15]
    stream, stream_sem, qkv, qkv_sem = rest[15:19]
    outgoing, rest = rest[19 : 19 + PERM], rest[19 + PERM :]
    qkv_copy = pltpu.make_async_copy(qkv_in, qkv, qkv_sem)
    qkv_copy.start()
    pre_send, pre_recv, post_send, post_recv = rest[:4]
    line_number = 4 * PERM + 3
    line_refs, reduction_refs = rest[4 : 4 + line_number], rest[4 + line_number :]
    reduction = Reduction(chunks, outs, reduction_refs)
    x, c, y, z = reduction.place
    h = half_of(y, z)
    own, dim = grad.shape
    padded = qkv.shape[0]
    tile = attention_tile(own)
    last = 3
    at_y, at_z = {"tp": 1 - y}, {"ctx": jnp.clip(z - 1 + 2 * h, 0, last)}
    has_z = ((h == 0) & (z > 0)) | ((h == 1) & (z < last))
    greet_all(wide_peers(), ((reduction.inner, {"ctx": 3 - z}),))

    def halos(where, same):
        first = (1 - h) if same else h
        side = h if same else 1 - h
        base = 0 if same else 4
        return (
            remote(
                grad.at[pl.ds(pl.multiple_of(first * (own - HALO), 64), HALO)],
                grad_win.at[pl.ds(pl.multiple_of(side * (HALO + own), 64), HALO)],
                halo_sem.at[base],
                halo_sem.at[base + 1],
                where,
            ),
            remote(stats, stats_side.at[side], halo_sem.at[base + 2], halo_sem.at[base + 3], where),
        )

    for item in halos(at_y, True):
        item.start()

    @pl.when(has_z)
    def _():
        for item in halos(at_z, False):
            item.start()

    grad_win[HALO : HALO + own, :] = grad[...]
    grad_win[2 * HALO + own :, :] = jnp.zeros((padded - 2 * HALO - own, dim), BF)
    for missing, side in (((h == 0) & (z == 0), 0), ((h == 1) & (z == last), 1)):

        @pl.when(missing)
        def _():
            grad_win[side * (HALO + own) : side * (HALO + own) + HALO, :] = jnp.zeros((HALO, dim), BF)
            stats_side[side] = jnp.zeros(stats.shape, F32)

    lefts, rights = (first_low, hidden_low, second_low), (attended, pre_low, act_low)

    def bring(k, of_y):
        a, first, columns = chunks[k]
        half = rights[a].shape[1] // 2
        return pltpu.make_async_copy(
            rights[a].at[:, of_y * half + first : of_y * half + first + columns],
            stream.at[k % 2, of_y],
            stream_sem.at[k % 2, of_y],
        )

    for k in range(min(2, len(chunks))):
        for of_y in range(2):
            bring(k, of_y).start()

    def produce(k):
        a, first, _ = chunks[k]
        if first == 0:
            turned[a][...] = lefts[a][...].T
        for of_y in range(2):
            bring(k, of_y).wait()
        reduction.product(k, turned[a], lambda of_y: stream[k % 2, of_y])
        if k + 2 < len(chunks):
            for of_y in range(2):
                bring(k + 2, of_y).start()

    lines = [line_of(j, PERM, z, dealt_row, True, line_refs) for j in range(PERM)]
    width = dim // 2 // PERM

    def layer_values(j, half):
        return layer_low[:, pl.ds(pl.multiple_of(half * (dim // 2) + j * width, 128), width)]

    def store(rows, p, part):
        at_query = places(p, dim)[0]
        qkv_low[rows, at_query : at_query + 128] = part

    def attention_task():
        yield
        qkv_copy.wait()
        yield from run_static(
            query_steps(
                dim, tile, qkv, seg_col, seg_tile, grad, stats_tile, store, query_sums, key_t, first_st, second_st, bias_query, acc
            ),
            tile,
            own // tile,
        )
        for item in halos(at_y, True):
            item.wait()

        @pl.when(has_z)
        def _():
            for item in halos(at_z, False):
                item.wait()

        stats_win[...] = jnp.concatenate(
            [
                stats_side[0][:, own - HALO :],
                stats[...],
                stats_side[1][:, :HALO],
                jnp.zeros((stats.shape[0], padded - 2 * HALO - own), F32),
            ],
            axis=1,
        )
        yield from run_static(
            key_steps(
                dim,
                tile,
                qkv,
                seg_col,
                seg_row,
                grad_win,
                stats_win,
                qkv_low,
                value_sums,
                first_st,
                second_st,
                bias_key,
                first_acc,
                second_acc,
            ),
            tile,
            own // tile,
        )

    tasks = [(chunk_round(k), timed(reduction.task(k, produce), chunk_gaps(k))) for k in range(len(chunks))]
    tasks += [
        (
            LAYER_AT[j],
            timed(
                slots_task(
                lines[j],
                j,
                y,
                layer_values,
                layer_out,
                (outgoing[j], pre_send.at[j], pre_recv.at[j]),
                (post_send.at[j], post_recv.at[j]),
                at_y,
            ), LAYER_GAPS),
        )
        for j in range(PERM)
    ]
    interleave(sorted([(0, attention_task())] + tasks, key=lambda item: item[0]))
    reduction.settle()


def backward_stage(first_low, attended, hidden_low, pre_low, second_low, act_low, grad, stats, qkv, seg_col, seg_row, layer_low, dealt):
    own, dim = grad.shape
    padded = qkv.shape[0]
    rows = dim // 4
    tile = attention_tile(own)
    pairs = dim // 128
    widths = (attended.shape[1] // 2, pre_low.shape[1] // 2, act_low.shape[1] // 2)
    chunks = chunks_of(widths)
    spec = pl.BlockSpec(memory_space=pltpu.VMEM)
    outs = [jax.ShapeDtypeStruct((rows, width), F32) for width in widths]
    outs += [
        jax.ShapeDtypeStruct((own, 3 * dim), BF),
        jax.ShapeDtypeStruct((1, dim), F32),
        jax.ShapeDtypeStruct((1, dim), F32),
        jax.ShapeDtypeStruct((2 * own, dim), BF),
    ]
    scratch = [pltpu.VMEM((dim, own), BF) for _ in range(3)]
    scratch += [
        pltpu.VMEM((padded, dim), BF),
        pltpu.VMEM((2, 32, own), F32),
        pltpu.VMEM((32, padded), F32),
        pltpu.SemaphoreType.DMA((8,)),
        pltpu.VMEM((dim, padded), BF),
        pltpu.VMEM((pairs, 2 * tile, 128), BF),
        pltpu.VMEM((pairs, 2 * tile, 128), BF),
        pltpu.VMEM((BLOCK, 2 * tile), F32),
        pltpu.VMEM((tile, BLOCK), F32),
        pltpu.VMEM((pairs, 128, 2 * tile), F32),
        pltpu.VMEM((pairs, 2 * tile, 128), F32),
        pltpu.VMEM((pairs, 2 * tile, 128), F32),
    ]
    scratch += [pltpu.VMEM((2, 2, own, CHUNK), BF), pltpu.SemaphoreType.DMA((2, 2))]
    scratch += [pltpu.VMEM((padded, 3 * dim), BF), pltpu.SemaphoreType.DMA]
    scratch += [pltpu.VMEM((own, dim // 2 // PERM), BF) for _ in range(PERM)]
    scratch += [pltpu.SemaphoreType.DMA((PERM,)) for _ in range(4)]
    scratch += line_scratch(lax.axis_size("ctx"), 2 * own, PERM, dim // 2 // PERM)
    scratch += reduction_scratch(rows, chunks)
    args = (
        first_low,
        attended,
        hidden_low,
        pre_low,
        second_low,
        act_low,
        grad,
        stats,
        by_tile(stats, own),
        qkv,
        seg_col,
        seg_row,
        segments_by_tile(seg_row, own),
        layer_low,
        dealt[None, :].astype(F32),
    )
    anywhere = pl.BlockSpec(memory_space=pl.ANY)
    return pl.pallas_call(
        functools.partial(backward_kernel, chunks),
        out_shape=outs,
        in_specs=[anywhere if i in (1, 3, 5, 9) else spec for i in range(len(args))],
        out_specs=[spec] * len(outs),
        scratch_shapes=scratch,
        compiler_params=pltpu.CompilerParams(
            collective_id=1, has_side_effects=True, vmem_limit_bytes=VMEM_LIMIT
        ),
        cost_estimate=pl.CostEstimate(flops=50000000000, bytes_accessed=100000000, transcendentals=0),
    )(*args)


def last_kernel(chunks, *refs):
    inputs, qkv_low, weight, grad_first, dealt_row, vector = refs[:6]
    outs, tokens_grad, vector_out = refs[6:9], refs[9], refs[10]
    rest = refs[11:]
    number = PERM
    turned, outgoing, pre_send, pre_recv, post_send, post_recv = (
        rest[0],
        rest[1 : 1 + number],
        rest[1 + number],
        rest[2 + number],
        rest[3 + number],
        rest[4 + number],
    )
    vector_in, vector_sum, vector_send, vector_recv = rest[5 + number : 9 + number]
    rest = rest[9 + number :]
    line_number = 4 * number + 3
    line_refs, reduction_refs = rest[:line_number], rest[line_number:]
    reduction = Reduction(chunks, outs, reduction_refs)
    x, c, y, z = reduction.place
    own, dim = inputs.shape
    at_y = {"tp": 1 - y}
    inner = (z == 1) | (z == 2)
    peers = wide_peers() + ({"ctx": (z + 2) % 4},)
    greet_all(peers, ((inner, {"ctx": 3 - z}),))
    lines = [line_of(j, number, z, dealt_row, True, line_refs) for j in range(number)]
    width = dim // 2 // PERM

    def vector_copy(stage):
        return remote(
            vector_sum.at[stage], vector_in.at[stage], vector_send.at[stage], vector_recv.at[stage], peers[stage]
        )

    def vector_task():
        vector_sum[0] = vector[...]
        for stage in range(5):
            vector_copy(stage).start()
            yield
            vector_copy(stage).wait_recv()
            total = vector_sum[stage] + vector_in[stage]
            if stage < 4:
                vector_sum[stage + 1] = total
            else:
                vector_out[...] = total

    def grad_values(j, half):
        first = pl.ds(pl.multiple_of(half * (dim // 2) + j * width, 128), width)
        return (grad_first[:, first] + matmul_second(qkv_low[...], weight[first, :])).astype(BF)

    def produce(k):
        if k == 0:
            turned[...] = inputs[...].T
        which, first, columns = chunks[k]
        half = qkv_low.shape[1] // 2
        third = half // 3

        def other(of_y):
            start = of_y * half + which * third + first
            return qkv_low[:, start : start + columns]

        reduction.product(k, turned, other)

    def slots(values, j, index, out_ref):
        return slots_task(
            lines[index],
            j,
            y,
            values,
            out_ref,
            (outgoing[index], pre_send.at[index], pre_recv.at[index]),
            (post_send.at[index], post_recv.at[index]),
            at_y,
        )

    tasks = [(j, slots(grad_values, j, j, tokens_grad)) for j in range(PERM)]
    tasks += [(k, reduction.task(k, produce)) for k in range(len(chunks))]
    tasks += [(1, vector_task())]
    interleave(sorted(tasks, key=lambda item: item[0]))
    reduction.settle()
    for stage in range(5):
        vector_copy(stage).wait_send()


def last_stage(inputs, qkv_low, weight, grad_first, dealt, vector):
    own, dim = inputs.shape
    ctx_size = lax.axis_size("ctx")
    rows = dim // 4
    width = qkv_low.shape[1] // 6
    chunks = chunks_of((width,) * 3)
    spec = pl.BlockSpec(memory_space=pltpu.VMEM)
    outs = [
        *[jax.ShapeDtypeStruct((rows, width), F32) for _ in range(3)],
        jax.ShapeDtypeStruct((2 * own, dim), BF),
        jax.ShapeDtypeStruct(vector.shape, F32),
    ]
    scratch = [pltpu.VMEM((dim, own), BF)]
    scratch += [pltpu.VMEM((own, dim // 2 // PERM), BF) for _ in range(PERM)]
    scratch += [pltpu.SemaphoreType.DMA((PERM,)) for _ in range(4)]
    scratch += [pltpu.VMEM((5,) + vector.shape, F32), pltpu.VMEM((5,) + vector.shape, F32)]
    scratch += [pltpu.SemaphoreType.DMA((5,)), pltpu.SemaphoreType.DMA((5,))]
    scratch += line_scratch(ctx_size, 2 * own, PERM, dim // 2 // PERM)
    scratch += reduction_scratch(rows, chunks)
    return pl.pallas_call(
        functools.partial(last_kernel, chunks),
        out_shape=outs,
        in_specs=[spec] * 6,
        out_specs=[spec] * len(outs),
        scratch_shapes=scratch,
        compiler_params=pltpu.CompilerParams(
            collective_id=2, has_side_effects=True, vmem_limit_bytes=VMEM_LIMIT
        ),
        cost_estimate=pl.CostEstimate(flops=10000000000, bytes_accessed=100000000, transcendentals=0),
    )(inputs, qkv_low, weight, grad_first, dealt[None, :].astype(F32), vector)


def project_kernel(dim, x_ref, weight, bias, out):
    step = 256
    third = weight.shape[1] // 3

    def body(i, carry):
        lines = pl.ds(pl.multiple_of(i * step, step), step)
        value = (matmul(x_ref[lines, :], weight[...]) + bias[0]).astype(BF)
        scale = jnp.where(lax.broadcasted_iota(jnp.int32, (1, 3 * third), 1) < third, 0.125, 1.0).astype(BF)
        out[lines, :] = value * scale
        return carry

    lax.fori_loop(0, x_ref.shape[0] // step, body, 0)


def project(x_window, weight, bias):
    rows, dim = x_window.shape
    width = 3 * dim // 2
    return pl.pallas_call(
        functools.partial(project_kernel, dim),
        grid=(2,),
        out_shape=jax.ShapeDtypeStruct((rows, 2 * width), BF),
        in_specs=[
            pl.BlockSpec((rows, dim), lambda i: (0, 0)),
            pl.BlockSpec((dim, width), lambda i: (0, i)),
            pl.BlockSpec((1, 1, width), lambda i: (i, 0, 0)),
        ],
        out_specs=pl.BlockSpec((rows, width), lambda i: (0, i)),
        compiler_params=pltpu.CompilerParams(vmem_limit_bytes=VMEM_LIMIT),
        cost_estimate=pl.CostEstimate(flops=6000000000, bytes_accessed=14000000, transcendentals=0),
    )(x_window, weight, bias)


def rows_to_slots(values, dealt, place_z, place_y):
    own, dim = values.shape
    half = dim // 2
    keep = lax.dynamic_slice_in_dim(values, place_y * half, half, axis=1)
    send = lax.dynamic_slice_in_dim(values, (1 - place_y) * half, half, axis=1)
    other = lax.ppermute(send, "tp", [(0, 1), (1, 0)])
    first = jnp.where(place_y == 0, keep, other)
    second = jnp.where(place_y == 0, other, keep)
    block = jnp.concatenate([first, second], axis=0)
    everything = lax.all_gather(block, "ctx", axis=0, tiled=True)
    slots = 2 * own
    mine = lax.dynamic_slice_in_dim(dealt, place_z * slots, slots)
    picked = jnp.take(everything, mine, axis=0, mode="clip")
    other_columns = lax.ppermute(picked, "tp", [(0, 1), (1, 0)])
    return jnp.concatenate(
        [jnp.where(place_y == 0, picked, other_columns), jnp.where(place_y == 0, other_columns, picked)], axis=1
    )


def slots_to_rows(values, dealt, place_z, place_y):
    slots, dim = values.shape
    half, own = dim // 2, slots // 2
    block = lax.dynamic_slice_in_dim(values, place_y * half, half, axis=1)
    everything = lax.all_gather(block, "ctx", axis=0, tiled=True)
    wanted = place_z * slots + lax.broadcasted_iota(jnp.int32, (slots, 1), 0)
    chosen = (wanted == dealt[None, :]).astype(BF)
    picked = matmul(chosen, everything).astype(BF)
    keep = lax.dynamic_slice_in_dim(picked, place_y * own, own, axis=0)
    send = lax.dynamic_slice_in_dim(picked, (1 - place_y) * own, own, axis=0)
    other = lax.ppermute(send, "tp", [(0, 1), (1, 0)])
    return jnp.concatenate([jnp.where(place_y == 0, keep, other), jnp.where(place_y == 0, other, keep)], axis=1)


def per_device(
    tokens,
    cotangent,
    seq_lengths,
    dealing,
    query_weight,
    query_bias,
    key_weight,
    value_weight,
    value_bias,
    output_weight,
    output_bias,
    first_gain,
    first_shift,
    up_weight,
    up_bias,
    down_weight,
    down_bias,
    second_gain,
    second_shift,
):
    rows, dim = tokens.shape
    ctx_size, tp_size = lax.axis_size("ctx"), lax.axis_size("tp")
    group_rows = rows * ctx_size
    own = rows // tp_size
    place_z, place_y = lax.axis_index("ctx"), lax.axis_index("tp")
    window = HALO + own + HALO
    padded = -(-window // BLOCK) * BLOCK
    dealt = dealing[0]

    lengths = seq_lengths[0]
    number = lengths.shape[0]
    upto = jnp.arange(number)[:, None] >= jnp.arange(number)[None, :]
    ends = jnp.sum(jnp.where(upto, lengths[None, :], 0), axis=1)
    starts = ends - lengths
    special = lax.axis_size("shard") == 4 and tp_size == 2 and ctx_size == 4
    place_h = half_of(place_y, place_z) if special else place_y
    first_row = place_z * rows + place_h * own
    index = jnp.arange(padded, dtype=jnp.int32)
    position = first_row - HALO + index
    valid = (position >= 0) & (position < group_rows) & (index < window)
    segment = jnp.sum((position[:, None] >= ends[None, :-1]).astype(jnp.int32), axis=1)
    segment = jnp.where(valid, segment, -1)
    seg_row, seg_col = segment[None, :], segment[:, None]
    tile = attention_tile(own)
    tile_first = first_row + tile * jnp.arange(own // tile, dtype=jnp.int32)
    tile_last = tile_first + tile - 1
    begin = jnp.max(jnp.where(starts[None, :] <= tile_first[:, None], starts[None, :], 0), axis=1)
    finish = jnp.min(jnp.where(ends[None, :] > tile_last[:, None], ends[None, :], group_rows), axis=1)
    shift = HALO - first_row
    bounds = jnp.stack([(begin + shift) // BLOCK, (finish + shift + BLOCK - 1) // BLOCK], axis=1).astype(jnp.int32)

    half_dim = dim // tp_size
    pieces = [
        jnp.concatenate([query_weight, key_weight, value_weight], axis=1),
        output_weight.T,
        up_weight,
        down_weight.T,
    ]
    flat = jnp.concatenate([query_bias, value_bias, up_bias])
    small = jnp.broadcast_to(flat[None, :], (16, flat.shape[0]))
    inputs = lax.dynamic_slice_in_dim(tokens, place_h * own, own, axis=0)
    if special:
        whole, biases, qkv, cot_rows, attended, logsum = first_stage(
            pieces, small, tokens, cotangent, dealt, seg_col, seg_row, padded
        )
        whole_up_bias = biases[::16, dim:].reshape(-1).astype(F32)
    else:
        whole = [
            lax.all_gather(lax.all_gather(piece, "shard", axis=0, tiled=True), "tp", axis=1, tiled=True)
            for piece in pieces
        ]
        biases = lax.all_gather(small, "tp", axis=0, tiled=True)[::16].astype(F32)
        qkv_bias = jnp.concatenate(
            [biases[:, :half_dim], jnp.zeros((tp_size, half_dim), F32), biases[:, half_dim:dim]], axis=1
        )[:, None, :]
        whole_up_bias = biases[:, dim:].reshape(-1)
        edge = jnp.where(place_y == 0, tokens[rows - HALO :], tokens[:HALO])
        hops = [(2 * z, 2 * z + 2) for z in range(ctx_size - 1)] + [(2 * z + 1, 2 * z - 1) for z in range(1, ctx_size)]
        arrived = lax.ppermute(edge, ("ctx", "tp"), hops)
        x_window = jnp.where(
            place_y == 0,
            jnp.concatenate([arrived, tokens[: own + HALO]], axis=0),
            jnp.concatenate([tokens[own - HALO :], arrived], axis=0),
        )
        x_window = jnp.pad(x_window, ((0, padded - window), (0, 0)))
        qkv = project(x_window, whole[0], qkv_bias)
        cot_rows = slots_to_rows(cotangent, dealt, place_z, place_y)
        attended, logsum = attention_forward(qkv, seg_col, seg_row, bounds, own, dim)
    wide_qkv, wide_output, wide_up, wide_down = whole
    output_bias = output_bias.astype(F32)
    first_gain = first_gain.astype(F32)
    first_shift = first_shift.astype(F32)
    down_bias = down_bias.astype(F32)
    second_gain = second_gain.astype(F32)
    second_shift = second_shift.astype(F32)

    grad_out = cot_rows.astype(F32)
    hidden_one, normed_one, inverse_one = norm_forward(
        inputs.astype(F32) + matmul_second(attended, wide_output) + output_bias, first_gain, first_shift
    )
    hidden_low = hidden_one.astype(BF)
    pre_act = matmul(hidden_low, wide_up) + whole_up_bias
    erf_part = 0.5 * (1.0 + jax.scipy.special.erf(pre_act * HALF_ROOT))
    act_low = (pre_act * erf_part).astype(BF)
    layer_value, normed_two, inverse_two = norm_forward(
        hidden_one + matmul_second(act_low, wide_down) + down_bias, second_gain, second_shift
    )
    layer_low = layer_value.astype(BF)

    second_shift_grad = jnp.sum(grad_out, axis=0)
    second_gain_grad = jnp.sum(grad_out * normed_two, axis=0)
    grad_second = norm_backward(grad_out, normed_two, inverse_two, second_gain)
    down_bias_grad = jnp.sum(grad_second, axis=0)
    second_low = grad_second.astype(BF)
    slope = erf_part + pre_act * DENSITY * jnp.exp(-0.5 * pre_act * pre_act)
    grad_pre = matmul(second_low, wide_down) * slope
    up_bias_grad = jnp.sum(grad_pre, axis=0)
    pre_low = grad_pre.astype(BF)
    grad_hidden = grad_second + matmul_second(pre_low, wide_up)
    first_shift_grad = jnp.sum(grad_hidden, axis=0)
    first_gain_grad = jnp.sum(grad_hidden * normed_one, axis=0)
    grad_first = norm_backward(grad_hidden, normed_one, inverse_one, first_gain)
    output_bias_grad = jnp.sum(grad_first, axis=0)
    first_low = grad_first.astype(BF)
    attended_grad = matmul(first_low, wide_output).astype(BF)
    head_of = (jnp.arange(dim)[None, :] // HEAD == jnp.arange(16)[:, None]).astype(F32)
    delta = lax.dot_general(
        head_of,
        attended_grad.astype(F32) * attended.astype(F32),
        (((1,), (1,)), ((), ())),
        precision=lax.Precision.HIGHEST,
        preferred_element_type=F32,
    )
    stats = jnp.concatenate([logsum, delta], axis=0)
    if special:
        output_own, up_own, down_own, qkv_low, query_bias_grad, value_bias_grad, layer_out = backward_stage(
            first_low,
            attended,
            hidden_low,
            pre_low,
            second_low,
            act_low,
            attended_grad,
            stats,
            qkv,
            seg_col,
            seg_row,
            layer_low,
            dealt,
        )
    else:
        layer_out = rows_to_slots(layer_low, dealt, place_z, place_y)
        up_hops = [(i, i + 1) for i in range(ctx_size * tp_size - 1)]
        down_hops = [(i + 1, i) for i in range(ctx_size * tp_size - 1)]
        grad_win, stats_win = [
            jnp.concatenate(
                [
                    lax.ppermute(lax.slice_in_dim(array, own - HALO, own, axis=axis), ("ctx", "tp"), up_hops),
                    array,
                    lax.ppermute(lax.slice_in_dim(array, 0, HALO, axis=axis), ("ctx", "tp"), down_hops),
                    jnp.zeros((padded - window, dim) if axis == 0 else (32, padded - window), array.dtype),
                ],
                axis=axis,
            )
            for array, axis in ((attended_grad, 0), (stats, 1))
        ]
        query_low, query_bias_grad = attention_query(qkv, seg_col, seg_row, bounds, attended_grad, stats, dim)
        qkv_low, value_bias_grad = attention_key(
            qkv, seg_col, seg_row, bounds, grad_win, stats_win, query_low, own, dim
        )
    vectors = jnp.concatenate(
        [
            query_bias_grad[0],
            value_bias_grad[0],
            up_bias_grad,
            output_bias_grad,
            first_gain_grad,
            first_shift_grad,
            down_bias_grad,
            second_gain_grad,
            second_shift_grad,
        ]
    )
    if special:
        *qkv_own, tokens_grad, small_sum = last_stage(
            inputs, qkv_low, wide_qkv, grad_first, dealt, vectors.reshape(-1, 128)
        )
        small_sum = small_sum.reshape(-1)
        owned = [*qkv_own, output_own, up_own, down_own]
    else:
        owned = []
        for full in (
            matmul_first(inputs, qkv_low),
            matmul_first(first_low, attended),
            matmul_first(hidden_low, pre_low),
            matmul_first(second_low, act_low),
        ):
            part = lax.psum_scatter(full.astype(BF), "tp", scatter_dimension=1, tiled=True)
            part = lax.psum_scatter(part, "shard", scatter_dimension=0, tiled=True)
            owned.append(lax.psum(part, "ctx").astype(F32))
        owned = [owned[0][:, i * half_dim : (i + 1) * half_dim] for i in range(3)] + owned[1:]
        small_sum = lax.psum(vectors, ("shard", "ctx", "tp"))
        tokens_grad = (grad_first + matmul_second(qkv_low, wide_qkv)).astype(BF)
        tokens_grad = rows_to_slots(tokens_grad, dealt, place_z, place_y)
    hidden = up_bias_grad.shape[0]
    sizes = [dim, dim, hidden] + [dim] * 6
    offsets = [sum(sizes[:i]) for i in range(len(sizes))]
    parts = [small_sum[o : o + s] for o, s in zip(offsets, sizes)]

    def by_tp(vector):
        part = vector.shape[0] // tp_size
        return lax.dynamic_slice_in_dim(vector, place_y * part, part)

    return (
        layer_out,
        tokens_grad,
        owned[0],
        by_tp(parts[0]),
        owned[1],
        owned[2],
        by_tp(parts[1]),
        owned[3].T,
        parts[3],
        parts[4],
        parts[5],
        owned[4],
        by_tp(parts[2]),
        owned[5].T,
        parts[6],
        parts[7],
        parts[8],
    )


def solution(mesh):
    return jax.shard_map(
        per_device,
        mesh=mesh,
        in_specs=(
            P(("shard", "ctx"), None),
            P(("shard", "ctx"), None),
            P("shard", None),
            P("shard", None),
            P("shard", "tp"),
            P("tp"),
            P("shard", "tp"),
            P("shard", "tp"),
            P("tp"),
            P("tp", "shard"),
            P(),
            P(),
            P(),
            P("shard", "tp"),
            P("tp"),
            P("tp", "shard"),
            P(),
            P(),
            P(),
        ),
        out_specs=(
            P(("shard", "ctx"), None),
            P(("shard", "ctx"), None),
            P("shard", "tp"),
            P("tp"),
            P("shard", "tp"),
            P("shard", "tp"),
            P("tp"),
            P("tp", "shard"),
            P(),
            P(),
            P(),
            P("shard", "tp"),
            P("tp"),
            P("tp", "shard"),
            P(),
            P(),
            P(),
        ),
        check_vma=False,
    )
```

```python
import functools

import jax
import jax.numpy as jnp
from jax import lax
from jax.experimental import pallas as pl
from jax.experimental.pallas import tpu as pltpu
from jax.sharding import PartitionSpec as P

HEAD = 64
HALO = 512
HALF_ROOT = 0.7071067811865476
DENSITY = 0.3989422804014327
NEG_FILL = -1000000000.0
BF = jnp.bfloat16
F32 = jnp.float32
BLOCK = 256
VMEM_LIMIT = 60 * 1024 * 1024


def matmul(former, latter):
    return jnp.dot(former, latter, preferred_element_type=F32)


def matmul_first(former, latter):
    return lax.dot_general(former, latter, (((0,), (0,)), ((), ())), preferred_element_type=F32)


def matmul_second(former, latter):
    return lax.dot_general(former, latter, (((1,), (1,)), ((), ())), preferred_element_type=F32)


def norm_forward(values, norm_gain, norm_shift):
    centre = values - jnp.mean(values, axis=1, keepdims=True)
    spread = jnp.mean(centre * centre, axis=1, keepdims=True)
    inverse = lax.rsqrt(spread + 1e-06)
    normed = centre * inverse
    return (norm_gain * normed + norm_shift, normed, inverse)


def norm_backward(gradient, normed, inverse, norm_gain):
    scaled = gradient * norm_gain
    bracket = (
        scaled
        - jnp.mean(scaled, axis=1, keepdims=True)
        - normed * jnp.mean(scaled * normed, axis=1, keepdims=True)
    )
    return inverse * bracket


def places(pair, dim):
    half, inner = divmod(pair, dim // 256)
    base = half * (3 * dim // 2) + inner * 128
    return base, base + dim // 2, base + dim


def take(qkv, rows, pair, dim, which):
    first = places(pair, dim)[which]
    return qkv[rows, first : first + 128]


def low_lanes(rows):
    return lax.broadcasted_iota(jnp.int32, (rows, 128), 1) < HEAD


def stacked(pair):
    low = low_lanes(pair.shape[0])
    zero = jnp.zeros_like(pair)
    return jnp.concatenate([jnp.where(low, pair, zero), jnp.where(low, zero, pair)], axis=0)


def unstacked(both):
    rows = both.shape[0] // 2
    return jnp.where(low_lanes(rows), both[:rows], both[rows:])


def bias_of(own_seg, other_seg):
    return jnp.where(own_seg == other_seg, 0.0, NEG_FILL)


def turn_columns(qkv, pair, dim, which, turned):
    turned[pair * 128 : pair * 128 + 128, :] = take(qkv, slice(0, qkv.shape[0]), pair, dim, which).T


def twice(row_pair):
    return jnp.concatenate([row_pair[0:1], row_pair[1:2]], axis=1)


def forward_steps(dim, tile, qkv, seg_col, seg_tile, out, logsum, value_t, query_st, bias_ref, acc, top, total):
    pairs = dim // 128

    def prepare():
        for p in range(pairs):
            turn_columns(qkv, p, dim, 2, value_t)

    def begin(i):
        rows = pl.ds(pl.multiple_of(HALO + i * tile, 64), tile)
        for p in range(pairs):
            query_st[p] = stacked(take(qkv, rows, p, dim, 0))
        acc[...] = jnp.zeros_like(acc)
        total[...] = jnp.zeros_like(total)
        top[...] = jnp.full_like(top, 2 * NEG_FILL)

    def block(i, j):
        start = pl.multiple_of(j * BLOCK, BLOCK)
        bias_ref[...] = bias_of(seg_col[pl.ds(start, BLOCK), :], seg_tile[i])
        for p in range(pairs):
            key = take(qkv, pl.ds(start, BLOCK), p, dim, 1)
            scores = matmul_second(key, query_st[p]) + bias_ref[...]
            old = top[p]
            new = jnp.maximum(old, jnp.max(scores, axis=0, keepdims=True))
            keep = jnp.exp(old - new)
            raised = jnp.exp(scores - new)
            total[p] = keep * total[p] + jnp.sum(raised, axis=0, keepdims=True)
            value = value_t[p * 128 : p * 128 + 128, pl.ds(start, BLOCK)]
            acc[p] = keep * acc[p] + matmul(value, raised.astype(BF))
            top[p] = new

    def finish(i):
        lines = pl.ds(pl.multiple_of(i * tile, tile), tile)
        for p in range(pairs):
            whole = total[p]
            out[lines, p * 128 : p * 128 + 128] = unstacked((acc[p] / whole).T).astype(BF)
            lse = top[p] + jnp.log(whole)
            logsum[i, 2 * p : 2 * p + 1, :] = lse[:, :tile]
            logsum[i, 2 * p + 1 : 2 * p + 2, :] = lse[:, tile:]
        for p in range(2 * pairs, 16):
            logsum[i, p : p + 1, :] = jnp.zeros((1, tile), F32)

    return prepare, begin, block, finish


def query_steps(dim, tile, qkv, seg_col, seg_tile, grad, stats, store, sums, key_t, query_st, grad_st, bias_ref, acc):
    pairs = dim // 128

    def prepare():
        sums[...] = jnp.zeros_like(sums)
        for p in range(pairs):
            turn_columns(qkv, p, dim, 1, key_t)

    def begin(i):
        own_rows = pl.ds(pl.multiple_of(i * tile, tile), tile)
        rows = pl.ds(pl.multiple_of(HALO + i * tile, 64), tile)
        for p in range(pairs):
            query_st[p] = stacked(take(qkv, rows, p, dim, 0))
            grad_st[p] = stacked(grad[own_rows, p * 128 : p * 128 + 128])
        acc[...] = jnp.zeros_like(acc)

    def block(i, j):
        there = pl.ds(pl.multiple_of(j * BLOCK, BLOCK), BLOCK)
        bias_ref[...] = bias_of(seg_col[there, :], seg_tile[i])
        for p in range(pairs):
            scores = matmul_second(take(qkv, there, p, dim, 1), query_st[p]) + bias_ref[...]
            probs = jnp.exp(scores - twice(stats[i, 2 * p : 2 * p + 2, :]))
            grad_probs = matmul_second(take(qkv, there, p, dim, 2), grad_st[p])
            grad_scores = (probs * (grad_probs - twice(stats[i, 16 + 2 * p : 18 + 2 * p, :]))).astype(BF)
            acc[p] += matmul(key_t[p * 128 : p * 128 + 128, there], grad_scores)

    def finish(i):
        own_rows = pl.ds(pl.multiple_of(i * tile, tile), tile)
        for p in range(pairs):
            part = 0.125 * unstacked(acc[p].T)
            store(own_rows, p, part.astype(BF))
            sums[:, p * 128 : p * 128 + 128] += jnp.sum(part, axis=0, keepdims=True)

    return prepare, begin, block, finish


def key_steps(dim, tile, qkv, seg_col, seg_row, grad, stats, out, sums, key_st, value_st, bias_ref, key_acc, value_acc):
    pairs = dim // 128

    def prepare():
        sums[...] = jnp.zeros_like(sums)

    def begin(i):
        rows = pl.ds(pl.multiple_of(HALO + i * tile, 64), tile)
        for p in range(pairs):
            key_st[p] = stacked(take(qkv, rows, p, dim, 1))
            value_st[p] = stacked(take(qkv, rows, p, dim, 2))
        key_acc[...] = jnp.zeros_like(key_acc)
        value_acc[...] = jnp.zeros_like(value_acc)

    def block(i, j):
        there = pl.ds(pl.multiple_of(j * BLOCK, BLOCK), BLOCK)
        seg_here = seg_col[pl.ds(pl.multiple_of(HALO + i * tile, 64), tile), :]
        bias_ref[...] = bias_of(seg_here, seg_row[:, there])
        for p in range(pairs):
            query = take(qkv, there, p, dim, 0)
            grad_pair = grad[there, p * 128 : p * 128 + 128]
            scores = matmul_second(key_st[p], query)
            grad_probs = matmul_second(value_st[p], grad_pair)
            probs_all, grads_all = [], []
            for half in range(2):
                head = 2 * p + half
                lines = slice(half * tile, half * tile + tile)
                probs = jnp.exp(scores[lines] + bias_ref[...] - stats[head : head + 1, there])
                grads_all.append((probs * (grad_probs[lines] - stats[16 + head : 17 + head, there])).astype(BF))
                probs_all.append(probs.astype(BF))
            key_acc[p] += matmul(jnp.concatenate(grads_all, axis=0), query)
            value_acc[p] += matmul(jnp.concatenate(probs_all, axis=0), grad_pair)

    def finish(i):
        own_rows = pl.ds(pl.multiple_of(i * tile, tile), tile)
        for p in range(pairs):
            _, at_key, at_value = places(p, dim)
            out[own_rows, at_key : at_key + 128] = unstacked(key_acc[p]).astype(BF)
            part = unstacked(value_acc[p])
            out[own_rows, at_value : at_value + 128] = part.astype(BF)
            sums[:, p * 128 : p * 128 + 128] += jnp.sum(part, axis=0, keepdims=True)

    return prepare, begin, block, finish


def run_dynamic(steps, bounds, tiles):
    prepare, begin, block, finish = steps
    prepare()

    def one_tile(i, carry):
        begin(i)

        def one_block(j, inner):
            block(i, j)
            return inner

        lax.fori_loop(bounds[i, 0], bounds[i, 1], one_block, 0)
        finish(i)
        return carry

    lax.fori_loop(0, tiles, one_tile, 0)


PIECE = 2


def run_static(steps, tile, tiles):
    prepare, begin, block, finish = steps
    prepare()
    yield
    for i in range(tiles):
        first = (HALO + i * tile - HALO + 1) // BLOCK
        after = -(-(HALO + i * tile + tile + HALO - 1) // BLOCK)
        begin(i)
        for piece in range(first, after, PIECE):

            def one_block(j, inner):
                block(i, j)
                return inner

            lax.fori_loop(piece, min(piece + PIECE, after), one_block, 0)
            if piece + PIECE >= after:
                finish(i)
            yield


def forward_kernel(dim, tile, bounds, *refs):
    run_dynamic(forward_steps(dim, tile, *refs), bounds, refs[3].shape[0] // tile)


def query_kernel(dim, tile, bounds, qkv, seg_col, seg_tile, grad, stats, out, sums, *scratch):
    def store(rows, p, part):
        out[rows, p * 128 : p * 128 + 128] = part

    run_dynamic(
        query_steps(dim, tile, qkv, seg_col, seg_tile, grad, stats, store, sums, *scratch), bounds, out.shape[0] // tile
    )


def key_kernel(dim, tile, bounds, qkv, seg_col, seg_row, grad, stats, query_low, out, sums, *scratch):
    for p in range(dim // 128):
        at_query = places(p, dim)[0]
        out[:, at_query : at_query + 128] = query_low[:, p * 128 : p * 128 + 128]
    run_dynamic(
        key_steps(dim, tile, qkv, seg_col, seg_row, grad, stats, out, sums, *scratch), bounds, out.shape[0] // tile
    )


def vmem_call(kernel, arrays, bounds, outs, scratch, flops):
    spec = pl.BlockSpec(memory_space=pltpu.VMEM)
    return pl.pallas_call(
        kernel,
        out_shape=outs,
        in_specs=[pl.BlockSpec(memory_space=pltpu.SMEM)] + [spec] * len(arrays),
        out_specs=jax.tree.map(lambda leaf: spec, outs),
        scratch_shapes=scratch,
        compiler_params=pltpu.CompilerParams(vmem_limit_bytes=VMEM_LIMIT),
        cost_estimate=pl.CostEstimate(flops=flops, bytes_accessed=12000000, transcendentals=6000000),
    )(bounds, *arrays)


def attention_tile(own):
    for tile in (192, 128, 64, 32, 16):
        if own % tile == 0:
            return tile
    raise ValueError("rows")


def by_tile(rows_last, own):
    tile = attention_tile(own)
    return rows_last.reshape(rows_last.shape[0], own // tile, tile).transpose(1, 0, 2)


def segments_by_tile(seg_row, own):
    tiles = by_tile(lax.slice_in_dim(seg_row, HALO, HALO + own, axis=1), own)
    return jnp.concatenate([tiles, tiles], axis=2)


def forward_scratch(padded, tile, dim):
    pairs = dim // 128
    return [
        pltpu.VMEM((dim, padded), BF),
        pltpu.VMEM((pairs, 2 * tile, 128), BF),
        pltpu.VMEM((BLOCK, 2 * tile), F32),
        pltpu.VMEM((pairs, 128, 2 * tile), F32),
        pltpu.VMEM((pairs, 1, 2 * tile), F32),
        pltpu.VMEM((pairs, 1, 2 * tile), F32),
    ]


def attention_forward(qkv, seg_col, seg_row, bounds, own, dim):
    tile = attention_tile(own)
    pairs = dim // 128
    out, logsum = vmem_call(
        functools.partial(forward_kernel, dim, tile),
        (qkv, seg_col, segments_by_tile(seg_row, own)),
        bounds,
        (jax.ShapeDtypeStruct((own, dim), BF), jax.ShapeDtypeStruct((own // tile, 16, tile), F32)),
        forward_scratch(qkv.shape[0], tile, dim),
        10_000_000_000,
    )
    return out, logsum.transpose(1, 0, 2).reshape(16, own)


def attention_query(qkv, seg_col, seg_row, bounds, grad, stats, dim):
    own = grad.shape[0]
    tile = attention_tile(own)
    pairs = dim // 128
    return vmem_call(
        functools.partial(query_kernel, dim, tile),
        (qkv, seg_col, segments_by_tile(seg_row, own), grad, by_tile(stats, own)),
        bounds,
        (jax.ShapeDtypeStruct((own, dim), BF), jax.ShapeDtypeStruct((1, dim), F32)),
        [
            pltpu.VMEM((dim, qkv.shape[0]), BF),
            pltpu.VMEM((pairs, 2 * tile, 128), BF),
            pltpu.VMEM((pairs, 2 * tile, 128), BF),
            pltpu.VMEM((BLOCK, 2 * tile), F32),
            pltpu.VMEM((pairs, 128, 2 * tile), F32),
        ],
        15_000_000_000,
    )


def attention_key(qkv, seg_col, seg_row, bounds, grad_win, stats_win, query_low, own, dim):
    tile = attention_tile(own)
    pairs = dim // 128
    return vmem_call(
        functools.partial(key_kernel, dim, tile),
        (qkv, seg_col, seg_row, grad_win, stats_win, query_low),
        bounds,
        (jax.ShapeDtypeStruct((own, 3 * dim), BF), jax.ShapeDtypeStruct((1, dim), F32)),
        [
            pltpu.VMEM((pairs, 2 * tile, 128), BF),
            pltpu.VMEM((pairs, 2 * tile, 128), BF),
            pltpu.VMEM((tile, BLOCK), F32),
            pltpu.VMEM((pairs, 2 * tile, 128), F32),
            pltpu.VMEM((pairs, 2 * tile, 128), F32),
        ],
        20_000_000_000,
    )


def remote(src, dst, send_sem, recv_sem, where):
    return pltpu.make_async_remote_copy(
        src_ref=src,
        dst_ref=dst,
        send_sem=send_sem,
        recv_sem=recv_sem,
        device_id=where,
        device_id_type=pl.DeviceIdType.MESH,
    )


def here():
    shard, z, y = lax.axis_index("shard"), lax.axis_index("ctx"), lax.axis_index("tp")
    return shard // 2, shard % 2, y, z


def half_of(y, z):
    return (y + z) % 2


def interleave(tasks):
    running, turn = [], 0
    while tasks or running:
        running += [task for first, task in tasks if first <= turn]
        tasks = [item for item in tasks if item[0] > turn]
        alive = []
        for task in running:
            try:
                next(task)
                alive.append(task)
            except StopIteration:
                pass
        running, turn = alive, turn + 1


def timed(task, gaps):
    for stage, _ in enumerate(task):
        yield
        for _ in range(gaps[min(stage, len(gaps) - 1)]):
            yield


def greet_all(always, sometimes):
    barrier = pltpu.get_barrier_semaphore()
    number = jnp.int32(len(always))
    for peer in always:
        pl.semaphore_signal(barrier, inc=1, device_id=peer, device_id_type=pl.DeviceIdType.MESH)
    for condition, peer in sometimes:

        @pl.when(condition)
        def _():
            pl.semaphore_signal(barrier, inc=1, device_id=peer, device_id_type=pl.DeviceIdType.MESH)

        number = number + condition.astype(jnp.int32)
    pl.semaphore_wait(barrier, number)


class Line:
    SCRATCH = 4

    def __init__(self, z, dealt, to_slots, refs, sems):
        self.z, self.dealt, self.to_slots = z, dealt, to_slots
        self.blocks, self.picked, self.away, self.arrived = refs
        self.send, self.block_recv, self.away_recv = sems
        self.inner = (z == 1) | (z == 2)
        self.outer = (z == 0) | (z == 3)
        self.near = 1 + z // 3
        self.end = jnp.maximum(3 * (z - 1), 0) % 6
        self.middle = 3 - z
        self.far = 3 - self.end
        self.slots = refs[0].shape[1]

    def copy(self, what):
        if what == "own_near":
            block, where, sem = self.z, self.near, 0
        elif what == "own_middle":
            block, where, sem = self.z, self.middle, 0
        elif what == "forward":
            block, where, sem = self.end, self.middle, 1
        else:
            where = self.end
            return remote(self.away, self.arrived, self.send.at[2], self.away_recv, {"ctx": where})
        there = self.blocks.at[block]
        return remote(there, there, self.send.at[sem], self.block_recv.at[block], {"ctx": where})

    def wait_block(self, block):
        there = self.blocks.at[block]
        remote(there, there, self.send.at[0], self.block_recv.at[block], {"ctx": self.middle}).wait_recv()

    def select(self, target, wanted_by, block, start):
        slots = self.slots
        wide = 384 if slots % 384 == 0 else 128

        def body(i, carry):
            lines = pl.ds(pl.multiple_of(i * wide, 128), wide)
            if self.to_slots:
                row = self.dealt[:, pl.ds(pl.multiple_of(wanted_by * slots + i * wide, 128), wide)]
                wanted = jnp.broadcast_to(row, (8, wide)).T[:, :1]
                offered = (block * slots + lax.broadcasted_iota(jnp.int32, (wide, slots), 1)).astype(F32)
            else:
                wanted = wanted_by * slots + i * wide + lax.broadcasted_iota(jnp.int32, (wide, slots), 0)
                offered = self.dealt[:, pl.ds(pl.multiple_of(block * slots, 128), slots)]
            chosen = jnp.where(wanted == offered, 1.0, 0.0).astype(BF)
            part = matmul(chosen, self.blocks[block]).astype(BF)
            target[lines, :] = part if start else target[lines, :] + part
            return carry

        lax.fori_loop(0, slots // wide, body, 0)

    def run(self):
        @pl.when(self.outer)
        def _():
            self.copy("own_near").start()

        @pl.when(self.inner)
        def _():
            self.copy("own_middle").start()

        self.select(self.picked, self.z, self.z, True)
        yield

        @pl.when(self.inner)
        def _():
            self.wait_block(self.end)
            self.copy("forward").start()
            self.select(self.picked, self.z, self.end, False)
            self.select(self.away, self.end, self.z, True)

        yield

        @pl.when(self.inner)
        def _():
            self.wait_block(self.middle)
            self.select(self.away, self.end, self.middle, False)
            self.select(self.picked, self.z, self.middle, False)

        yield

        @pl.when(self.inner)
        def _():
            self.wait_block(self.far)
            self.select(self.away, self.end, self.far, False)
            self.copy("away").start()
            self.select(self.picked, self.z, self.far, False)

        yield

        @pl.when(self.outer)
        def _():
            self.copy("away").wait_recv()
            self.picked[...] = self.picked[...] + self.arrived[...]

    def settle(self):
        @pl.when(self.outer)
        def _():
            self.copy("own_near").wait_send()

        @pl.when(self.inner)
        def _():
            self.copy("own_middle").wait_send()
            self.copy("forward").wait_send()
            self.copy("away").wait_send()


def line_scratch(ctx_size, slots, chunks, columns):
    blocks = [pltpu.VMEM((ctx_size, slots, columns), BF) for _ in range(chunks)]
    others = [pltpu.VMEM((slots, columns), BF) for _ in range(3 * chunks)]
    sems = [pltpu.SemaphoreType.DMA((chunks, 3)), pltpu.SemaphoreType.DMA((chunks, ctx_size)), pltpu.SemaphoreType.DMA((chunks,))]
    return blocks + others + sems


def line_of(j, chunks, z, dealt, to_slots, refs):
    blocks, others, sems = refs[:chunks], refs[chunks : 4 * chunks], refs[4 * chunks :]
    return Line(
        z,
        dealt,
        to_slots,
        (blocks[j], others[3 * j], others[3 * j + 1], others[3 * j + 2]),
        (sems[0].at[j], sems[1].at[j], sems[2].at[j]),
    )


PERM = 3


MIDDLE_AT = (4, 8, 12)
COTANGENT_AT = (1, 2, 3)
COTANGENT_PAUSE = 1


def first_kernel(widths, padded, *refs):
    count = len(widths)
    pieces, (small, tokens, cotangent, dealt_row, seg_col, seg_tile) = refs[:count], refs[count : count + 6]
    refs = refs[count + 6 :]
    wholes, (small_whole, qkv_out, cot_rows, attended, logsum) = refs[:count], refs[count : count + 5]
    rest = refs[count + 5 :]
    attention_refs, qkv, qkv_sem, rest = rest[:6], rest[6], rest[7], rest[8:]
    weight, window, send, recv, own_sem, small_sem, halo_sem, post_send, post_recv, bring = rest[:10]
    line_refs = rest[10:]
    x, c, y, z = here()
    h = half_of(y, z)
    rows, dim = tokens.shape
    own = rows // 2
    half = dim // 2
    last = 3
    tile = attention_tile(own)
    at_x, at_y, at_c = {"shard": 2 * (1 - x) + c}, {"tp": 1 - y}, {"shard": 2 * x + 1 - c}
    left, right = {"ctx": jnp.maximum(z - 1, 0)}, {"ctx": jnp.minimum(z + 1, last)}
    greet_all((at_x, at_y, at_c), ((z > 0, left), (z < last, right)))

    def slot(a, of_y, of_x, of_c, lines=None):
        cols = pl.ds(pl.multiple_of(of_y * widths[a], 128), widths[a])
        depth = wholes[a].shape[2]
        lines = slice(0, depth) if lines is None else slice(lines * depth // 2, (lines + 1) * depth // 2)
        return (weight if a == 0 else wholes[a]).at[of_x, of_c, lines, cols]

    def moves(a):
        table = [
            (pieces[a], slot(a, y, x, c), at_x),
            (pieces[a], slot(a, y, x, c), at_y),
            (pieces[a], slot(a, y, x, c), at_c),
            (slot(a, y, 1 - x, c, 0), slot(a, y, 1 - x, c, 0), at_y),
            (slot(a, 1 - y, x, c, 1), slot(a, 1 - y, x, c, 1), at_x),
            (slot(a, y, 1 - x, c), slot(a, y, 1 - x, c), at_c),
            (slot(a, 1 - y, x, c), slot(a, 1 - y, x, c), at_c),
            (slot(a, 1 - y, 1 - x, c, 0), slot(a, 1 - y, 1 - x, c, 0), at_c),
            (slot(a, 1 - y, 1 - x, c, 1), slot(a, 1 - y, 1 - x, c, 1), at_c),
        ]
        return [remote(s, d, send.at[a, kind], recv.at[a, kind], w) for kind, (s, d, w) in enumerate(table)]

    tables = [moves(a) for a in range(count)]
    depth = small_whole.shape[0] // 2
    small_at = small_whole.at[pl.ds(pl.multiple_of(y * depth, 16), depth)]
    small_copy = remote(small, small_at, small_sem.at[0], small_sem.at[1], at_y)
    sends_right, sends_left = (h == 1) & (z < last), (h == 0) & (z > 0)
    gets_left, gets_right = (h == 0) & (z > 0), (h == 1) & (z < last)

    def halo(where):
        src = tokens.at[pl.ds(pl.multiple_of(h * (rows - HALO), 64), HALO)]
        dst = window.at[pl.ds(pl.multiple_of((1 - h) * (HALO + own), 64), HALO)]
        return remote(src, dst, halo_sem.at[0], halo_sem.at[1], where)

    inside = pltpu.make_async_copy(
        tokens.at[pl.ds(pl.multiple_of(h * (own - HALO), 64), own + HALO)],
        window.at[pl.ds(pl.multiple_of((1 - h) * HALO, 64), own + HALO)],
        halo_sem.at[2],
    )
    small_local = pltpu.make_async_copy(small, small_at, small_sem.at[2])
    piece_local = [pltpu.make_async_copy(pieces[a], slot(a, y, x, c), own_sem.at[a]) for a in range(count)]
    lines = [line_of(j, PERM, z, dealt_row, False, line_refs) for j in range(PERM)]

    def columns_of(j):
        return pl.ds(pl.multiple_of(y * half + j * (half // PERM), 128), half // PERM)

    bring_cot = [
        pltpu.make_async_copy(cotangent.at[:, columns_of(j)], lines[j].blocks.at[z], bring.at[j]) for j in range(PERM)
    ]
    def spread(a):
        for kind in range(3):
            tables[a][kind].start()

    spread(0)
    small_copy.start()

    @pl.when(sends_right)
    def _():
        halo(right).start()

    @pl.when(sends_left)
    def _():
        halo(left).start()

    for item in (small_local, *piece_local, inside, *bring_cot):
        item.start()
    window[padded - (padded - 2 * HALO - own) :, :] = jnp.zeros((padded - 2 * HALO - own, dim), BF)

    @pl.when((h == 0) & (z == 0))
    def _():
        window[:HALO, :] = jnp.zeros((HALO, dim), BF)

    @pl.when((h == 1) & (z == last))
    def _():
        window[HALO + own : 2 * HALO + own, :] = jnp.zeros((HALO, dim), BF)

    def pause(number):
        for _ in range(number):
            yield

    def forward_first(a):
        tables[a][0].wait_recv()
        tables[a][3].start()
        tables[a][5].start()
        tables[a][1].wait_recv()
        tables[a][4].start()
        tables[a][6].start()

    def forward_second(a):
        tables[a][3].wait_recv()
        tables[a][7].start()
        tables[a][4].wait_recv()
        tables[a][8].start()

    def collect(a):
        for kind in (2, 5, 6, 7, 8):
            tables[a][kind].wait_recv()

    early, late = tuple(range(1, count - 1)), count - 1

    def qkv_task():
        forward_first(0)
        yield
        forward_second(0)
        for a in early:
            spread(a)
        yield
        collect(0)
        yield from project_task()
        qkv_copy.start()
        yield from run_static(
            forward_steps(dim, tile, qkv, seg_col, seg_tile, attended, logsum, *attention_refs), tile, own // tile
        )

    def others_task():
        for a in early:
            forward_first(a)
        spread(late)
        yield from pause(MIDDLE_AT[1] - MIDDLE_AT[0])
        forward_first(late)
        for a in early:
            forward_second(a)
        yield from pause(MIDDLE_AT[2] - MIDDLE_AT[1])
        forward_second(late)
        for a in (*early, late):
            collect(a)

    qkv_copy = pltpu.make_async_copy(qkv, qkv_out, qkv_sem)

    def project_task():
        piece_local[0].wait()
        pltpu.make_async_copy(weight, wholes[0], own_sem.at[0]).start()
        inside.wait()
        small_copy.wait()
        small_local.wait()

        @pl.when(gets_left | gets_right)
        def _():
            halo(left).wait_recv()

        depth_w, width = weight.shape[2], widths[0]
        third = width // 3
        step = 256
        for of_y in range(2):
            bias = small_whole[of_y * depth : of_y * depth + 1, :].astype(F32)
            bias = jnp.concatenate([bias[:, :third], jnp.zeros((1, third), F32), bias[:, third : 2 * third]], axis=1)
            scale = jnp.where(lax.broadcasted_iota(jnp.int32, (1, width), 1) < third, 0.125, 1.0).astype(BF)
            full = jnp.concatenate(
                [weight[i // 2, i % 2, :, of_y * width : (of_y + 1) * width] for i in range(4)], axis=0
            )

            def body(i, carry):
                there = pl.ds(pl.multiple_of(i * step, step), step)
                value = (matmul(window[there, :], full) + bias).astype(BF)
                qkv[there, of_y * width : (of_y + 1) * width] = value * scale
                return carry

            lax.fori_loop(0, padded // step, body, 0)
            yield

    def post(j):
        there = lines[j].picked.at[pl.ds(pl.multiple_of((1 - h) * own, 64), own)]
        return remote(there, cot_rows.at[:, columns_of(j)], post_send.at[j], post_recv.at[j], at_y)

    def cotangent_task(j):
        bring_cot[j].wait()
        for _ in lines[j].run():
            yield
            yield from pause(COTANGENT_PAUSE)
        post(j).start()
        cot_rows[:, columns_of(j)] = lines[j].picked[pl.ds(pl.multiple_of(h * own, 64), own), :]
        yield
        post(j).wait_recv()

    tasks = [(0, qkv_task()), (MIDDLE_AT[0], others_task())]
    tasks += [(COTANGENT_AT[j], cotangent_task(j)) for j in range(PERM)]
    interleave(sorted(tasks, key=lambda item: item[0]))
    for a in range(count):
        for kind in range(9):
            tables[a][kind].wait_send()
        if a:
            piece_local[a].wait()
    pltpu.make_async_copy(weight, wholes[0], own_sem.at[0]).wait()
    qkv_copy.wait()

    @pl.when(sends_right | sends_left)
    def _():
        halo(left).wait_send()

    for j in range(PERM):
        lines[j].settle()
        post(j).wait_send()


def first_stage(pieces, small, tokens, cotangent, dealt, seg_col, seg_row, padded):
    rows, dim = tokens.shape
    depth = pieces[0].shape[0]
    own = rows // 2
    tile = attention_tile(own)
    widths = tuple(piece.shape[1] for piece in pieces)
    count = len(pieces)
    ctx_size = lax.axis_size("ctx")
    outs = [jax.ShapeDtypeStruct((2, 2, depth, 2 * width), BF) for width in widths]
    outs += [
        jax.ShapeDtypeStruct((2 * small.shape[0], small.shape[1]), BF),
        jax.ShapeDtypeStruct((padded, 3 * dim), BF),
        jax.ShapeDtypeStruct((own, dim), BF),
        jax.ShapeDtypeStruct((own, dim), BF),
        jax.ShapeDtypeStruct((own // tile, 16, tile), F32),
    ]
    anywhere, vmem = pl.BlockSpec(memory_space=pl.ANY), pl.BlockSpec(memory_space=pltpu.VMEM)
    result = pl.pallas_call(
        functools.partial(first_kernel, widths, padded),
        out_shape=outs,
        in_specs=[anywhere] * (count + 3) + [vmem] * 3,
        out_specs=[anywhere] * count + [vmem, anywhere] + [vmem] * 3,
        scratch_shapes=forward_scratch(padded, tile, dim)
        + [
            pltpu.VMEM((padded, 3 * dim), BF),
            pltpu.SemaphoreType.DMA,
            pltpu.VMEM((2, 2, depth, 2 * widths[0]), BF),
            pltpu.VMEM((padded, dim), BF),
            pltpu.SemaphoreType.DMA((count, 9)),
            pltpu.SemaphoreType.DMA((count, 9)),
            pltpu.SemaphoreType.DMA((count,)),
            pltpu.SemaphoreType.DMA((3,)),
            pltpu.SemaphoreType.DMA((3,)),
            pltpu.SemaphoreType.DMA((PERM,)),
            pltpu.SemaphoreType.DMA((PERM,)),
            pltpu.SemaphoreType.DMA((PERM,)),
        ]
        + line_scratch(ctx_size, rows, PERM, dim // 2 // PERM),
        compiler_params=pltpu.CompilerParams(
            collective_id=0, has_side_effects=True, vmem_limit_bytes=VMEM_LIMIT
        ),
        cost_estimate=pl.CostEstimate(flops=10000000000, bytes_accessed=100000000, transcendentals=0),
    )(*pieces, small, tokens, cotangent, dealt[None, :], seg_col, segments_by_tile(seg_row, own))
    whole = [full.reshape(4 * depth, full.shape[3]) for full in result[:count]]
    logsum = result[count + 4].transpose(1, 0, 2).reshape(16, own)
    return whole, result[count], result[count + 1], result[count + 2], result[count + 3], logsum


def add_lines(dst, first, second):
    rows = dst.shape[0]
    step = 48 if rows % 48 == 0 else 16

    def body(i, carry):
        lines = pl.ds(pl.multiple_of(i * step, 16), step)
        dst[lines, :] = (first[lines, :].astype(F32) + second[lines, :].astype(F32)).astype(dst.dtype)
        return carry

    lax.fori_loop(0, rows // step, body, 0)


RING = 4


class Reduction:
    STAGES = 7

    def __init__(self, chunks, outs, refs):
        number = len(chunks)
        self.chunks, self.outs = chunks, outs
        ring = min(RING, number)
        self.full = [refs[k % ring] for k in range(number)]
        refs = refs[ring:]
        self.by_core, self.by_x, self.plane, self.from_end, self.half_z, self.final = (
            refs[i * number : (i + 1) * number] for i in range(6)
        )
        self.send, self.recv = refs[6 * number :]
        self.place = here()
        z = self.place[3]
        self.inner, self.outer = (z == 1) | (z == 2), (z == 0) | (z == 3)
        self.near, self.end, self.middle = 1 + z // 3, jnp.maximum(3 * (z - 1), 0) % 6, 3 - z
        self.rows = self.full[0].shape[3]

    def copy(self, k, stage):
        x, c, y, z = self.place
        half = self.rows // 2
        side = z // 2
        if stage == 0:
            src, dst, where = self.full[k].at[:, :, 1 - c], self.by_core[k], {"shard": 2 * x + 1 - c}
        elif stage == 1:
            src, dst, where = self.by_core[k].at[:, 1 - x], self.by_x[k], {"shard": 2 * (1 - x) + c}
        elif stage == 2:
            src, dst, where = self.by_x[k].at[1 - y], self.plane[k], {"tp": 1 - y}
        elif stage == 3:
            src, dst, where = self.plane[k], self.from_end[k], {"ctx": self.near}
        elif stage == 4:
            src = self.plane[k].at[pl.ds(pl.multiple_of((1 - side) * half, 16), half)]
            dst, where = self.half_z[k], {"ctx": self.middle}
        elif stage == 5:
            src = dst = self.final[k].at[pl.ds(pl.multiple_of(side * half, 16), half)]
            where = {"ctx": self.middle}
        else:
            src = dst = self.final[k]
            where = {"ctx": self.end}
        return remote(src, dst, self.send.at[k, stage], self.recv.at[k, stage], where)

    def sender(self, stage):
        return None if stage < 3 else (self.outer if stage == 3 else self.inner)

    def receiver(self, stage):
        return None if stage < 3 else (self.outer if stage == 6 else self.inner)

    def guarded(self, condition, action):
        if condition is None:
            action()
        else:
            pl.when(condition)(action)

    def start(self, k, stage):
        self.guarded(self.sender(stage), lambda: self.copy(k, stage).start())

    def absorb(self, k, stage):
        x, c, y, z = self.place
        half = self.rows // 2
        side = z // 2
        self.copy(k, stage).wait_recv()
        if stage == 0:
            for of_y in range(2):
                for of_x in range(2):
                    there = self.by_core[k].at[of_y, of_x]
                    add_lines(there, there, self.full[k].at[of_y, of_x, c])
            self.copy(k, 0).wait_send()
        elif stage == 1:
            for i in range(2):
                add_lines(self.by_x[k].at[i], self.by_x[k].at[i], self.by_core[k].at[i, x])
        elif stage == 2:
            add_lines(self.plane[k], self.plane[k], self.by_x[k].at[y])
        elif stage == 3:
            add_lines(self.plane[k], self.plane[k], self.from_end[k])
        elif stage == 4:
            lines = pl.ds(pl.multiple_of(side * half, 16), half)
            add_lines(self.final[k].at[lines], self.half_z[k], self.plane[k].at[lines])

    def task(self, k, produce):
        produce(k)
        for stage in range(self.STAGES):
            self.start(k, stage)
            yield
            self.guarded(self.receiver(stage), lambda: self.absorb(k, stage))
        a, first, width = self.chunks[k]
        self.outs[a][:, first : first + width] = self.final[k][...].astype(F32)

    def settle(self):
        for k in range(len(self.chunks)):
            for stage in range(1, self.STAGES):
                self.guarded(self.sender(stage), lambda: self.copy(k, stage).wait_send())

    def product(self, k, turned, other):
        for of_y in range(2):
            right = other(of_y)
            for i in range(4):
                value = matmul(turned[i * self.rows : (i + 1) * self.rows, :], right)
                self.full[k][of_y, i // 2, i % 2] = value.astype(BF)


def reduction_scratch(rows, chunks):
    shapes = [
        lambda w: (2, 2, rows, w),
        lambda w: (2, rows, w),
        lambda w: (rows, w),
        lambda w: (rows, w),
        lambda w: (rows // 2, w),
        lambda w: (rows, w),
    ]
    scratch = [pltpu.VMEM((2, 2, 2, rows, CHUNK), BF) for _ in range(min(RING, len(chunks)))]
    scratch += [pltpu.VMEM(shape(width), BF) for shape in shapes for _, _, width in chunks]
    return scratch + [pltpu.SemaphoreType.DMA((len(chunks), 7)), pltpu.SemaphoreType.DMA((len(chunks), 7))]


def wide_peers():
    x, c, y, z = here()
    return (
        {"shard": 2 * x + 1 - c},
        {"shard": 2 * (1 - x) + c},
        {"tp": 1 - y},
        {"ctx": z + 1 - 2 * (z % 2)},
    )


CHUNK = 384


def chunks_of(widths):
    return tuple((a, first, CHUNK) for a, width in enumerate(widths) for first in range(0, width, CHUNK))


def slots_task(line, j, y, values, out, pre, post_sem, at_y):
    slots = line.slots
    own = slots // 2
    outgoing, pre_send, pre_recv = pre
    post_send, post_recv = post_sem
    width = line.picked.shape[1]
    mine_rows = pl.ds(pl.multiple_of(half_of(y, line.z) * own, 64), own)
    half = out.shape[1] // 2
    outgoing[...] = values(j, 1 - y)
    before = remote(outgoing, line.blocks.at[line.z, mine_rows], pre_send, pre_recv, at_y)
    before.start()
    line.blocks[line.z, mine_rows, :] = values(j, y)
    yield
    before.wait_recv()
    yield from line.run()
    cols = pl.ds(pl.multiple_of(y * half + j * width, 128), width)
    after = remote(line.picked, out.at[:, cols], post_send, post_recv, at_y)
    after.start()
    out[:, cols] = line.picked[...]
    yield
    after.wait_recv()
    before.wait_send()
    after.wait_send()
    line.settle()


LAYER_AT = (2, 5, 8)
LAYER_GAPS = (1, 1, 1, 1, 1, 1)
AHEAD = 2
X_FIRST = 3
LATER_GAPS = (1, 1, 1, 0, 1)


def chunk_round(k):
    return k // AHEAD


def chunk_gaps(k):
    return (0, max(0, X_FIRST + 5 * k // 4 - chunk_round(k) - 2)) + LATER_GAPS


def backward_kernel(chunks, *refs):
    first_low, attended, hidden_low, pre_low, second_low, act_low, grad, stats, stats_tile, qkv_in, seg_col, seg_row, seg_tile, layer_low, dealt_row = refs[:15]
    outs, qkv_low, query_sums, value_sums, layer_out = refs[15:18], refs[18], refs[19], refs[20], refs[21]
    rest = refs[22:]
    turned, grad_win, stats_side, stats_win, halo_sem = rest[0:3], rest[3], rest[4], rest[5], rest[6]
    key_t, first_st, second_st, bias_query, bias_key, acc, first_acc, second_acc = rest[7:15]
    stream, stream_sem, qkv, qkv_sem = rest[15:19]
    outgoing, rest = rest[19 : 19 + PERM], rest[19 + PERM :]
    qkv_copy = pltpu.make_async_copy(qkv_in, qkv, qkv_sem)
    qkv_copy.start()
    pre_send, pre_recv, post_send, post_recv = rest[:4]
    line_number = 4 * PERM + 3
    line_refs, reduction_refs = rest[4 : 4 + line_number], rest[4 + line_number :]
    reduction = Reduction(chunks, outs, reduction_refs)
    x, c, y, z = reduction.place
    h = half_of(y, z)
    own, dim = grad.shape
    padded = qkv.shape[0]
    tile = attention_tile(own)
    last = 3
    at_y, at_z = {"tp": 1 - y}, {"ctx": jnp.clip(z - 1 + 2 * h, 0, last)}
    has_z = ((h == 0) & (z > 0)) | ((h == 1) & (z < last))
    greet_all(wide_peers(), ((reduction.inner, {"ctx": 3 - z}),))

    def halos(where, same):
        first = (1 - h) if same else h
        side = h if same else 1 - h
        base = 0 if same else 4
        return (
            remote(
                grad.at[pl.ds(pl.multiple_of(first * (own - HALO), 64), HALO)],
                grad_win.at[pl.ds(pl.multiple_of(side * (HALO + own), 64), HALO)],
                halo_sem.at[base],
                halo_sem.at[base + 1],
                where,
            ),
            remote(stats, stats_side.at[side], halo_sem.at[base + 2], halo_sem.at[base + 3], where),
        )

    for item in halos(at_y, True):
        item.start()

    @pl.when(has_z)
    def _():
        for item in halos(at_z, False):
            item.start()

    grad_win[HALO : HALO + own, :] = grad[...]
    grad_win[2 * HALO + own :, :] = jnp.zeros((padded - 2 * HALO - own, dim), BF)
    for missing, side in (((h == 0) & (z == 0), 0), ((h == 1) & (z == last), 1)):

        @pl.when(missing)
        def _():
            grad_win[side * (HALO + own) : side * (HALO + own) + HALO, :] = jnp.zeros((HALO, dim), BF)
            stats_side[side] = jnp.zeros(stats.shape, F32)

    lefts, rights = (first_low, hidden_low, second_low), (attended, pre_low, act_low)

    def bring(k, of_y):
        a, first, columns = chunks[k]
        half = rights[a].shape[1] // 2
        return pltpu.make_async_copy(
            rights[a].at[:, of_y * half + first : of_y * half + first + columns],
            stream.at[k % 2, of_y],
            stream_sem.at[k % 2, of_y],
        )

    for k in range(min(2, len(chunks))):
        for of_y in range(2):
            bring(k, of_y).start()

    def produce(k):
        a, first, _ = chunks[k]
        if first == 0:
            turned[a][...] = lefts[a][...].T
        for of_y in range(2):
            bring(k, of_y).wait()
        reduction.product(k, turned[a], lambda of_y: stream[k % 2, of_y])
        if k + 2 < len(chunks):
            for of_y in range(2):
                bring(k + 2, of_y).start()

    lines = [line_of(j, PERM, z, dealt_row, True, line_refs) for j in range(PERM)]
    width = dim // 2 // PERM

    def layer_values(j, half):
        return layer_low[:, pl.ds(pl.multiple_of(half * (dim // 2) + j * width, 128), width)]

    def store(rows, p, part):
        at_query = places(p, dim)[0]
        qkv_low[rows, at_query : at_query + 128] = part

    def attention_task():
        yield
        qkv_copy.wait()
        yield from run_static(
            query_steps(
                dim, tile, qkv, seg_col, seg_tile, grad, stats_tile, store, query_sums, key_t, first_st, second_st, bias_query, acc
            ),
            tile,
            own // tile,
        )
        for item in halos(at_y, True):
            item.wait()

        @pl.when(has_z)
        def _():
            for item in halos(at_z, False):
                item.wait()

        stats_win[...] = jnp.concatenate(
            [
                stats_side[0][:, own - HALO :],
                stats[...],
                stats_side[1][:, :HALO],
                jnp.zeros((stats.shape[0], padded - 2 * HALO - own), F32),
            ],
            axis=1,
        )
        yield from run_static(
            key_steps(
                dim,
                tile,
                qkv,
                seg_col,
                seg_row,
                grad_win,
                stats_win,
                qkv_low,
                value_sums,
                first_st,
                second_st,
                bias_key,
                first_acc,
                second_acc,
            ),
            tile,
            own // tile,
        )

    tasks = [(chunk_round(k), timed(reduction.task(k, produce), chunk_gaps(k))) for k in range(len(chunks))]
    tasks += [
        (
            LAYER_AT[j],
            timed(
                slots_task(
                lines[j],
                j,
                y,
                layer_values,
                layer_out,
                (outgoing[j], pre_send.at[j], pre_recv.at[j]),
                (post_send.at[j], post_recv.at[j]),
                at_y,
            ), LAYER_GAPS),
        )
        for j in range(PERM)
    ]
    interleave(sorted([(0, attention_task())] + tasks, key=lambda item: item[0]))
    reduction.settle()


def backward_stage(first_low, attended, hidden_low, pre_low, second_low, act_low, grad, stats, qkv, seg_col, seg_row, layer_low, dealt):
    own, dim = grad.shape
    padded = qkv.shape[0]
    rows = dim // 4
    tile = attention_tile(own)
    pairs = dim // 128
    widths = (attended.shape[1] // 2, pre_low.shape[1] // 2, act_low.shape[1] // 2)
    chunks = chunks_of(widths)
    spec = pl.BlockSpec(memory_space=pltpu.VMEM)
    outs = [jax.ShapeDtypeStruct((rows, width), F32) for width in widths]
    outs += [
        jax.ShapeDtypeStruct((own, 3 * dim), BF),
        jax.ShapeDtypeStruct((1, dim), F32),
        jax.ShapeDtypeStruct((1, dim), F32),
        jax.ShapeDtypeStruct((2 * own, dim), BF),
    ]
    scratch = [pltpu.VMEM((dim, own), BF) for _ in range(3)]
    scratch += [
        pltpu.VMEM((padded, dim), BF),
        pltpu.VMEM((2, 32, own), F32),
        pltpu.VMEM((32, padded), F32),
        pltpu.SemaphoreType.DMA((8,)),
        pltpu.VMEM((dim, padded), BF),
        pltpu.VMEM((pairs, 2 * tile, 128), BF),
        pltpu.VMEM((pairs, 2 * tile, 128), BF),
        pltpu.VMEM((BLOCK, 2 * tile), F32),
        pltpu.VMEM((tile, BLOCK), F32),
        pltpu.VMEM((pairs, 128, 2 * tile), F32),
        pltpu.VMEM((pairs, 2 * tile, 128), F32),
        pltpu.VMEM((pairs, 2 * tile, 128), F32),
    ]
    scratch += [pltpu.VMEM((2, 2, own, CHUNK), BF), pltpu.SemaphoreType.DMA((2, 2))]
    scratch += [pltpu.VMEM((padded, 3 * dim), BF), pltpu.SemaphoreType.DMA]
    scratch += [pltpu.VMEM((own, dim // 2 // PERM), BF) for _ in range(PERM)]
    scratch += [pltpu.SemaphoreType.DMA((PERM,)) for _ in range(4)]
    scratch += line_scratch(lax.axis_size("ctx"), 2 * own, PERM, dim // 2 // PERM)
    scratch += reduction_scratch(rows, chunks)
    args = (
        first_low,
        attended,
        hidden_low,
        pre_low,
        second_low,
        act_low,
        grad,
        stats,
        by_tile(stats, own),
        qkv,
        seg_col,
        seg_row,
        segments_by_tile(seg_row, own),
        layer_low,
        dealt[None, :].astype(F32),
    )
    anywhere = pl.BlockSpec(memory_space=pl.ANY)
    return pl.pallas_call(
        functools.partial(backward_kernel, chunks),
        out_shape=outs,
        in_specs=[anywhere if i in (1, 3, 5, 9) else spec for i in range(len(args))],
        out_specs=[spec] * len(outs),
        scratch_shapes=scratch,
        compiler_params=pltpu.CompilerParams(
            collective_id=1, has_side_effects=True, vmem_limit_bytes=VMEM_LIMIT
        ),
        cost_estimate=pl.CostEstimate(flops=50000000000, bytes_accessed=100000000, transcendentals=0),
    )(*args)


def last_kernel(chunks, *refs):
    inputs, qkv_low, weight, grad_first, dealt_row, vector = refs[:6]
    outs, tokens_grad, vector_out = refs[6:9], refs[9], refs[10]
    rest = refs[11:]
    number = PERM
    turned, outgoing, pre_send, pre_recv, post_send, post_recv = (
        rest[0],
        rest[1 : 1 + number],
        rest[1 + number],
        rest[2 + number],
        rest[3 + number],
        rest[4 + number],
    )
    vector_in, vector_sum, vector_send, vector_recv = rest[5 + number : 9 + number]
    rest = rest[9 + number :]
    line_number = 4 * number + 3
    line_refs, reduction_refs = rest[:line_number], rest[line_number:]
    reduction = Reduction(chunks, outs, reduction_refs)
    x, c, y, z = reduction.place
    own, dim = inputs.shape
    at_y = {"tp": 1 - y}
    inner = (z == 1) | (z == 2)
    peers = wide_peers() + ({"ctx": (z + 2) % 4},)
    greet_all(peers, ((inner, {"ctx": 3 - z}),))
    lines = [line_of(j, number, z, dealt_row, True, line_refs) for j in range(number)]
    width = dim // 2 // PERM

    def vector_copy(stage):
        return remote(
            vector_sum.at[stage], vector_in.at[stage], vector_send.at[stage], vector_recv.at[stage], peers[stage]
        )

    def vector_task():
        vector_sum[0] = vector[...]
        for stage in range(5):
            vector_copy(stage).start()
            yield
            vector_copy(stage).wait_recv()
            total = vector_sum[stage] + vector_in[stage]
            if stage < 4:
                vector_sum[stage + 1] = total
            else:
                vector_out[...] = total

    def grad_values(j, half):
        first = pl.ds(pl.multiple_of(half * (dim // 2) + j * width, 128), width)
        return (grad_first[:, first] + matmul_second(qkv_low[...], weight[first, :])).astype(BF)

    def produce(k):
        if k == 0:
            turned[...] = inputs[...].T
        which, first, columns = chunks[k]
        half = qkv_low.shape[1] // 2
        third = half // 3

        def other(of_y):
            start = of_y * half + which * third + first
            return qkv_low[:, start : start + columns]

        reduction.product(k, turned, other)

    def slots(values, j, index, out_ref):
        return slots_task(
            lines[index],
            j,
            y,
            values,
            out_ref,
            (outgoing[index], pre_send.at[index], pre_recv.at[index]),
            (post_send.at[index], post_recv.at[index]),
            at_y,
        )

    tasks = [(j, slots(grad_values, j, j, tokens_grad)) for j in range(PERM)]
    tasks += [(k, reduction.task(k, produce)) for k in range(len(chunks))]
    tasks += [(1, vector_task())]
    interleave(sorted(tasks, key=lambda item: item[0]))
    reduction.settle()
    for stage in range(5):
        vector_copy(stage).wait_send()


def last_stage(inputs, qkv_low, weight, grad_first, dealt, vector):
    own, dim = inputs.shape
    ctx_size = lax.axis_size("ctx")
    rows = dim // 4
    width = qkv_low.shape[1] // 6
    chunks = chunks_of((width,) * 3)
    spec = pl.BlockSpec(memory_space=pltpu.VMEM)
    outs = [
        *[jax.ShapeDtypeStruct((rows, width), F32) for _ in range(3)],
        jax.ShapeDtypeStruct((2 * own, dim), BF),
        jax.ShapeDtypeStruct(vector.shape, F32),
    ]
    scratch = [pltpu.VMEM((dim, own), BF)]
    scratch += [pltpu.VMEM((own, dim // 2 // PERM), BF) for _ in range(PERM)]
    scratch += [pltpu.SemaphoreType.DMA((PERM,)) for _ in range(4)]
    scratch += [pltpu.VMEM((5,) + vector.shape, F32), pltpu.VMEM((5,) + vector.shape, F32)]
    scratch += [pltpu.SemaphoreType.DMA((5,)), pltpu.SemaphoreType.DMA((5,))]
    scratch += line_scratch(ctx_size, 2 * own, PERM, dim // 2 // PERM)
    scratch += reduction_scratch(rows, chunks)
    return pl.pallas_call(
        functools.partial(last_kernel, chunks),
        out_shape=outs,
        in_specs=[spec] * 6,
        out_specs=[spec] * len(outs),
        scratch_shapes=scratch,
        compiler_params=pltpu.CompilerParams(
            collective_id=2, has_side_effects=True, vmem_limit_bytes=VMEM_LIMIT
        ),
        cost_estimate=pl.CostEstimate(flops=10000000000, bytes_accessed=100000000, transcendentals=0),
    )(inputs, qkv_low, weight, grad_first, dealt[None, :].astype(F32), vector)


def project_kernel(dim, x_ref, weight, bias, out):
    step = 256
    third = weight.shape[1] // 3

    def body(i, carry):
        lines = pl.ds(pl.multiple_of(i * step, step), step)
        value = (matmul(x_ref[lines, :], weight[...]) + bias[0]).astype(BF)
        scale = jnp.where(lax.broadcasted_iota(jnp.int32, (1, 3 * third), 1) < third, 0.125, 1.0).astype(BF)
        out[lines, :] = value * scale
        return carry

    lax.fori_loop(0, x_ref.shape[0] // step, body, 0)


def project(x_window, weight, bias):
    rows, dim = x_window.shape
    width = 3 * dim // 2
    return pl.pallas_call(
        functools.partial(project_kernel, dim),
        grid=(2,),
        out_shape=jax.ShapeDtypeStruct((rows, 2 * width), BF),
        in_specs=[
            pl.BlockSpec((rows, dim), lambda i: (0, 0)),
            pl.BlockSpec((dim, width), lambda i: (0, i)),
            pl.BlockSpec((1, 1, width), lambda i: (i, 0, 0)),
        ],
        out_specs=pl.BlockSpec((rows, width), lambda i: (0, i)),
        compiler_params=pltpu.CompilerParams(vmem_limit_bytes=VMEM_LIMIT),
        cost_estimate=pl.CostEstimate(flops=6000000000, bytes_accessed=14000000, transcendentals=0),
    )(x_window, weight, bias)


def rows_to_slots(values, dealt, place_z, place_y):
    own, dim = values.shape
    half = dim // 2
    keep = lax.dynamic_slice_in_dim(values, place_y * half, half, axis=1)
    send = lax.dynamic_slice_in_dim(values, (1 - place_y) * half, half, axis=1)
    other = lax.ppermute(send, "tp", [(0, 1), (1, 0)])
    first = jnp.where(place_y == 0, keep, other)
    second = jnp.where(place_y == 0, other, keep)
    block = jnp.concatenate([first, second], axis=0)
    everything = lax.all_gather(block, "ctx", axis=0, tiled=True)
    slots = 2 * own
    mine = lax.dynamic_slice_in_dim(dealt, place_z * slots, slots)
    picked = jnp.take(everything, mine, axis=0, mode="clip")
    other_columns = lax.ppermute(picked, "tp", [(0, 1), (1, 0)])
    return jnp.concatenate(
        [jnp.where(place_y == 0, picked, other_columns), jnp.where(place_y == 0, other_columns, picked)], axis=1
    )


def slots_to_rows(values, dealt, place_z, place_y):
    slots, dim = values.shape
    half, own = dim // 2, slots // 2
    block = lax.dynamic_slice_in_dim(values, place_y * half, half, axis=1)
    everything = lax.all_gather(block, "ctx", axis=0, tiled=True)
    wanted = place_z * slots + lax.broadcasted_iota(jnp.int32, (slots, 1), 0)
    chosen = (wanted == dealt[None, :]).astype(BF)
    picked = matmul(chosen, everything).astype(BF)
    keep = lax.dynamic_slice_in_dim(picked, place_y * own, own, axis=0)
    send = lax.dynamic_slice_in_dim(picked, (1 - place_y) * own, own, axis=0)
    other = lax.ppermute(send, "tp", [(0, 1), (1, 0)])
    return jnp.concatenate([jnp.where(place_y == 0, keep, other), jnp.where(place_y == 0, other, keep)], axis=1)


def per_device(
    tokens,
    cotangent,
    seq_lengths,
    dealing,
    query_weight,
    query_bias,
    key_weight,
    value_weight,
    value_bias,
    output_weight,
    output_bias,
    first_gain,
    first_shift,
    up_weight,
    up_bias,
    down_weight,
    down_bias,
    second_gain,
    second_shift,
):
    rows, dim = tokens.shape
    ctx_size, tp_size = lax.axis_size("ctx"), lax.axis_size("tp")
    group_rows = rows * ctx_size
    own = rows // tp_size
    place_z, place_y = lax.axis_index("ctx"), lax.axis_index("tp")
    window = HALO + own + HALO
    padded = -(-window // BLOCK) * BLOCK
    dealt = dealing[0]

    lengths = seq_lengths[0]
    number = lengths.shape[0]
    upto = jnp.arange(number)[:, None] >= jnp.arange(number)[None, :]
    ends = jnp.sum(jnp.where(upto, lengths[None, :], 0), axis=1)
    starts = ends - lengths
    special = lax.axis_size("shard") == 4 and tp_size == 2 and ctx_size == 4
    place_h = half_of(place_y, place_z) if special else place_y
    first_row = place_z * rows + place_h * own
    index = jnp.arange(padded, dtype=jnp.int32)
    position = first_row - HALO + index
    valid = (position >= 0) & (position < group_rows) & (index < window)
    segment = jnp.sum((position[:, None] >= ends[None, :-1]).astype(jnp.int32), axis=1)
    segment = jnp.where(valid, segment, -1)
    seg_row, seg_col = segment[None, :], segment[:, None]
    tile = attention_tile(own)
    tile_first = first_row + tile * jnp.arange(own // tile, dtype=jnp.int32)
    tile_last = tile_first + tile - 1
    begin = jnp.max(jnp.where(starts[None, :] <= tile_first[:, None], starts[None, :], 0), axis=1)
    finish = jnp.min(jnp.where(ends[None, :] > tile_last[:, None], ends[None, :], group_rows), axis=1)
    shift = HALO - first_row
    bounds = jnp.stack([(begin + shift) // BLOCK, (finish + shift + BLOCK - 1) // BLOCK], axis=1).astype(jnp.int32)

    half_dim = dim // tp_size
    pieces = [
        jnp.concatenate([query_weight, key_weight, value_weight], axis=1),
        output_weight.T,
        up_weight,
        down_weight.T,
    ]
    flat = jnp.concatenate([query_bias, value_bias, up_bias])
    small = jnp.broadcast_to(flat[None, :], (16, flat.shape[0]))
    inputs = lax.dynamic_slice_in_dim(tokens, place_h * own, own, axis=0)
    if special:
        whole, biases, qkv, cot_rows, attended, logsum = first_stage(
            pieces, small, tokens, cotangent, dealt, seg_col, seg_row, padded
        )
        whole_up_bias = biases[::16, dim:].reshape(-1).astype(F32)
    else:
        whole = [
            lax.all_gather(lax.all_gather(piece, "shard", axis=0, tiled=True), "tp", axis=1, tiled=True)
            for piece in pieces
        ]
        biases = lax.all_gather(small, "tp", axis=0, tiled=True)[::16].astype(F32)
        qkv_bias = jnp.concatenate(
            [biases[:, :half_dim], jnp.zeros((tp_size, half_dim), F32), biases[:, half_dim:dim]], axis=1
        )[:, None, :]
        whole_up_bias = biases[:, dim:].reshape(-1)
        edge = jnp.where(place_y == 0, tokens[rows - HALO :], tokens[:HALO])
        hops = [(2 * z, 2 * z + 2) for z in range(ctx_size - 1)] + [(2 * z + 1, 2 * z - 1) for z in range(1, ctx_size)]
        arrived = lax.ppermute(edge, ("ctx", "tp"), hops)
        x_window = jnp.where(
            place_y == 0,
            jnp.concatenate([arrived, tokens[: own + HALO]], axis=0),
            jnp.concatenate([tokens[own - HALO :], arrived], axis=0),
        )
        x_window = jnp.pad(x_window, ((0, padded - window), (0, 0)))
        qkv = project(x_window, whole[0], qkv_bias)
        cot_rows = slots_to_rows(cotangent, dealt, place_z, place_y)
        attended, logsum = attention_forward(qkv, seg_col, seg_row, bounds, own, dim)
    wide_qkv, wide_output, wide_up, wide_down = whole
    output_bias = output_bias.astype(F32)
    first_gain = first_gain.astype(F32)
    first_shift = first_shift.astype(F32)
    down_bias = down_bias.astype(F32)
    second_gain = second_gain.astype(F32)
    second_shift = second_shift.astype(F32)

    grad_out = cot_rows.astype(F32)
    hidden_one, normed_one, inverse_one = norm_forward(
        inputs.astype(F32) + matmul_second(attended, wide_output) + output_bias, first_gain, first_shift
    )
    hidden_low = hidden_one.astype(BF)
    pre_act = matmul(hidden_low, wide_up) + whole_up_bias
    erf_part = 0.5 * (1.0 + jax.scipy.special.erf(pre_act * HALF_ROOT))
    act_low = (pre_act * erf_part).astype(BF)
    layer_value, normed_two, inverse_two = norm_forward(
        hidden_one + matmul_second(act_low, wide_down) + down_bias, second_gain, second_shift
    )
    layer_low = layer_value.astype(BF)

    second_shift_grad = jnp.sum(grad_out, axis=0)
    second_gain_grad = jnp.sum(grad_out * normed_two, axis=0)
    grad_second = norm_backward(grad_out, normed_two, inverse_two, second_gain)
    down_bias_grad = jnp.sum(grad_second, axis=0)
    second_low = grad_second.astype(BF)
    slope = erf_part + pre_act * DENSITY * jnp.exp(-0.5 * pre_act * pre_act)
    grad_pre = matmul(second_low, wide_down) * slope
    up_bias_grad = jnp.sum(grad_pre, axis=0)
    pre_low = grad_pre.astype(BF)
    grad_hidden = grad_second + matmul_second(pre_low, wide_up)
    first_shift_grad = jnp.sum(grad_hidden, axis=0)
    first_gain_grad = jnp.sum(grad_hidden * normed_one, axis=0)
    grad_first = norm_backward(grad_hidden, normed_one, inverse_one, first_gain)
    output_bias_grad = jnp.sum(grad_first, axis=0)
    first_low = grad_first.astype(BF)
    attended_grad = matmul(first_low, wide_output).astype(BF)
    head_of = (jnp.arange(dim)[None, :] // HEAD == jnp.arange(16)[:, None]).astype(F32)
    delta = lax.dot_general(
        head_of,
        attended_grad.astype(F32) * attended.astype(F32),
        (((1,), (1,)), ((), ())),
        precision=lax.Precision.HIGHEST,
        preferred_element_type=F32,
    )
    stats = jnp.concatenate([logsum, delta], axis=0)
    if special:
        output_own, up_own, down_own, qkv_low, query_bias_grad, value_bias_grad, layer_out = backward_stage(
            first_low,
            attended,
            hidden_low,
            pre_low,
            second_low,
            act_low,
            attended_grad,
            stats,
            qkv,
            seg_col,
            seg_row,
            layer_low,
            dealt,
        )
    else:
        layer_out = rows_to_slots(layer_low, dealt, place_z, place_y)
        up_hops = [(i, i + 1) for i in range(ctx_size * tp_size - 1)]
        down_hops = [(i + 1, i) for i in range(ctx_size * tp_size - 1)]
        grad_win, stats_win = [
            jnp.concatenate(
                [
                    lax.ppermute(lax.slice_in_dim(array, own - HALO, own, axis=axis), ("ctx", "tp"), up_hops),
                    array,
                    lax.ppermute(lax.slice_in_dim(array, 0, HALO, axis=axis), ("ctx", "tp"), down_hops),
                    jnp.zeros((padded - window, dim) if axis == 0 else (32, padded - window), array.dtype),
                ],
                axis=axis,
            )
            for array, axis in ((attended_grad, 0), (stats, 1))
        ]
        query_low, query_bias_grad = attention_query(qkv, seg_col, seg_row, bounds, attended_grad, stats, dim)
        qkv_low, value_bias_grad = attention_key(
            qkv, seg_col, seg_row, bounds, grad_win, stats_win, query_low, own, dim
        )
    vectors = jnp.concatenate(
        [
            query_bias_grad[0],
            value_bias_grad[0],
            up_bias_grad,
            output_bias_grad,
            first_gain_grad,
            first_shift_grad,
            down_bias_grad,
            second_gain_grad,
            second_shift_grad,
        ]
    )
    if special:
        *qkv_own, tokens_grad, small_sum = last_stage(
            inputs, qkv_low, wide_qkv, grad_first, dealt, vectors.reshape(-1, 128)
        )
        small_sum = small_sum.reshape(-1)
        owned = [*qkv_own, output_own, up_own, down_own]
    else:
        owned = []
        for full in (
            matmul_first(inputs, qkv_low),
            matmul_first(first_low, attended),
            matmul_first(hidden_low, pre_low),
            matmul_first(second_low, act_low),
        ):
            part = lax.psum_scatter(full.astype(BF), "tp", scatter_dimension=1, tiled=True)
            part = lax.psum_scatter(part, "shard", scatter_dimension=0, tiled=True)
            owned.append(lax.psum(part, "ctx").astype(F32))
        owned = [owned[0][:, i * half_dim : (i + 1) * half_dim] for i in range(3)] + owned[1:]
        small_sum = lax.psum(vectors, ("shard", "ctx", "tp"))
        tokens_grad = (grad_first + matmul_second(qkv_low, wide_qkv)).astype(BF)
        tokens_grad = rows_to_slots(tokens_grad, dealt, place_z, place_y)
    hidden = up_bias_grad.shape[0]
    sizes = [dim, dim, hidden] + [dim] * 6
    offsets = [sum(sizes[:i]) for i in range(len(sizes))]
    parts = [small_sum[o : o + s] for o, s in zip(offsets, sizes)]

    def by_tp(vector):
        part = vector.shape[0] // tp_size
        mine = vector[:part]
        for of_y in range(1, tp_size):
            mine = jnp.where(place_y == of_y, vector[of_y * part : (of_y + 1) * part], mine)
        return mine

    return (
        layer_out,
        tokens_grad,
        owned[0],
        by_tp(parts[0]),
        owned[1],
        owned[2],
        by_tp(parts[1]),
        owned[3].T,
        parts[3],
        parts[4],
        parts[5],
        owned[4],
        by_tp(parts[2]),
        owned[5].T,
        parts[6],
        parts[7],
        parts[8],
    )


def solution(mesh):
    return jax.shard_map(
        per_device,
        mesh=mesh,
        in_specs=(
            P(("shard", "ctx"), None),
            P(("shard", "ctx"), None),
            P("shard", None),
            P("shard", None),
            P("shard", "tp"),
            P("tp"),
            P("shard", "tp"),
            P("shard", "tp"),
            P("tp"),
            P("tp", "shard"),
            P(),
            P(),
            P(),
            P("shard", "tp"),
            P("tp"),
            P("tp", "shard"),
            P(),
            P(),
            P(),
        ),
        out_specs=(
            P(("shard", "ctx"), None),
            P(("shard", "ctx"), None),
            P("shard", "tp"),
            P("tp"),
            P("shard", "tp"),
            P("shard", "tp"),
            P("tp"),
            P("tp", "shard"),
            P(),
            P(),
            P(),
            P("shard", "tp"),
            P("tp"),
            P("tp", "shard"),
            P(),
            P(),
            P(),
        ),
        check_vma=False,
    )
```

```python
import functools

import jax
import jax.numpy as jnp
from jax import lax
from jax.experimental import pallas as pl
from jax.experimental.pallas import tpu as pltpu
from jax.sharding import PartitionSpec as P

HEAD = 64
HALO = 512
HALF_ROOT = 0.7071067811865476
DENSITY = 0.3989422804014327
NEG_FILL = -1000000000.0
BF = jnp.bfloat16
F32 = jnp.float32
BLOCK = 256
VMEM_LIMIT = 60 * 1024 * 1024


def matmul(former, latter):
    return jnp.dot(former, latter, preferred_element_type=F32)


def matmul_first(former, latter):
    return lax.dot_general(former, latter, (((0,), (0,)), ((), ())), preferred_element_type=F32)


def matmul_second(former, latter):
    return lax.dot_general(former, latter, (((1,), (1,)), ((), ())), preferred_element_type=F32)


def norm_forward(values, norm_gain, norm_shift):
    centre = values - jnp.mean(values, axis=1, keepdims=True)
    spread = jnp.mean(centre * centre, axis=1, keepdims=True)
    inverse = lax.rsqrt(spread + 1e-06)
    normed = centre * inverse
    return (norm_gain * normed + norm_shift, normed, inverse)


def norm_backward(gradient, normed, inverse, norm_gain):
    scaled = gradient * norm_gain
    bracket = (
        scaled
        - jnp.mean(scaled, axis=1, keepdims=True)
        - normed * jnp.mean(scaled * normed, axis=1, keepdims=True)
    )
    return inverse * bracket


def places(pair, dim):
    half, inner = divmod(pair, dim // 256)
    base = half * (3 * dim // 2) + inner * 128
    return base, base + dim // 2, base + dim


def take(qkv, rows, pair, dim, which):
    first = places(pair, dim)[which]
    return qkv[rows, first : first + 128]


def low_lanes(rows):
    return lax.broadcasted_iota(jnp.int32, (rows, 128), 1) < HEAD


def stacked(pair):
    low = low_lanes(pair.shape[0])
    zero = jnp.zeros_like(pair)
    return jnp.concatenate([jnp.where(low, pair, zero), jnp.where(low, zero, pair)], axis=0)


def unstacked(both):
    rows = both.shape[0] // 2
    return jnp.where(low_lanes(rows), both[:rows], both[rows:])


def bias_of(own_seg, other_seg):
    return jnp.where(own_seg == other_seg, 0.0, NEG_FILL)


def turn_columns(qkv, pair, dim, which, turned):
    turned[pair * 128 : pair * 128 + 128, :] = take(qkv, slice(0, qkv.shape[0]), pair, dim, which).T


def twice(row_pair):
    return jnp.concatenate([row_pair[0:1], row_pair[1:2]], axis=1)


def forward_steps(dim, tile, qkv, seg_col, seg_tile, out, logsum, value_t, query_st, bias_ref, acc, top, total):
    pairs = dim // 128

    def prepare():
        for p in range(pairs):
            turn_columns(qkv, p, dim, 2, value_t)

    def begin(i):
        rows = pl.ds(pl.multiple_of(HALO + i * tile, 64), tile)
        for p in range(pairs):
            query_st[p] = stacked(take(qkv, rows, p, dim, 0))
        acc[...] = jnp.zeros_like(acc)
        total[...] = jnp.zeros_like(total)
        top[...] = jnp.full_like(top, 2 * NEG_FILL)

    def block(i, j):
        start = pl.multiple_of(j * BLOCK, BLOCK)
        bias_ref[...] = bias_of(seg_col[pl.ds(start, BLOCK), :], seg_tile[i])
        for p in range(pairs):
            key = take(qkv, pl.ds(start, BLOCK), p, dim, 1)
            scores = matmul_second(key, query_st[p]) + bias_ref[...]
            old = top[p]
            new = jnp.maximum(old, jnp.max(scores, axis=0, keepdims=True))
            keep = jnp.exp(old - new)
            raised = jnp.exp(scores - new)
            total[p] = keep * total[p] + jnp.sum(raised, axis=0, keepdims=True)
            value = value_t[p * 128 : p * 128 + 128, pl.ds(start, BLOCK)]
            acc[p] = keep * acc[p] + matmul(value, raised.astype(BF))
            top[p] = new

    def finish(i):
        lines = pl.ds(pl.multiple_of(i * tile, tile), tile)
        for p in range(pairs):
            whole = total[p]
            out[lines, p * 128 : p * 128 + 128] = unstacked((acc[p] / whole).T).astype(BF)
            lse = top[p] + jnp.log(whole)
            logsum[i, 2 * p : 2 * p + 1, :] = lse[:, :tile]
            logsum[i, 2 * p + 1 : 2 * p + 2, :] = lse[:, tile:]
        for p in range(2 * pairs, 16):
            logsum[i, p : p + 1, :] = jnp.zeros((1, tile), F32)

    return prepare, begin, block, finish


def query_steps(dim, tile, qkv, seg_col, seg_tile, grad, stats, store, sums, key_t, query_st, grad_st, bias_ref, acc):
    pairs = dim // 128

    def prepare():
        sums[...] = jnp.zeros_like(sums)
        for p in range(pairs):
            turn_columns(qkv, p, dim, 1, key_t)

    def begin(i):
        own_rows = pl.ds(pl.multiple_of(i * tile, tile), tile)
        rows = pl.ds(pl.multiple_of(HALO + i * tile, 64), tile)
        for p in range(pairs):
            query_st[p] = stacked(take(qkv, rows, p, dim, 0))
            grad_st[p] = stacked(grad[own_rows, p * 128 : p * 128 + 128])
        acc[...] = jnp.zeros_like(acc)

    def block(i, j):
        there = pl.ds(pl.multiple_of(j * BLOCK, BLOCK), BLOCK)
        bias_ref[...] = bias_of(seg_col[there, :], seg_tile[i])
        for p in range(pairs):
            scores = matmul_second(take(qkv, there, p, dim, 1), query_st[p]) + bias_ref[...]
            probs = jnp.exp(scores - twice(stats[i, 2 * p : 2 * p + 2, :]))
            grad_probs = matmul_second(take(qkv, there, p, dim, 2), grad_st[p])
            grad_scores = (probs * (grad_probs - twice(stats[i, 16 + 2 * p : 18 + 2 * p, :]))).astype(BF)
            acc[p] += matmul(key_t[p * 128 : p * 128 + 128, there], grad_scores)

    def finish(i):
        own_rows = pl.ds(pl.multiple_of(i * tile, tile), tile)
        for p in range(pairs):
            part = 0.125 * unstacked(acc[p].T)
            store(own_rows, p, part.astype(BF))
            sums[:, p * 128 : p * 128 + 128] += jnp.sum(part, axis=0, keepdims=True)

    return prepare, begin, block, finish


def key_steps(dim, tile, qkv, seg_col, seg_row, grad, stats, out, sums, key_st, value_st, bias_ref, key_acc, value_acc):
    pairs = dim // 128

    def prepare():
        sums[...] = jnp.zeros_like(sums)

    def begin(i):
        rows = pl.ds(pl.multiple_of(HALO + i * tile, 64), tile)
        for p in range(pairs):
            key_st[p] = stacked(take(qkv, rows, p, dim, 1))
            value_st[p] = stacked(take(qkv, rows, p, dim, 2))
        key_acc[...] = jnp.zeros_like(key_acc)
        value_acc[...] = jnp.zeros_like(value_acc)

    def block(i, j):
        there = pl.ds(pl.multiple_of(j * BLOCK, BLOCK), BLOCK)
        seg_here = seg_col[pl.ds(pl.multiple_of(HALO + i * tile, 64), tile), :]
        bias_ref[...] = bias_of(seg_here, seg_row[:, there])
        for p in range(pairs):
            query = take(qkv, there, p, dim, 0)
            grad_pair = grad[there, p * 128 : p * 128 + 128]
            scores = matmul_second(key_st[p], query)
            grad_probs = matmul_second(value_st[p], grad_pair)
            probs_all, grads_all = [], []
            for half in range(2):
                head = 2 * p + half
                lines = slice(half * tile, half * tile + tile)
                probs = jnp.exp(scores[lines] + bias_ref[...] - stats[head : head + 1, there])
                grads_all.append((probs * (grad_probs[lines] - stats[16 + head : 17 + head, there])).astype(BF))
                probs_all.append(probs.astype(BF))
            key_acc[p] += matmul(jnp.concatenate(grads_all, axis=0), query)
            value_acc[p] += matmul(jnp.concatenate(probs_all, axis=0), grad_pair)

    def finish(i):
        own_rows = pl.ds(pl.multiple_of(i * tile, tile), tile)
        for p in range(pairs):
            _, at_key, at_value = places(p, dim)
            out[own_rows, at_key : at_key + 128] = unstacked(key_acc[p]).astype(BF)
            part = unstacked(value_acc[p])
            out[own_rows, at_value : at_value + 128] = part.astype(BF)
            sums[:, p * 128 : p * 128 + 128] += jnp.sum(part, axis=0, keepdims=True)

    return prepare, begin, block, finish


def run_dynamic(steps, bounds, tiles):
    prepare, begin, block, finish = steps
    prepare()

    def one_tile(i, carry):
        begin(i)

        def one_block(j, inner):
            block(i, j)
            return inner

        lax.fori_loop(bounds[i, 0], bounds[i, 1], one_block, 0)
        finish(i)
        return carry

    lax.fori_loop(0, tiles, one_tile, 0)


PIECE = 2


def run_static(steps, tile, tiles):
    prepare, begin, block, finish = steps
    prepare()
    yield
    for i in range(tiles):
        first = (HALO + i * tile - HALO + 1) // BLOCK
        after = -(-(HALO + i * tile + tile + HALO - 1) // BLOCK)
        begin(i)
        for piece in range(first, after, PIECE):

            def one_block(j, inner):
                block(i, j)
                return inner

            lax.fori_loop(piece, min(piece + PIECE, after), one_block, 0)
            if piece + PIECE >= after:
                finish(i)
            yield


def forward_kernel(dim, tile, bounds, *refs):
    run_dynamic(forward_steps(dim, tile, *refs), bounds, refs[3].shape[0] // tile)


def query_kernel(dim, tile, bounds, qkv, seg_col, seg_tile, grad, stats, out, sums, *scratch):
    def store(rows, p, part):
        out[rows, p * 128 : p * 128 + 128] = part

    run_dynamic(
        query_steps(dim, tile, qkv, seg_col, seg_tile, grad, stats, store, sums, *scratch), bounds, out.shape[0] // tile
    )


def key_kernel(dim, tile, bounds, qkv, seg_col, seg_row, grad, stats, query_low, out, sums, *scratch):
    for p in range(dim // 128):
        at_query = places(p, dim)[0]
        out[:, at_query : at_query + 128] = query_low[:, p * 128 : p * 128 + 128]
    run_dynamic(
        key_steps(dim, tile, qkv, seg_col, seg_row, grad, stats, out, sums, *scratch), bounds, out.shape[0] // tile
    )


def vmem_call(kernel, arrays, bounds, outs, scratch, flops):
    spec = pl.BlockSpec(memory_space=pltpu.VMEM)
    return pl.pallas_call(
        kernel,
        out_shape=outs,
        in_specs=[pl.BlockSpec(memory_space=pltpu.SMEM)] + [spec] * len(arrays),
        out_specs=jax.tree.map(lambda leaf: spec, outs),
        scratch_shapes=scratch,
        compiler_params=pltpu.CompilerParams(vmem_limit_bytes=VMEM_LIMIT),
        cost_estimate=pl.CostEstimate(flops=flops, bytes_accessed=12000000, transcendentals=6000000),
    )(bounds, *arrays)


def attention_tile(own):
    for tile in (192, 128, 64, 32, 16):
        if own % tile == 0:
            return tile
    raise ValueError("rows")


def by_tile(rows_last, own):
    tile = attention_tile(own)
    return rows_last.reshape(rows_last.shape[0], own // tile, tile).transpose(1, 0, 2)


def segments_by_tile(seg_row, own):
    tiles = by_tile(lax.slice_in_dim(seg_row, HALO, HALO + own, axis=1), own)
    return jnp.concatenate([tiles, tiles], axis=2)


def forward_scratch(padded, tile, dim):
    pairs = dim // 128
    return [
        pltpu.VMEM((dim, padded), BF),
        pltpu.VMEM((pairs, 2 * tile, 128), BF),
        pltpu.VMEM((BLOCK, 2 * tile), F32),
        pltpu.VMEM((pairs, 128, 2 * tile), F32),
        pltpu.VMEM((pairs, 1, 2 * tile), F32),
        pltpu.VMEM((pairs, 1, 2 * tile), F32),
    ]


def attention_forward(qkv, seg_col, seg_row, bounds, own, dim):
    tile = attention_tile(own)
    pairs = dim // 128
    out, logsum = vmem_call(
        functools.partial(forward_kernel, dim, tile),
        (qkv, seg_col, segments_by_tile(seg_row, own)),
        bounds,
        (jax.ShapeDtypeStruct((own, dim), BF), jax.ShapeDtypeStruct((own // tile, 16, tile), F32)),
        forward_scratch(qkv.shape[0], tile, dim),
        10_000_000_000,
    )
    return out, logsum.transpose(1, 0, 2).reshape(16, own)


def attention_query(qkv, seg_col, seg_row, bounds, grad, stats, dim):
    own = grad.shape[0]
    tile = attention_tile(own)
    pairs = dim // 128
    return vmem_call(
        functools.partial(query_kernel, dim, tile),
        (qkv, seg_col, segments_by_tile(seg_row, own), grad, by_tile(stats, own)),
        bounds,
        (jax.ShapeDtypeStruct((own, dim), BF), jax.ShapeDtypeStruct((1, dim), F32)),
        [
            pltpu.VMEM((dim, qkv.shape[0]), BF),
            pltpu.VMEM((pairs, 2 * tile, 128), BF),
            pltpu.VMEM((pairs, 2 * tile, 128), BF),
            pltpu.VMEM((BLOCK, 2 * tile), F32),
            pltpu.VMEM((pairs, 128, 2 * tile), F32),
        ],
        15_000_000_000,
    )


def attention_key(qkv, seg_col, seg_row, bounds, grad_win, stats_win, query_low, own, dim):
    tile = attention_tile(own)
    pairs = dim // 128
    return vmem_call(
        functools.partial(key_kernel, dim, tile),
        (qkv, seg_col, seg_row, grad_win, stats_win, query_low),
        bounds,
        (jax.ShapeDtypeStruct((own, 3 * dim), BF), jax.ShapeDtypeStruct((1, dim), F32)),
        [
            pltpu.VMEM((pairs, 2 * tile, 128), BF),
            pltpu.VMEM((pairs, 2 * tile, 128), BF),
            pltpu.VMEM((tile, BLOCK), F32),
            pltpu.VMEM((pairs, 2 * tile, 128), F32),
            pltpu.VMEM((pairs, 2 * tile, 128), F32),
        ],
        20_000_000_000,
    )


def remote(src, dst, send_sem, recv_sem, where):
    return pltpu.make_async_remote_copy(
        src_ref=src,
        dst_ref=dst,
        send_sem=send_sem,
        recv_sem=recv_sem,
        device_id=where,
        device_id_type=pl.DeviceIdType.MESH,
    )


def here():
    shard, z, y = lax.axis_index("shard"), lax.axis_index("ctx"), lax.axis_index("tp")
    return shard // 2, shard % 2, y, z


def half_of(y, z):
    return (y + z) % 2


def interleave(tasks):
    running, turn = [], 0
    while tasks or running:
        running += [task for first, task in tasks if first <= turn]
        tasks = [item for item in tasks if item[0] > turn]
        alive = []
        for task in running:
            try:
                next(task)
                alive.append(task)
            except StopIteration:
                pass
        running, turn = alive, turn + 1


def timed(task, gaps):
    for stage, _ in enumerate(task):
        yield
        for _ in range(gaps[min(stage, len(gaps) - 1)]):
            yield


def greet_all(always, sometimes):
    barrier = pltpu.get_barrier_semaphore()
    number = jnp.int32(len(always))
    for peer in always:
        pl.semaphore_signal(barrier, inc=1, device_id=peer, device_id_type=pl.DeviceIdType.MESH)
    for condition, peer in sometimes:

        @pl.when(condition)
        def _():
            pl.semaphore_signal(barrier, inc=1, device_id=peer, device_id_type=pl.DeviceIdType.MESH)

        number = number + condition.astype(jnp.int32)
    pl.semaphore_wait(barrier, number)


class Line:
    SCRATCH = 4

    def __init__(self, z, dealt, to_slots, refs, sems):
        self.z, self.dealt, self.to_slots = z, dealt, to_slots
        self.blocks, self.picked, self.away, self.arrived = refs
        self.send, self.block_recv, self.away_recv = sems
        self.inner = (z == 1) | (z == 2)
        self.outer = (z == 0) | (z == 3)
        self.near = 1 + z // 3
        self.end = jnp.maximum(3 * (z - 1), 0) % 6
        self.middle = 3 - z
        self.far = 3 - self.end
        self.slots = refs[0].shape[1]

    def copy(self, what):
        if what == "own_near":
            block, where, sem = self.z, self.near, 0
        elif what == "own_middle":
            block, where, sem = self.z, self.middle, 0
        elif what == "forward":
            block, where, sem = self.end, self.middle, 1
        else:
            where = self.end
            return remote(self.away, self.arrived, self.send.at[2], self.away_recv, {"ctx": where})
        there = self.blocks.at[block]
        return remote(there, there, self.send.at[sem], self.block_recv.at[block], {"ctx": where})

    def wait_block(self, block):
        there = self.blocks.at[block]
        remote(there, there, self.send.at[0], self.block_recv.at[block], {"ctx": self.middle}).wait_recv()

    def select(self, target, wanted_by, block, start):
        slots = self.slots
        wide = 384 if slots % 384 == 0 else 128

        def body(i, carry):
            lines = pl.ds(pl.multiple_of(i * wide, 128), wide)
            if self.to_slots:
                row = self.dealt[:, pl.ds(pl.multiple_of(wanted_by * slots + i * wide, 128), wide)]
                wanted = jnp.broadcast_to(row, (8, wide)).T[:, :1]
                offered = (block * slots + lax.broadcasted_iota(jnp.int32, (wide, slots), 1)).astype(F32)
            else:
                wanted = wanted_by * slots + i * wide + lax.broadcasted_iota(jnp.int32, (wide, slots), 0)
                offered = self.dealt[:, pl.ds(pl.multiple_of(block * slots, 128), slots)]
            chosen = jnp.where(wanted == offered, 1.0, 0.0).astype(BF)
            part = matmul(chosen, self.blocks[block]).astype(BF)
            target[lines, :] = part if start else target[lines, :] + part
            return carry

        lax.fori_loop(0, slots // wide, body, 0)

    def run(self):
        @pl.when(self.outer)
        def _():
            self.copy("own_near").start()

        @pl.when(self.inner)
        def _():
            self.copy("own_middle").start()

        self.select(self.picked, self.z, self.z, True)
        yield

        @pl.when(self.inner)
        def _():
            self.wait_block(self.end)
            self.copy("forward").start()
            self.select(self.picked, self.z, self.end, False)
            self.select(self.away, self.end, self.z, True)

        yield

        @pl.when(self.inner)
        def _():
            self.wait_block(self.middle)
            self.select(self.away, self.end, self.middle, False)
            self.select(self.picked, self.z, self.middle, False)

        yield

        @pl.when(self.inner)
        def _():
            self.wait_block(self.far)
            self.select(self.away, self.end, self.far, False)
            self.copy("away").start()
            self.select(self.picked, self.z, self.far, False)

        yield

        @pl.when(self.outer)
        def _():
            self.copy("away").wait_recv()
            self.picked[...] = self.picked[...] + self.arrived[...]

    def settle(self):
        @pl.when(self.outer)
        def _():
            self.copy("own_near").wait_send()

        @pl.when(self.inner)
        def _():
            self.copy("own_middle").wait_send()
            self.copy("forward").wait_send()
            self.copy("away").wait_send()


def line_scratch(ctx_size, slots, chunks, columns):
    blocks = [pltpu.VMEM((ctx_size, slots, columns), BF) for _ in range(chunks)]
    others = [pltpu.VMEM((slots, columns), BF) for _ in range(3 * chunks)]
    sems = [pltpu.SemaphoreType.DMA((chunks, 3)), pltpu.SemaphoreType.DMA((chunks, ctx_size)), pltpu.SemaphoreType.DMA((chunks,))]
    return blocks + others + sems


def line_of(j, chunks, z, dealt, to_slots, refs):
    blocks, others, sems = refs[:chunks], refs[chunks : 4 * chunks], refs[4 * chunks :]
    return Line(
        z,
        dealt,
        to_slots,
        (blocks[j], others[3 * j], others[3 * j + 1], others[3 * j + 2]),
        (sems[0].at[j], sems[1].at[j], sems[2].at[j]),
    )


PERM = 3


MIDDLE_AT = (4, 8, 12)
COTANGENT_AT = (1, 2, 3)
COTANGENT_PAUSE = 1


def first_kernel(widths, padded, *refs):
    count = len(widths)
    thirds, pieces = refs[:3], (None, *refs[3 : count + 2])
    small, tokens, cotangent, dealt_row, seg_col, seg_tile = refs[count + 2 : count + 8]
    refs = refs[count + 8 :]
    wholes, (small_whole, qkv_out, cot_rows, attended, logsum) = refs[:count], refs[count : count + 5]
    rest = refs[count + 5 :]
    attention_refs, qkv, qkv_sem, rest = rest[:6], rest[6], rest[7], rest[8:]
    weight, window, send, recv, own_sem, small_sem, halo_sem, post_send, post_recv, bring = rest[:10]
    line_refs = rest[10:]
    x, c, y, z = here()
    h = half_of(y, z)
    rows, dim = tokens.shape
    own = rows // 2
    half = dim // 2
    last = 3
    tile = attention_tile(own)
    at_x, at_y, at_c = {"shard": 2 * (1 - x) + c}, {"tp": 1 - y}, {"shard": 2 * x + 1 - c}
    left, right = {"ctx": jnp.maximum(z - 1, 0)}, {"ctx": jnp.minimum(z + 1, last)}
    greet_all((at_x, at_y, at_c), ((z > 0, left), (z < last, right)))

    def slot(a, of_y, of_x, of_c, lines=None):
        cols = pl.ds(pl.multiple_of(of_y * widths[a], 128), widths[a])
        depth = wholes[a].shape[2]
        lines = slice(0, depth) if lines is None else slice(lines * depth // 2, (lines + 1) * depth // 2)
        return (weight if a == 0 else wholes[a]).at[of_x, of_c, lines, cols]

    def third_of(i):
        columns = widths[0] // 3
        return weight.at[x, c, :, pl.ds(pl.multiple_of(y * widths[0] + i * columns, 128), columns)]

    def moves(a):
        source = slot(0, y, x, c) if a == 0 else pieces[a]
        table = [
            (source, slot(a, y, x, c), at_x),
            (source, slot(a, y, x, c), at_y),
            (source, slot(a, y, x, c), at_c),
            (slot(a, y, 1 - x, c, 0), slot(a, y, 1 - x, c, 0), at_y),
            (slot(a, 1 - y, x, c, 1), slot(a, 1 - y, x, c, 1), at_x),
            (slot(a, y, 1 - x, c), slot(a, y, 1 - x, c), at_c),
            (slot(a, 1 - y, x, c), slot(a, 1 - y, x, c), at_c),
            (slot(a, 1 - y, 1 - x, c, 0), slot(a, 1 - y, 1 - x, c, 0), at_c),
            (slot(a, 1 - y, 1 - x, c, 1), slot(a, 1 - y, 1 - x, c, 1), at_c),
        ]
        return [remote(s, d, send.at[a, kind], recv.at[a, kind], w) for kind, (s, d, w) in enumerate(table)]

    tables = [moves(a) for a in range(count)]
    depth = small_whole.shape[0] // 2
    small_at = small_whole.at[pl.ds(pl.multiple_of(y * depth, 16), depth)]
    small_copy = remote(small, small_at, small_sem.at[0], small_sem.at[1], at_y)
    sends_right, sends_left = (h == 1) & (z < last), (h == 0) & (z > 0)
    gets_left, gets_right = (h == 0) & (z > 0), (h == 1) & (z < last)

    def halo(where):
        src = tokens.at[pl.ds(pl.multiple_of(h * (rows - HALO), 64), HALO)]
        dst = window.at[pl.ds(pl.multiple_of((1 - h) * (HALO + own), 64), HALO)]
        return remote(src, dst, halo_sem.at[0], halo_sem.at[1], where)

    inside = pltpu.make_async_copy(
        tokens.at[pl.ds(pl.multiple_of(h * (own - HALO), 64), own + HALO)],
        window.at[pl.ds(pl.multiple_of((1 - h) * HALO, 64), own + HALO)],
        halo_sem.at[2],
    )
    small_local = pltpu.make_async_copy(small, small_at, small_sem.at[2])
    third_local = [pltpu.make_async_copy(thirds[i], third_of(i), own_sem.at[0]) for i in range(3)]
    piece_local = [
        pltpu.make_async_copy(slot(a, y, x, c) if a == 0 else pieces[a], slot(a, y, x, c), own_sem.at[a])
        for a in range(count)
    ]
    lines = [line_of(j, PERM, z, dealt_row, False, line_refs) for j in range(PERM)]

    def columns_of(j):
        return pl.ds(pl.multiple_of(y * half + j * (half // PERM), 128), half // PERM)

    bring_cot = [
        pltpu.make_async_copy(cotangent.at[:, columns_of(j)], lines[j].blocks.at[z], bring.at[j]) for j in range(PERM)
    ]
    def spread(a):
        for kind in range(3):
            tables[a][kind].start()

    for kind, where in enumerate((at_x, at_y, at_c)):
        for i in range(3):
            remote(thirds[i], third_of(i), send.at[0, kind], recv.at[0, kind], where).start()
    small_copy.start()

    @pl.when(sends_right)
    def _():
        halo(right).start()

    @pl.when(sends_left)
    def _():
        halo(left).start()

    for item in (small_local, *third_local, *piece_local[1:], inside, *bring_cot):
        item.start()
    window[padded - (padded - 2 * HALO - own) :, :] = jnp.zeros((padded - 2 * HALO - own, dim), BF)

    @pl.when((h == 0) & (z == 0))
    def _():
        window[:HALO, :] = jnp.zeros((HALO, dim), BF)

    @pl.when((h == 1) & (z == last))
    def _():
        window[HALO + own : 2 * HALO + own, :] = jnp.zeros((HALO, dim), BF)

    def pause(number):
        for _ in range(number):
            yield

    def forward_first(a):
        tables[a][0].wait_recv()
        tables[a][3].start()
        tables[a][5].start()
        tables[a][1].wait_recv()
        tables[a][4].start()
        tables[a][6].start()

    def forward_second(a):
        tables[a][3].wait_recv()
        tables[a][7].start()
        tables[a][4].wait_recv()
        tables[a][8].start()

    def collect(a):
        for kind in (2, 5, 6, 7, 8):
            tables[a][kind].wait_recv()

    early, late = tuple(range(1, count - 1)), count - 1

    def qkv_task():
        forward_first(0)
        yield
        forward_second(0)
        for a in early:
            spread(a)
        yield
        collect(0)
        yield from project_task()
        qkv_copy.start()
        yield from run_static(
            forward_steps(dim, tile, qkv, seg_col, seg_tile, attended, logsum, *attention_refs), tile, own // tile
        )

    def others_task():
        for a in early:
            forward_first(a)
        spread(late)
        yield from pause(MIDDLE_AT[1] - MIDDLE_AT[0])
        forward_first(late)
        for a in early:
            forward_second(a)
        yield from pause(MIDDLE_AT[2] - MIDDLE_AT[1])
        forward_second(late)
        for a in (*early, late):
            collect(a)

    qkv_copy = pltpu.make_async_copy(qkv, qkv_out, qkv_sem)

    def project_task():
        piece_local[0].wait()
        pltpu.make_async_copy(weight, wholes[0], own_sem.at[0]).start()
        inside.wait()
        small_copy.wait()
        small_local.wait()

        @pl.when(gets_left | gets_right)
        def _():
            halo(left).wait_recv()

        depth_w, width = weight.shape[2], widths[0]
        third = width // 3
        step = 256
        for of_y in range(2):
            bias = small_whole[of_y * depth : of_y * depth + 1, :].astype(F32)
            bias = jnp.concatenate([bias[:, :third], jnp.zeros((1, third), F32), bias[:, third : 2 * third]], axis=1)
            scale = jnp.where(lax.broadcasted_iota(jnp.int32, (1, width), 1) < third, 0.125, 1.0).astype(BF)
            full = jnp.concatenate(
                [weight[i // 2, i % 2, :, of_y * width : (of_y + 1) * width] for i in range(4)], axis=0
            )

            def body(i, carry):
                there = pl.ds(pl.multiple_of(i * step, step), step)
                value = (matmul(window[there, :], full) + bias).astype(BF)
                qkv[there, of_y * width : (of_y + 1) * width] = value * scale
                return carry

            lax.fori_loop(0, padded // step, body, 0)
            yield

    def post(j):
        there = lines[j].picked.at[pl.ds(pl.multiple_of((1 - h) * own, 64), own)]
        return remote(there, cot_rows.at[:, columns_of(j)], post_send.at[j], post_recv.at[j], at_y)

    def cotangent_task(j):
        bring_cot[j].wait()
        for _ in lines[j].run():
            yield
            yield from pause(COTANGENT_PAUSE)
        post(j).start()
        cot_rows[:, columns_of(j)] = lines[j].picked[pl.ds(pl.multiple_of(h * own, 64), own), :]
        yield
        post(j).wait_recv()

    tasks = [(0, qkv_task()), (MIDDLE_AT[0], others_task())]
    tasks += [(COTANGENT_AT[j], cotangent_task(j)) for j in range(PERM)]
    interleave(sorted(tasks, key=lambda item: item[0]))
    for a in range(count):
        for kind in range(9):
            tables[a][kind].wait_send()
        if a:
            piece_local[a].wait()
    pltpu.make_async_copy(weight, wholes[0], own_sem.at[0]).wait()
    qkv_copy.wait()

    @pl.when(sends_right | sends_left)
    def _():
        halo(left).wait_send()

    for j in range(PERM):
        lines[j].settle()
        post(j).wait_send()


def first_stage(pieces, small, tokens, cotangent, dealt, seg_col, seg_row, padded):
    rows, dim = tokens.shape
    thirds, pieces = pieces[:3], pieces[3:]
    depth = pieces[0].shape[0]
    own = rows // 2
    tile = attention_tile(own)
    widths = (3 * thirds[0].shape[1], *(piece.shape[1] for piece in pieces))
    count = len(widths)
    ctx_size = lax.axis_size("ctx")
    outs = [jax.ShapeDtypeStruct((2, 2, depth, 2 * width), BF) for width in widths]
    outs += [
        jax.ShapeDtypeStruct((2 * small.shape[0], small.shape[1]), BF),
        jax.ShapeDtypeStruct((padded, 3 * dim), BF),
        jax.ShapeDtypeStruct((own, dim), BF),
        jax.ShapeDtypeStruct((own, dim), BF),
        jax.ShapeDtypeStruct((own // tile, 16, tile), F32),
    ]
    anywhere, vmem = pl.BlockSpec(memory_space=pl.ANY), pl.BlockSpec(memory_space=pltpu.VMEM)
    result = pl.pallas_call(
        functools.partial(first_kernel, widths, padded),
        out_shape=outs,
        in_specs=[anywhere] * (count + 5) + [vmem] * 3,
        out_specs=[anywhere] * count + [vmem, anywhere] + [vmem] * 3,
        scratch_shapes=forward_scratch(padded, tile, dim)
        + [
            pltpu.VMEM((padded, 3 * dim), BF),
            pltpu.SemaphoreType.DMA,
            pltpu.VMEM((2, 2, depth, 2 * widths[0]), BF),
            pltpu.VMEM((padded, dim), BF),
            pltpu.SemaphoreType.DMA((count, 9)),
            pltpu.SemaphoreType.DMA((count, 9)),
            pltpu.SemaphoreType.DMA((count,)),
            pltpu.SemaphoreType.DMA((3,)),
            pltpu.SemaphoreType.DMA((3,)),
            pltpu.SemaphoreType.DMA((PERM,)),
            pltpu.SemaphoreType.DMA((PERM,)),
            pltpu.SemaphoreType.DMA((PERM,)),
        ]
        + line_scratch(ctx_size, rows, PERM, dim // 2 // PERM),
        compiler_params=pltpu.CompilerParams(
            collective_id=0, has_side_effects=True, vmem_limit_bytes=VMEM_LIMIT
        ),
        cost_estimate=pl.CostEstimate(flops=10000000000, bytes_accessed=100000000, transcendentals=0),
    )(*thirds, *pieces, small, tokens, cotangent, dealt[None, :], seg_col, segments_by_tile(seg_row, own))
    whole = [full.reshape(4 * depth, full.shape[3]) for full in result[:count]]
    logsum = result[count + 4].transpose(1, 0, 2).reshape(16, own)
    return whole, result[count], result[count + 1], result[count + 2], result[count + 3], logsum


def add_lines(dst, first, second):
    rows = dst.shape[0]
    step = 48 if rows % 48 == 0 else 16

    def body(i, carry):
        lines = pl.ds(pl.multiple_of(i * step, 16), step)
        dst[lines, :] = (first[lines, :].astype(F32) + second[lines, :].astype(F32)).astype(dst.dtype)
        return carry

    lax.fori_loop(0, rows // step, body, 0)


RING = 4


class Reduction:
    STAGES = 7

    def __init__(self, chunks, outs, refs):
        number = len(chunks)
        self.chunks, self.outs = chunks, outs
        ring = min(RING, number)
        self.full = [refs[k % ring] for k in range(number)]
        refs = refs[ring:]
        self.by_core, self.by_x, self.plane, self.from_end, self.half_z, self.final = (
            refs[i * number : (i + 1) * number] for i in range(6)
        )
        self.send, self.recv = refs[6 * number :]
        self.place = here()
        z = self.place[3]
        self.inner, self.outer = (z == 1) | (z == 2), (z == 0) | (z == 3)
        self.near, self.end, self.middle = 1 + z // 3, jnp.maximum(3 * (z - 1), 0) % 6, 3 - z
        self.rows = self.full[0].shape[3]

    def copy(self, k, stage):
        x, c, y, z = self.place
        half = self.rows // 2
        side = z // 2
        if stage == 0:
            src, dst, where = self.full[k].at[:, :, 1 - c], self.by_core[k], {"shard": 2 * x + 1 - c}
        elif stage == 1:
            src, dst, where = self.by_core[k].at[:, 1 - x], self.by_x[k], {"shard": 2 * (1 - x) + c}
        elif stage == 2:
            src, dst, where = self.by_x[k].at[1 - y], self.plane[k], {"tp": 1 - y}
        elif stage == 3:
            src, dst, where = self.plane[k], self.from_end[k], {"ctx": self.near}
        elif stage == 4:
            src = self.plane[k].at[pl.ds(pl.multiple_of((1 - side) * half, 16), half)]
            dst, where = self.half_z[k], {"ctx": self.middle}
        elif stage == 5:
            src = dst = self.final[k].at[pl.ds(pl.multiple_of(side * half, 16), half)]
            where = {"ctx": self.middle}
        else:
            src = dst = self.final[k]
            where = {"ctx": self.end}
        return remote(src, dst, self.send.at[k, stage], self.recv.at[k, stage], where)

    def sender(self, stage):
        return None if stage < 3 else (self.outer if stage == 3 else self.inner)

    def receiver(self, stage):
        return None if stage < 3 else (self.outer if stage == 6 else self.inner)

    def guarded(self, condition, action):
        if condition is None:
            action()
        else:
            pl.when(condition)(action)

    def start(self, k, stage):
        self.guarded(self.sender(stage), lambda: self.copy(k, stage).start())

    def absorb(self, k, stage):
        x, c, y, z = self.place
        half = self.rows // 2
        side = z // 2
        self.copy(k, stage).wait_recv()
        if stage == 0:
            for of_y in range(2):
                for of_x in range(2):
                    there = self.by_core[k].at[of_y, of_x]
                    add_lines(there, there, self.full[k].at[of_y, of_x, c])
            self.copy(k, 0).wait_send()
        elif stage == 1:
            for i in range(2):
                add_lines(self.by_x[k].at[i], self.by_x[k].at[i], self.by_core[k].at[i, x])
        elif stage == 2:
            add_lines(self.plane[k], self.plane[k], self.by_x[k].at[y])
        elif stage == 3:
            add_lines(self.plane[k], self.plane[k], self.from_end[k])
        elif stage == 4:
            lines = pl.ds(pl.multiple_of(side * half, 16), half)
            add_lines(self.final[k].at[lines], self.half_z[k], self.plane[k].at[lines])

    def task(self, k, produce):
        produce(k)
        for stage in range(self.STAGES):
            self.start(k, stage)
            yield
            self.guarded(self.receiver(stage), lambda: self.absorb(k, stage))
        a, first, width = self.chunks[k]
        self.outs[a][:, first : first + width] = self.final[k][...].astype(F32)

    def settle(self):
        for k in range(len(self.chunks)):
            for stage in range(1, self.STAGES):
                self.guarded(self.sender(stage), lambda: self.copy(k, stage).wait_send())

    def product(self, k, turned, other):
        for of_y in range(2):
            right = other(of_y)
            for i in range(4):
                value = matmul(turned[i * self.rows : (i + 1) * self.rows, :], right)
                self.full[k][of_y, i // 2, i % 2] = value.astype(BF)


def reduction_scratch(rows, chunks):
    shapes = [
        lambda w: (2, 2, rows, w),
        lambda w: (2, rows, w),
        lambda w: (rows, w),
        lambda w: (rows, w),
        lambda w: (rows // 2, w),
        lambda w: (rows, w),
    ]
    scratch = [pltpu.VMEM((2, 2, 2, rows, CHUNK), BF) for _ in range(min(RING, len(chunks)))]
    scratch += [pltpu.VMEM(shape(width), BF) for shape in shapes for _, _, width in chunks]
    return scratch + [pltpu.SemaphoreType.DMA((len(chunks), 7)), pltpu.SemaphoreType.DMA((len(chunks), 7))]


def wide_peers():
    x, c, y, z = here()
    return (
        {"shard": 2 * x + 1 - c},
        {"shard": 2 * (1 - x) + c},
        {"tp": 1 - y},
        {"ctx": z + 1 - 2 * (z % 2)},
    )


CHUNK = 384


def chunks_of(widths):
    return tuple((a, first, CHUNK) for a, width in enumerate(widths) for first in range(0, width, CHUNK))


def slots_task(line, j, y, values, out, pre, post_sem, at_y):
    slots = line.slots
    own = slots // 2
    outgoing, pre_send, pre_recv = pre
    post_send, post_recv = post_sem
    width = line.picked.shape[1]
    mine_rows = pl.ds(pl.multiple_of(half_of(y, line.z) * own, 64), own)
    half = out.shape[1] // 2
    outgoing[...] = values(j, 1 - y)
    before = remote(outgoing, line.blocks.at[line.z, mine_rows], pre_send, pre_recv, at_y)
    before.start()
    line.blocks[line.z, mine_rows, :] = values(j, y)
    yield
    before.wait_recv()
    yield from line.run()
    cols = pl.ds(pl.multiple_of(y * half + j * width, 128), width)
    after = remote(line.picked, out.at[:, cols], post_send, post_recv, at_y)
    after.start()
    out[:, cols] = line.picked[...]
    yield
    after.wait_recv()
    before.wait_send()
    after.wait_send()
    line.settle()


LAYER_AT = (2, 5, 8)
LAYER_GAPS = (1, 1, 1, 1, 1, 1)
AHEAD = 2
X_FIRST = 3
LATER_GAPS = (1, 1, 1, 0, 1)


def chunk_round(k):
    return k // AHEAD


def chunk_gaps(k):
    return (0, max(0, X_FIRST + 5 * k // 4 - chunk_round(k) - 2)) + LATER_GAPS


def backward_kernel(chunks, *refs):
    first_low, attended, hidden_low, pre_low, second_low, act_low, grad, stats, stats_tile, qkv_in, seg_col, seg_row, seg_tile, layer_low, dealt_row = refs[:15]
    outs, qkv_low, query_sums, value_sums, layer_out = refs[15:18], refs[18], refs[19], refs[20], refs[21]
    rest = refs[22:]
    turned, grad_win, stats_side, stats_win, halo_sem = rest[0:3], rest[3], rest[4], rest[5], rest[6]
    key_t, first_st, second_st, bias_query, bias_key, acc, first_acc, second_acc = rest[7:15]
    stream, stream_sem, qkv, qkv_sem = rest[15:19]
    outgoing, rest = rest[19 : 19 + PERM], rest[19 + PERM :]
    qkv_copy = pltpu.make_async_copy(qkv_in, qkv, qkv_sem)
    qkv_copy.start()
    pre_send, pre_recv, post_send, post_recv = rest[:4]
    line_number = 4 * PERM + 3
    line_refs, reduction_refs = rest[4 : 4 + line_number], rest[4 + line_number :]
    reduction = Reduction(chunks, outs, reduction_refs)
    x, c, y, z = reduction.place
    h = half_of(y, z)
    own, dim = grad.shape
    padded = qkv.shape[0]
    tile = attention_tile(own)
    last = 3
    at_y, at_z = {"tp": 1 - y}, {"ctx": jnp.clip(z - 1 + 2 * h, 0, last)}
    has_z = ((h == 0) & (z > 0)) | ((h == 1) & (z < last))
    greet_all(wide_peers(), ((reduction.inner, {"ctx": 3 - z}),))

    def halos(where, same):
        first = (1 - h) if same else h
        side = h if same else 1 - h
        base = 0 if same else 4
        return (
            remote(
                grad.at[pl.ds(pl.multiple_of(first * (own - HALO), 64), HALO)],
                grad_win.at[pl.ds(pl.multiple_of(side * (HALO + own), 64), HALO)],
                halo_sem.at[base],
                halo_sem.at[base + 1],
                where,
            ),
            remote(stats, stats_side.at[side], halo_sem.at[base + 2], halo_sem.at[base + 3], where),
        )

    for item in halos(at_y, True):
        item.start()

    @pl.when(has_z)
    def _():
        for item in halos(at_z, False):
            item.start()

    grad_win[HALO : HALO + own, :] = grad[...]
    grad_win[2 * HALO + own :, :] = jnp.zeros((padded - 2 * HALO - own, dim), BF)
    for missing, side in (((h == 0) & (z == 0), 0), ((h == 1) & (z == last), 1)):

        @pl.when(missing)
        def _():
            grad_win[side * (HALO + own) : side * (HALO + own) + HALO, :] = jnp.zeros((HALO, dim), BF)
            stats_side[side] = jnp.zeros(stats.shape, F32)

    lefts, rights = (first_low, hidden_low, second_low), (attended, pre_low, act_low)

    def bring(k, of_y):
        a, first, columns = chunks[k]
        half = rights[a].shape[1] // 2
        return pltpu.make_async_copy(
            rights[a].at[:, of_y * half + first : of_y * half + first + columns],
            stream.at[k % 2, of_y],
            stream_sem.at[k % 2, of_y],
        )

    for k in range(min(2, len(chunks))):
        for of_y in range(2):
            bring(k, of_y).start()

    def produce(k):
        a, first, _ = chunks[k]
        if first == 0:
            turned[a][...] = lefts[a][...].T
        for of_y in range(2):
            bring(k, of_y).wait()
        reduction.product(k, turned[a], lambda of_y: stream[k % 2, of_y])
        if k + 2 < len(chunks):
            for of_y in range(2):
                bring(k + 2, of_y).start()

    lines = [line_of(j, PERM, z, dealt_row, True, line_refs) for j in range(PERM)]
    width = dim // 2 // PERM

    def layer_values(j, half):
        return layer_low[:, pl.ds(pl.multiple_of(half * (dim // 2) + j * width, 128), width)]

    def store(rows, p, part):
        at_query = places(p, dim)[0]
        qkv_low[rows, at_query : at_query + 128] = part

    def attention_task():
        yield
        qkv_copy.wait()
        yield from run_static(
            query_steps(
                dim, tile, qkv, seg_col, seg_tile, grad, stats_tile, store, query_sums, key_t, first_st, second_st, bias_query, acc
            ),
            tile,
            own // tile,
        )
        for item in halos(at_y, True):
            item.wait()

        @pl.when(has_z)
        def _():
            for item in halos(at_z, False):
                item.wait()

        stats_win[...] = jnp.concatenate(
            [
                stats_side[0][:, own - HALO :],
                stats[...],
                stats_side[1][:, :HALO],
                jnp.zeros((stats.shape[0], padded - 2 * HALO - own), F32),
            ],
            axis=1,
        )
        yield from run_static(
            key_steps(
                dim,
                tile,
                qkv,
                seg_col,
                seg_row,
                grad_win,
                stats_win,
                qkv_low,
                value_sums,
                first_st,
                second_st,
                bias_key,
                first_acc,
                second_acc,
            ),
            tile,
            own // tile,
        )

    tasks = [(chunk_round(k), timed(reduction.task(k, produce), chunk_gaps(k))) for k in range(len(chunks))]
    tasks += [
        (
            LAYER_AT[j],
            timed(
                slots_task(
                lines[j],
                j,
                y,
                layer_values,
                layer_out,
                (outgoing[j], pre_send.at[j], pre_recv.at[j]),
                (post_send.at[j], post_recv.at[j]),
                at_y,
            ), LAYER_GAPS),
        )
        for j in range(PERM)
    ]
    interleave(sorted([(0, attention_task())] + tasks, key=lambda item: item[0]))
    reduction.settle()


def backward_stage(first_low, attended, hidden_low, pre_low, second_low, act_low, grad, stats, qkv, seg_col, seg_row, layer_low, dealt):
    own, dim = grad.shape
    padded = qkv.shape[0]
    rows = dim // 4
    tile = attention_tile(own)
    pairs = dim // 128
    widths = (attended.shape[1] // 2, pre_low.shape[1] // 2, act_low.shape[1] // 2)
    chunks = chunks_of(widths)
    spec = pl.BlockSpec(memory_space=pltpu.VMEM)
    outs = [jax.ShapeDtypeStruct((rows, width), F32) for width in widths]
    outs += [
        jax.ShapeDtypeStruct((own, 3 * dim), BF),
        jax.ShapeDtypeStruct((1, dim), F32),
        jax.ShapeDtypeStruct((1, dim), F32),
        jax.ShapeDtypeStruct((2 * own, dim), BF),
    ]
    scratch = [pltpu.VMEM((dim, own), BF) for _ in range(3)]
    scratch += [
        pltpu.VMEM((padded, dim), BF),
        pltpu.VMEM((2, 32, own), F32),
        pltpu.VMEM((32, padded), F32),
        pltpu.SemaphoreType.DMA((8,)),
        pltpu.VMEM((dim, padded), BF),
        pltpu.VMEM((pairs, 2 * tile, 128), BF),
        pltpu.VMEM((pairs, 2 * tile, 128), BF),
        pltpu.VMEM((BLOCK, 2 * tile), F32),
        pltpu.VMEM((tile, BLOCK), F32),
        pltpu.VMEM((pairs, 128, 2 * tile), F32),
        pltpu.VMEM((pairs, 2 * tile, 128), F32),
        pltpu.VMEM((pairs, 2 * tile, 128), F32),
    ]
    scratch += [pltpu.VMEM((2, 2, own, CHUNK), BF), pltpu.SemaphoreType.DMA((2, 2))]
    scratch += [pltpu.VMEM((padded, 3 * dim), BF), pltpu.SemaphoreType.DMA]
    scratch += [pltpu.VMEM((own, dim // 2 // PERM), BF) for _ in range(PERM)]
    scratch += [pltpu.SemaphoreType.DMA((PERM,)) for _ in range(4)]
    scratch += line_scratch(lax.axis_size("ctx"), 2 * own, PERM, dim // 2 // PERM)
    scratch += reduction_scratch(rows, chunks)
    args = (
        first_low,
        attended,
        hidden_low,
        pre_low,
        second_low,
        act_low,
        grad,
        stats,
        by_tile(stats, own),
        qkv,
        seg_col,
        seg_row,
        segments_by_tile(seg_row, own),
        layer_low,
        dealt[None, :].astype(F32),
    )
    anywhere = pl.BlockSpec(memory_space=pl.ANY)
    return pl.pallas_call(
        functools.partial(backward_kernel, chunks),
        out_shape=outs,
        in_specs=[anywhere if i in (1, 3, 5, 9) else spec for i in range(len(args))],
        out_specs=[spec] * len(outs),
        scratch_shapes=scratch,
        compiler_params=pltpu.CompilerParams(
            collective_id=1, has_side_effects=True, vmem_limit_bytes=VMEM_LIMIT
        ),
        cost_estimate=pl.CostEstimate(flops=50000000000, bytes_accessed=100000000, transcendentals=0),
    )(*args)


def last_kernel(chunks, *refs):
    inputs, qkv_low, weight, grad_first, dealt_row, vector = refs[:6]
    outs, tokens_grad, vector_out = refs[6:9], refs[9], refs[10]
    rest = refs[11:]
    number = PERM
    turned, outgoing, pre_send, pre_recv, post_send, post_recv = (
        rest[0],
        rest[1 : 1 + number],
        rest[1 + number],
        rest[2 + number],
        rest[3 + number],
        rest[4 + number],
    )
    vector_in, vector_sum, vector_send, vector_recv = rest[5 + number : 9 + number]
    rest = rest[9 + number :]
    line_number = 4 * number + 3
    line_refs, reduction_refs = rest[:line_number], rest[line_number:]
    reduction = Reduction(chunks, outs, reduction_refs)
    x, c, y, z = reduction.place
    own, dim = inputs.shape
    at_y = {"tp": 1 - y}
    inner = (z == 1) | (z == 2)
    peers = wide_peers() + ({"ctx": (z + 2) % 4},)
    greet_all(peers, ((inner, {"ctx": 3 - z}),))
    lines = [line_of(j, number, z, dealt_row, True, line_refs) for j in range(number)]
    width = dim // 2 // PERM

    def vector_copy(stage):
        return remote(
            vector_sum.at[stage], vector_in.at[stage], vector_send.at[stage], vector_recv.at[stage], peers[stage]
        )

    def vector_task():
        vector_sum[0] = vector[...]
        for stage in range(5):
            vector_copy(stage).start()
            yield
            vector_copy(stage).wait_recv()
            total = vector_sum[stage] + vector_in[stage]
            if stage < 4:
                vector_sum[stage + 1] = total
            else:
                vector_out[...] = total

    def grad_values(j, half):
        first = pl.ds(pl.multiple_of(half * (dim // 2) + j * width, 128), width)
        return (grad_first[:, first] + matmul_second(qkv_low[...], weight[first, :])).astype(BF)

    def produce(k):
        if k == 0:
            turned[...] = inputs[...].T
        which, first, columns = chunks[k]
        half = qkv_low.shape[1] // 2
        third = half // 3

        def other(of_y):
            start = of_y * half + which * third + first
            return qkv_low[:, start : start + columns]

        reduction.product(k, turned, other)

    def slots(values, j, index, out_ref):
        return slots_task(
            lines[index],
            j,
            y,
            values,
            out_ref,
            (outgoing[index], pre_send.at[index], pre_recv.at[index]),
            (post_send.at[index], post_recv.at[index]),
            at_y,
        )

    tasks = [(j, slots(grad_values, j, j, tokens_grad)) for j in range(PERM)]
    tasks += [(k, reduction.task(k, produce)) for k in range(len(chunks))]
    tasks += [(1, vector_task())]
    interleave(sorted(tasks, key=lambda item: item[0]))
    reduction.settle()
    for stage in range(5):
        vector_copy(stage).wait_send()


def last_stage(inputs, qkv_low, weight, grad_first, dealt, vector):
    own, dim = inputs.shape
    ctx_size = lax.axis_size("ctx")
    rows = dim // 4
    width = qkv_low.shape[1] // 6
    chunks = chunks_of((width,) * 3)
    spec = pl.BlockSpec(memory_space=pltpu.VMEM)
    outs = [
        *[jax.ShapeDtypeStruct((rows, width), F32) for _ in range(3)],
        jax.ShapeDtypeStruct((2 * own, dim), BF),
        jax.ShapeDtypeStruct(vector.shape, F32),
    ]
    scratch = [pltpu.VMEM((dim, own), BF)]
    scratch += [pltpu.VMEM((own, dim // 2 // PERM), BF) for _ in range(PERM)]
    scratch += [pltpu.SemaphoreType.DMA((PERM,)) for _ in range(4)]
    scratch += [pltpu.VMEM((5,) + vector.shape, F32), pltpu.VMEM((5,) + vector.shape, F32)]
    scratch += [pltpu.SemaphoreType.DMA((5,)), pltpu.SemaphoreType.DMA((5,))]
    scratch += line_scratch(ctx_size, 2 * own, PERM, dim // 2 // PERM)
    scratch += reduction_scratch(rows, chunks)
    return pl.pallas_call(
        functools.partial(last_kernel, chunks),
        out_shape=outs,
        in_specs=[spec] * 6,
        out_specs=[spec] * len(outs),
        scratch_shapes=scratch,
        compiler_params=pltpu.CompilerParams(
            collective_id=2, has_side_effects=True, vmem_limit_bytes=VMEM_LIMIT
        ),
        cost_estimate=pl.CostEstimate(flops=10000000000, bytes_accessed=100000000, transcendentals=0),
    )(inputs, qkv_low, weight, grad_first, dealt[None, :].astype(F32), vector)


def project_kernel(dim, x_ref, weight, bias, out):
    step = 256
    third = weight.shape[1] // 3

    def body(i, carry):
        lines = pl.ds(pl.multiple_of(i * step, step), step)
        value = (matmul(x_ref[lines, :], weight[...]) + bias[0]).astype(BF)
        scale = jnp.where(lax.broadcasted_iota(jnp.int32, (1, 3 * third), 1) < third, 0.125, 1.0).astype(BF)
        out[lines, :] = value * scale
        return carry

    lax.fori_loop(0, x_ref.shape[0] // step, body, 0)


def project(x_window, weight, bias):
    rows, dim = x_window.shape
    width = 3 * dim // 2
    return pl.pallas_call(
        functools.partial(project_kernel, dim),
        grid=(2,),
        out_shape=jax.ShapeDtypeStruct((rows, 2 * width), BF),
        in_specs=[
            pl.BlockSpec((rows, dim), lambda i: (0, 0)),
            pl.BlockSpec((dim, width), lambda i: (0, i)),
            pl.BlockSpec((1, 1, width), lambda i: (i, 0, 0)),
        ],
        out_specs=pl.BlockSpec((rows, width), lambda i: (0, i)),
        compiler_params=pltpu.CompilerParams(vmem_limit_bytes=VMEM_LIMIT),
        cost_estimate=pl.CostEstimate(flops=6000000000, bytes_accessed=14000000, transcendentals=0),
    )(x_window, weight, bias)


def rows_to_slots(values, dealt, place_z, place_y):
    own, dim = values.shape
    half = dim // 2
    keep = lax.dynamic_slice_in_dim(values, place_y * half, half, axis=1)
    send = lax.dynamic_slice_in_dim(values, (1 - place_y) * half, half, axis=1)
    other = lax.ppermute(send, "tp", [(0, 1), (1, 0)])
    first = jnp.where(place_y == 0, keep, other)
    second = jnp.where(place_y == 0, other, keep)
    block = jnp.concatenate([first, second], axis=0)
    everything = lax.all_gather(block, "ctx", axis=0, tiled=True)
    slots = 2 * own
    mine = lax.dynamic_slice_in_dim(dealt, place_z * slots, slots)
    picked = jnp.take(everything, mine, axis=0, mode="clip")
    other_columns = lax.ppermute(picked, "tp", [(0, 1), (1, 0)])
    return jnp.concatenate(
        [jnp.where(place_y == 0, picked, other_columns), jnp.where(place_y == 0, other_columns, picked)], axis=1
    )


def slots_to_rows(values, dealt, place_z, place_y):
    slots, dim = values.shape
    half, own = dim // 2, slots // 2
    block = lax.dynamic_slice_in_dim(values, place_y * half, half, axis=1)
    everything = lax.all_gather(block, "ctx", axis=0, tiled=True)
    wanted = place_z * slots + lax.broadcasted_iota(jnp.int32, (slots, 1), 0)
    chosen = (wanted == dealt[None, :]).astype(BF)
    picked = matmul(chosen, everything).astype(BF)
    keep = lax.dynamic_slice_in_dim(picked, place_y * own, own, axis=0)
    send = lax.dynamic_slice_in_dim(picked, (1 - place_y) * own, own, axis=0)
    other = lax.ppermute(send, "tp", [(0, 1), (1, 0)])
    return jnp.concatenate([jnp.where(place_y == 0, keep, other), jnp.where(place_y == 0, other, keep)], axis=1)


def per_device(
    tokens,
    cotangent,
    seq_lengths,
    dealing,
    query_weight,
    query_bias,
    key_weight,
    value_weight,
    value_bias,
    output_weight,
    output_bias,
    first_gain,
    first_shift,
    up_weight,
    up_bias,
    down_weight,
    down_bias,
    second_gain,
    second_shift,
):
    rows, dim = tokens.shape
    ctx_size, tp_size = lax.axis_size("ctx"), lax.axis_size("tp")
    group_rows = rows * ctx_size
    own = rows // tp_size
    place_z, place_y = lax.axis_index("ctx"), lax.axis_index("tp")
    window = HALO + own + HALO
    padded = -(-window // BLOCK) * BLOCK
    dealt = dealing[0]

    lengths = seq_lengths[0]
    number = lengths.shape[0]
    upto = jnp.arange(number)[:, None] >= jnp.arange(number)[None, :]
    ends = jnp.sum(jnp.where(upto, lengths[None, :], 0), axis=1)
    starts = ends - lengths
    special = lax.axis_size("shard") == 4 and tp_size == 2 and ctx_size == 4
    place_h = half_of(place_y, place_z) if special else place_y
    first_row = place_z * rows + place_h * own
    index = jnp.arange(padded, dtype=jnp.int32)
    position = first_row - HALO + index
    valid = (position >= 0) & (position < group_rows) & (index < window)
    segment = jnp.sum((position[:, None] >= ends[None, :-1]).astype(jnp.int32), axis=1)
    segment = jnp.where(valid, segment, -1)
    seg_row, seg_col = segment[None, :], segment[:, None]
    tile = attention_tile(own)
    tile_first = first_row + tile * jnp.arange(own // tile, dtype=jnp.int32)
    tile_last = tile_first + tile - 1
    begin = jnp.max(jnp.where(starts[None, :] <= tile_first[:, None], starts[None, :], 0), axis=1)
    finish = jnp.min(jnp.where(ends[None, :] > tile_last[:, None], ends[None, :], group_rows), axis=1)
    shift = HALO - first_row
    bounds = jnp.stack([(begin + shift) // BLOCK, (finish + shift + BLOCK - 1) // BLOCK], axis=1).astype(jnp.int32)

    half_dim = dim // tp_size
    pieces = [
        query_weight,
        key_weight,
        value_weight,
        output_weight.T,
        up_weight,
        down_weight.T,
    ]
    flat = jnp.concatenate([query_bias, value_bias, up_bias])
    small = jnp.broadcast_to(flat[None, :], (16, flat.shape[0]))
    inputs = lax.dynamic_slice_in_dim(tokens, place_h * own, own, axis=0)
    if special:
        whole, biases, qkv, cot_rows, attended, logsum = first_stage(
            pieces, small, tokens, cotangent, dealt, seg_col, seg_row, padded
        )
        whole_up_bias = biases[::16, dim:].reshape(-1).astype(F32)
    else:
        whole = [
            lax.all_gather(lax.all_gather(piece, "shard", axis=0, tiled=True), "tp", axis=1, tiled=True)
            for piece in (jnp.concatenate(pieces[:3], axis=1), *pieces[3:])
        ]
        biases = lax.all_gather(small, "tp", axis=0, tiled=True)[::16].astype(F32)
        qkv_bias = jnp.concatenate(
            [biases[:, :half_dim], jnp.zeros((tp_size, half_dim), F32), biases[:, half_dim:dim]], axis=1
        )[:, None, :]
        whole_up_bias = biases[:, dim:].reshape(-1)
        edge = jnp.where(place_y == 0, tokens[rows - HALO :], tokens[:HALO])
        hops = [(2 * z, 2 * z + 2) for z in range(ctx_size - 1)] + [(2 * z + 1, 2 * z - 1) for z in range(1, ctx_size)]
        arrived = lax.ppermute(edge, ("ctx", "tp"), hops)
        x_window = jnp.where(
            place_y == 0,
            jnp.concatenate([arrived, tokens[: own + HALO]], axis=0),
            jnp.concatenate([tokens[own - HALO :], arrived], axis=0),
        )
        x_window = jnp.pad(x_window, ((0, padded - window), (0, 0)))
        qkv = project(x_window, whole[0], qkv_bias)
        cot_rows = slots_to_rows(cotangent, dealt, place_z, place_y)
        attended, logsum = attention_forward(qkv, seg_col, seg_row, bounds, own, dim)
    wide_qkv, wide_output, wide_up, wide_down = whole
    output_bias = output_bias.astype(F32)
    first_gain = first_gain.astype(F32)
    first_shift = first_shift.astype(F32)
    down_bias = down_bias.astype(F32)
    second_gain = second_gain.astype(F32)
    second_shift = second_shift.astype(F32)

    grad_out = cot_rows.astype(F32)
    hidden_one, normed_one, inverse_one = norm_forward(
        inputs.astype(F32) + matmul_second(attended, wide_output) + output_bias, first_gain, first_shift
    )
    hidden_low = hidden_one.astype(BF)
    pre_act = matmul(hidden_low, wide_up) + whole_up_bias
    erf_part = 0.5 * (1.0 + jax.scipy.special.erf(pre_act * HALF_ROOT))
    act_low = (pre_act * erf_part).astype(BF)
    layer_value, normed_two, inverse_two = norm_forward(
        hidden_one + matmul_second(act_low, wide_down) + down_bias, second_gain, second_shift
    )
    layer_low = layer_value.astype(BF)

    second_shift_grad = jnp.sum(grad_out, axis=0)
    second_gain_grad = jnp.sum(grad_out * normed_two, axis=0)
    grad_second = norm_backward(grad_out, normed_two, inverse_two, second_gain)
    down_bias_grad = jnp.sum(grad_second, axis=0)
    second_low = grad_second.astype(BF)
    slope = erf_part + pre_act * DENSITY * jnp.exp(-0.5 * pre_act * pre_act)
    grad_pre = matmul(second_low, wide_down) * slope
    up_bias_grad = jnp.sum(grad_pre, axis=0)
    pre_low = grad_pre.astype(BF)
    grad_hidden = grad_second + matmul_second(pre_low, wide_up)
    first_shift_grad = jnp.sum(grad_hidden, axis=0)
    first_gain_grad = jnp.sum(grad_hidden * normed_one, axis=0)
    grad_first = norm_backward(grad_hidden, normed_one, inverse_one, first_gain)
    output_bias_grad = jnp.sum(grad_first, axis=0)
    first_low = grad_first.astype(BF)
    attended_grad = matmul(first_low, wide_output).astype(BF)
    head_of = (jnp.arange(dim)[None, :] // HEAD == jnp.arange(16)[:, None]).astype(F32)
    delta = lax.dot_general(
        head_of,
        attended_grad.astype(F32) * attended.astype(F32),
        (((1,), (1,)), ((), ())),
        precision=lax.Precision.HIGHEST,
        preferred_element_type=F32,
    )
    stats = jnp.concatenate([logsum, delta], axis=0)
    if special:
        output_own, up_own, down_own, qkv_low, query_bias_grad, value_bias_grad, layer_out = backward_stage(
            first_low,
            attended,
            hidden_low,
            pre_low,
            second_low,
            act_low,
            attended_grad,
            stats,
            qkv,
            seg_col,
            seg_row,
            layer_low,
            dealt,
        )
    else:
        layer_out = rows_to_slots(layer_low, dealt, place_z, place_y)
        up_hops = [(i, i + 1) for i in range(ctx_size * tp_size - 1)]
        down_hops = [(i + 1, i) for i in range(ctx_size * tp_size - 1)]
        grad_win, stats_win = [
            jnp.concatenate(
                [
                    lax.ppermute(lax.slice_in_dim(array, own - HALO, own, axis=axis), ("ctx", "tp"), up_hops),
                    array,
                    lax.ppermute(lax.slice_in_dim(array, 0, HALO, axis=axis), ("ctx", "tp"), down_hops),
                    jnp.zeros((padded - window, dim) if axis == 0 else (32, padded - window), array.dtype),
                ],
                axis=axis,
            )
            for array, axis in ((attended_grad, 0), (stats, 1))
        ]
        query_low, query_bias_grad = attention_query(qkv, seg_col, seg_row, bounds, attended_grad, stats, dim)
        qkv_low, value_bias_grad = attention_key(
            qkv, seg_col, seg_row, bounds, grad_win, stats_win, query_low, own, dim
        )
    vectors = jnp.concatenate(
        [
            query_bias_grad[0],
            value_bias_grad[0],
            up_bias_grad,
            output_bias_grad,
            first_gain_grad,
            first_shift_grad,
            down_bias_grad,
            second_gain_grad,
            second_shift_grad,
        ]
    )
    if special:
        *qkv_own, tokens_grad, small_sum = last_stage(
            inputs, qkv_low, wide_qkv, grad_first, dealt, vectors.reshape(-1, 128)
        )
        small_sum = small_sum.reshape(-1)
        owned = [*qkv_own, output_own, up_own, down_own]
    else:
        owned = []
        for full in (
            matmul_first(inputs, qkv_low),
            matmul_first(first_low, attended),
            matmul_first(hidden_low, pre_low),
            matmul_first(second_low, act_low),
        ):
            part = lax.psum_scatter(full.astype(BF), "tp", scatter_dimension=1, tiled=True)
            part = lax.psum_scatter(part, "shard", scatter_dimension=0, tiled=True)
            owned.append(lax.psum(part, "ctx").astype(F32))
        owned = [owned[0][:, i * half_dim : (i + 1) * half_dim] for i in range(3)] + owned[1:]
        small_sum = lax.psum(vectors, ("shard", "ctx", "tp"))
        tokens_grad = (grad_first + matmul_second(qkv_low, wide_qkv)).astype(BF)
        tokens_grad = rows_to_slots(tokens_grad, dealt, place_z, place_y)
    hidden = up_bias_grad.shape[0]
    sizes = [dim, dim, hidden] + [dim] * 6
    offsets = [sum(sizes[:i]) for i in range(len(sizes))]
    parts = [small_sum[o : o + s] for o, s in zip(offsets, sizes)]

    def by_tp(vector):
        part = vector.shape[0] // tp_size
        return lax.dynamic_slice_in_dim(vector, place_y * part, part)

    return (
        layer_out,
        tokens_grad,
        owned[0],
        by_tp(parts[0]),
        owned[1],
        owned[2],
        by_tp(parts[1]),
        owned[3].T,
        parts[3],
        parts[4],
        parts[5],
        owned[4],
        by_tp(parts[2]),
        owned[5].T,
        parts[6],
        parts[7],
        parts[8],
    )


def solution(mesh):
    return jax.shard_map(
        per_device,
        mesh=mesh,
        in_specs=(
            P(("shard", "ctx"), None),
            P(("shard", "ctx"), None),
            P("shard", None),
            P("shard", None),
            P("shard", "tp"),
            P("tp"),
            P("shard", "tp"),
            P("shard", "tp"),
            P("tp"),
            P("tp", "shard"),
            P(),
            P(),
            P(),
            P("shard", "tp"),
            P("tp"),
            P("tp", "shard"),
            P(),
            P(),
            P(),
        ),
        out_specs=(
            P(("shard", "ctx"), None),
            P(("shard", "ctx"), None),
            P("shard", "tp"),
            P("tp"),
            P("shard", "tp"),
            P("shard", "tp"),
            P("tp"),
            P("tp", "shard"),
            P(),
            P(),
            P(),
            P("shard", "tp"),
            P("tp"),
            P("tp", "shard"),
            P(),
            P(),
            P(),
        ),
        check_vma=False,
    )
```
